32 devices in a mesh: runs: 2 (over y), dom: 8 (over z, x), sub: 2 (over core).
Axes of the slice: x: 2, y: 2, z: 4, core: 2. Of those that a mesh axis runs over, the one named last changes fastest.
Arguments:
- displacement: float32 [3, 64, 32, 256], P(None, ('runs', 'dom', 'sub')), parts along dimension 1, may hold values from -6 to 6
- modulus: float32 [64, 32, 256], P(('runs', 'dom', 'sub')), parts along dimension 0, may hold values from 0.3 to 3
- node_mass: float32 [64, 32, 256], P(('runs', 'dom', 'sub')), parts along dimension 0, may hold values from 0.5 to 2
- stiffness: float32 [24, 24], replicated
- face_nodes: int32 [4, 16384], P(None, ('runs', 'dom', 'sub')), parts along dimension 1, may hold values from 0 to 16383
- pair_mortar: int32 [8192], P(('runs', 'dom', 'sub')), parts along dimension 0, may hold values from 0 to 511
- pair_rank: int32 [8192, 1], P(('runs', 'dom', 'sub')), parts along dimension 0, may hold values from 0 to 7; in each aligned block of 256 rows (0 to 255, 256 to 511, ...) at most 64 rows name the same one
- pair_face: int32 [8192], P(('runs', 'dom', 'sub')), parts along dimension 0, may hold values from 0 to 511
- pair_count: int32 [8192], P(('runs', 'dom', 'sub')), parts along dimension 0, may hold values from 4 to 25
- pair_shape: float32 [8, 25, 8192], P(None, None, ('runs', 'dom', 'sub')), parts along dimension 2, may hold values from 0 to 1
- pair_weight: float32 [25, 8192], P(None, ('runs', 'dom', 'sub')), parts along dimension 1, may hold values from 0.05 to 0.5
- pair_gap: float32 [25, 8192], P(None, ('runs', 'dom', 'sub')), parts along dimension 1, may hold values from -4 to 4
- pair_normal: float32 [3, 8192], P(None, ('runs', 'dom', 'sub')), parts along dimension 1, may hold values from -4 to 4
Outputs:
- acceleration: float32 [3, 64, 32, 256], P(None, ('runs', 'dom', 'sub')), parts along dimension 1
The draws below stay inside these ranges and needn't reach their ends.
There are 2 independent parts, one for each index of `runs`. The reference program is written for one: setup_inputs(seed, part) draws one part's arguments, and reference() takes and returns one part's arrays. A program takes and returns all parts, laid end to end along the dimension named above; an argument that names none is the same for every part. Nothing has to cross between parts.
Inputs may be any that keep to these rules, and one draw needn't show every extreme that they name: `pair_rank`: in every partition at most 64 pairs name the same remote partition.
All inputs are finite; a program needn't handle non-finite values.
Results may differ from the reference program's by a relative error of at most 0.00005.
Values sent between devices are 32-bit elements; how exact they have to be, the bound alone decides.
No kernel may reach another device: no remote copies, remote signals or barrier semaphores. Data moves between devices by JAX's collectives and lax.ppermute only.
A program may use at most 64 MiB of HBM per device.

```python
import math
import jax
import jax.numpy as jnp
import numpy as np
from jax import lax

NX = 256
NY = 32
NZ = 2
PAIRS_DEV = 256
QP = 25
FACES_DEV = 512
CAP = 64
NODES_DEV = 16384
NZT = 32
PAIRS = 4096
FACES = 8192
N_DOM = 8
N_SUB = 2


def draw_stiffness(key, part):
    key = jax.random.fold_in(key, 7)
    first_key, second_key = jax.random.split(key)
    coupling = jax.random.normal(first_key, (24, 24), jnp.float32) * 0.06
    diagonal = jax.random.uniform(second_key, (24,), jnp.float32, 1.2, 2.0)
    return (coupling + coupling.T) * 0.5 + jnp.diag(diagonal)


def with_ends(entries, own_key, smallest, top_value):
    longest = entries.shape.index(max(entries.shape))
    spots = []
    for shift in (0, 1):
        where = [jax.random.randint(jax.random.fold_in(own_key, axis), (), 0, length) for axis, length in enumerate(entries.shape)]
        where[longest] = (where[longest] + shift) % entries.shape[longest]
        spots.append(tuple(where))
    return entries.at[spots[0]].set(smallest).at[spots[1]].set(top_value)


def level_of(own_key, extent, cuts, smallest, high):
    loudness, own = 1.0, jax.random.fold_in(own_key, 6)
    for axis_at, parts in cuts:
        draws = jnp.exp(jax.random.uniform(jax.random.fold_in(own, axis_at), (parts,), jnp.float32, smallest / len(cuts), high / len(cuts)))
        loudness = loudness * jnp.repeat(draws, extent[axis_at] // parts).reshape([-1 if axis == axis_at else 1 for axis in range(len(extent))])
    return loudness


def deal_out(key, own, number, rows, count, top, limit, skew):
    sequence = jax.random.permutation(key, count)
    crowded, ordinary = portions_of(count, rows * top, limit, skew, True), portions_of(count, rows * top, limit, skew, False)
    places = jnp.arange(count)

    def named(tallies, rotation):
        used = int((tallies > 0).sum())
        fixed = max(1, used // 4)
        passed = fixed + (places - fixed + rotation * (used - fixed)) % max(1, count - fixed)
        return jnp.zeros((count,), jnp.int32).at[sequence[jnp.where(places < fixed, places, passed)]].set(jnp.asarray(tallies, jnp.int32))

    tallies = jnp.where(number % 4 == 0, named(crowded, number // 4), named(ordinary, number - number // 4 - 1))
    mixed = jax.random.permutation(jax.random.fold_in(own, 3), count)
    giver, sink = mixed[0:count // 2 * 2:2], mixed[1:count // 2 * 2:2]
    room = jnp.minimum(tallies[giver] - 1, limit - tallies[sink]) // 2
    room = jnp.where((giver == sequence[0]) | (sink == sequence[0]) | (tallies[sink] == 0), 0, jnp.maximum(room, 0))
    passed = jax.random.randint(jax.random.fold_in(own, 4), (count // 2,), 0, 1 << 20) % (room + 1)
    tallies = tallies.at[giver].add(-passed).at[sink].add(passed)
    members = jnp.searchsorted(jnp.cumsum(tallies), jnp.arange(rows * top), side="right").astype(jnp.int32)
    grid = members.reshape(top, rows).T
    grid = grid[jax.random.permutation(jax.random.fold_in(own, 1), rows)]
    rotation = jax.random.randint(jax.random.fold_in(own, 2), (rows, 1), 0, top)
    return jnp.take_along_axis(grid, (jnp.arange(top)[None, :] + rotation) % top, axis=1)


def portions_of(count, total, bound, slope, full):
    portions = [(1 << 20) // math.isqrt(standing ** slope) + 1 for standing in range(1, count + 1)]
    largest = bound if full else min(bound, max(-(-total // count), total * portions[0] // sum(portions)))
    least = 1 if total - largest >= count - 1 else 0
    given, surplus = [largest] + [least] * (count - 1), total - largest - least * (count - 1)
    while surplus > 0:
        candidates = [i for i in range(1, count) if given[i] < largest] or [i for i in range(1, count) if given[i] < bound]
        mass, budget = sum([portions[i] for i in candidates]), surplus
        for i in candidates:
            extra = min(bound - given[i], max(1, budget * portions[i] // mass), surplus)
            given[i] = given[i] + extra
            surplus = surplus - extra
    return np.array(given)


def centred(own_key, dims, spread, bound, cuts=(), kind=jnp.bfloat16):
    factor_of = level_of(own_key, dims, cuts, -0.22, 0.18) if cuts else 1.0
    entries = jax.random.normal(own_key, dims, jnp.float32) * spread * factor_of
    return jnp.minimum(jnp.maximum(entries, -bound), bound).astype(kind)


def setup_inputs(seed: int = 0, part: int = 0) -> dict:
    key_list = jax.random.split(jax.random.key(seed), 14)
    own_keys = jax.random.split(jax.random.fold_in(key_list[13], part), 14)
    displacement = centred(own_keys[0], (3, NZT, NY, NX), 1.0, 6.0, ((1, 16),), jnp.float32)
    modulus = jnp.clip(jnp.exp(math.log(3.0) - 2.3025851 * jax.random.uniform(own_keys[1], (NZT, NY, NX), jnp.float32) ** level_of(own_keys[1], (NZT, NY, NX), ((0, 16),), -0.2, 0.2)), 0.3, 3.0)
    node_mass = jnp.clip(jnp.exp(math.log(2.0) - 1.3862944 * jax.random.uniform(own_keys[2], (NZT, NY, NX), jnp.float32) ** level_of(own_keys[2], (NZT, NY, NX), ((0, 16),), -0.2, 0.2)), 0.5, 2.0)
    stiffness = draw_stiffness(jax.random.fold_in(key_list[13], 71), part)
    face_nodes = with_ends(jax.random.randint(own_keys[4], (4, FACES), 0, NODES_DEV), jax.random.fold_in(own_keys[4], 1), 0, NODES_DEV - 1).astype(jnp.int32)
    pair_mortar = with_ends(jax.random.randint(own_keys[5], (PAIRS,), 0, FACES_DEV), jax.random.fold_in(own_keys[5], 1), 0, FACES_DEV - 1).astype(jnp.int32)
    pair_rank_keys = jax.random.split(jax.random.fold_in(own_keys[6], 1), PAIRS // PAIRS_DEV)
    pair_rank_turns = jax.random.permutation(jax.random.fold_in(own_keys[6], 3), PAIRS // PAIRS_DEV)
    pair_rank = jax.vmap(lambda own, number: deal_out(jax.random.fold_in(own_keys[6], 2), own, number, PAIRS_DEV, N_DOM, 1, CAP, 2))(pair_rank_keys, pair_rank_turns).reshape((PAIRS, 1))
    pair_face = with_ends(jax.random.randint(own_keys[7], (PAIRS,), 0, FACES_DEV), jax.random.fold_in(own_keys[7], 1), 0, FACES_DEV - 1).astype(jnp.int32)
    pair_count = with_ends(jax.random.randint(own_keys[8], (PAIRS,), 4, QP + 1), jax.random.fold_in(own_keys[8], 1), 4, QP).astype(jnp.int32)
    pair_shape = jnp.clip(1.0 * jax.random.uniform(own_keys[9], (8, QP, PAIRS), jnp.float32) ** level_of(own_keys[9], (8, QP, PAIRS), ((2, 16),), -0.2, 0.2), 0.0, 1.0)
    pair_weight = jnp.clip(jnp.exp(math.log(0.5) - 2.3025851 * jax.random.uniform(own_keys[10], (QP, PAIRS), jnp.float32) ** level_of(own_keys[10], (QP, PAIRS), ((1, 16),), -0.2, 0.2)), 0.05, 0.5)
    pair_gap = centred(own_keys[11], (QP, PAIRS), 0.7, 4.0, ((1, 16),), jnp.float32)
    pair_normal = centred(own_keys[12], (3, PAIRS), 0.8, 4.0, ((1, 16),), jnp.float32)
    return dict(displacement=displacement, modulus=modulus, node_mass=node_mass, stiffness=stiffness, face_nodes=face_nodes, pair_mortar=pair_mortar, pair_rank=pair_rank, pair_face=pair_face, pair_count=pair_count, pair_shape=pair_shape, pair_weight=pair_weight, pair_gap=pair_gap, pair_normal=pair_normal)


def element_forces(extended, modulus, stiffness):
    layers = extended.shape[1] - 1
    rows_y = extended.shape[2]
    cols_x = extended.shape[3]
    mask_y = lax.broadcasted_iota(jnp.int32, (rows_y, cols_x), 0) < rows_y - 1
    mask_x = lax.broadcasted_iota(jnp.int32, (rows_y, cols_x), 1) < cols_x - 1
    elastic = modulus * (mask_y & mask_x).astype(jnp.float32)[None]
    corners = []
    for component in range(3):
        for corner in range(8):
            offset_z, offset_y, offset_x = corner // 4, (corner // 2) % 2, corner % 2
            layer_part = extended[component, offset_z:offset_z + layers]
            corners.append(jnp.roll(layer_part, (-offset_y, -offset_x), axis=(1, 2)))
    stacked = jnp.stack(corners)
    elem_force = jnp.einsum("ij,jzyx->izyx", stiffness, stacked, precision=lax.Precision.HIGHEST) * elastic[None]
    nodal_force = jnp.zeros((3, layers + 1, rows_y, cols_x), jnp.float32)
    for component in range(3):
        for corner in range(8):
            offset_z, offset_y, offset_x = corner // 4, (corner // 2) % 2, corner % 2
            moved = jnp.roll(elem_force[component * 8 + corner], (offset_y, offset_x), axis=(1, 2))
            nodal_force = nodal_force.at[component, offset_z:offset_z + layers].add(-moved)
    return nodal_force


def penalty(mortar_rows, remote_rows, pair_count, pair_shape, pair_weight, pair_gap, pair_normal):
    points, pair_total = pair_weight.shape
    remote_shape = pair_shape[:4]
    mortar_shape = pair_shape[4:]
    remote_points = jnp.sum(remote_rows.reshape(3, 4, 1, pair_total) * remote_shape[None], axis=1)
    mortar_points = jnp.sum(mortar_rows.reshape(3, 4, 1, pair_total) * mortar_shape[None], axis=1)
    gap_value = pair_gap + jnp.sum(pair_normal[:, None, :] * (remote_points - mortar_points), axis=0)
    live_mask = lax.broadcasted_iota(jnp.int32, (points, pair_total), 0) < pair_count[None, :]
    pressure = jnp.where(live_mask, pair_weight * jnp.maximum(-gap_value, 0.0), 0.0)
    remote_load = jnp.sum(pressure[None] * remote_shape, axis=1)
    mortar_load = jnp.sum(pressure[None] * mortar_shape, axis=1)
    remote_force = (pair_normal[:, None, :] * remote_load[None]).reshape(12, pair_total)
    mortar_force = -(pair_normal[:, None, :] * mortar_load[None]).reshape(12, pair_total)
    return mortar_force, remote_force


def reference(displacement, modulus, node_mass, stiffness, face_nodes, pair_mortar, pair_rank, pair_face, pair_count, pair_shape, pair_weight, pair_gap, pair_normal):
    slab_count = N_DOM * N_SUB
    blocks = displacement.reshape(3, slab_count, NZ, NY, NX).transpose(1, 0, 2, 3, 4)
    following = jnp.concatenate([blocks[1:, :, :1], jnp.zeros((1, 3, 1, NY, NX), jnp.float32)], axis=0)
    extended = jnp.concatenate([blocks, following], axis=2)
    modulus_blocks = modulus.reshape(slab_count, NZ, NY, NX)

    def slab_forces(operands):
        return element_forces(operands[0], operands[1], stiffness)

    nodal_force = lax.map(slab_forces, (extended, modulus_blocks))
    carried = jnp.concatenate([jnp.zeros((1, 3, 1, NY, NX), jnp.float32), nodal_force[:-1, :, NZ:]], axis=0)
    owned_part = nodal_force[:, :, :NZ].at[:, :, :1].add(carried)
    internal = owned_part.transpose(1, 0, 2, 3, 4).reshape(3, NZT, NY, NX)

    flat_disp = displacement.reshape(3, -1)
    device_face = jnp.arange(FACES, dtype=jnp.int32) // FACES_DEV
    global_nodes = device_face[None, :] * NODES_DEV + face_nodes
    face_rows = flat_disp[:, global_nodes].reshape(12, FACES)
    owner_device = jnp.arange(PAIRS, dtype=jnp.int32) // PAIRS_DEV
    mortar_face = owner_device * FACES_DEV + pair_mortar
    remote_face = (pair_rank[:, 0] * N_SUB + owner_device % N_SUB) * FACES_DEV + pair_face
    mortar_force, remote_force = penalty(face_rows[:, mortar_face], face_rows[:, remote_face], pair_count, pair_shape, pair_weight, pair_gap, pair_normal)
    face_force = jnp.zeros((12, FACES), jnp.float32).at[:, mortar_face].add(mortar_force).at[:, remote_face].add(remote_force)
    contact = jnp.zeros(flat_disp.shape, jnp.float32).at[:, global_nodes.reshape(-1)].add(face_force.reshape(3, -1))
    return (internal + contact.reshape(internal.shape)) / node_mass[None]
```

```python
import jax
import jax.numpy as jnp
from jax import lax
from jax.experimental import pallas as pl
from jax.experimental.pallas import tpu as pltpu
from jax.sharding import PartitionSpec as P

F32 = jnp.float32
BF16 = jnp.bfloat16
LANES = 128
WORDS = 8


def passed_along(block, axis, distance):
    devices = range(lax.axis_size(axis))
    route = [(i - distance, i) for i in devices if i - distance in devices]
    return lax.ppermute(block, axis, route)


def thirds(x):
    high = x.astype(BF16)
    rest = x - high.astype(F32)
    middle = rest.astype(BF16)
    low = (rest - middle.astype(F32)).astype(BF16)
    return jnp.concatenate([high, middle, low], axis=0)


def summed(stacked):
    rows = stacked.shape[0] // 3
    return (stacked[:rows] + stacked[rows : 2 * rows]) + stacked[2 * rows :]


def marks(index, count):
    rows = lax.broadcasted_iota(jnp.int32, (count, index.shape[1]), 0)
    return (rows == index).astype(F32).astype(BF16)


def times(left, right):
    return jnp.dot(left, right, preferred_element_type=F32)


def times_turned(left, right):
    return lax.dot_general(left, right, (((1,), (1,)), ((), ())), preferred_element_type=F32)


def halves(power):
    return power.bit_length() - 1


def face_rows_kernel(disp_ref, nodes_ref, rows_ref):
    components, layers, rows_y, cols_x = disp_ref.shape
    strips = layers * rows_y
    parts = thirds(disp_ref[...].reshape(components * strips, cols_x))
    face_count = nodes_ref.shape[1]
    folds = face_count // cols_x
    for corner in range(4):
        index = nodes_ref[corner : corner + 1, :]
        along_x = marks(index & (cols_x - 1), cols_x)
        strip = index >> halves(cols_x)
        found = summed(times(parts, along_x)).reshape(components, strips, face_count)
        numbers = lax.broadcasted_iota(jnp.int32, (strips, face_count), 0)
        values = jnp.sum(jnp.where((numbers == strip)[None], found, 0.0), axis=1)
        for fold in range(folds):
            for k in range(components):
                at = fold * 12 + k * 4 + corner
                rows_ref[at : at + 1, :] = values[k : k + 1, fold * cols_x : (fold + 1) * cols_x]


def looked_up(table, face, width):
    at = marks(face & (width - 1), width)
    both = summed(times(thirds(table), at))
    return jnp.where(face < width, both[:12], both[12:])


def pairs_kernel(
    all_ref, own_ref, mortar_ref, rank_ref, face_ref, count_ref, shape_ref, weight_ref, gap_ref,
    normal_ref, sent_ref, kept_ref,
):
    domains, folded, width = all_ref.shape
    pair_total = mortar_ref.shape[1]
    mortar, rank, face = mortar_ref[...], rank_ref[...], face_ref[...]
    mortar_rows = looked_up(own_ref[...], mortar, width)

    at = marks(face & (width - 1), width)
    step = min(domains, 8)

    def add_step(turn, total):
        block = all_ref[pl.ds(turn * step, step)].reshape(step * folded, width)
        found = summed(times(thirds(block), at)).reshape(step, folded, pair_total)
        for i in range(step):
            total = total + jnp.where(rank == turn * step + i, found[i], 0.0)
        return total

    both = jnp.zeros((folded, pair_total), F32)
    if domains == step:
        both = add_step(0, both)
    else:
        both = lax.fori_loop(0, domains // step, add_step, both)
    remote_rows = jnp.where(face < width, both[:12], both[12:])

    normal = normal_ref[...]
    gap = gap_ref[...]
    points = gap.shape[0]
    for node in range(4):
        across = sum(normal[k : k + 1] * remote_rows[k * 4 + node : k * 4 + node + 1] for k in range(3))
        gap = gap + shape_ref[node] * across
        across = sum(normal[k : k + 1] * mortar_rows[k * 4 + node : k * 4 + node + 1] for k in range(3))
        gap = gap - shape_ref[4 + node] * across
    live = lax.broadcasted_iota(jnp.int32, (points, pair_total), 0) < count_ref[...]
    pressure = jnp.where(live, weight_ref[...] * jnp.maximum(-gap, 0.0), 0.0)
    loads = [jnp.sum(pressure * shape_ref[i], axis=0, keepdims=True) for i in range(8)]

    ranks = lax.broadcasted_iota(jnp.int32, (domains, pair_total), 0)
    chosen = ranks == rank
    before = lax.broadcasted_iota(jnp.int32, (pair_total, pair_total), 0) < lax.broadcasted_iota(
        jnp.int32, (pair_total, pair_total), 1
    )
    earlier = times(chosen.astype(F32).astype(BF16), before.astype(F32).astype(BF16))
    slot = jnp.sum(jnp.where(chosen, earlier, 0.0), axis=0, keepdims=True).astype(jnp.int32)
    place = marks(slot, LANES)

    words = jnp.concatenate([normal] + loads[:4] + [face.astype(F32)], axis=0)
    parts = thirds(words).astype(F32)

    def send_step(turn):
        picked = [jnp.where(rank == turn * step + i, parts, 0.0) for i in range(step)]
        stacked = jnp.concatenate(picked, axis=0).astype(BF16)
        placed = times_turned(stacked, place).reshape(step, 3, WORDS, LANES)
        sent_ref[pl.ds(turn * step, step)] = (placed[:, 0] + placed[:, 1]) + placed[:, 2]

    if domains == step:
        send_step(0)
    else:
        pl.loop(0, domains // step)(send_step)
    kept_ref[...] = jnp.concatenate([-normal] + loads[4:] + [mortar.astype(F32)], axis=0)


def face_forces(words, face_count):
    loads = words[3:7]
    forces = jnp.concatenate([words[k : k + 1] * loads for k in range(3)], axis=0)
    at = marks(words[7:8].astype(jnp.int32), face_count)
    return summed(times_turned(thirds(forces), at))


def mortar_kernel(kept_ref, faces_ref):
    faces_ref[...] = face_forces(kept_ref[...], faces_ref.shape[1])


def nodes_kernel(capacity, got_ref, faces_ref, nodes_ref, internal_ref, mass_ref, out_ref):
    domains = got_ref.shape[0]
    components, layers, rows_y, cols_x = out_ref.shape
    strips = layers * rows_y
    face_count = faces_ref.shape[1]
    group = LANES // capacity
    tiles = []
    for start in range(0, domains, group):
        tile = got_ref[start]
        for i in range(1, group):
            tile = tile + pltpu.roll(got_ref[start + i], i * capacity, 1)
        tiles.append(tile)
    words = jnp.concatenate(tiles, axis=1)
    forces = faces_ref[...] + face_forces(words, face_count)
    total = jnp.zeros((3 * components * strips, cols_x), F32)
    parts = thirds(forces).astype(F32)
    numbers = lax.broadcasted_iota(jnp.int32, (strips, face_count), 0)
    for corner in range(4):
        index = nodes_ref[corner : corner + 1, :]
        along_x = marks(index & (cols_x - 1), cols_x)
        strip = numbers == (index >> halves(cols_x))
        spread = []
        for part in range(3):
            for k in range(components):
                at = part * 12 + k * 4 + corner
                spread.append(jnp.where(strip, parts[at : at + 1], 0.0).astype(BF16))
        total = total + times_turned(jnp.concatenate(spread, axis=0), along_x)
    contact = summed(total).reshape(components, layers, rows_y, cols_x)
    out_ref[...] = (internal_ref[...] + contact) / mass_ref[...][None]


def internal_kernel(disp_ref, above_ref, below_ref, modulus_ref, stiffness_ref, out_ref):
    components, layers, rows_y, cols_x = disp_ref.shape
    group = 8
    dofs = 8 * components
    half = dofs // 2

    row = lax.broadcasted_iota(jnp.int32, (dofs * group, dofs), 0) >> halves(group)
    upper = (row >= half).astype(jnp.int32)
    inner = row - half * upper
    dof = (inner >> 2) * 8 + upper * 4 + (inner & 3)
    pick = (dof == lax.broadcasted_iota(jnp.int32, (dofs * group, dofs), 1)).astype(F32)
    tall = jnp.dot(pick, stiffness_ref[...], precision=lax.Precision.HIGHEST)
    wide = lax.dot_general(
        tall, pick, (((1,), (1,)), ((), ())), precision=lax.Precision.HIGHEST,
        preferred_element_type=F32,
    )
    size = dofs * group
    diagonal = (lax.broadcasted_iota(jnp.int32, (size, size), 0) & (group - 1)) == (
        lax.broadcasted_iota(jnp.int32, (size, size), 1) & (group - 1)
    )
    blocks = jnp.where(diagonal, wide, 0.0)

    def shifted(layer):
        views = []
        for k in range(components):
            for b in range(2):
                moved = layer[k] if b == 0 else pltpu.roll(layer[k], rows_y - 1, 0)
                views.append(moved)
                views.append(pltpu.roll(moved, cols_x - 1, 1))
        return views

    views = [shifted(below_ref)]
    for layer in range(layers):
        views.append(shifted([disp_ref[k, layer] for k in range(components)]))
    views.append(shifted(above_ref))
    inside = (lax.broadcasted_iota(jnp.int32, (rows_y, cols_x), 0) < rows_y - 1) & (
        lax.broadcasted_iota(jnp.int32, (rows_y, cols_x), 1) < cols_x - 1
    )
    scales = [below_ref[components]] + [modulus_ref[layer] for layer in range(layers)]
    scales = [jnp.where(inside, scale, 0.0) for scale in scales]

    lower, higher = [], []
    for e in range(layers + 1):
        matrix = blocks
        if e == 0:
            matrix = blocks[half * group :]
        elif e == layers:
            matrix = blocks[: half * group]
        strips = []
        for y in range(0, rows_y, group):
            stacked = jnp.concatenate(
                [view[y : y + group] for view in views[e] + views[e + 1]], axis=0
            )
            force = jnp.dot(matrix, stacked, precision=lax.Precision.HIGHEST)
            force = force.reshape(-1, group, cols_x) * scales[e][y : y + group][None]
            strips.append(force)
        forces = jnp.concatenate(strips, axis=1)
        if e < layers:
            higher.append(forces[-half:])
        if e > 0:
            lower.append(forces[:half])
    for layer in range(layers):
        nodal = lower[layer] + higher[layer]
        for k in range(components):
            straight, crossed = [
                nodal[k * 4 + c] + pltpu.roll(nodal[k * 4 + 2 + c], 1, 0) for c in range(2)
            ]
            out_ref[k, layer] = -(straight + pltpu.roll(crossed, 1, 1))


def on_core(kernel, outs, flops, moved):
    return pl.pallas_call(
        kernel,
        out_shape=outs,
        compiler_params=pltpu.CompilerParams(vmem_limit_bytes=48 * 1024 * 1024),
        cost_estimate=pl.CostEstimate(flops=flops, bytes_accessed=moved, transcendentals=0),
    )


def shards(
    displacement,
    modulus,
    node_mass,
    stiffness,
    face_nodes,
    pair_mortar,
    pair_rank,
    pair_face,
    pair_count,
    pair_shape,
    pair_weight,
    pair_gap,
    pair_normal,
):
    components, layers, rows_y, cols_x = displacement.shape
    face_count = face_nodes.shape[1]
    pair_total = pair_mortar.shape[0]
    domains = lax.axis_size("dom")
    capacity = max(2, 2 * pair_total // domains)
    nodes = layers * rows_y * cols_x

    rows_shape = jax.ShapeDtypeStruct((12 * face_count // cols_x, cols_x), F32)
    own_rows = on_core(face_rows_kernel, rows_shape, 600_000_000, 400_000)(displacement, face_nodes)
    all_rows = lax.all_gather(own_rows, "dom")

    above = passed_along(displacement[:, 0], ("dom", "sub"), -1)
    below = passed_along(
        jnp.concatenate([displacement[:, -1], modulus[-1:]], axis=0), ("dom", "sub"), 1
    )

    line = (1, pair_total)
    sent, kept = on_core(
        pairs_kernel,
        [
            jax.ShapeDtypeStruct((domains, WORDS, LANES), F32),
            jax.ShapeDtypeStruct((WORDS, pair_total), F32),
        ],
        200_000_000,
        800_000,
    )(
        all_rows,
        own_rows,
        pair_mortar.reshape(line),
        pair_rank.reshape(line),
        pair_face.reshape(line),
        pair_count.reshape(line),
        pair_shape,
        pair_weight,
        pair_gap,
        pair_normal,
    )
    got = lax.all_to_all(sent, "dom", split_axis=0, concat_axis=0, tiled=True)

    internal = on_core(
        internal_kernel, jax.ShapeDtypeStruct(displacement.shape, F32), 3_000_000_000, 700_000
    )(displacement, above, below, modulus, stiffness)
    faces = on_core(
        mortar_kernel, jax.ShapeDtypeStruct((12, face_count), F32), 10_000_000, 30_000
    )(kept)

    def last(*refs):
        nodes_kernel(capacity, *refs)

    return on_core(
        last, jax.ShapeDtypeStruct(displacement.shape, F32), 600_000_000, 900_000
    )(got, faces, face_nodes, internal, node_mass)


def solution(mesh):
    placed = (
        P(None, ("runs", "dom", "sub"), None, None),
        P(("runs", "dom", "sub"), None, None),
        P(("runs", "dom", "sub"), None, None),
        P(),
        P(None, ("runs", "dom", "sub")),
        P(("runs", "dom", "sub")),
        P(("runs", "dom", "sub"), None),
        P(("runs", "dom", "sub")),
        P(("runs", "dom", "sub")),
        P(None, None, ("runs", "dom", "sub")),
        P(None, ("runs", "dom", "sub")),
        P(None, ("runs", "dom", "sub")),
        P(None, ("runs", "dom", "sub")),
    )
    return jax.shard_map(
        shards,
        mesh=mesh,
        in_specs=placed,
        out_specs=P(None, ("runs", "dom", "sub"), None, None),
        check_vma=False,
    )
```

```python
import jax
import jax.numpy as jnp
from jax import lax
from jax.experimental import pallas as pl
from jax.experimental.pallas import tpu as pltpu
from jax.sharding import PartitionSpec as P

F32 = jnp.float32
BF16 = jnp.bfloat16
LANES = 128
WORDS = 8


def passed_along(block, axis, distance):
    devices = range(lax.axis_size(axis))
    route = [(i - distance, i) for i in devices if i - distance in devices]
    return lax.ppermute(block, axis, route)


def thirds(x):
    high = x.astype(BF16)
    rest = x - high.astype(F32)
    middle = rest.astype(BF16)
    low = (rest - middle.astype(F32)).astype(BF16)
    return jnp.concatenate([high, middle, low], axis=0)


def summed(stacked):
    rows = stacked.shape[0] // 3
    return (stacked[:rows] + stacked[rows : 2 * rows]) + stacked[2 * rows :]


def marks(index, count):
    rows = lax.broadcasted_iota(jnp.int32, (count, index.shape[1]), 0)
    return (rows == index).astype(F32).astype(BF16)


def times(left, right):
    return jnp.dot(left, right, preferred_element_type=F32)


def times_turned(left, right):
    return lax.dot_general(left, right, (((1,), (1,)), ((), ())), preferred_element_type=F32)


def halves(power):
    return power.bit_length() - 1


def face_rows_kernel(disp_ref, nodes_ref, modulus_ref, rows_ref, copies_ref, down_ref, up_ref):
    down_ref[...] = disp_ref[:, 0]
    up_ref[: disp_ref.shape[0]] = disp_ref[:, disp_ref.shape[1] - 1]
    up_ref[disp_ref.shape[0]] = modulus_ref[disp_ref.shape[1] - 1]
    components, layers, rows_y, cols_x = disp_ref.shape
    strips = layers * rows_y
    parts = thirds(disp_ref[...].reshape(components * strips, cols_x))
    face_count = nodes_ref.shape[1]
    folds = face_count // cols_x
    for corner in range(4):
        index = nodes_ref[corner : corner + 1, :]
        along_x = marks(index & (cols_x - 1), cols_x)
        strip = index >> halves(cols_x)
        found = summed(times(parts, along_x)).reshape(components, strips, face_count)
        numbers = lax.broadcasted_iota(jnp.int32, (strips, face_count), 0)
        values = jnp.sum(jnp.where((numbers == strip)[None], found, 0.0), axis=1)
        for fold in range(folds):
            for k in range(components):
                at = fold * 12 + k * 4 + corner
                rows_ref[at : at + 1, :] = values[k : k + 1, fold * cols_x : (fold + 1) * cols_x]
    rows = rows_ref[...]

    def copy(i):
        copies_ref[i] = rows

    pl.loop(0, copies_ref.shape[0])(copy)


def looked_up(table, face, width):
    at = marks(face & (width - 1), width)
    both = summed(times(thirds(table), at))
    return jnp.where(face < width, both[:12], both[12:])


def pairs_kernel(
    all_ref, own_ref, mortar_ref, rank_ref, face_ref, count_ref, shape_ref, weight_ref, gap_ref,
    normal_ref, sent_ref, kept_ref,
):
    domains, folded, width = all_ref.shape
    pair_total = mortar_ref.shape[1]
    mortar, rank, face = mortar_ref[...], rank_ref[...], face_ref[...]
    mortar_rows = looked_up(own_ref[...], mortar, width)

    at = marks(face & (width - 1), width)
    step = min(domains, 8)

    def add_step(turn, total):
        block = all_ref[pl.ds(turn * step, step)].reshape(step * folded, width)
        found = summed(times(thirds(block), at)).reshape(step, folded, pair_total)
        for i in range(step):
            total = total + jnp.where(rank == turn * step + i, found[i], 0.0)
        return total

    both = jnp.zeros((folded, pair_total), F32)
    if domains == step:
        both = add_step(0, both)
    else:
        both = lax.fori_loop(0, domains // step, add_step, both)
    remote_rows = jnp.where(face < width, both[:12], both[12:])

    normal = normal_ref[...]
    gap = gap_ref[...]
    points = gap.shape[0]
    for node in range(4):
        across = sum(normal[k : k + 1] * remote_rows[k * 4 + node : k * 4 + node + 1] for k in range(3))
        gap = gap + shape_ref[node] * across
        across = sum(normal[k : k + 1] * mortar_rows[k * 4 + node : k * 4 + node + 1] for k in range(3))
        gap = gap - shape_ref[4 + node] * across
    live = lax.broadcasted_iota(jnp.int32, (points, pair_total), 0) < count_ref[...]
    pressure = jnp.where(live, weight_ref[...] * jnp.maximum(-gap, 0.0), 0.0)
    loads = [jnp.sum(pressure * shape_ref[i], axis=0, keepdims=True) for i in range(8)]

    ranks = lax.broadcasted_iota(jnp.int32, (domains, pair_total), 0)
    chosen = ranks == rank
    before = lax.broadcasted_iota(jnp.int32, (pair_total, pair_total), 0) < lax.broadcasted_iota(
        jnp.int32, (pair_total, pair_total), 1
    )
    earlier = times(chosen.astype(F32).astype(BF16), before.astype(F32).astype(BF16))
    slot = jnp.sum(jnp.where(chosen, earlier, 0.0), axis=0, keepdims=True).astype(jnp.int32)
    place = marks(slot, LANES)

    words = jnp.concatenate([normal] + loads[:4] + [face.astype(F32)], axis=0)
    parts = thirds(words).astype(F32)

    def send_step(turn):
        picked = [jnp.where(rank == turn * step + i, parts, 0.0) for i in range(step)]
        stacked = jnp.concatenate(picked, axis=0).astype(BF16)
        placed = times_turned(stacked, place).reshape(step, 3, WORDS, LANES)
        sent_ref[pl.ds(turn * step, step)] = (placed[:, 0] + placed[:, 1]) + placed[:, 2]

    if domains == step:
        send_step(0)
    else:
        pl.loop(0, domains // step)(send_step)
    kept_ref[...] = jnp.concatenate([-normal] + loads[4:] + [mortar.astype(F32)], axis=0)


def face_forces(words, face_count):
    loads = words[3:7]
    forces = jnp.concatenate([words[k : k + 1] * loads for k in range(3)], axis=0)
    at = marks(words[7:8].astype(jnp.int32), face_count)
    return summed(times_turned(thirds(forces), at))


def mortar_kernel(kept_ref, faces_ref):
    faces_ref[...] = face_forces(kept_ref[...], faces_ref.shape[1])


def nodes_kernel(capacity, got_ref, faces_ref, nodes_ref, internal_ref, mass_ref, out_ref):
    domains = got_ref.shape[0]
    components, layers, rows_y, cols_x = out_ref.shape
    strips = layers * rows_y
    face_count = faces_ref.shape[1]
    group = LANES // capacity
    tiles = []
    for start in range(0, domains, group):
        tile = got_ref[start]
        for i in range(1, group):
            tile = tile + pltpu.roll(got_ref[start + i], i * capacity, 1)
        tiles.append(tile)
    words = jnp.concatenate(tiles, axis=1)
    forces = faces_ref[...] + face_forces(words, face_count)
    total = jnp.zeros((3 * components * strips, cols_x), F32)
    parts = thirds(forces).astype(F32)
    numbers = lax.broadcasted_iota(jnp.int32, (strips, face_count), 0)
    for corner in range(4):
        index = nodes_ref[corner : corner + 1, :]
        along_x = marks(index & (cols_x - 1), cols_x)
        strip = numbers == (index >> halves(cols_x))
        spread = []
        for part in range(3):
            for k in range(components):
                at = part * 12 + k * 4 + corner
                spread.append(jnp.where(strip, parts[at : at + 1], 0.0).astype(BF16))
        total = total + times_turned(jnp.concatenate(spread, axis=0), along_x)
    contact = summed(total).reshape(components, layers, rows_y, cols_x)
    out_ref[...] = (internal_ref[...] + contact) / mass_ref[...][None]


def internal_kernel(disp_ref, above_ref, below_ref, modulus_ref, stiffness_ref, out_ref):
    components, layers, rows_y, cols_x = disp_ref.shape
    group = 8
    dofs = 8 * components
    half = dofs // 2

    row = lax.broadcasted_iota(jnp.int32, (dofs * group, dofs), 0) >> halves(group)
    upper = (row >= half).astype(jnp.int32)
    inner = row - half * upper
    dof = (inner >> 2) * 8 + upper * 4 + (inner & 3)
    pick = (dof == lax.broadcasted_iota(jnp.int32, (dofs * group, dofs), 1)).astype(F32)
    tall = jnp.dot(pick, stiffness_ref[...], precision=lax.Precision.HIGHEST)
    wide = lax.dot_general(
        tall, pick, (((1,), (1,)), ((), ())), precision=lax.Precision.HIGHEST,
        preferred_element_type=F32,
    )
    size = dofs * group
    diagonal = (lax.broadcasted_iota(jnp.int32, (size, size), 0) & (group - 1)) == (
        lax.broadcasted_iota(jnp.int32, (size, size), 1) & (group - 1)
    )
    blocks = jnp.where(diagonal, wide, 0.0)

    def shifted(layer):
        views = []
        for k in range(components):
            for b in range(2):
                moved = layer[k] if b == 0 else pltpu.roll(layer[k], rows_y - 1, 0)
                views.append(moved)
                views.append(pltpu.roll(moved, cols_x - 1, 1))
        return views

    views = [shifted(below_ref)]
    for layer in range(layers):
        views.append(shifted([disp_ref[k, layer] for k in range(components)]))
    views.append(shifted(above_ref))
    inside = (lax.broadcasted_iota(jnp.int32, (rows_y, cols_x), 0) < rows_y - 1) & (
        lax.broadcasted_iota(jnp.int32, (rows_y, cols_x), 1) < cols_x - 1
    )
    scales = [below_ref[components]] + [modulus_ref[layer] for layer in range(layers)]
    scales = [jnp.where(inside, scale, 0.0) for scale in scales]

    lower, higher = [], []
    for e in range(layers + 1):
        matrix = blocks
        if e == 0:
            matrix = blocks[half * group :]
        elif e == layers:
            matrix = blocks[: half * group]
        strips = []
        for y in range(0, rows_y, group):
            stacked = jnp.concatenate(
                [view[y : y + group] for view in views[e] + views[e + 1]], axis=0
            )
            force = jnp.dot(matrix, stacked, precision=lax.Precision.HIGHEST)
            force = force.reshape(-1, group, cols_x) * scales[e][y : y + group][None]
            strips.append(force)
        forces = jnp.concatenate(strips, axis=1)
        if e < layers:
            higher.append(forces[-half:])
        if e > 0:
            lower.append(forces[:half])
    for layer in range(layers):
        nodal = lower[layer] + higher[layer]
        for k in range(components):
            straight, crossed = [
                nodal[k * 4 + c] + pltpu.roll(nodal[k * 4 + 2 + c], 1, 0) for c in range(2)
            ]
            out_ref[k, layer] = -(straight + pltpu.roll(crossed, 1, 1))


def on_core(kernel, outs, flops, moved):
    return pl.pallas_call(
        kernel,
        out_shape=outs,
        compiler_params=pltpu.CompilerParams(vmem_limit_bytes=48 * 1024 * 1024),
        cost_estimate=pl.CostEstimate(flops=flops, bytes_accessed=moved, transcendentals=0),
    )


def shards(
    displacement,
    modulus,
    node_mass,
    stiffness,
    face_nodes,
    pair_mortar,
    pair_rank,
    pair_face,
    pair_count,
    pair_shape,
    pair_weight,
    pair_gap,
    pair_normal,
):
    components, layers, rows_y, cols_x = displacement.shape
    face_count = face_nodes.shape[1]
    pair_total = pair_mortar.shape[0]
    domains = lax.axis_size("dom")
    capacity = max(2, 2 * pair_total // domains)

    rows_shape = (12 * face_count // cols_x, cols_x)
    own_rows, copies, down, up = on_core(
        face_rows_kernel,
        [
            jax.ShapeDtypeStruct(rows_shape, F32),
            jax.ShapeDtypeStruct((domains,) + rows_shape, F32),
            jax.ShapeDtypeStruct((components, rows_y, cols_x), F32),
            jax.ShapeDtypeStruct((components + 1, rows_y, cols_x), F32),
        ],
        600_000_000,
        900_000,
    )(displacement, face_nodes, modulus)
    all_rows = lax.all_to_all(copies, "dom", split_axis=0, concat_axis=0, tiled=True)
    above = passed_along(down, ("dom", "sub"), -1)
    below = passed_along(up, ("dom", "sub"), 1)

    line = (1, pair_total)
    sent, kept = on_core(
        pairs_kernel,
        [
            jax.ShapeDtypeStruct((domains, WORDS, LANES), F32),
            jax.ShapeDtypeStruct((WORDS, pair_total), F32),
        ],
        200_000_000,
        800_000,
    )(
        all_rows,
        own_rows,
        pair_mortar.reshape(line),
        pair_rank.reshape(line),
        pair_face.reshape(line),
        pair_count.reshape(line),
        pair_shape,
        pair_weight,
        pair_gap,
        pair_normal,
    )
    got = lax.all_to_all(sent, "dom", split_axis=0, concat_axis=0, tiled=True)

    internal = on_core(
        internal_kernel, jax.ShapeDtypeStruct(displacement.shape, F32), 3_000_000_000, 700_000
    )(displacement, above, below, modulus, stiffness)
    faces = on_core(
        mortar_kernel, jax.ShapeDtypeStruct((12, face_count), F32), 10_000_000, 30_000
    )(kept)

    def last(*refs):
        nodes_kernel(capacity, *refs)

    return on_core(
        last, jax.ShapeDtypeStruct(displacement.shape, F32), 600_000_000, 900_000
    )(got, faces, face_nodes, internal, node_mass)


def solution(mesh):
    placed = (
        P(None, ("runs", "dom", "sub"), None, None),
        P(("runs", "dom", "sub"), None, None),
        P(("runs", "dom", "sub"), None, None),
        P(),
        P(None, ("runs", "dom", "sub")),
        P(("runs", "dom", "sub")),
        P(("runs", "dom", "sub"), None),
        P(("runs", "dom", "sub")),
        P(("runs", "dom", "sub")),
        P(None, None, ("runs", "dom", "sub")),
        P(None, ("runs", "dom", "sub")),
        P(None, ("runs", "dom", "sub")),
        P(None, ("runs", "dom", "sub")),
    )
    return jax.shard_map(
        shards,
        mesh=mesh,
        in_specs=placed,
        out_specs=P(None, ("runs", "dom", "sub"), None, None),
        check_vma=False,
    )
```

```python
import jax
import jax.numpy as jnp
from jax import lax
from jax.experimental import pallas as pl
from jax.experimental.pallas import tpu as pltpu
from jax.sharding import PartitionSpec as P

F32 = jnp.float32
BF16 = jnp.bfloat16
LANES = 128
WORDS = 8


def terms_of(x, count):
    terms = []
    for _ in range(count):
        terms.append(x.astype(BF16))
        x = x - terms[-1].astype(F32)
    return terms


def thirds(x):
    return jnp.concatenate(terms_of(x, 3), axis=0)


def summed(stacked):
    rows = stacked.shape[0] // 3
    return (stacked[:rows] + stacked[rows : 2 * rows]) + stacked[2 * rows :]


def marks(index, count):
    rows = lax.broadcasted_iota(jnp.int32, (count, index.shape[1]), 0)
    return (rows == index).astype(F32).astype(BF16)


def times(left, right):
    return jnp.dot(left, right, preferred_element_type=F32)


def times_turned(left, right):
    return lax.dot_general(left, right, (((1,), (1,)), ((), ())), preferred_element_type=F32)


def halves(power):
    return power.bit_length() - 1


def face_rows_kernel(
    passed, disp_ref, nodes_ref, modulus_ref, *refs
):
    ins, refs = refs[:passed], refs[passed:]
    outs, refs = refs[:passed], refs[passed:]
    rows_ref, copies_ref, inner_ref, outer_ref, disp, nodes, modulus, sems, copy_sems = refs
    components, layers, rows_y, cols_x = disp_ref.shape

    def bring(number, source, target):
        return pltpu.make_async_copy(source, target, sems.at[number])

    loads = [
        bring(0, nodes_ref, nodes),
        bring(1, disp_ref, disp),
        bring(2, modulus_ref, modulus),
    ]
    loads += [bring(3 + i, ins[i], outs[i]) for i in range(passed)]
    for load in loads:
        load.start()
    loads[0].wait()
    strips = layers * rows_y
    face_count = nodes.shape[1]
    folds = face_count // cols_x
    indices = [nodes[corner : corner + 1, :] for corner in range(4)]
    along_x = [marks(index & (cols_x - 1), cols_x) for index in indices]
    loads[1].wait()
    parts = thirds(disp[...].reshape(components * strips, cols_x))
    numbers = lax.broadcasted_iota(jnp.int32, (strips, face_count), 0)
    for corner in range(4):
        strip = indices[corner] >> halves(cols_x)
        found = summed(times(parts, along_x[corner])).reshape(components, strips, face_count)
        values = jnp.sum(jnp.where((numbers == strip)[None], found, 0.0), axis=1)
        for fold in range(folds):
            for k in range(components):
                at = fold * 12 + k * 4 + corner
                rows_ref[at : at + 1, :] = values[k : k + 1, fold * cols_x : (fold + 1) * cols_x]
    copies = [
        pltpu.make_async_copy(rows_ref, copies_ref.at[i], copy_sems.at[i])
        for i in range(copies_ref.shape[0])
    ]
    for copy in copies:
        copy.start()
    loads[2].wait()
    sub = lax.axis_index("sub")
    for target, layer in ((inner_ref, (1 - sub) * (layers - 1)), (outer_ref, sub * (layers - 1))):
        for k in range(components):
            target[k] = disp[k, layer]
        target[components] = modulus[layer]
    for load in loads[3:]:
        load.wait()
    for copy in copies:
        copy.wait()


def looked_up(table, face, width):
    at = marks(face & (width - 1), width)
    both = summed(times(thirds(table), at))
    return jnp.where(face < width, both[:12], both[12:])


def pairs_kernel(
    all_ref, own_ref, mortar_ref, rank_ref, face_ref, count_ref, shape_ref, weight_ref, gap_ref,
    normal_ref, sent_ref, kept_ref,
):
    domains, folded, width = all_ref.shape
    pair_total = mortar_ref.shape[1]
    mortar, rank, face = mortar_ref[...], rank_ref[...], face_ref[...]
    mortar_rows = looked_up(own_ref[...], mortar, width)

    at = marks(face & (width - 1), width)
    step = min(domains, 8)

    def add_step(turn, total):
        block = all_ref[pl.ds(turn * step, step)].reshape(step * folded, width)
        found = summed(times(thirds(block), at)).reshape(step, folded, pair_total)
        for i in range(step):
            total = total + jnp.where(rank == turn * step + i, found[i], 0.0)
        return total

    both = jnp.zeros((folded, pair_total), F32)
    if domains == step:
        both = add_step(0, both)
    else:
        both = lax.fori_loop(0, domains // step, add_step, both)
    remote_rows = jnp.where(face < width, both[:12], both[12:])

    normal = normal_ref[...]
    gap = gap_ref[...]
    points = gap.shape[0]
    for node in range(4):
        across = sum(normal[k : k + 1] * remote_rows[k * 4 + node : k * 4 + node + 1] for k in range(3))
        gap = gap + shape_ref[:, node] * across
        across = sum(normal[k : k + 1] * mortar_rows[k * 4 + node : k * 4 + node + 1] for k in range(3))
        gap = gap - shape_ref[:, 4 + node] * across
    live = lax.broadcasted_iota(jnp.int32, (points, pair_total), 0) < count_ref[...]
    pressure = jnp.where(live, weight_ref[...] * jnp.maximum(-gap, 0.0), 0.0)
    loads = [jnp.sum(pressure * shape_ref[:, i], axis=0, keepdims=True) for i in range(8)]

    ranks = lax.broadcasted_iota(jnp.int32, (domains, pair_total), 0)
    chosen = ranks == rank
    before = lax.broadcasted_iota(jnp.int32, (pair_total, pair_total), 0) < lax.broadcasted_iota(
        jnp.int32, (pair_total, pair_total), 1
    )
    earlier = times(chosen.astype(F32).astype(BF16), before.astype(F32).astype(BF16))
    slot = jnp.sum(jnp.where(chosen, earlier, 0.0), axis=0, keepdims=True).astype(jnp.int32)
    place = marks(slot, LANES)

    words = jnp.concatenate([normal] + loads[:4] + [face.astype(F32)], axis=0)
    parts = thirds(words).astype(F32)

    def send_step(turn):
        picked = [jnp.where(rank == turn * step + i, parts, 0.0) for i in range(step)]
        stacked = jnp.concatenate(picked, axis=0).astype(BF16)
        placed = times_turned(stacked, place).reshape(step, 3, WORDS, LANES)
        sent_ref[pl.ds(turn * step, step)] = (placed[:, 0] + placed[:, 1]) + placed[:, 2]

    if domains == step:
        send_step(0)
    else:
        pl.loop(0, domains // step)(send_step)
    kept_ref[...] = jnp.concatenate([-normal] + loads[4:] + [mortar.astype(F32)], axis=0)


def face_forces(words, face_count):
    loads = words[3:7]
    forces = jnp.concatenate([words[k : k + 1] * loads for k in range(3)], axis=0)
    at = marks(words[7:8].astype(jnp.int32), face_count)
    return summed(times_turned(thirds(forces), at))


def nodes_kernel(capacity, got_ref, faces_ref, nodes_ref, internal_ref, mass_ref, out_ref):
    domains = got_ref.shape[0]
    components, layers, rows_y, cols_x = out_ref.shape
    strips = layers * rows_y
    face_count = faces_ref.shape[1]
    group = LANES // capacity
    tiles = []
    for start in range(0, domains, group):
        tile = got_ref[start]
        for i in range(1, group):
            tile = tile + pltpu.roll(got_ref[start + i], i * capacity, 1)
        tiles.append(tile)
    words = jnp.concatenate(tiles, axis=1)
    forces = faces_ref[...] + face_forces(words, face_count)
    total = jnp.zeros((2 * components * strips, cols_x), F32)
    parts = [term.astype(F32) for term in terms_of(forces, 2)]
    numbers = lax.broadcasted_iota(jnp.int32, (strips, face_count), 0)
    for corner in range(4):
        index = nodes_ref[corner : corner + 1, :]
        along_x = marks(index & (cols_x - 1), cols_x)
        strip = numbers == (index >> halves(cols_x))
        spread = []
        for part in parts:
            for k in range(components):
                at = k * 4 + corner
                spread.append(jnp.where(strip, part[at : at + 1], 0.0).astype(BF16))
        total = total + times_turned(jnp.concatenate(spread, axis=0), along_x)
    half = components * strips
    contact = (total[:half] + total[half:]).reshape(components, layers, rows_y, cols_x)
    out_ref[...] = (internal_ref[...] + contact) / mass_ref[...][None]


def internal_kernel(
    disp_ref, inner_ref, outer_ref, modulus_ref, stiffness_ref, kept_ref, out_ref, faces_ref
):
    components, layers, rows_y, cols_x = disp_ref.shape
    group = 8
    dofs = 8 * components
    half = dofs // 2

    row = lax.broadcasted_iota(jnp.int32, (dofs * group, dofs), 0) >> halves(group)
    upper = (row >= half).astype(jnp.int32)
    inner = row - half * upper
    dof = (inner >> 2) * 8 + upper * 4 + (inner & 3)
    pick = (dof == lax.broadcasted_iota(jnp.int32, (dofs * group, dofs), 1)).astype(F32).astype(BF16)
    size = dofs * group
    diagonal = (lax.broadcasted_iota(jnp.int32, (size, size), 0) & (group - 1)) == (
        lax.broadcasted_iota(jnp.int32, (size, size), 1) & (group - 1)
    )
    blocks = []
    for term in terms_of(stiffness_ref[...], 2):
        wide = times_turned(times(pick, term).astype(BF16), pick)
        blocks.append(jnp.where(diagonal, wide, 0.0).astype(BF16))

    sub = lax.axis_index("sub")
    below_ref = [jnp.where(sub == 0, outer_ref[k], inner_ref[k]) for k in range(components + 1)]
    above_ref = [jnp.where(sub == 0, inner_ref[k], outer_ref[k]) for k in range(components)]

    def shifted(layer):
        views = []
        for k in range(components):
            for b in range(2):
                moved = layer[k] if b == 0 else pltpu.roll(layer[k], rows_y - 1, 0)
                views.append(moved)
                views.append(pltpu.roll(moved, cols_x - 1, 1))
        return views

    views = [shifted(below_ref)]
    for layer in range(layers):
        views.append(shifted([disp_ref[k, layer] for k in range(components)]))
    views.append(shifted(above_ref))
    inside = (lax.broadcasted_iota(jnp.int32, (rows_y, cols_x), 0) < rows_y - 1) & (
        lax.broadcasted_iota(jnp.int32, (rows_y, cols_x), 1) < cols_x - 1
    )
    scales = [below_ref[components]] + [modulus_ref[layer] for layer in range(layers)]
    scales = [jnp.where(inside, scale, 0.0) for scale in scales]

    lower, higher = [], []
    for e in range(layers + 1):
        kept = slice(half * group, None) if e == 0 else slice(0, half * group if e == layers else None)
        both = jnp.concatenate([block[kept] for block in blocks], axis=0)
        count = both.shape[0] // 2
        strips = []
        for y in range(0, rows_y, group):
            stacked = jnp.concatenate(
                [view[y : y + group] for view in views[e] + views[e + 1]], axis=0
            )
            high, low = terms_of(stacked, 2)
            leading = times(both, high)
            force = leading[:count] + (leading[count:] + times(both[:count], low))
            force = force.reshape(-1, group, cols_x) * scales[e][y : y + group][None]
            strips.append(force)
        forces = jnp.concatenate(strips, axis=1)
        if e < layers:
            higher.append(forces[-half:])
        if e > 0:
            lower.append(forces[:half])
    for layer in range(layers):
        nodal = lower[layer] + higher[layer]
        for k in range(components):
            straight, crossed = [
                nodal[k * 4 + c] + pltpu.roll(nodal[k * 4 + 2 + c], 1, 0) for c in range(2)
            ]
            out_ref[k, layer] = -(straight + pltpu.roll(crossed, 1, 1))
    faces_ref[...] = face_forces(kept_ref[...], faces_ref.shape[1])


def on_core(kernel, outs, flops, moved, **more):
    return pl.pallas_call(
        kernel,
        out_shape=outs,
        compiler_params=pltpu.CompilerParams(vmem_limit_bytes=48 * 1024 * 1024),
        cost_estimate=pl.CostEstimate(flops=flops, bytes_accessed=moved, transcendentals=0),
        **more,
    )


def swapped(block, axis, first):
    size = lax.axis_size(axis)
    route = []
    for i in range(first, size - 1, 2):
        route += [(i, i + 1), (i + 1, i)]
    return lax.ppermute(block, axis, route)


def shards(
    displacement,
    modulus,
    node_mass,
    stiffness,
    face_nodes,
    pair_mortar,
    pair_rank,
    pair_face,
    pair_count,
    pair_shape,
    pair_weight,
    pair_gap,
    pair_normal,
):
    components, layers, rows_y, cols_x = displacement.shape
    face_count = face_nodes.shape[1]
    pair_total = pair_mortar.shape[0]
    domains = lax.axis_size("dom")
    capacity = max(2, 2 * pair_total // domains)

    line = (1, pair_total)
    pairs = [
        pair_mortar.reshape(line),
        pair_rank.reshape(line),
        pair_face.reshape(line),
        pair_count.reshape(line),
        jnp.swapaxes(pair_shape, 0, 1),
        pair_weight,
        pair_gap,
        pair_normal,
    ]

    def first(*refs):
        face_rows_kernel(len(pairs), *refs)

    rows_shape = (12 * face_count // cols_x, cols_x)
    edge = jax.ShapeDtypeStruct((components + 1, rows_y, cols_x), F32)
    in_hbm = pl.BlockSpec(memory_space=pltpu.HBM)
    in_vmem = pl.BlockSpec(memory_space=pltpu.VMEM)
    held = [pltpu.with_memory_space_constraint(x, pltpu.HBM) for x in (displacement, face_nodes, modulus, *pairs)]
    *pairs, own_rows, copies, inner, outer = on_core(
        first,
        [jax.ShapeDtypeStruct(x.shape, x.dtype) for x in pairs]
        + [
            jax.ShapeDtypeStruct(rows_shape, F32),
            jax.ShapeDtypeStruct((domains,) + rows_shape, F32),
            edge,
            edge,
        ],
        600_000_000,
        900_000,
        in_specs=[in_hbm] * (3 + len(pairs)),
        out_specs=[in_vmem] * (len(pairs) + 1) + [in_hbm, in_vmem, in_vmem],
        scratch_shapes=[
            pltpu.VMEM(displacement.shape, F32),
            pltpu.VMEM(face_nodes.shape, jnp.int32),
            pltpu.VMEM(modulus.shape, F32),
            pltpu.SemaphoreType.DMA((3 + len(pairs),)),
            pltpu.SemaphoreType.DMA((domains,)),
        ],
    )(*held)
    all_rows = lax.all_to_all(copies, "dom", split_axis=0, concat_axis=0, tiled=True)
    outer = swapped(outer, ("dom", "sub"), 1)
    inner = swapped(inner, ("dom", "sub"), 0)

    sent, kept = on_core(
        pairs_kernel,
        [
            jax.ShapeDtypeStruct((domains, WORDS, LANES), F32),
            jax.ShapeDtypeStruct((WORDS, pair_total), F32),
        ],
        200_000_000,
        800_000,
    )(all_rows, own_rows, *pairs)
    got = lax.all_to_all(sent, "dom", split_axis=0, concat_axis=0, tiled=True)

    internal, faces = on_core(
        internal_kernel,
        [
            jax.ShapeDtypeStruct(displacement.shape, F32),
            jax.ShapeDtypeStruct((12, face_count), F32),
        ],
        1_500_000_000,
        700_000,
    )(displacement, inner, outer, modulus, stiffness, kept)

    def last(*refs):
        nodes_kernel(capacity, *refs)

    return on_core(
        last, jax.ShapeDtypeStruct(displacement.shape, F32), 600_000_000, 900_000
    )(got, faces, face_nodes, internal, node_mass)


def solution(mesh):
    placed = (
        P(None, ("runs", "dom", "sub"), None, None),
        P(("runs", "dom", "sub"), None, None),
        P(("runs", "dom", "sub"), None, None),
        P(),
        P(None, ("runs", "dom", "sub")),
        P(("runs", "dom", "sub")),
        P(("runs", "dom", "sub"), None),
        P(("runs", "dom", "sub")),
        P(("runs", "dom", "sub")),
        P(None, None, ("runs", "dom", "sub")),
        P(None, ("runs", "dom", "sub")),
        P(None, ("runs", "dom", "sub")),
        P(None, ("runs", "dom", "sub")),
    )
    return jax.shard_map(
        shards,
        mesh=mesh,
        in_specs=placed,
        out_specs=P(None, ("runs", "dom", "sub"), None, None),
        check_vma=False,
    )
```

```python
import jax
import jax.numpy as jnp
from jax import lax
from jax.experimental import pallas as pl
from jax.experimental.pallas import tpu as pltpu
from jax.sharding import PartitionSpec as P

F32 = jnp.float32
BF16 = jnp.bfloat16
LANES = 128


def terms_of(x, count):
    terms = []
    for _ in range(count):
        terms.append(x.astype(BF16))
        x = x - terms[-1].astype(F32)
    return terms


def thirds(x):
    return jnp.concatenate(terms_of(x, 3), axis=0)


def summed(stacked):
    rows = stacked.shape[0] // 3
    return (stacked[:rows] + stacked[rows : 2 * rows]) + stacked[2 * rows :]


def marks(index, count):
    rows = lax.broadcasted_iota(jnp.int32, (count, index.shape[1]), 0)
    return (rows == index).astype(F32).astype(BF16)


def times(left, right):
    return jnp.dot(left, right, preferred_element_type=F32)


def times_turned(left, right):
    return lax.dot_general(left, right, (((1,), (1,)), ((), ())), preferred_element_type=F32)


def halves(power):
    return power.bit_length() - 1


def looked_up(table, face, width):
    at = marks(face & (width - 1), width)
    both = summed(times(thirds(table), at))
    return jnp.where(face < width, both[:12], both[12:])


def words_of(shapes, gap, normal, face):
    full = gap.shape[0] // 8 * 8
    last = [x[full:] for x in shapes + [gap]]
    blank = jnp.zeros((7, face.shape[1]), F32)
    return jnp.concatenate(
        [x[:full] for x in shapes + [gap]] + last + [normal, face.astype(F32), blank], axis=0
    )


def weighted_pressure(words, full, remote_rows):
    tail = 5 * full
    normal = words[tail + 5 : tail + 8]
    gap, last = words[4 * full : tail], words[tail + 4 : tail + 5]
    for node in range(4):
        across = sum(
            normal[k : k + 1] * remote_rows[k * 4 + node : k * 4 + node + 1] for k in range(3)
        )
        gap = gap + words[node * full : (node + 1) * full] * across
        last = last + words[tail + node : tail + node + 1] * across
    return jnp.maximum(-gap, 0.0), jnp.maximum(-last, 0.0), normal


def loads_on(shapes, full, tail, pressure, last):
    return [
        jnp.sum(pressure * shapes[i * full : (i + 1) * full], axis=0, keepdims=True)
        + last * shapes[tail + i : tail + i + 1]
        for i in range(4)
    ]


def forces_of(normal, loads):
    loads = jnp.concatenate(loads, axis=0)
    return jnp.concatenate([normal[k : k + 1] * loads for k in range(3)], axis=0)


def first_kernel(capacity, *refs):
    (
        nodes_hbm, disp_hbm, mortar_hbm, rank_hbm, face_hbm, count_hbm, weight_hbm, normal_hbm,
        gap_hbm, shape_hbm, modulus_hbm,
        sent_ref, rows_ref, words_ref, turned_ref, mortar_ref, rank_ref, face_ref, inner_ref, outer_ref,
        nodes, disp, count, weight, normal_v, gap_v, shape, modulus, blocks, sems, copy_sems,
    ) = refs
    components, layers, rows_y, cols_x = disp.shape
    sources = (
        nodes_hbm, rank_hbm, face_hbm, mortar_hbm, count_hbm, weight_hbm, normal_hbm, gap_hbm,
        shape_hbm, disp_hbm, modulus_hbm,
    )
    targets = (
        nodes, rank_ref, face_ref, mortar_ref, count, weight, normal_v, gap_v, shape, disp, modulus,
    )
    brought = [
        pltpu.make_async_copy(source, target, sems.at[i])
        for i, (source, target) in enumerate(zip(sources, targets))
    ]
    for copy in brought:
        copy.start()

    domains = sent_ref.shape[0]
    pair_total = rank_ref.shape[1]
    face_count = nodes.shape[1]
    strips = layers * rows_y
    brought[0].wait()
    indices = [nodes[corner : corner + 1, :] for corner in range(4)]
    along_x = [marks(index & (cols_x - 1), cols_x) for index in indices]

    for copy in brought[1:4]:
        copy.wait()
    rank, face, mortar = rank_ref[...], face_ref[...], mortar_ref[...]
    chosen = lax.broadcasted_iota(jnp.int32, (domains, pair_total), 0) == rank
    before = lax.broadcasted_iota(jnp.int32, (pair_total, pair_total), 0) < lax.broadcasted_iota(
        jnp.int32, (pair_total, pair_total), 1
    )
    earlier = times(chosen.astype(F32).astype(BF16), before.astype(F32).astype(BF16))
    slot = jnp.sum(jnp.where(chosen, earlier, 0.0), axis=0, keepdims=True).astype(jnp.int32)
    place = marks(rank * capacity + slot, domains * capacity)

    for copy in brought[4:]:
        copy.wait()
    parts = thirds(disp[...].reshape(components * strips, cols_x))
    numbers = lax.broadcasted_iota(jnp.int32, (strips, face_count), 0)
    folds = face_count // cols_x
    for corner in range(4):
        strip = indices[corner] >> halves(cols_x)
        found = summed(times(parts, along_x[corner])).reshape(components, strips, face_count)
        values = jnp.sum(jnp.where((numbers == strip)[None], found, 0.0), axis=1)
        for fold in range(folds):
            for k in range(components):
                at = fold * 12 + k * 4 + corner
                rows_ref[at : at + 1, :] = values[k : k + 1, fold * cols_x : (fold + 1) * cols_x]

    mortar_rows = looked_up(rows_ref[...], mortar, cols_x)
    normal = normal_v[...]
    gap = gap_v[...]
    points = gap.shape[0]
    full = points // 8 * 8
    live = lax.broadcasted_iota(jnp.int32, (points, pair_total), 0) < count[...]
    root = jnp.where(live, jnp.sqrt(weight[...]), 0.0)
    turned = []
    for node in range(4):
        mortar_shape = shape[:, 4 + node]
        across = sum(
            normal[k : k + 1] * mortar_rows[k * 4 + node : k * 4 + node + 1] for k in range(3)
        )
        gap = gap - mortar_shape * across
        turned.append(root * mortar_shape)
    for node in range(4):
        turned_ref[node * full : (node + 1) * full] = turned[node][:full]
        turned_ref[4 * full + node : 4 * full + node + 1] = turned[node][full:]
    words = words_of([root * shape[:, node] for node in range(4)], root * gap, normal, face)
    words_ref[...] = words

    group = LANES // capacity
    rows_high = rows_ref.shape[0] * cols_x // LANES
    height = blocks.shape[1] - rows_high
    extra = group * height - words.shape[0]
    if extra:
        words = jnp.concatenate([words, jnp.zeros((extra, pair_total), F32)], axis=0)
    placed = summed(times_turned(thirds(words), place))
    rows = rows_ref[...]
    part = lax.broadcasted_iota(jnp.int32, (height, LANES), 1) >> halves(capacity)
    copies = []
    for domain in range(domains):
        tile, spot = domain // group, domain % group
        block = None
        for j in range(group):
            piece = placed[j * height : (j + 1) * height, tile * LANES : (tile + 1) * LANES]
            if j != spot:
                piece = pltpu.roll(piece, (j - spot) * capacity % LANES, 1)
            block = piece if block is None else jnp.where(part == j, piece, block)
        for i in range(cols_x // LANES):
            high = rows_ref.shape[0]
            blocks[domain, i * high : (i + 1) * high] = rows[:, i * LANES : (i + 1) * LANES]
        blocks[domain, rows_high:] = block
        copies.append(
            pltpu.make_async_copy(blocks.at[domain], sent_ref.at[domain], copy_sems.at[domain])
        )
        copies[-1].start()

    sub = lax.axis_index("sub")
    for target, layer in ((inner_ref, (1 - sub) * (layers - 1)), (outer_ref, sub * (layers - 1))):
        for k in range(components):
            target[k] = disp[k, layer]
        target[components] = modulus[layer]
    for copy in copies:
        copy.wait()


def last_kernel(
    capacity, got_ref, rows_ref, words_ref, turned_ref, mortar_ref, rank_ref, face_ref, nodes_ref,
    internal_ref, mass_ref, out_ref,
):
    domains = got_ref.shape[0]
    components, layers, rows_y, cols_x = out_ref.shape
    strips = layers * rows_y
    face_count = nodes_ref.shape[1]
    pair_total = rank_ref.shape[1]
    folded = rows_ref.shape[0]
    rows_high = folded * cols_x // LANES
    height = got_ref.shape[1] - rows_high
    group = LANES // capacity
    full = (turned_ref.shape[0] - 8) // 4
    own_rows = rows_ref[...]

    rank, face = rank_ref[...], face_ref[...]
    at = marks(face & (cols_x - 1), cols_x)
    step = min(domains, 8)

    def add_step(turn, total):
        block = jnp.concatenate(
            [
                got_ref[pl.ds(turn * step, step), i * folded : (i + 1) * folded].reshape(
                    step * folded, LANES
                )
                for i in range(cols_x // LANES)
            ],
            axis=1,
        )
        found = summed(times(thirds(block), at)).reshape(step, folded, pair_total)
        for i in range(step):
            total = total + jnp.where(rank == turn * step + i, found[i], 0.0)
        return total

    both = jnp.zeros((folded, pair_total), F32)
    if domains == step:
        both = add_step(0, both)
    else:
        both = lax.fori_loop(0, domains // step, add_step, both)
    remote_rows = jnp.where(face < cols_x, both[:12], both[12:])
    pressure, last, normal = weighted_pressure(words_ref[...], full, remote_rows)
    turned = turned_ref[...]
    mortar_forces = forces_of(-normal, loads_on(turned, full, 4 * full, pressure, last))

    part = lax.broadcasted_iota(jnp.int32, (height, LANES), 1) >> halves(capacity)
    pieces = []
    for j in range(group):
        tiles = []
        for tile in range(domains // group):
            block = None
            for spot in range(group):
                piece = got_ref[tile * group + spot, rows_high:]
                if j != spot:
                    piece = pltpu.roll(piece, (spot - j) * capacity % LANES, 1)
                block = piece if block is None else jnp.where(part == spot, piece, block)
            tiles.append(block)
        pieces.append(jnp.concatenate(tiles, axis=1))
    words = jnp.concatenate(pieces, axis=0)
    asked = words[5 * full + 8 : 5 * full + 9].astype(jnp.int32)
    pressure, last, normal = weighted_pressure(words, full, looked_up(own_rows, asked, cols_x))
    remote_forces = forces_of(normal, loads_on(words, full, 5 * full, pressure, last))

    forces = jnp.concatenate([mortar_forces, remote_forces], axis=1)
    at = marks(jnp.concatenate([mortar_ref[...], asked], axis=1), face_count)
    forces = summed(times_turned(thirds(forces), at))
    total = jnp.zeros((2 * components * strips, cols_x), F32)
    parts = [term.astype(F32) for term in terms_of(forces, 2)]
    numbers = lax.broadcasted_iota(jnp.int32, (strips, face_count), 0)
    for corner in range(4):
        index = nodes_ref[corner : corner + 1, :]
        along_x = marks(index & (cols_x - 1), cols_x)
        strip = numbers == (index >> halves(cols_x))
        spread = []
        for part in parts:
            for k in range(components):
                at = k * 4 + corner
                spread.append(jnp.where(strip, part[at : at + 1], 0.0).astype(BF16))
        total = total + times_turned(jnp.concatenate(spread, axis=0), along_x)
    half = components * strips
    contact = (total[:half] + total[half:]).reshape(components, layers, rows_y, cols_x)
    out_ref[...] = (internal_ref[...] + contact) / mass_ref[...][None]


def internal_kernel(
    disp_ref, inner_ref, outer_ref, modulus_ref, stiffness_ref, out_ref
):
    components, layers, rows_y, cols_x = disp_ref.shape
    group = 8
    dofs = 8 * components
    half = dofs // 2

    row = lax.broadcasted_iota(jnp.int32, (dofs * group, dofs), 0) >> halves(group)
    upper = (row >= half).astype(jnp.int32)
    inner = row - half * upper
    dof = (inner >> 2) * 8 + upper * 4 + (inner & 3)
    pick = (dof == lax.broadcasted_iota(jnp.int32, (dofs * group, dofs), 1)).astype(F32).astype(BF16)
    size = dofs * group
    diagonal = (lax.broadcasted_iota(jnp.int32, (size, size), 0) & (group - 1)) == (
        lax.broadcasted_iota(jnp.int32, (size, size), 1) & (group - 1)
    )
    blocks = []
    for term in terms_of(stiffness_ref[...], 2):
        wide = times_turned(times(pick, term).astype(BF16), pick)
        blocks.append(jnp.where(diagonal, wide, 0.0).astype(BF16))

    sub = lax.axis_index("sub")
    below_ref = [jnp.where(sub == 0, outer_ref[k], inner_ref[k]) for k in range(components + 1)]
    above_ref = [jnp.where(sub == 0, inner_ref[k], outer_ref[k]) for k in range(components)]

    def shifted(layer):
        views = []
        for k in range(components):
            for b in range(2):
                moved = layer[k] if b == 0 else pltpu.roll(layer[k], rows_y - 1, 0)
                views.append(moved)
                views.append(pltpu.roll(moved, cols_x - 1, 1))
        return views

    views = [shifted(below_ref)]
    for layer in range(layers):
        views.append(shifted([disp_ref[k, layer] for k in range(components)]))
    views.append(shifted(above_ref))
    inside = (lax.broadcasted_iota(jnp.int32, (rows_y, cols_x), 0) < rows_y - 1) & (
        lax.broadcasted_iota(jnp.int32, (rows_y, cols_x), 1) < cols_x - 1
    )
    scales = [below_ref[components]] + [modulus_ref[layer] for layer in range(layers)]
    scales = [jnp.where(inside, scale, 0.0) for scale in scales]

    lower, higher = [], []
    for e in range(layers + 1):
        kept = slice(half * group, None) if e == 0 else slice(0, half * group if e == layers else None)
        both = jnp.concatenate([block[kept] for block in blocks], axis=0)
        count = both.shape[0] // 2
        strips = []
        for y in range(0, rows_y, group):
            stacked = jnp.concatenate(
                [view[y : y + group] for view in views[e] + views[e + 1]], axis=0
            )
            high, low = terms_of(stacked, 2)
            leading = times(both, high)
            force = leading[:count] + (leading[count:] + times(both[:count], low))
            force = force.reshape(-1, group, cols_x) * scales[e][y : y + group][None]
            strips.append(force)
        forces = jnp.concatenate(strips, axis=1)
        if e < layers:
            higher.append(forces[-half:])
        if e > 0:
            lower.append(forces[:half])
    for layer in range(layers):
        nodal = lower[layer] + higher[layer]
        for k in range(components):
            straight, crossed = [
                nodal[k * 4 + c] + pltpu.roll(nodal[k * 4 + 2 + c], 1, 0) for c in range(2)
            ]
            out_ref[k, layer] = -(straight + pltpu.roll(crossed, 1, 1))


def on_core(kernel, outs, flops, moved, **more):
    return pl.pallas_call(
        kernel,
        out_shape=outs,
        compiler_params=pltpu.CompilerParams(vmem_limit_bytes=48 * 1024 * 1024),
        cost_estimate=pl.CostEstimate(flops=flops, bytes_accessed=moved, transcendentals=0),
        **more,
    )


def swapped(block, axis, first):
    size = lax.axis_size(axis)
    route = []
    for i in range(first, size - 1, 2):
        route += [(i, i + 1), (i + 1, i)]
    return lax.ppermute(block, axis, route)


def shards(
    displacement,
    modulus,
    node_mass,
    stiffness,
    face_nodes,
    pair_mortar,
    pair_rank,
    pair_face,
    pair_count,
    pair_shape,
    pair_weight,
    pair_gap,
    pair_normal,
):
    components, layers, rows_y, cols_x = displacement.shape
    face_count = face_nodes.shape[1]
    pair_total = pair_mortar.shape[0]
    domains = lax.axis_size("dom")
    capacity = max(2, 2 * pair_total // domains)

    points = pair_weight.shape[0]
    full = points // 8 * 8
    group = LANES // capacity
    word_rows = 5 * full + 16
    height = -(-word_rows // (8 * group)) * 8
    rows_high = 12 * face_count // LANES
    line = (1, pair_total)

    def first(*refs):
        first_kernel(capacity, *refs)

    def last(*refs):
        last_kernel(capacity, *refs)

    def shaped(shape, dtype=F32):
        return jax.ShapeDtypeStruct(shape, dtype)

    arrays = [
        face_nodes,
        displacement,
        pair_mortar.reshape(line),
        pair_rank.reshape(line),
        pair_face.reshape(line),
        pair_count.reshape(line),
        pair_weight,
        pair_normal,
        pair_gap,
        jnp.swapaxes(pair_shape, 0, 1),
        modulus,
    ]
    edge = shaped((components + 1, rows_y, cols_x))
    in_hbm = pl.BlockSpec(memory_space=pltpu.HBM)
    in_vmem = pl.BlockSpec(memory_space=pltpu.VMEM)
    kept = [face_nodes, displacement, *arrays[5:]]
    sent, rows, words, turned, mortar, rank, face, inner, outer = on_core(
        first,
        [
            shaped((domains, rows_high + height, LANES)),
            shaped((12 * face_count // cols_x, cols_x)),
            shaped((word_rows, pair_total)),
            shaped((4 * full + 8, pair_total)),
            shaped(line, jnp.int32),
            shaped(line, jnp.int32),
            shaped(line, jnp.int32),
            edge,
            edge,
        ],
        900_000_000,
        1_500_000,
        in_specs=[in_hbm] * len(arrays),
        out_specs=[in_hbm] + [in_vmem] * 8,
        scratch_shapes=[pltpu.VMEM(x.shape, x.dtype) for x in kept]
        + [
            pltpu.VMEM((domains, rows_high + height, LANES), F32),
            pltpu.SemaphoreType.DMA((len(arrays),)),
            pltpu.SemaphoreType.DMA((domains,)),
        ],
    )(*[pltpu.with_memory_space_constraint(x, pltpu.HBM) for x in arrays])
    got = lax.all_to_all(sent, "dom", split_axis=0, concat_axis=0, tiled=True)
    outer = swapped(outer, ("dom", "sub"), 1)
    inner = swapped(inner, ("dom", "sub"), 0)
    internal = on_core(
        internal_kernel, shaped(displacement.shape), 1_500_000_000, 700_000
    )(displacement, inner, outer, modulus, stiffness)
    return on_core(last, shaped(displacement.shape), 900_000_000, 1_500_000)(
        got, rows, words, turned, mortar, rank, face, face_nodes, internal, node_mass
    )


def solution(mesh):
    placed = (
        P(None, ("runs", "dom", "sub"), None, None),
        P(("runs", "dom", "sub"), None, None),
        P(("runs", "dom", "sub"), None, None),
        P(),
        P(None, ("runs", "dom", "sub")),
        P(("runs", "dom", "sub")),
        P(("runs", "dom", "sub"), None),
        P(("runs", "dom", "sub")),
        P(("runs", "dom", "sub")),
        P(None, None, ("runs", "dom", "sub")),
        P(None, ("runs", "dom", "sub")),
        P(None, ("runs", "dom", "sub")),
        P(None, ("runs", "dom", "sub")),
    )
    return jax.shard_map(
        shards,
        mesh=mesh,
        in_specs=placed,
        out_specs=P(None, ("runs", "dom", "sub"), None, None),
        check_vma=False,
    )
```

```python
import jax
import jax.numpy as jnp
from jax import lax
from jax.experimental import pallas as pl
from jax.experimental.pallas import tpu as pltpu
from jax.sharding import PartitionSpec as P

F32 = jnp.float32
BF16 = jnp.bfloat16
LANES = 128


def terms_of(x, count):
    terms = []
    for _ in range(count):
        terms.append(x.astype(BF16))
        x = x - terms[-1].astype(F32)
    return terms


def stacked_terms(x):
    return jnp.concatenate(terms_of(x, 2), axis=0)


def summed(stacked):
    rows = stacked.shape[0] // 2
    return stacked[:rows] + stacked[rows:]


def marks(index, count):
    rows = lax.broadcasted_iota(jnp.int32, (count, index.shape[1]), 0)
    return (rows == index).astype(F32).astype(BF16)


def times(left, right):
    return jnp.dot(left, right, preferred_element_type=F32)


def times_turned(left, right):
    return lax.dot_general(left, right, (((1,), (1,)), ((), ())), preferred_element_type=F32)


def halves(power):
    return power.bit_length() - 1


def looked_up(table, face, width):
    at = marks(face & (width - 1), width)
    both = summed(times(stacked_terms(table), at))
    return jnp.where(face < width, both[:12], both[12:])


def words_of(shapes, gap, normal, face):
    full = gap.shape[0] // 8 * 8
    last = [x[full:] for x in shapes + [gap]]
    blank = jnp.zeros((7, face.shape[1]), F32)
    return jnp.concatenate(
        [x[:full] for x in shapes + [gap]] + last + [normal, face.astype(F32), blank], axis=0
    )


def weighted_pressure(words, full, remote_rows):
    tail = 5 * full
    normal = words[tail + 5 : tail + 8]
    gap, last = words[4 * full : tail], words[tail + 4 : tail + 5]
    for node in range(4):
        across = sum(
            normal[k : k + 1] * remote_rows[k * 4 + node : k * 4 + node + 1] for k in range(3)
        )
        gap = gap + words[node * full : (node + 1) * full] * across
        last = last + words[tail + node : tail + node + 1] * across
    return jnp.maximum(-gap, 0.0), jnp.maximum(-last, 0.0), normal


def loads_on(shapes, full, tail, pressure, last):
    return [
        jnp.sum(pressure * shapes[i * full : (i + 1) * full], axis=0, keepdims=True)
        + last * shapes[tail + i : tail + i + 1]
        for i in range(4)
    ]


def forces_of(normal, loads):
    loads = jnp.concatenate(loads, axis=0)
    return jnp.concatenate([normal[k : k + 1] * loads for k in range(3)], axis=0)


def first_kernel(capacity, *refs):
    (
        nodes_hbm, disp_hbm, mortar_hbm, rank_hbm, face_hbm, count_hbm, weight_hbm, normal_hbm,
        gap_hbm, shape_hbm, modulus_hbm,
        sent_ref, rows_ref, words_ref, turned_ref, mortar_ref, rank_ref, face_ref, inner_ref, outer_ref,
        marks_ref,
        nodes, disp, count, weight, normal_v, gap_v, shape, modulus, halved, blocks, sems, copy_sems,
    ) = refs
    components, layers, rows_y, cols_x = disp.shape
    sources = (
        nodes_hbm, disp_hbm, rank_hbm, face_hbm, mortar_hbm, count_hbm, weight_hbm, normal_hbm,
        gap_hbm, shape_hbm, modulus_hbm,
    )
    targets = (
        nodes, disp, rank_ref, face_ref, mortar_ref, count, weight, normal_v, gap_v, shape, modulus,
    )
    brought = [
        pltpu.make_async_copy(source, target, sems.at[i])
        for i, (source, target) in enumerate(zip(sources, targets))
    ]
    for copy in brought:
        copy.start()

    domains = sent_ref.shape[0]
    pair_total = rank_ref.shape[1]
    face_count = nodes.shape[1]
    strips = layers * rows_y
    brought[0].wait()
    indices = [nodes[corner : corner + 1, :] for corner in range(4)]
    for corner in range(4):
        marks_ref[corner] = marks(indices[corner] & (cols_x - 1), cols_x)

    for copy in brought[2:5]:
        copy.wait()
    rank, face, mortar = rank_ref[...], face_ref[...], mortar_ref[...]
    chosen = lax.broadcasted_iota(jnp.int32, (domains, pair_total), 0) == rank
    before = lax.broadcasted_iota(jnp.int32, (pair_total, pair_total), 0) < lax.broadcasted_iota(
        jnp.int32, (pair_total, pair_total), 1
    )
    earlier = times(chosen.astype(F32).astype(BF16), before.astype(F32).astype(BF16))
    slot = jnp.sum(jnp.where(chosen, earlier, 0.0), axis=0, keepdims=True).astype(jnp.int32)
    place = marks(rank * capacity + slot, domains * capacity)

    brought[1].wait()
    parts = stacked_terms(disp[...].reshape(components * strips, cols_x))
    numbers = lax.broadcasted_iota(jnp.int32, (strips, face_count), 0)
    folds = face_count // cols_x
    for corner in range(4):
        strip = indices[corner] >> halves(cols_x)
        found = summed(times(parts, marks_ref[corner])).reshape(components, strips, face_count)
        values = jnp.sum(jnp.where((numbers == strip)[None], found, 0.0), axis=1)
        for fold in range(folds):
            for k in range(components):
                at = fold * 12 + k * 4 + corner
                rows_ref[at : at + 1, :] = values[k : k + 1, fold * cols_x : (fold + 1) * cols_x]

    rows = rows_ref[...]
    high = rows.shape[0]
    rows_high = high * cols_x // LANES
    copies = []
    for i in range(cols_x // LANES):
        halved[i * high : (i + 1) * high] = rows[:, i * LANES : (i + 1) * LANES]
    for domain in range(domains):
        copies.append(
            pltpu.make_async_copy(
                halved, sent_ref.at[domain, :rows_high], copy_sems.at[0, domain]
            )
        )
        copies[-1].start()

    for copy in brought[5:]:
        copy.wait()
    mortar_rows = looked_up(rows, mortar, cols_x)
    normal = normal_v[...]
    gap = gap_v[...]
    points = gap.shape[0]
    full = points // 8 * 8
    live = lax.broadcasted_iota(jnp.int32, (points, pair_total), 0) < count[...]
    root = jnp.where(live, jnp.sqrt(weight[...]), 0.0)
    turned = []
    for node in range(4):
        mortar_shape = shape[:, 4 + node]
        across = sum(
            normal[k : k + 1] * mortar_rows[k * 4 + node : k * 4 + node + 1] for k in range(3)
        )
        gap = gap - mortar_shape * across
        turned.append(root * mortar_shape)
    for node in range(4):
        turned_ref[node * full : (node + 1) * full] = turned[node][:full]
        turned_ref[4 * full + node : 4 * full + node + 1] = turned[node][full:]
    words = words_of([root * shape[:, node] for node in range(4)], root * gap, normal, face)
    words_ref[...] = words

    group = LANES // capacity
    height = blocks.shape[1]
    extra = group * height - words.shape[0]
    if extra:
        words = jnp.concatenate([words, jnp.zeros((extra, pair_total), F32)], axis=0)
    placed = summed(times_turned(stacked_terms(words), place))
    part = lax.broadcasted_iota(jnp.int32, (height, LANES), 1) >> halves(capacity)
    for domain in range(domains):
        tile, spot = domain // group, domain % group
        block = None
        for j in range(group):
            piece = placed[j * height : (j + 1) * height, tile * LANES : (tile + 1) * LANES]
            if j != spot:
                piece = pltpu.roll(piece, (j - spot) * capacity % LANES, 1)
            block = piece if block is None else jnp.where(part == j, piece, block)
        blocks[domain] = block
        copies.append(
            pltpu.make_async_copy(
                blocks.at[domain], sent_ref.at[domain, rows_high:], copy_sems.at[1, domain]
            )
        )
        copies[-1].start()

    sub = lax.axis_index("sub")
    for target, layer in ((inner_ref, (1 - sub) * (layers - 1)), (outer_ref, sub * (layers - 1))):
        for k in range(components):
            target[k] = disp[k, layer]
        target[components] = modulus[layer]
    for copy in copies:
        copy.wait()


def last_kernel(
    capacity, got_ref, rows_ref, words_ref, turned_ref, mortar_ref, rank_ref, face_ref, nodes_ref,
    marks_ref, internal_ref, mass_ref, out_ref,
):
    domains = got_ref.shape[0]
    components, layers, rows_y, cols_x = out_ref.shape
    strips = layers * rows_y
    face_count = nodes_ref.shape[1]
    pair_total = rank_ref.shape[1]
    folded = rows_ref.shape[0]
    rows_high = folded * cols_x // LANES
    height = got_ref.shape[1] - rows_high
    group = LANES // capacity
    full = (turned_ref.shape[0] - 8) // 4
    own_rows = rows_ref[...]

    rank, face = rank_ref[...], face_ref[...]
    at = marks(face & (cols_x - 1), cols_x)
    step = min(domains, 8)

    def add_step(turn, total):
        block = jnp.concatenate(
            [
                got_ref[pl.ds(turn * step, step), i * folded : (i + 1) * folded].reshape(
                    step * folded, LANES
                )
                for i in range(cols_x // LANES)
            ],
            axis=1,
        )
        found = summed(times(stacked_terms(block), at)).reshape(step, folded, pair_total)
        for i in range(step):
            total = total + jnp.where(rank == turn * step + i, found[i], 0.0)
        return total

    both = jnp.zeros((folded, pair_total), F32)
    if domains == step:
        both = add_step(0, both)
    else:
        both = lax.fori_loop(0, domains // step, add_step, both)
    remote_rows = jnp.where(face < cols_x, both[:12], both[12:])
    pressure, last, normal = weighted_pressure(words_ref[...], full, remote_rows)
    turned = turned_ref[...]
    mortar_forces = forces_of(-normal, loads_on(turned, full, 4 * full, pressure, last))

    part = lax.broadcasted_iota(jnp.int32, (height, LANES), 1) >> halves(capacity)
    pieces = []
    for j in range(group):
        tiles = []
        for tile in range(domains // group):
            block = None
            for spot in range(group):
                piece = got_ref[tile * group + spot, rows_high:]
                if j != spot:
                    piece = pltpu.roll(piece, (spot - j) * capacity % LANES, 1)
                block = piece if block is None else jnp.where(part == spot, piece, block)
            tiles.append(block)
        pieces.append(jnp.concatenate(tiles, axis=1))
    words = jnp.concatenate(pieces, axis=0)
    asked = words[5 * full + 8 : 5 * full + 9].astype(jnp.int32)
    pressure, last, normal = weighted_pressure(words, full, looked_up(own_rows, asked, cols_x))
    remote_forces = forces_of(normal, loads_on(words, full, 5 * full, pressure, last))

    forces = jnp.concatenate([mortar_forces, remote_forces], axis=1)
    at = marks(jnp.concatenate([mortar_ref[...], asked], axis=1), face_count)
    forces = summed(times_turned(stacked_terms(forces), at))
    total = jnp.zeros((2 * components * strips, cols_x), F32)
    parts = [term.astype(F32) for term in terms_of(forces, 2)]
    numbers = lax.broadcasted_iota(jnp.int32, (strips, face_count), 0)
    for corner in range(4):
        index = nodes_ref[corner : corner + 1, :]
        strip = numbers == (index >> halves(cols_x))
        spread = []
        for part in parts:
            for k in range(components):
                at = k * 4 + corner
                spread.append(jnp.where(strip, part[at : at + 1], 0.0).astype(BF16))
        total = total + times_turned(jnp.concatenate(spread, axis=0), marks_ref[corner])
    contact = summed(total).reshape(components, layers, rows_y, cols_x)
    out_ref[...] = (internal_ref[...] + contact) / mass_ref[...][None]


def internal_kernel(
    disp_ref, inner_ref, outer_ref, modulus_ref, stiffness_ref, out_ref
):
    components, layers, rows_y, cols_x = disp_ref.shape
    group = 8
    dofs = 8 * components
    half = dofs // 2

    row = lax.broadcasted_iota(jnp.int32, (dofs * group, dofs), 0) >> halves(group)
    upper = (row >= half).astype(jnp.int32)
    inner = row - half * upper
    dof = (inner >> 2) * 8 + upper * 4 + (inner & 3)
    pick = (dof == lax.broadcasted_iota(jnp.int32, (dofs * group, dofs), 1)).astype(F32).astype(BF16)
    size = dofs * group
    diagonal = (lax.broadcasted_iota(jnp.int32, (size, size), 0) & (group - 1)) == (
        lax.broadcasted_iota(jnp.int32, (size, size), 1) & (group - 1)
    )
    blocks = []
    for term in terms_of(stiffness_ref[...], 2):
        wide = times_turned(times(pick, term).astype(BF16), pick)
        blocks.append(jnp.where(diagonal, wide, 0.0).astype(BF16))

    sub = lax.axis_index("sub")
    below_ref = [jnp.where(sub == 0, outer_ref[k], inner_ref[k]) for k in range(components + 1)]
    above_ref = [jnp.where(sub == 0, inner_ref[k], outer_ref[k]) for k in range(components)]

    def shifted(layer):
        views = []
        for k in range(components):
            for b in range(2):
                moved = layer[k] if b == 0 else pltpu.roll(layer[k], rows_y - 1, 0)
                views.append(moved)
                views.append(pltpu.roll(moved, cols_x - 1, 1))
        return views

    views = [shifted(below_ref)]
    for layer in range(layers):
        views.append(shifted([disp_ref[k, layer] for k in range(components)]))
    views.append(shifted(above_ref))
    inside = (lax.broadcasted_iota(jnp.int32, (rows_y, cols_x), 0) < rows_y - 1) & (
        lax.broadcasted_iota(jnp.int32, (rows_y, cols_x), 1) < cols_x - 1
    )
    scales = [below_ref[components]] + [modulus_ref[layer] for layer in range(layers)]
    scales = [jnp.where(inside, scale, 0.0) for scale in scales]

    lower, higher = [], []
    for e in range(layers + 1):
        kept = slice(half * group, None) if e == 0 else slice(0, half * group if e == layers else None)
        both = jnp.concatenate([block[kept] for block in blocks], axis=0)
        count = both.shape[0] // 2
        strips = []
        for y in range(0, rows_y, group):
            stacked = jnp.concatenate(
                [view[y : y + group] for view in views[e] + views[e + 1]], axis=0
            )
            high, low = terms_of(stacked, 2)
            leading = times(both, high)
            force = leading[:count] + (leading[count:] + times(both[:count], low))
            force = force.reshape(-1, group, cols_x) * scales[e][y : y + group][None]
            strips.append(force)
        forces = jnp.concatenate(strips, axis=1)
        if e < layers:
            higher.append(forces[-half:])
        if e > 0:
            lower.append(forces[:half])
    for layer in range(layers):
        nodal = lower[layer] + higher[layer]
        for k in range(components):
            straight, crossed = [
                nodal[k * 4 + c] + pltpu.roll(nodal[k * 4 + 2 + c], 1, 0) for c in range(2)
            ]
            out_ref[k, layer] = -(straight + pltpu.roll(crossed, 1, 1))


def on_core(kernel, outs, flops, moved, **more):
    return pl.pallas_call(
        kernel,
        out_shape=outs,
        compiler_params=pltpu.CompilerParams(vmem_limit_bytes=48 * 1024 * 1024),
        cost_estimate=pl.CostEstimate(flops=flops, bytes_accessed=moved, transcendentals=0),
        **more,
    )


def swapped(block, axis, first):
    size = lax.axis_size(axis)
    route = []
    for i in range(first, size - 1, 2):
        route += [(i, i + 1), (i + 1, i)]
    return lax.ppermute(block, axis, route)


def shards(
    displacement,
    modulus,
    node_mass,
    stiffness,
    face_nodes,
    pair_mortar,
    pair_rank,
    pair_face,
    pair_count,
    pair_shape,
    pair_weight,
    pair_gap,
    pair_normal,
):
    components, layers, rows_y, cols_x = displacement.shape
    face_count = face_nodes.shape[1]
    pair_total = pair_mortar.shape[0]
    domains = lax.axis_size("dom")
    capacity = max(2, 2 * pair_total // domains)

    points = pair_weight.shape[0]
    full = points // 8 * 8
    group = LANES // capacity
    word_rows = 5 * full + 16
    height = -(-word_rows // (8 * group)) * 8
    rows_high = 12 * face_count // LANES
    line = (1, pair_total)

    def first(*refs):
        first_kernel(capacity, *refs)

    def last(*refs):
        last_kernel(capacity, *refs)

    def shaped(shape, dtype=F32):
        return jax.ShapeDtypeStruct(shape, dtype)

    arrays = [
        face_nodes,
        displacement,
        pair_mortar.reshape(line),
        pair_rank.reshape(line),
        pair_face.reshape(line),
        pair_count.reshape(line),
        pair_weight,
        pair_normal,
        pair_gap,
        jnp.swapaxes(pair_shape, 0, 1),
        modulus,
    ]
    edge = shaped((components + 1, rows_y, cols_x))
    in_hbm = pl.BlockSpec(memory_space=pltpu.HBM)
    in_vmem = pl.BlockSpec(memory_space=pltpu.VMEM)
    kept = [face_nodes, displacement, *arrays[5:]]
    sent, rows, words, turned, mortar, rank, face, inner, outer, along_x = on_core(
        first,
        [
            shaped((domains, rows_high + height, LANES)),
            shaped((12 * face_count // cols_x, cols_x)),
            shaped((word_rows, pair_total)),
            shaped((4 * full + 8, pair_total)),
            shaped(line, jnp.int32),
            shaped(line, jnp.int32),
            shaped(line, jnp.int32),
            edge,
            edge,
            shaped((4, cols_x, face_count), BF16),
        ],
        900_000_000,
        1_500_000,
        in_specs=[in_hbm] * len(arrays),
        out_specs=[in_hbm] + [in_vmem] * 9,
        scratch_shapes=[pltpu.VMEM(x.shape, x.dtype) for x in kept]
        + [
            pltpu.VMEM((rows_high, LANES), F32),
            pltpu.VMEM((domains, height, LANES), F32),
            pltpu.SemaphoreType.DMA((len(arrays),)),
            pltpu.SemaphoreType.DMA((2, domains)),
        ],
    )(*[pltpu.with_memory_space_constraint(x, pltpu.HBM) for x in arrays])
    got = lax.all_to_all(sent, "dom", split_axis=0, concat_axis=0, tiled=True)
    outer = swapped(outer, ("dom", "sub"), 1)
    inner = swapped(inner, ("dom", "sub"), 0)
    internal = on_core(
        internal_kernel, shaped(displacement.shape), 2_000_000_000_000, 700_000
    )(displacement, inner, outer, modulus, stiffness)
    return on_core(last, shaped(displacement.shape), 900_000_000, 1_500_000)(
        got, rows, words, turned, mortar, rank, face, face_nodes, along_x, internal, node_mass
    )


def solution(mesh):
    placed = (
        P(None, ("runs", "dom", "sub"), None, None),
        P(("runs", "dom", "sub"), None, None),
        P(("runs", "dom", "sub"), None, None),
        P(),
        P(None, ("runs", "dom", "sub")),
        P(("runs", "dom", "sub")),
        P(("runs", "dom", "sub"), None),
        P(("runs", "dom", "sub")),
        P(("runs", "dom", "sub")),
        P(None, None, ("runs", "dom", "sub")),
        P(None, ("runs", "dom", "sub")),
        P(None, ("runs", "dom", "sub")),
        P(None, ("runs", "dom", "sub")),
    )
    return jax.shard_map(
        shards,
        mesh=mesh,
        in_specs=placed,
        out_specs=P(None, ("runs", "dom", "sub"), None, None),
        check_vma=False,
    )
```

```python
import jax
import jax.numpy as jnp
from jax import lax
from jax.experimental import pallas as pl
from jax.experimental.pallas import tpu as pltpu
from jax.sharding import PartitionSpec as P

F32 = jnp.float32
BF16 = jnp.bfloat16
LANES = 128


def terms_of(x, count):
    terms = []
    for _ in range(count):
        terms.append(x.astype(BF16))
        x = x - terms[-1].astype(F32)
    return terms


def stacked_terms(x):
    return jnp.concatenate(terms_of(x, 2), axis=0)


def summed(stacked):
    rows = stacked.shape[0] // 2
    return stacked[:rows] + stacked[rows:]


def marks(index, count):
    rows = lax.broadcasted_iota(jnp.int32, (count, index.shape[1]), 0)
    return (rows == index).astype(F32).astype(BF16)


def times(left, right):
    return jnp.dot(left, right, preferred_element_type=F32)


def times_turned(left, right):
    return lax.dot_general(left, right, (((1,), (1,)), ((), ())), preferred_element_type=F32)


def halves(power):
    return power.bit_length() - 1


def looked_up(table, face, width):
    at = marks(face & (width - 1), width)
    both = summed(times(stacked_terms(table), at))
    return jnp.where(face < width, both[:12], both[12:])


def words_of(shapes, gap, normal, face):
    full = gap.shape[0] // 8 * 8
    last = [x[full:] for x in shapes + [gap]]
    blank = jnp.zeros((7, face.shape[1]), F32)
    return jnp.concatenate(
        [x[:full] for x in shapes + [gap]] + last + [normal, face.astype(F32), blank], axis=0
    )


def weighted_pressure(words, full, remote_rows):
    tail = 5 * full
    normal = words[tail + 5 : tail + 8]
    gap, last = words[4 * full : tail], words[tail + 4 : tail + 5]
    for node in range(4):
        across = sum(
            normal[k : k + 1] * remote_rows[k * 4 + node : k * 4 + node + 1] for k in range(3)
        )
        gap = gap + words[node * full : (node + 1) * full] * across
        last = last + words[tail + node : tail + node + 1] * across
    return jnp.maximum(-gap, 0.0), jnp.maximum(-last, 0.0), normal


def loads_on(shapes, full, tail, pressure, last):
    return [
        jnp.sum(pressure * shapes[i * full : (i + 1) * full], axis=0, keepdims=True)
        + last * shapes[tail + i : tail + i + 1]
        for i in range(4)
    ]


def forces_of(normal, loads):
    loads = jnp.concatenate(loads, axis=0)
    return jnp.concatenate([normal[k : k + 1] * loads for k in range(3)], axis=0)


def place_in_group(domain, domains):
    inner = domains // 4
    return {0: inner, inner: 0}.get(domain, domain)


def first_kernel(capacity, *refs):
    (
        nodes_hbm, disp_hbm, mortar_hbm, rank_hbm, face_hbm, count_hbm, weight_hbm, normal_hbm,
        gap_hbm, shape_hbm, modulus_hbm,
        sent_ref, rows_ref, words_ref, turned_ref, mortar_ref, rank_ref, face_ref, inner_ref, outer_ref,
        nodes, disp, count, weight, normal_v, gap_v, shape, modulus, halved, blocks, sems, copy_sems,
    ) = refs
    components, layers, rows_y, cols_x = disp.shape
    sources = (
        nodes_hbm, disp_hbm, rank_hbm, face_hbm, mortar_hbm, count_hbm, weight_hbm, normal_hbm,
        gap_hbm, shape_hbm, modulus_hbm,
    )
    targets = (
        nodes, disp, rank_ref, face_ref, mortar_ref, count, weight, normal_v, gap_v, shape, modulus,
    )
    brought = [
        pltpu.make_async_copy(source, target, sems.at[i])
        for i, (source, target) in enumerate(zip(sources, targets))
    ]
    for copy in brought:
        copy.start()

    domains = sent_ref.shape[0]
    pair_total = rank_ref.shape[1]
    face_count = nodes.shape[1]
    strips = layers * rows_y
    brought[0].wait()
    indices = [nodes[corner : corner + 1, :] for corner in range(4)]
    along_x = [marks(index & (cols_x - 1), cols_x) for index in indices]

    for copy in brought[2:5]:
        copy.wait()
    rank, face, mortar = rank_ref[...], face_ref[...], mortar_ref[...]
    chosen = lax.broadcasted_iota(jnp.int32, (domains, pair_total), 0) == rank
    before = lax.broadcasted_iota(jnp.int32, (pair_total, pair_total), 0) < lax.broadcasted_iota(
        jnp.int32, (pair_total, pair_total), 1
    )
    earlier = times(chosen.astype(F32).astype(BF16), before.astype(F32).astype(BF16))
    slot = jnp.sum(jnp.where(chosen, earlier, 0.0), axis=0, keepdims=True).astype(jnp.int32)
    place = marks(rank * capacity + slot, domains * capacity)

    brought[1].wait()
    parts = stacked_terms(disp[...].reshape(components * strips, cols_x))
    numbers = lax.broadcasted_iota(jnp.int32, (strips, face_count), 0)
    folds = face_count // cols_x
    for corner in range(4):
        strip = indices[corner] >> halves(cols_x)
        found = summed(times(parts, along_x[corner])).reshape(components, strips, face_count)
        values = jnp.sum(jnp.where((numbers == strip)[None], found, 0.0), axis=1)
        for fold in range(folds):
            for k in range(components):
                at = fold * 12 + k * 4 + corner
                rows_ref[at : at + 1, :] = values[k : k + 1, fold * cols_x : (fold + 1) * cols_x]

    rows = rows_ref[...]
    high = rows.shape[0]
    rows_high = high * cols_x // LANES
    copies = []
    for i in range(cols_x // LANES):
        halved[i * high : (i + 1) * high] = rows[:, i * LANES : (i + 1) * LANES]
    for domain in range(domains):
        copies.append(
            pltpu.make_async_copy(
                halved, sent_ref.at[domain, :rows_high], copy_sems.at[0, domain]
            )
        )
        copies[-1].start()

    for copy in brought[5:]:
        copy.wait()
    mortar_rows = looked_up(rows, mortar, cols_x)
    normal = normal_v[...]
    gap = gap_v[...]
    points = gap.shape[0]
    full = points // 8 * 8
    live = lax.broadcasted_iota(jnp.int32, (points, pair_total), 0) < count[...]
    root = jnp.where(live, jnp.sqrt(weight[...]), 0.0)
    turned = []
    for node in range(4):
        mortar_shape = shape[:, 4 + node]
        across = sum(
            normal[k : k + 1] * mortar_rows[k * 4 + node : k * 4 + node + 1] for k in range(3)
        )
        gap = gap - mortar_shape * across
        turned.append(root * mortar_shape)
    for node in range(4):
        turned_ref[node * full : (node + 1) * full] = turned[node][:full]
        turned_ref[4 * full + node : 4 * full + node + 1] = turned[node][full:]
    words = words_of([root * shape[:, node] for node in range(4)], root * gap, normal, face)
    words_ref[...] = words

    group = LANES // capacity
    height = blocks.shape[1]
    extra = group * height - words.shape[0]
    if extra:
        words = jnp.concatenate([words, jnp.zeros((extra, pair_total), F32)], axis=0)
    placed = summed(times_turned(stacked_terms(words), place))
    part = lax.broadcasted_iota(jnp.int32, (height, LANES), 1) >> halves(capacity)
    for domain in range(domains):
        tile, spot = domain // group, domain % group
        block = None
        for j in range(group):
            piece = placed[j * height : (j + 1) * height, tile * LANES : (tile + 1) * LANES]
            if j != spot:
                piece = pltpu.roll(piece, (j - spot) * capacity % LANES, 1)
            block = piece if block is None else jnp.where(part == j, piece, block)
        blocks[domain] = block
        copies.append(
            pltpu.make_async_copy(
                blocks.at[domain],
                sent_ref.at[place_in_group(domain, domains), rows_high:],
                copy_sems.at[1, domain],
            )
        )
        copies[-1].start()

    sub = lax.axis_index("sub")
    for target, layer in ((inner_ref, (1 - sub) * (layers - 1)), (outer_ref, sub * (layers - 1))):
        for k in range(components):
            target[k] = disp[k, layer]
        target[components] = modulus[layer]
    for copy in copies:
        copy.wait()


def last_kernel(
    capacity, got_ref, rows_ref, words_ref, turned_ref, mortar_ref, rank_ref, face_ref, nodes_ref,
    internal_ref, mass_ref, out_ref,
):
    domains = got_ref.shape[0]
    components, layers, rows_y, cols_x = out_ref.shape
    strips = layers * rows_y
    face_count = nodes_ref.shape[1]
    pair_total = rank_ref.shape[1]
    folded = rows_ref.shape[0]
    rows_high = folded * cols_x // LANES
    height = got_ref.shape[1] - rows_high
    group = LANES // capacity
    full = (turned_ref.shape[0] - 8) // 4
    own_rows = rows_ref[...]

    rank, face = rank_ref[...], face_ref[...]
    inner = place_in_group(0, domains)
    place = jnp.where(rank == 0, inner, jnp.where(rank == inner, 0, rank))
    at = marks(face & (cols_x - 1), cols_x)
    step = min(domains, 8)

    def add_step(turn, total):
        block = jnp.concatenate(
            [
                got_ref[pl.ds(turn * step, step), i * folded : (i + 1) * folded].reshape(
                    step * folded, LANES
                )
                for i in range(cols_x // LANES)
            ],
            axis=1,
        )
        found = summed(times(stacked_terms(block), at)).reshape(step, folded, pair_total)
        for i in range(step):
            total = total + jnp.where(place == turn * step + i, found[i], 0.0)
        return total

    both = jnp.zeros((folded, pair_total), F32)
    if domains == step:
        both = add_step(0, both)
    else:
        both = lax.fori_loop(0, domains // step, add_step, both)
    remote_rows = jnp.where(face < cols_x, both[:12], both[12:])
    pressure, last, normal = weighted_pressure(words_ref[...], full, remote_rows)
    turned = turned_ref[...]
    mortar_forces = forces_of(-normal, loads_on(turned, full, 4 * full, pressure, last))

    part = lax.broadcasted_iota(jnp.int32, (height, LANES), 1) >> halves(capacity)
    pieces = []
    for j in range(group):
        tiles = []
        for tile in range(domains // group):
            block = None
            for spot in range(group):
                piece = got_ref[tile * group + spot, rows_high:]
                if j != spot:
                    piece = pltpu.roll(piece, (spot - j) * capacity % LANES, 1)
                block = piece if block is None else jnp.where(part == spot, piece, block)
            tiles.append(block)
        pieces.append(jnp.concatenate(tiles, axis=1))
    words = jnp.concatenate(pieces, axis=0)
    asked = words[5 * full + 8 : 5 * full + 9].astype(jnp.int32)
    pressure, last, normal = weighted_pressure(words, full, looked_up(own_rows, asked, cols_x))
    remote_forces = forces_of(normal, loads_on(words, full, 5 * full, pressure, last))

    forces = jnp.concatenate([mortar_forces, remote_forces], axis=1)
    at = marks(jnp.concatenate([mortar_ref[...], asked], axis=1), face_count)
    forces = summed(times_turned(stacked_terms(forces), at))
    total = jnp.zeros((2 * components * strips, cols_x), F32)
    parts = [term.astype(F32) for term in terms_of(forces, 2)]
    numbers = lax.broadcasted_iota(jnp.int32, (strips, face_count), 0)
    for corner in range(4):
        index = nodes_ref[corner : corner + 1, :]
        along_x = marks(index & (cols_x - 1), cols_x)
        strip = numbers == (index >> halves(cols_x))
        spread = []
        for part in parts:
            for k in range(components):
                at = k * 4 + corner
                spread.append(jnp.where(strip, part[at : at + 1], 0.0).astype(BF16))
        total = total + times_turned(jnp.concatenate(spread, axis=0), along_x)
    contact = summed(total).reshape(components, layers, rows_y, cols_x)
    out_ref[...] = (internal_ref[...] + contact) / mass_ref[...][None]


def internal_kernel(
    disp_ref, inner_ref, outer_ref, modulus_ref, stiffness_ref, out_ref
):
    components, layers, rows_y, cols_x = disp_ref.shape
    group = 8
    dofs = 8 * components
    half = dofs // 2

    row = lax.broadcasted_iota(jnp.int32, (dofs * group, dofs), 0) >> halves(group)
    upper = (row >= half).astype(jnp.int32)
    inner = row - half * upper
    dof = (inner >> 2) * 8 + upper * 4 + (inner & 3)
    pick = (dof == lax.broadcasted_iota(jnp.int32, (dofs * group, dofs), 1)).astype(F32).astype(BF16)
    size = dofs * group
    diagonal = (lax.broadcasted_iota(jnp.int32, (size, size), 0) & (group - 1)) == (
        lax.broadcasted_iota(jnp.int32, (size, size), 1) & (group - 1)
    )
    blocks = []
    for term in terms_of(stiffness_ref[...], 2):
        wide = times_turned(times(pick, term).astype(BF16), pick)
        blocks.append(jnp.where(diagonal, wide, 0.0).astype(BF16))

    sub = lax.axis_index("sub")
    below_ref = [jnp.where(sub == 0, outer_ref[k], inner_ref[k]) for k in range(components + 1)]
    above_ref = [jnp.where(sub == 0, inner_ref[k], outer_ref[k]) for k in range(components)]

    def shifted(layer):
        views = []
        for k in range(components):
            for b in range(2):
                moved = layer[k] if b == 0 else pltpu.roll(layer[k], rows_y - 1, 0)
                views.append(moved)
                views.append(pltpu.roll(moved, cols_x - 1, 1))
        return views

    views = [shifted(below_ref)]
    for layer in range(layers):
        views.append(shifted([disp_ref[k, layer] for k in range(components)]))
    views.append(shifted(above_ref))
    inside = (lax.broadcasted_iota(jnp.int32, (rows_y, cols_x), 0) < rows_y - 1) & (
        lax.broadcasted_iota(jnp.int32, (rows_y, cols_x), 1) < cols_x - 1
    )
    scales = [below_ref[components]] + [modulus_ref[layer] for layer in range(layers)]
    scales = [jnp.where(inside, scale, 0.0) for scale in scales]

    lower, higher = [], []
    for e in range(layers + 1):
        kept = slice(half * group, None) if e == 0 else slice(0, half * group if e == layers else None)
        both = jnp.concatenate([block[kept] for block in blocks], axis=0)
        count = both.shape[0] // 2
        strips = []
        for y in range(0, rows_y, group):
            stacked = jnp.concatenate(
                [view[y : y + group] for view in views[e] + views[e + 1]], axis=0
            )
            high, low = terms_of(stacked, 2)
            leading = times(both, high)
            force = leading[:count] + (leading[count:] + times(both[:count], low))
            force = force.reshape(-1, group, cols_x) * scales[e][y : y + group][None]
            strips.append(force)
        forces = jnp.concatenate(strips, axis=1)
        if e < layers:
            higher.append(forces[-half:])
        if e > 0:
            lower.append(forces[:half])
    for layer in range(layers):
        nodal = lower[layer] + higher[layer]
        for k in range(components):
            straight, crossed = [
                nodal[k * 4 + c] + pltpu.roll(nodal[k * 4 + 2 + c], 1, 0) for c in range(2)
            ]
            out_ref[k, layer] = -(straight + pltpu.roll(crossed, 1, 1))


def on_core(kernel, outs, flops, moved, **more):
    return pl.pallas_call(
        kernel,
        out_shape=outs,
        compiler_params=pltpu.CompilerParams(vmem_limit_bytes=48 * 1024 * 1024),
        cost_estimate=pl.CostEstimate(flops=flops, bytes_accessed=moved, transcendentals=0),
        **more,
    )


def swapped(block, axis, first):
    size = lax.axis_size(axis)
    route = []
    for i in range(first, size - 1, 2):
        route += [(i, i + 1), (i + 1, i)]
    return lax.ppermute(block, axis, route)


def shards(
    displacement,
    modulus,
    node_mass,
    stiffness,
    face_nodes,
    pair_mortar,
    pair_rank,
    pair_face,
    pair_count,
    pair_shape,
    pair_weight,
    pair_gap,
    pair_normal,
):
    components, layers, rows_y, cols_x = displacement.shape
    face_count = face_nodes.shape[1]
    pair_total = pair_mortar.shape[0]
    domains = lax.axis_size("dom")
    capacity = max(2, 2 * pair_total // domains)

    points = pair_weight.shape[0]
    full = points // 8 * 8
    group = LANES // capacity
    word_rows = 5 * full + 16
    height = -(-word_rows // (8 * group)) * 8
    rows_high = 12 * face_count // LANES
    line = (1, pair_total)

    def first(*refs):
        first_kernel(capacity, *refs)

    def last(*refs):
        last_kernel(capacity, *refs)

    def shaped(shape, dtype=F32):
        return jax.ShapeDtypeStruct(shape, dtype)

    arrays = [
        face_nodes,
        displacement,
        pair_mortar.reshape(line),
        pair_rank.reshape(line),
        pair_face.reshape(line),
        pair_count.reshape(line),
        pair_weight,
        pair_normal,
        pair_gap,
        jnp.swapaxes(pair_shape, 0, 1),
        modulus,
    ]
    edge = shaped((components + 1, rows_y, cols_x))
    in_hbm = pl.BlockSpec(memory_space=pltpu.HBM)
    in_vmem = pl.BlockSpec(memory_space=pltpu.VMEM)
    kept = [face_nodes, displacement, *arrays[5:]]
    sent, rows, words, turned, mortar, rank, face, inner, outer = on_core(
        first,
        [
            shaped((domains, rows_high + height, LANES)),
            shaped((12 * face_count // cols_x, cols_x)),
            shaped((word_rows, pair_total)),
            shaped((4 * full + 8, pair_total)),
            shaped(line, jnp.int32),
            shaped(line, jnp.int32),
            shaped(line, jnp.int32),
            edge,
            edge,
        ],
        900_000_000,
        1_500_000,
        in_specs=[in_hbm] * len(arrays),
        out_specs=[in_hbm] + [in_vmem] * 8,
        scratch_shapes=[pltpu.VMEM(x.shape, x.dtype) for x in kept]
        + [
            pltpu.VMEM((rows_high, LANES), F32),
            pltpu.VMEM((domains, height, LANES), F32),
            pltpu.SemaphoreType.DMA((len(arrays),)),
            pltpu.SemaphoreType.DMA((2, domains)),
        ],
    )(*[pltpu.with_memory_space_constraint(x, pltpu.HBM) for x in arrays])
    order = [place_in_group(domain, domains) for domain in range(domains)]
    got = lax.all_to_all(
        sent, "dom", split_axis=0, concat_axis=0, axis_index_groups=[order], tiled=True
    )
    outer = swapped(outer, ("dom", "sub"), 1)
    inner = swapped(inner, ("dom", "sub"), 0)
    internal = on_core(
        internal_kernel, shaped(displacement.shape), 1_500_000_000, 700_000
    )(displacement, inner, outer, modulus, stiffness)
    return on_core(last, shaped(displacement.shape), 900_000_000, 1_500_000)(
        got, rows, words, turned, mortar, rank, face, face_nodes, internal, node_mass
    )


def solution(mesh):
    placed = (
        P(None, ("runs", "dom", "sub"), None, None),
        P(("runs", "dom", "sub"), None, None),
        P(("runs", "dom", "sub"), None, None),
        P(),
        P(None, ("runs", "dom", "sub")),
        P(("runs", "dom", "sub")),
        P(("runs", "dom", "sub"), None),
        P(("runs", "dom", "sub")),
        P(("runs", "dom", "sub")),
        P(None, None, ("runs", "dom", "sub")),
        P(None, ("runs", "dom", "sub")),
        P(None, ("runs", "dom", "sub")),
        P(None, ("runs", "dom", "sub")),
    )
    return jax.shard_map(
        shards,
        mesh=mesh,
        in_specs=placed,
        out_specs=P(None, ("runs", "dom", "sub"), None, None),
        check_vma=False,
    )
```

```python
import jax
import jax.numpy as jnp
from jax import lax
from jax.experimental import pallas as pl
from jax.experimental.pallas import tpu as pltpu
from jax.sharding import PartitionSpec as P

F32 = jnp.float32
BF16 = jnp.bfloat16
LANES = 128


def terms_of(x, count):
    terms = []
    for _ in range(count):
        terms.append(x.astype(BF16))
        x = x - terms[-1].astype(F32)
    return terms


def stacked_terms(x):
    return jnp.concatenate(terms_of(x, 2), axis=0)


def summed(stacked):
    rows = stacked.shape[0] // 2
    return stacked[:rows] + stacked[rows:]


def marks(index, count):
    rows = lax.broadcasted_iota(jnp.int32, (count, index.shape[1]), 0)
    return (rows == index).astype(F32).astype(BF16)


def times(left, right):
    return jnp.dot(left, right, preferred_element_type=F32)


def times_turned(left, right):
    return lax.dot_general(left, right, (((1,), (1,)), ((), ())), preferred_element_type=F32)


def halves(power):
    return power.bit_length() - 1


def looked_up(table, face, width):
    at = marks(face & (width - 1), width)
    both = summed(times(stacked_terms(table), at))
    return jnp.where(face < width, both[:12], both[12:])


def words_of(shapes, gap, normal, face):
    full = gap.shape[0] // 8 * 8
    last = [x[full:] for x in shapes + [gap]]
    blank = jnp.zeros((7, face.shape[1]), F32)
    return jnp.concatenate(
        [x[:full] for x in shapes + [gap]] + last + [normal, face.astype(F32), blank], axis=0
    )


def weighted_pressure(words, full, remote_rows):
    tail = 5 * full
    normal = words[tail + 5 : tail + 8]
    gap, last = words[4 * full : tail], words[tail + 4 : tail + 5]
    for node in range(4):
        across = sum(
            normal[k : k + 1] * remote_rows[k * 4 + node : k * 4 + node + 1] for k in range(3)
        )
        gap = gap + words[node * full : (node + 1) * full] * across
        last = last + words[tail + node : tail + node + 1] * across
    return jnp.maximum(-gap, 0.0), jnp.maximum(-last, 0.0), normal


def loads_on(shapes, full, tail, pressure, last):
    return [
        jnp.sum(pressure * shapes[i * full : (i + 1) * full], axis=0, keepdims=True)
        + last * shapes[tail + i : tail + i + 1]
        for i in range(4)
    ]


def forces_of(normal, loads):
    loads = jnp.concatenate(loads, axis=0)
    return jnp.concatenate([normal[k : k + 1] * loads for k in range(3)], axis=0)


def place_in_group(domain, domains):
    return {0: domains - 1, domains - 1: 0}.get(domain, domain)


def first_kernel(capacity, *refs):
    (
        nodes_hbm, disp_hbm, mortar_hbm, rank_hbm, face_hbm, count_hbm, weight_hbm, normal_hbm,
        gap_hbm, shape_hbm, modulus_hbm, mass_hbm,
        sent_ref, rows_ref, words_ref, turned_ref, mortar_ref, rank_ref, face_ref, nodes, mass_ref,
        inner_ref, outer_ref,
        disp, count, weight, normal_v, gap_v, shape, modulus, halved, blocks, sems, copy_sems,
    ) = refs
    components, layers, rows_y, cols_x = disp.shape
    sources = (
        nodes_hbm, disp_hbm, rank_hbm, face_hbm, mortar_hbm, shape_hbm, count_hbm, weight_hbm,
        normal_hbm, gap_hbm, modulus_hbm, mass_hbm,
    )
    targets = (
        nodes, disp, rank_ref, face_ref, mortar_ref, shape, count, weight, normal_v, gap_v, modulus,
        mass_ref,
    )
    brought = [
        pltpu.make_async_copy(source, target, sems.at[i])
        for i, (source, target) in enumerate(zip(sources, targets))
    ]
    for copy in brought:
        copy.start()

    domains = sent_ref.shape[0]
    pair_total = rank_ref.shape[1]
    face_count = nodes.shape[1]
    strips = layers * rows_y
    for copy in brought[:-2]:
        copy.wait()
    indices = [nodes[corner : corner + 1, :] for corner in range(4)]
    along_x = [marks(index & (cols_x - 1), cols_x) for index in indices]

    rank, face, mortar = rank_ref[...], face_ref[...], mortar_ref[...]
    chosen = lax.broadcasted_iota(jnp.int32, (domains, pair_total), 0) == rank
    before = lax.broadcasted_iota(jnp.int32, (pair_total, pair_total), 0) < lax.broadcasted_iota(
        jnp.int32, (pair_total, pair_total), 1
    )
    earlier = times(chosen.astype(F32).astype(BF16), before.astype(F32).astype(BF16))
    slot = jnp.sum(jnp.where(chosen, earlier, 0.0), axis=0, keepdims=True).astype(jnp.int32)
    place = marks(rank * capacity + slot, domains * capacity)

    parts = stacked_terms(disp[...].reshape(components * strips, cols_x))
    numbers = lax.broadcasted_iota(jnp.int32, (strips, face_count), 0)
    folds = face_count // cols_x
    for corner in range(4):
        strip = indices[corner] >> halves(cols_x)
        found = summed(times(parts, along_x[corner])).reshape(components, strips, face_count)
        values = jnp.sum(jnp.where((numbers == strip)[None], found, 0.0), axis=1)
        for fold in range(folds):
            for k in range(components):
                at = fold * 12 + k * 4 + corner
                rows_ref[at : at + 1, :] = values[k : k + 1, fold * cols_x : (fold + 1) * cols_x]

    rows = rows_ref[...]
    high = rows.shape[0]
    rows_high = high * cols_x // LANES
    copies = []
    for i in range(cols_x // LANES):
        halved[i * high : (i + 1) * high] = rows[:, i * LANES : (i + 1) * LANES]
    for domain in range(domains):
        copies.append(
            pltpu.make_async_copy(
                halved, sent_ref.at[domain, :rows_high], copy_sems.at[0, domain]
            )
        )
        copies[-1].start()

    mortar_rows = looked_up(rows, mortar, cols_x)
    normal = normal_v[...]
    gap = gap_v[...]
    points = gap.shape[0]
    full = points // 8 * 8
    live = lax.broadcasted_iota(jnp.int32, (points, pair_total), 0) < count[...]
    root = jnp.where(live, jnp.sqrt(weight[...]), 0.0)
    turned = []
    for node in range(4):
        mortar_shape = shape[:, 4 + node]
        across = sum(
            normal[k : k + 1] * mortar_rows[k * 4 + node : k * 4 + node + 1] for k in range(3)
        )
        gap = gap - mortar_shape * across
        turned.append(root * mortar_shape)
    for node in range(4):
        turned_ref[node * full : (node + 1) * full] = turned[node][:full]
        turned_ref[4 * full + node : 4 * full + node + 1] = turned[node][full:]
    words = words_of([root * shape[:, node] for node in range(4)], root * gap, normal, face)
    words_ref[...] = words

    group = LANES // capacity
    height = blocks.shape[1]
    extra = group * height - words.shape[0]
    if extra:
        words = jnp.concatenate([words, jnp.zeros((extra, pair_total), F32)], axis=0)
    placed = summed(times_turned(stacked_terms(words), place))
    part = lax.broadcasted_iota(jnp.int32, (height, LANES), 1) >> halves(capacity)
    for domain in range(domains):
        tile, spot = domain // group, domain % group
        block = None
        for j in range(group):
            piece = placed[j * height : (j + 1) * height, tile * LANES : (tile + 1) * LANES]
            if j != spot:
                piece = pltpu.roll(piece, (j - spot) * capacity % LANES, 1)
            block = piece if block is None else jnp.where(part == j, piece, block)
        blocks[domain] = block
        copies.append(
            pltpu.make_async_copy(
                blocks.at[domain],
                sent_ref.at[place_in_group(domain, domains), rows_high:],
                copy_sems.at[1, domain],
            )
        )
        copies[-1].start()

    for copy in brought[-2:]:
        copy.wait()
    sub = lax.axis_index("sub")
    for target, layer in ((inner_ref, (1 - sub) * (layers - 1)), (outer_ref, sub * (layers - 1))):
        for k in range(components):
            target[k] = disp[k, layer]
        target[components] = modulus[layer]
    for copy in copies:
        copy.wait()


def last_kernel(
    capacity, got_ref, rows_ref, words_ref, turned_ref, mortar_ref, rank_ref, face_ref, nodes_ref,
    mass_ref, internal_ref, blocks_ref, own_ref, halo_ref, out_ref,
):
    domains = got_ref.shape[0]
    components, layers, rows_y, cols_x = out_ref.shape
    strips = layers * rows_y
    face_count = nodes_ref.shape[1]
    pair_total = rank_ref.shape[1]
    folded = rows_ref.shape[0]
    rows_high = folded * cols_x // LANES
    height = got_ref.shape[1] - rows_high
    group = LANES // capacity
    full = (turned_ref.shape[0] - 8) // 4
    own_rows = rows_ref[...]

    rank, face = rank_ref[...], face_ref[...]
    end = domains - 1
    place = jnp.where(rank == 0, end, jnp.where(rank == end, 0, rank))
    at = marks(face & (cols_x - 1), cols_x)
    step = min(domains, 8)

    def add_step(turn, total):
        block = jnp.concatenate(
            [
                got_ref[pl.ds(turn * step, step), i * folded : (i + 1) * folded].reshape(
                    step * folded, LANES
                )
                for i in range(cols_x // LANES)
            ],
            axis=1,
        )
        found = summed(times(stacked_terms(block), at)).reshape(step, folded, pair_total)
        for i in range(step):
            total = total + jnp.where(place == turn * step + i, found[i], 0.0)
        return total

    both = jnp.zeros((folded, pair_total), F32)
    if domains == step:
        both = add_step(0, both)
    else:
        both = lax.fori_loop(0, domains // step, add_step, both)
    remote_rows = jnp.where(face < cols_x, both[:12], both[12:])
    pressure, last, normal = weighted_pressure(words_ref[...], full, remote_rows)
    turned = turned_ref[...]
    mortar_forces = forces_of(-normal, loads_on(turned, full, 4 * full, pressure, last))

    part = lax.broadcasted_iota(jnp.int32, (height, LANES), 1) >> halves(capacity)
    pieces = []
    for j in range(group):
        tiles = []
        for tile in range(domains // group):
            block = None
            for spot in range(group):
                piece = got_ref[tile * group + spot, rows_high:]
                if j != spot:
                    piece = pltpu.roll(piece, (spot - j) * capacity % LANES, 1)
                block = piece if block is None else jnp.where(part == spot, piece, block)
            tiles.append(block)
        pieces.append(jnp.concatenate(tiles, axis=1))
    words = jnp.concatenate(pieces, axis=0)
    asked = words[5 * full + 8 : 5 * full + 9].astype(jnp.int32)
    pressure, last, normal = weighted_pressure(words, full, looked_up(own_rows, asked, cols_x))
    remote_forces = forces_of(normal, loads_on(words, full, 5 * full, pressure, last))

    forces = jnp.concatenate([mortar_forces, remote_forces], axis=1)
    at = marks(jnp.concatenate([mortar_ref[...], asked], axis=1), face_count)
    forces = summed(times_turned(stacked_terms(forces), at))
    total = jnp.zeros((2 * components * strips, cols_x), F32)
    parts = [term.astype(F32) for term in terms_of(forces, 2)]
    numbers = lax.broadcasted_iota(jnp.int32, (strips, face_count), 0)
    for corner in range(4):
        index = nodes_ref[corner : corner + 1, :]
        along_x = marks(index & (cols_x - 1), cols_x)
        strip = numbers == (index >> halves(cols_x))
        spread = []
        for part in parts:
            for k in range(components):
                at = k * 4 + corner
                spread.append(jnp.where(strip, part[at : at + 1], 0.0).astype(BF16))
        total = total + times_turned(jnp.concatenate(spread, axis=0), along_x)
    contact = summed(total).reshape(components, layers, rows_y, cols_x)
    upward = lax.axis_index("sub") == 1
    edge = edge_part(upward, own_ref, halo_ref, blocks_ref)
    at = jnp.where(upward, layers - 1, 0)
    for layer in range(layers):
        for k in range(components):
            nodal = internal_ref[k, layer] + jnp.where(at == layer, edge[k], 0.0)
            out_ref[k, layer] = (nodal + contact[k, layer]) / mass_ref[layer]


GROUP = 8


def shifted(layer):
    views = []
    for part in layer:
        rows_y, cols_x = part.shape
        for moved in (part, pltpu.roll(part, rows_y - 1, 0)):
            views += [moved, pltpu.roll(moved, cols_x - 1, 1)]
    return views


def element_forces(matrices, low, high, modulus):
    rows_y, cols_x = modulus.shape
    inside = (lax.broadcasted_iota(jnp.int32, (rows_y, cols_x), 0) < rows_y - 1) & (
        lax.broadcasted_iota(jnp.int32, (rows_y, cols_x), 1) < cols_x - 1
    )
    scale = jnp.where(inside, modulus, 0.0)
    views = shifted(low) + shifted(high)
    both = jnp.concatenate(matrices, axis=0)
    count = both.shape[0] // 2
    strips = []
    for y in range(0, rows_y, GROUP):
        leading, second = terms_of(jnp.concatenate([view[y : y + GROUP] for view in views], axis=0), 2)
        found = times(both, leading)
        force = found[:count] + (found[count:] + times(matrices[0], second))
        strips.append(force.reshape(-1, GROUP, cols_x) * scale[y : y + GROUP][None])
    return jnp.concatenate(strips, axis=1)


def on_nodes(forces):
    sums = []
    for k in range(forces.shape[0] // 4):
        straight, crossed = [
            forces[k * 4 + c] + pltpu.roll(forces[k * 4 + 2 + c], 1, 0) for c in range(2)
        ]
        sums.append(-(straight + pltpu.roll(crossed, 1, 1)))
    return sums


def edge_part(upward, own_ref, halo_ref, blocks_ref):
    components = own_ref.shape[0] - 1
    size = blocks_ref.shape[1]
    rows = size // 2
    start = jnp.where(upward, 0, rows)
    matrices = [
        blocks_ref[pl.ds(pl.multiple_of(term * size + start, 16), rows)] for term in range(2)
    ]
    low = [jnp.where(upward, own_ref[k], halo_ref[k]) for k in range(components + 1)]
    high = [jnp.where(upward, halo_ref[k], own_ref[k]) for k in range(components)]
    return on_nodes(element_forces(matrices, low[:components], high, low[components]))


def internal_kernel(disp_ref, modulus_ref, stiffness_ref, own_ref, halo_ref, out_ref, blocks_ref):
    components, layers, rows_y, cols_x = disp_ref.shape
    dofs = 8 * components
    half = dofs // 2
    size = dofs * GROUP

    row = lax.broadcasted_iota(jnp.int32, (size, dofs), 0) >> halves(GROUP)
    upper = (row >= half).astype(jnp.int32)
    inner = row - half * upper
    dof = (inner >> 2) * 8 + upper * 4 + (inner & 3)
    pick = (dof == lax.broadcasted_iota(jnp.int32, (size, dofs), 1)).astype(F32).astype(BF16)
    diagonal = (lax.broadcasted_iota(jnp.int32, (size, size), 0) & (GROUP - 1)) == (
        lax.broadcasted_iota(jnp.int32, (size, size), 1) & (GROUP - 1)
    )
    for i, term in enumerate(terms_of(stiffness_ref[...], 2)):
        wide = times_turned(times(pick, term).astype(BF16), pick)
        blocks_ref[i * size : (i + 1) * size] = jnp.where(diagonal, wide, 0.0).astype(BF16)

    blocks = [blocks_ref[i * size : (i + 1) * size] for i in range(2)]
    sums = [[0.0] * components for _ in range(layers)]
    for e in range(layers - 1):
        pair = [[disp_ref[k, e + a] for k in range(components)] for a in range(2)]
        forces = element_forces(blocks, pair[0], pair[1], modulus_ref[e])
        for a in range(2):
            part = on_nodes(forces[a * half : (a + 1) * half])
            sums[e + a] = [x + y for x, y in zip(sums[e + a], part)]
    upward = lax.axis_index("sub") == 0
    edge = edge_part(upward, own_ref, halo_ref, blocks_ref)
    at = jnp.where(upward, layers - 1, 0)
    for layer in range(layers):
        for k in range(components):
            out_ref[k, layer] = sums[layer][k] + jnp.where(at == layer, edge[k], 0.0)


def on_core(kernel, outs, flops, moved, **more):
    return pl.pallas_call(
        kernel,
        out_shape=outs,
        compiler_params=pltpu.CompilerParams(vmem_limit_bytes=48 * 1024 * 1024),
        cost_estimate=pl.CostEstimate(flops=flops, bytes_accessed=moved, transcendentals=0),
        **more,
    )


def swapped(block, axis, first):
    size = lax.axis_size(axis)
    route = []
    for i in range(first, size - 1, 2):
        route += [(i, i + 1), (i + 1, i)]
    return lax.ppermute(block, axis, route)


def shards(
    displacement,
    modulus,
    node_mass,
    stiffness,
    face_nodes,
    pair_mortar,
    pair_rank,
    pair_face,
    pair_count,
    pair_shape,
    pair_weight,
    pair_gap,
    pair_normal,
):
    components, layers, rows_y, cols_x = displacement.shape
    face_count = face_nodes.shape[1]
    pair_total = pair_mortar.shape[0]
    domains = lax.axis_size("dom")
    capacity = max(2, 2 * pair_total // domains)

    points = pair_weight.shape[0]
    full = points // 8 * 8
    group = LANES // capacity
    word_rows = 5 * full + 16
    height = -(-word_rows // (8 * group)) * 8
    rows_high = 12 * face_count // LANES
    line = (1, pair_total)

    def first(*refs):
        first_kernel(capacity, *refs)

    def last(*refs):
        last_kernel(capacity, *refs)

    def shaped(shape, dtype=F32):
        return jax.ShapeDtypeStruct(shape, dtype)

    arrays = [
        face_nodes,
        displacement,
        pair_mortar.reshape(line),
        pair_rank.reshape(line),
        pair_face.reshape(line),
        pair_count.reshape(line),
        pair_weight,
        pair_normal,
        pair_gap,
        jnp.swapaxes(pair_shape, 0, 1),
        modulus,
        node_mass,
    ]
    edge = shaped((components + 1, rows_y, cols_x))
    in_hbm = pl.BlockSpec(memory_space=pltpu.HBM)
    in_vmem = pl.BlockSpec(memory_space=pltpu.VMEM)
    kept = [displacement, *arrays[5:-1]]
    sent, rows, words, turned, mortar, rank, face, nodes, mass, inner, outer = on_core(
        first,
        [
            shaped((domains, rows_high + height, LANES)),
            shaped((12 * face_count // cols_x, cols_x)),
            shaped((word_rows, pair_total)),
            shaped((4 * full + 8, pair_total)),
            shaped(line, jnp.int32),
            shaped(line, jnp.int32),
            shaped(line, jnp.int32),
            shaped(face_nodes.shape, jnp.int32),
            shaped(node_mass.shape),
            edge,
            edge,
        ],
        900_000_000,
        1_500_000,
        in_specs=[in_hbm] * len(arrays),
        out_specs=[in_hbm] + [in_vmem] * 10,
        scratch_shapes=[pltpu.VMEM(x.shape, x.dtype) for x in kept]
        + [
            pltpu.VMEM((rows_high, LANES), F32),
            pltpu.VMEM((domains, height, LANES), F32),
            pltpu.SemaphoreType.DMA((len(arrays),)),
            pltpu.SemaphoreType.DMA((2, domains)),
        ],
    )(*[pltpu.with_memory_space_constraint(x, pltpu.HBM) for x in arrays])
    order = [place_in_group(domain, domains) for domain in range(domains)]
    got = lax.all_to_all(
        sent, "dom", split_axis=0, concat_axis=0, axis_index_groups=[order], tiled=True
    )
    inner_halo = swapped(inner, ("dom", "sub"), 0)
    outer_halo = swapped(outer, ("dom", "sub"), 1)
    size = 8 * components * GROUP
    internal, blocks = on_core(
        internal_kernel,
        [shaped(displacement.shape), shaped((2 * size, size), BF16)],
        1_000_000_000,
        700_000,
    )(displacement, modulus, stiffness, inner, inner_halo)
    return on_core(last, shaped(displacement.shape), 1_000_000_000, 1_500_000)(
        got, rows, words, turned, mortar, rank, face, nodes, mass, internal, blocks, outer, outer_halo
    )


def solution(mesh):
    placed = (
        P(None, ("runs", "dom", "sub"), None, None),
        P(("runs", "dom", "sub"), None, None),
        P(("runs", "dom", "sub"), None, None),
        P(),
        P(None, ("runs", "dom", "sub")),
        P(("runs", "dom", "sub")),
        P(("runs", "dom", "sub"), None),
        P(("runs", "dom", "sub")),
        P(("runs", "dom", "sub")),
        P(None, None, ("runs", "dom", "sub")),
        P(None, ("runs", "dom", "sub")),
        P(None, ("runs", "dom", "sub")),
        P(None, ("runs", "dom", "sub")),
    )
    return jax.shard_map(
        shards,
        mesh=mesh,
        in_specs=placed,
        out_specs=P(None, ("runs", "dom", "sub"), None, None),
        check_vma=False,
    )
```

```python
import jax
import jax.numpy as jnp
from jax import lax
from jax.experimental import pallas as pl
from jax.experimental.pallas import tpu as pltpu
from jax.sharding import PartitionSpec as P

F32 = jnp.float32
BF16 = jnp.bfloat16
LANES = 128


def terms_of(x, count):
    terms = []
    for _ in range(count):
        terms.append(x.astype(BF16))
        x = x - terms[-1].astype(F32)
    return terms


def stacked_terms(x):
    return jnp.concatenate(terms_of(x, 2), axis=0)


def summed(stacked):
    rows = stacked.shape[0] // 2
    return stacked[:rows] + stacked[rows:]


def marks(index, count):
    rows = lax.broadcasted_iota(jnp.int32, (count, index.shape[1]), 0)
    return (rows == index).astype(F32).astype(BF16)


def times(left, right):
    return jnp.dot(left, right, preferred_element_type=F32)


def times_turned(left, right):
    return lax.dot_general(left, right, (((1,), (1,)), ((), ())), preferred_element_type=F32)


def halves(power):
    return power.bit_length() - 1


def looked_up(table, face, width):
    at = marks(face & (width - 1), width)
    both = summed(times(stacked_terms(table), at))
    return jnp.where(face < width, both[:12], both[12:])


def words_of(shapes, gap, normal, face):
    full = gap.shape[0] // 8 * 8
    last = [x[full:] for x in shapes + [gap]]
    blank = jnp.zeros((7, face.shape[1]), F32)
    return jnp.concatenate(
        [x[:full] for x in shapes + [gap]] + last + [normal, face.astype(F32), blank], axis=0
    )


def weighted_pressure(words, full, remote_rows):
    tail = 5 * full
    normal = words[tail + 5 : tail + 8]
    gap, last = words[4 * full : tail], words[tail + 4 : tail + 5]
    for node in range(4):
        across = sum(
            normal[k : k + 1] * remote_rows[k * 4 + node : k * 4 + node + 1] for k in range(3)
        )
        gap = gap + words[node * full : (node + 1) * full] * across
        last = last + words[tail + node : tail + node + 1] * across
    return jnp.maximum(-gap, 0.0), jnp.maximum(-last, 0.0), normal


def loads_on(shapes, full, tail, pressure, last):
    return [
        jnp.sum(pressure * shapes[i * full : (i + 1) * full], axis=0, keepdims=True)
        + last * shapes[tail + i : tail + i + 1]
        for i in range(4)
    ]


def forces_of(normal, loads):
    loads = jnp.concatenate(loads, axis=0)
    return jnp.concatenate([normal[k : k + 1] * loads for k in range(3)], axis=0)


def place_in_group(domain, domains):
    return {0: domains - 1, domains - 1: 0}.get(domain, domain)


def first_kernel(passed, *refs):
    nodes_hbm, disp_hbm, modulus_hbm, *refs = refs
    ins, refs = refs[:passed], refs[passed:]
    sent_ref, rows_ref, inner_ref, outer_ref, nodes, *refs = refs
    outs, refs = refs[:passed], refs[passed:]
    disp, modulus, sems, copy_sems = refs
    components, layers, rows_y, cols_x = disp.shape
    sources = [nodes_hbm, disp_hbm, modulus_hbm, *ins]
    brought = [
        pltpu.make_async_copy(source, target, sems.at[i])
        for i, (source, target) in enumerate(zip(sources, [nodes, disp, modulus, *outs]))
    ]
    for copy in brought:
        copy.start()

    domains = sent_ref.shape[0]
    face_count = nodes.shape[1]
    strips = layers * rows_y
    brought[0].wait()
    indices = [nodes[corner : corner + 1, :] for corner in range(4)]
    along_x = [marks(index & (cols_x - 1), cols_x) for index in indices]
    brought[1].wait()
    parts = stacked_terms(disp[...].reshape(components * strips, cols_x))
    numbers = lax.broadcasted_iota(jnp.int32, (strips, face_count), 0)
    folds = face_count // cols_x
    for corner in range(4):
        strip = indices[corner] >> halves(cols_x)
        found = summed(times(parts, along_x[corner])).reshape(components, strips, face_count)
        values = jnp.sum(jnp.where((numbers == strip)[None], found, 0.0), axis=1)
        for fold in range(folds):
            for k in range(components):
                at = fold * 12 + k * 4 + corner
                rows_ref[at : at + 1, :] = values[k : k + 1, fold * cols_x : (fold + 1) * cols_x]
    copies = [
        pltpu.make_async_copy(rows_ref, sent_ref.at[domain], copy_sems.at[domain])
        for domain in range(domains)
    ]
    for copy in copies:
        copy.start()

    brought[2].wait()
    sub = lax.axis_index("sub")
    for target, layer in ((inner_ref, (1 - sub) * (layers - 1)), (outer_ref, sub * (layers - 1))):
        for k in range(components):
            target[k] = disp[k, layer]
        target[components] = modulus[layer]
    for copy in brought[3:] + copies:
        copy.wait()


def words_kernel(
    capacity, rows_ref, mortar_ref, rank_ref, face_ref, count_ref, weight_ref, normal_ref, gap_ref,
    shape_ref, sent_ref, words_ref, turned_ref,
):
    domains, height = sent_ref.shape[:2]
    pair_total = rank_ref.shape[1]
    cols_x = rows_ref.shape[1]
    rank, face = rank_ref[...], face_ref[...]

    chosen = lax.broadcasted_iota(jnp.int32, (domains, pair_total), 0) == rank
    before = lax.broadcasted_iota(jnp.int32, (pair_total, pair_total), 0) < lax.broadcasted_iota(
        jnp.int32, (pair_total, pair_total), 1
    )
    earlier = times(chosen.astype(F32).astype(BF16), before.astype(F32).astype(BF16))
    slot = jnp.sum(jnp.where(chosen, earlier, 0.0), axis=0, keepdims=True).astype(jnp.int32)
    place = marks(rank * capacity + slot, domains * capacity)

    mortar_rows = looked_up(rows_ref[...], mortar_ref[...], cols_x)
    normal = normal_ref[...]
    gap = gap_ref[...]
    points = gap.shape[0]
    full = points // 8 * 8
    live = lax.broadcasted_iota(jnp.int32, (points, pair_total), 0) < count_ref[...]
    root = jnp.where(live, jnp.sqrt(weight_ref[...]), 0.0)
    turned = []
    for node in range(4):
        mortar_shape = shape_ref[:, 4 + node]
        across = sum(
            normal[k : k + 1] * mortar_rows[k * 4 + node : k * 4 + node + 1] for k in range(3)
        )
        gap = gap - mortar_shape * across
        turned.append(root * mortar_shape)
    words = words_of([root * shape_ref[:, node] for node in range(4)], root * gap, normal, face)
    words_ref[...] = words
    for node in range(4):
        turned_ref[node * full : (node + 1) * full] = turned[node][:full]
        turned_ref[4 * full + node : 4 * full + node + 1] = turned[node][full:]

    group = LANES // capacity
    extra = group * height - words.shape[0]
    if extra:
        words = jnp.concatenate([words, jnp.zeros((extra, pair_total), F32)], axis=0)
    placed = summed(times_turned(stacked_terms(words), place))
    part = lax.broadcasted_iota(jnp.int32, (height, LANES), 1) >> halves(capacity)
    for domain in range(domains):
        tile, spot = domain // group, domain % group
        block = None
        for j in range(group):
            piece = placed[j * height : (j + 1) * height, tile * LANES : (tile + 1) * LANES]
            if j != spot:
                piece = pltpu.roll(piece, (j - spot) * capacity % LANES, 1)
            block = piece if block is None else jnp.where(part == j, piece, block)
        sent_ref[domain] = block


def summed_on_faces(forces, faces, face_count):
    return summed(times_turned(stacked_terms(forces), marks(faces, face_count)))


def own_pairs_kernel(
    got_ref, words_ref, turned_ref, mortar_ref, rank_ref, face_ref, faces_ref
):
    domains, folded, cols_x = got_ref.shape
    pair_total = rank_ref.shape[1]
    full = (turned_ref.shape[0] - 8) // 4
    rank, face = rank_ref[...], face_ref[...]
    end = domains - 1
    place = jnp.where(rank == 0, end, jnp.where(rank == end, 0, rank))
    at = marks(face & (cols_x - 1), cols_x)
    step = min(domains, 8)

    def add_step(turn, total):
        block = got_ref[pl.ds(turn * step, step)].reshape(step * folded, cols_x)
        found = summed(times(stacked_terms(block), at)).reshape(step, folded, pair_total)
        for i in range(step):
            total = total + jnp.where(place == turn * step + i, found[i], 0.0)
        return total

    both = jnp.zeros((folded, pair_total), F32)
    if domains == step:
        both = add_step(0, both)
    else:
        both = lax.fori_loop(0, domains // step, add_step, both)
    remote_rows = jnp.where(face < cols_x, both[:12], both[12:])
    pressure, last, normal = weighted_pressure(words_ref[...], full, remote_rows)
    forces = forces_of(-normal, loads_on(turned_ref[...], full, 4 * full, pressure, last))
    faces_ref[...] = summed_on_faces(forces, mortar_ref[...], faces_ref.shape[1])


def last_kernel(
    capacity, full, got_ref, rows_ref, faces_ref, nodes_ref, mass_ref, internal_ref, blocks_ref, own_ref,
    halo_ref, out_ref,
):
    domains, height = got_ref.shape[:2]
    components, layers, rows_y, cols_x = out_ref.shape
    strips = layers * rows_y
    face_count = nodes_ref.shape[1]
    group = LANES // capacity

    part = lax.broadcasted_iota(jnp.int32, (height, LANES), 1) >> halves(capacity)
    pieces = []
    for j in range(group):
        tiles = []
        for tile in range(domains // group):
            block = None
            for spot in range(group):
                piece = got_ref[tile * group + spot]
                if j != spot:
                    piece = pltpu.roll(piece, (spot - j) * capacity % LANES, 1)
                block = piece if block is None else jnp.where(part == spot, piece, block)
            tiles.append(block)
        pieces.append(jnp.concatenate(tiles, axis=1))
    words = jnp.concatenate(pieces, axis=0)
    asked = words[5 * full + 8 : 5 * full + 9].astype(jnp.int32)
    pressure, last, normal = weighted_pressure(words, full, looked_up(rows_ref[...], asked, cols_x))
    remote_forces = forces_of(normal, loads_on(words, full, 5 * full, pressure, last))

    forces = faces_ref[...] + summed_on_faces(remote_forces, asked, face_count)
    total = jnp.zeros((2 * components * strips, cols_x), F32)
    parts = [term.astype(F32) for term in terms_of(forces, 2)]
    numbers = lax.broadcasted_iota(jnp.int32, (strips, face_count), 0)
    for corner in range(4):
        index = nodes_ref[corner : corner + 1, :]
        along_x = marks(index & (cols_x - 1), cols_x)
        strip = numbers == (index >> halves(cols_x))
        spread = []
        for part in parts:
            for k in range(components):
                at = k * 4 + corner
                spread.append(jnp.where(strip, part[at : at + 1], 0.0).astype(BF16))
        total = total + times_turned(jnp.concatenate(spread, axis=0), along_x)
    contact = summed(total).reshape(components, layers, rows_y, cols_x)
    upward = lax.axis_index("sub") == 1
    edge = edge_part(upward, own_ref, halo_ref, blocks_ref)
    at = jnp.where(upward, layers - 1, 0)
    for layer in range(layers):
        for k in range(components):
            nodal = internal_ref[k, layer] + jnp.where(at == layer, edge[k], 0.0)
            out_ref[k, layer] = (nodal + contact[k, layer]) / mass_ref[layer]


GROUP = 8


def shifted(layer):
    views = []
    for part in layer:
        rows_y, cols_x = part.shape
        for moved in (part, pltpu.roll(part, rows_y - 1, 0)):
            views += [moved, pltpu.roll(moved, cols_x - 1, 1)]
    return views


def element_forces(matrices, low, high, modulus):
    rows_y, cols_x = modulus.shape
    inside = (lax.broadcasted_iota(jnp.int32, (rows_y, cols_x), 0) < rows_y - 1) & (
        lax.broadcasted_iota(jnp.int32, (rows_y, cols_x), 1) < cols_x - 1
    )
    scale = jnp.where(inside, modulus, 0.0)
    views = shifted(low) + shifted(high)
    both = jnp.concatenate(matrices, axis=0)
    count = both.shape[0] // 2
    strips = []
    for y in range(0, rows_y, GROUP):
        leading, second = terms_of(jnp.concatenate([view[y : y + GROUP] for view in views], axis=0), 2)
        found = times(both, leading)
        force = found[:count] + (found[count:] + times(matrices[0], second))
        strips.append(force.reshape(-1, GROUP, cols_x) * scale[y : y + GROUP][None])
    return jnp.concatenate(strips, axis=1)


def on_nodes(forces):
    sums = []
    for k in range(forces.shape[0] // 4):
        straight, crossed = [
            forces[k * 4 + c] + pltpu.roll(forces[k * 4 + 2 + c], 1, 0) for c in range(2)
        ]
        sums.append(-(straight + pltpu.roll(crossed, 1, 1)))
    return sums


def edge_part(upward, own_ref, halo_ref, blocks_ref):
    components = own_ref.shape[0] - 1
    size = blocks_ref.shape[1]
    rows = size // 2
    start = jnp.where(upward, 0, rows)
    matrices = [
        blocks_ref[pl.ds(pl.multiple_of(term * size + start, 16), rows)] for term in range(2)
    ]
    low = [jnp.where(upward, own_ref[k], halo_ref[k]) for k in range(components + 1)]
    high = [jnp.where(upward, halo_ref[k], own_ref[k]) for k in range(components)]
    return on_nodes(element_forces(matrices, low[:components], high, low[components]))


def internal_kernel(disp_ref, modulus_ref, stiffness_ref, own_ref, halo_ref, out_ref, blocks_ref):
    components, layers, rows_y, cols_x = disp_ref.shape
    dofs = 8 * components
    half = dofs // 2
    size = dofs * GROUP

    row = lax.broadcasted_iota(jnp.int32, (size, dofs), 0) >> halves(GROUP)
    upper = (row >= half).astype(jnp.int32)
    inner = row - half * upper
    dof = (inner >> 2) * 8 + upper * 4 + (inner & 3)
    pick = (dof == lax.broadcasted_iota(jnp.int32, (size, dofs), 1)).astype(F32).astype(BF16)
    diagonal = (lax.broadcasted_iota(jnp.int32, (size, size), 0) & (GROUP - 1)) == (
        lax.broadcasted_iota(jnp.int32, (size, size), 1) & (GROUP - 1)
    )
    for i, term in enumerate(terms_of(stiffness_ref[...], 2)):
        wide = times_turned(times(pick, term).astype(BF16), pick)
        blocks_ref[i * size : (i + 1) * size] = jnp.where(diagonal, wide, 0.0).astype(BF16)

    blocks = [blocks_ref[i * size : (i + 1) * size] for i in range(2)]
    sums = [[0.0] * components for _ in range(layers)]
    for e in range(layers - 1):
        pair = [[disp_ref[k, e + a] for k in range(components)] for a in range(2)]
        forces = element_forces(blocks, pair[0], pair[1], modulus_ref[e])
        for a in range(2):
            part = on_nodes(forces[a * half : (a + 1) * half])
            sums[e + a] = [x + y for x, y in zip(sums[e + a], part)]
    upward = lax.axis_index("sub") == 0
    edge = edge_part(upward, own_ref, halo_ref, blocks_ref)
    at = jnp.where(upward, layers - 1, 0)
    for layer in range(layers):
        for k in range(components):
            out_ref[k, layer] = sums[layer][k] + jnp.where(at == layer, edge[k], 0.0)


def on_core(kernel, outs, flops, moved, **more):
    return pl.pallas_call(
        kernel,
        out_shape=outs,
        compiler_params=pltpu.CompilerParams(vmem_limit_bytes=48 * 1024 * 1024),
        cost_estimate=pl.CostEstimate(flops=flops, bytes_accessed=moved, transcendentals=0),
        **more,
    )


def swapped(block, axis, first):
    size = lax.axis_size(axis)
    route = []
    for i in range(first, size - 1, 2):
        route += [(i, i + 1), (i + 1, i)]
    return lax.ppermute(block, axis, route)


def shards(
    displacement,
    modulus,
    node_mass,
    stiffness,
    face_nodes,
    pair_mortar,
    pair_rank,
    pair_face,
    pair_count,
    pair_shape,
    pair_weight,
    pair_gap,
    pair_normal,
):
    components, layers, rows_y, cols_x = displacement.shape
    face_count = face_nodes.shape[1]
    pair_total = pair_mortar.shape[0]
    domains = lax.axis_size("dom")
    capacity = max(2, 2 * pair_total // domains)

    points = pair_weight.shape[0]
    full = points // 8 * 8
    group = LANES // capacity
    word_rows = 5 * full + 16
    height = -(-word_rows // (8 * group)) * 8
    line = (1, pair_total)
    pairs = [
        pair_mortar.reshape(line),
        pair_rank.reshape(line),
        pair_face.reshape(line),
        pair_count.reshape(line),
        pair_weight,
        pair_normal,
        pair_gap,
        jnp.swapaxes(pair_shape, 0, 1),
    ]
    passed = [*pairs, node_mass]
    ins = [face_nodes, displacement, modulus, *passed]

    def first(*refs):
        first_kernel(len(passed), *refs)

    def routed(*refs):
        words_kernel(capacity, *refs)

    def last(*refs):
        last_kernel(capacity, full, *refs)

    def shaped(shape, dtype=F32):
        return jax.ShapeDtypeStruct(shape, dtype)

    edge = shaped((components + 1, rows_y, cols_x))
    rows_shape = (12 * face_count // cols_x, cols_x)
    in_hbm = pl.BlockSpec(memory_space=pltpu.HBM)
    in_vmem = pl.BlockSpec(memory_space=pltpu.VMEM)
    sent_rows, rows, inner, outer, nodes, *pairs, mass = on_core(
        first,
        [
            shaped((domains,) + rows_shape),
            shaped(rows_shape),
            edge,
            edge,
            shaped(face_nodes.shape, jnp.int32),
        ]
        + [shaped(x.shape, x.dtype) for x in passed],
        600_000_000,
        1_500_000,
        in_specs=[in_hbm] * len(ins),
        out_specs=[in_hbm] + [in_vmem] * (4 + len(passed)),
        scratch_shapes=[
            pltpu.VMEM(displacement.shape, F32),
            pltpu.VMEM(modulus.shape, F32),
            pltpu.SemaphoreType.DMA((len(ins),)),
            pltpu.SemaphoreType.DMA((domains,)),
        ],
    )(*[pltpu.with_memory_space_constraint(x, pltpu.HBM) for x in ins])
    order = [place_in_group(domain, domains) for domain in range(domains)]
    got_rows = lax.all_to_all(
        sent_rows, "dom", split_axis=0, concat_axis=0, axis_index_groups=[order], tiled=True
    )
    sent_words, words, turned = on_core(
        routed,
        [
            shaped((domains, height, LANES)),
            shaped((word_rows, pair_total)),
            shaped((4 * full + 8, pair_total)),
        ],
        200_000_000,
        1_000_000,
    )(rows, *pairs)
    got_words = lax.all_to_all(sent_words, "dom", split_axis=0, concat_axis=0, tiled=True)
    inner_halo = swapped(inner, ("dom", "sub"), 0)
    outer_halo = swapped(outer, ("dom", "sub"), 1)
    faces = on_core(own_pairs_kernel, shaped((12, face_count)), 100_000_000, 500_000)(
        got_rows, words, turned, *pairs[:3]
    )
    size = 8 * components * GROUP
    internal, blocks = on_core(
        internal_kernel,
        [shaped(displacement.shape), shaped((2 * size, size), BF16)],
        1_000_000_000,
        700_000,
    )(displacement, modulus, stiffness, inner, inner_halo)
    return on_core(last, shaped(displacement.shape), 1_000_000_000, 1_500_000)(
        got_words, rows, faces, nodes, mass, internal, blocks, outer, outer_halo
    )


def solution(mesh):
    placed = (
        P(None, ("runs", "dom", "sub"), None, None),
        P(("runs", "dom", "sub"), None, None),
        P(("runs", "dom", "sub"), None, None),
        P(),
        P(None, ("runs", "dom", "sub")),
        P(("runs", "dom", "sub")),
        P(("runs", "dom", "sub"), None),
        P(("runs", "dom", "sub")),
        P(("runs", "dom", "sub")),
        P(None, None, ("runs", "dom", "sub")),
        P(None, ("runs", "dom", "sub")),
        P(None, ("runs", "dom", "sub")),
        P(None, ("runs", "dom", "sub")),
    )
    return jax.shard_map(
        shards,
        mesh=mesh,
        in_specs=placed,
        out_specs=P(None, ("runs", "dom", "sub"), None, None),
        check_vma=False,
    )
```

```python
import jax
import jax.numpy as jnp
from jax import lax
from jax.experimental import pallas as pl
from jax.experimental.pallas import tpu as pltpu
from jax.sharding import PartitionSpec as P

F32 = jnp.float32
BF16 = jnp.bfloat16
LANES = 128


def terms_of(x, count):
    terms = []
    for _ in range(count):
        terms.append(x.astype(BF16))
        x = x - terms[-1].astype(F32)
    return terms


def stacked_terms(x):
    return jnp.concatenate(terms_of(x, 2), axis=0)


def summed(stacked):
    rows = stacked.shape[0] // 2
    return stacked[:rows] + stacked[rows:]


def marks(index, count):
    shape = (16, index.shape[1])
    rows = lax.broadcasted_iota(jnp.int32, shape, 0).astype(jnp.int16)
    index = jnp.broadcast_to(index, shape).astype(jnp.int16)
    tiles = [
        jnp.where(rows == index - jnp.int16(start), jnp.ones((), BF16), jnp.zeros((), BF16))
        for start in range(0, count, 16)
    ]
    return jnp.concatenate(tiles, axis=0)


def times(left, right):
    return jnp.dot(left, right, preferred_element_type=F32)


def times_turned(left, right):
    return lax.dot_general(left, right, (((1,), (1,)), ((), ())), preferred_element_type=F32)


def halves(power):
    return power.bit_length() - 1


def looked_up(table, face, at):
    both = summed(times(stacked_terms(table), at))
    return jnp.where(face < table.shape[1], both[:12], both[12:])


def folded(placed, height, capacity, domain):
    group = LANES // capacity
    tile, spot = domain // group, domain % group
    part = lax.broadcasted_iota(jnp.int32, (height, LANES), 1) >> halves(capacity)
    block = None
    for j in range(group):
        piece = placed[j * height : (j + 1) * height, tile * LANES : (tile + 1) * LANES]
        if j != spot:
            piece = pltpu.roll(piece, (j - spot) * capacity % LANES, 1)
        block = piece if block is None else jnp.where(part == j, piece, block)
    return block


def unfolded(got_ref, start, height, capacity):
    group = LANES // capacity
    part = lax.broadcasted_iota(jnp.int32, (height, LANES), 1) >> halves(capacity)
    pieces = []
    for j in range(group):
        tiles = []
        for first in range(0, got_ref.shape[0], group):
            block = None
            for spot in range(group):
                piece = got_ref[first + spot, start : start + height]
                if j != spot:
                    piece = pltpu.roll(piece, (spot - j) * capacity % LANES, 1)
                block = piece if block is None else jnp.where(part == spot, piece, block)
            tiles.append(block)
        pieces.append(jnp.concatenate(tiles, axis=1))
    return jnp.concatenate(pieces, axis=0)


def routed(words, rows, place):
    extra = rows - words.shape[0]
    if extra:
        words = jnp.concatenate([words, jnp.zeros((extra, words.shape[1]), F32)], axis=0)
    return summed(times_turned(stacked_terms(words), place))


def weighted_pressure(words, full, remote_rows):
    tail = 5 * full
    normal = words[tail + 5 : tail + 8]
    gap, last = words[4 * full : tail], words[tail + 4 : tail + 5]
    for node in range(4):
        across = sum(
            normal[k : k + 1] * remote_rows[k * 4 + node : k * 4 + node + 1] for k in range(3)
        )
        gap = gap + words[node * full : (node + 1) * full] * across
        last = last + words[tail + node : tail + node + 1] * across
    return jnp.maximum(-gap, 0.0), jnp.maximum(-last, 0.0), normal


def loads_on(shapes, full, tail, pressure, last):
    return [
        jnp.sum(pressure * shapes[i * full : (i + 1) * full], axis=0, keepdims=True)
        + last * shapes[tail + i : tail + i + 1]
        for i in range(4)
    ]


def forces_of(normal, loads):
    loads = jnp.concatenate(loads, axis=0)
    return jnp.concatenate([normal[k : k + 1] * loads for k in range(3)], axis=0)


def place_in_group(domain, domains):
    return {0: domains - 1, domains - 1: 0}.get(domain, domain)


def first_kernel(capacity, heights, *refs):
    (
        nodes_hbm, disp_hbm, mortar_hbm, rank_hbm, face_hbm, count_hbm, weight_hbm, normal_hbm,
        gap_hbm, shape_hbm, modulus_hbm, mass_hbm,
        sent_ref, rows_ref, words_ref, turned_ref, mortar_ref, rank_ref, face_ref, nodes, mass_ref,
        inner_ref, outer_ref,
        disp, count, weight, normal_v, gap_v, shape, modulus, halved, shapes, gaps, sems, copy_sems,
    ) = refs
    components, layers, rows_y, cols_x = disp.shape
    sources = (
        nodes_hbm, disp_hbm, rank_hbm, face_hbm, mortar_hbm, shape_hbm, count_hbm, weight_hbm,
        normal_hbm, gap_hbm, modulus_hbm, mass_hbm,
    )
    targets = (
        nodes, disp, rank_ref, face_ref, mortar_ref, shape, count, weight, normal_v, gap_v, modulus,
        mass_ref,
    )
    brought = [
        pltpu.make_async_copy(source, target, sems.at[i])
        for i, (source, target) in enumerate(zip(sources, targets))
    ]
    for copy in brought:
        copy.start()

    domains = sent_ref.shape[0]
    pair_total = rank_ref.shape[1]
    face_count = nodes.shape[1]
    strips = layers * rows_y
    for copy in brought[:-2]:
        copy.wait()
    rank, face, mortar = rank_ref[...], face_ref[...], mortar_ref[...]
    normal = normal_v[...]
    gap = gap_v[...]

    chosen = lax.broadcasted_iota(jnp.int32, (domains, pair_total), 0) == rank
    before = lax.broadcasted_iota(jnp.int32, (pair_total, pair_total), 0) < lax.broadcasted_iota(
        jnp.int32, (pair_total, pair_total), 1
    )
    earlier = times(chosen.astype(F32).astype(BF16), before.astype(F32).astype(BF16))
    slot = jnp.sum(jnp.where(chosen, earlier, 0.0), axis=0, keepdims=True).astype(jnp.int32)
    place = marks(rank * capacity + slot, domains * capacity)

    parts = stacked_terms(disp[...].reshape(components * strips, cols_x))
    numbers = lax.broadcasted_iota(jnp.int32, (strips, face_count), 0)
    folds = face_count // cols_x
    for corner in range(4):
        index = nodes[corner : corner + 1, :]
        strip = index >> halves(cols_x)
        found = summed(times(parts, marks(index & (cols_x - 1), cols_x)))
        found = found.reshape(components, strips, face_count)
        values = jnp.sum(jnp.where((numbers == strip)[None], found, 0.0), axis=1)
        for fold in range(folds):
            for k in range(components):
                at = fold * 12 + k * 4 + corner
                rows_ref[at : at + 1, :] = values[k : k + 1, fold * cols_x : (fold + 1) * cols_x]

    points = gap.shape[0]
    full = points // 8 * 8
    live = lax.broadcasted_iota(jnp.int32, (points, pair_total), 0) < count[...]
    root = jnp.where(live, jnp.sqrt(weight[...]), 0.0)
    weighted = [root * shape[:, node] for node in range(4)]
    long_words = jnp.concatenate([x[:full] for x in weighted], axis=0)
    group = LANES // capacity
    placed = routed(long_words, group * heights[0], place)

    rows = rows_ref[...]
    high = rows.shape[0]
    rows_high = high * cols_x // LANES
    for i in range(cols_x // LANES):
        halved[i * high : (i + 1) * high] = rows[:, i * LANES : (i + 1) * LANES]
    starts = (rows_high, rows_high + heights[0], rows_high + sum(heights))
    copies = []
    for domain in range(domains):
        spot = place_in_group(domain, domains)
        shapes[domain] = folded(placed, heights[0], capacity, domain)
        copies += [
            pltpu.make_async_copy(halved, sent_ref.at[spot, :rows_high], copy_sems.at[0, domain]),
            pltpu.make_async_copy(
                shapes.at[domain],
                sent_ref.at[spot, starts[0] : starts[1]],
                copy_sems.at[1, domain],
            ),
        ]
        for copy in copies[-2:]:
            copy.start()

    mortar_rows = looked_up(rows, mortar, marks(mortar & (cols_x - 1), cols_x))
    for node in range(4):
        across = sum(
            normal[k : k + 1] * mortar_rows[k * 4 + node : k * 4 + node + 1] for k in range(3)
        )
        gap = gap - shape[:, 4 + node] * across
    gap = root * gap
    short_words = jnp.concatenate(
        [gap[:full]]
        + [x[full:] for x in weighted + [gap]]
        + [normal, face.astype(F32), jnp.zeros((7, pair_total), F32)],
        axis=0,
    )
    placed = routed(short_words, group * heights[1], place)
    for domain in range(domains):
        spot = place_in_group(domain, domains)
        gaps[domain] = folded(placed, heights[1], capacity, domain)
        copies.append(
            pltpu.make_async_copy(
                gaps.at[domain], sent_ref.at[spot, starts[1] : starts[2]], copy_sems.at[2, domain]
            )
        )
        copies[-1].start()

    words_ref[: 4 * full] = long_words
    words_ref[4 * full :] = short_words
    for node in range(4):
        turned = root * shape[:, 4 + node]
        turned_ref[node * full : (node + 1) * full] = turned[:full]
        turned_ref[4 * full + node : 4 * full + node + 1] = turned[full:]

    for copy in brought[-2:]:
        copy.wait()
    sub = lax.axis_index("sub")
    for target, layer in ((inner_ref, (1 - sub) * (layers - 1)), (outer_ref, sub * (layers - 1))):
        for k in range(components):
            target[k] = disp[k, layer]
        target[components] = modulus[layer]
    for copy in copies:
        copy.wait()


def last_kernel(
    capacity, heights, got_ref, rows_ref, words_ref, turned_ref, mortar_ref, rank_ref, face_ref, nodes_ref,
    inverse_ref, internal_ref, blocks_ref, own_ref, halo_ref, out_ref,
):
    domains = got_ref.shape[0]
    components, layers, rows_y, cols_x = out_ref.shape
    strips = layers * rows_y
    face_count = nodes_ref.shape[1]
    pair_total = rank_ref.shape[1]
    folded = rows_ref.shape[0]
    rows_high = folded * cols_x // LANES
    full = (turned_ref.shape[0] - 8) // 4
    own_rows = rows_ref[...]

    rank, face = rank_ref[...], face_ref[...]
    end = domains - 1
    place = jnp.where(rank == 0, end, jnp.where(rank == end, 0, rank))
    at = marks(face & (cols_x - 1), cols_x)
    step = min(domains, 8)

    def add_step(turn, total):
        block = jnp.concatenate(
            [
                got_ref[pl.ds(turn * step, step), i * folded : (i + 1) * folded].reshape(
                    step * folded, LANES
                )
                for i in range(cols_x // LANES)
            ],
            axis=1,
        )
        found = summed(times(stacked_terms(block), at)).reshape(step, folded, pair_total)
        for i in range(step):
            total = total + jnp.where(place == turn * step + i, found[i], 0.0)
        return total

    both = jnp.zeros((folded, pair_total), F32)
    if domains == step:
        both = add_step(0, both)
    else:
        both = lax.fori_loop(0, domains // step, add_step, both)
    remote_rows = jnp.where(face < cols_x, both[:12], both[12:])
    pressure, last, normal = weighted_pressure(words_ref[...], full, remote_rows)
    turned = turned_ref[...]
    mortar_forces = forces_of(-normal, loads_on(turned, full, 4 * full, pressure, last))

    words = jnp.concatenate(
        [
            unfolded(got_ref, rows_high, heights[0], capacity)[: 4 * full],
            unfolded(got_ref, rows_high + heights[0], heights[1], capacity)[: full + 16],
        ],
        axis=0,
    )
    asked = words[5 * full + 8 : 5 * full + 9].astype(jnp.int32)
    asked_at = marks(asked & (cols_x - 1), cols_x)
    remote_rows = looked_up(own_rows, asked, asked_at)
    pressure, last, normal = weighted_pressure(words, full, remote_rows)
    remote_forces = forces_of(normal, loads_on(words, full, 5 * full, pressure, last))

    forces = jnp.concatenate([mortar_forces, remote_forces], axis=1)
    into = jnp.concatenate([mortar_ref[...], asked], axis=1)
    at = jnp.concatenate([marks(mortar_ref[...] & (cols_x - 1), cols_x), asked_at], axis=1)
    forces = jnp.concatenate(
        [jnp.where(into < cols_x, forces, 0.0), jnp.where(into < cols_x, 0.0, forces)], axis=0
    )
    forces = summed(times_turned(stacked_terms(forces), at))
    forces = jnp.concatenate([forces[:12], forces[12:]], axis=1)
    total = jnp.zeros((2 * components * strips, cols_x), F32)
    parts = [term.astype(F32) for term in terms_of(forces, 2)]
    for corner in range(4):
        index = nodes_ref[corner : corner + 1, :]
        strip = marks(index >> halves(cols_x), strips)
        spread = []
        for part in parts:
            for k in range(components):
                at = k * 4 + corner
                row = jnp.broadcast_to(part[at : at + 1], (16, face_count)).astype(BF16)
                spread.append(strip * jnp.concatenate([row] * (strips // 16), axis=0))
        along_x = marks(index & (cols_x - 1), cols_x)
        total = total + times_turned(jnp.concatenate(spread, axis=0), along_x)
    contact = summed(total).reshape(components, layers, rows_y, cols_x)
    upward = lax.axis_index("sub") == 1
    edge = edge_part(upward, own_ref, halo_ref, blocks_ref)
    at = jnp.where(upward, layers - 1, 0)
    for layer in range(layers):
        for k in range(components):
            nodal = internal_ref[k, layer] + jnp.where(at == layer, edge[k], 0.0)
            out_ref[k, layer] = (nodal + contact[k, layer]) * inverse_ref[layer]


GROUP = 8


def shifted(layer):
    views = []
    for part in layer:
        rows_y, cols_x = part.shape
        for moved in (part, pltpu.roll(part, rows_y - 1, 0)):
            views += [moved, pltpu.roll(moved, cols_x - 1, 1)]
    return views


def element_forces(matrices, low, high, modulus):
    rows_y, cols_x = modulus.shape
    inside = (lax.broadcasted_iota(jnp.int32, (rows_y, cols_x), 0) < rows_y - 1) & (
        lax.broadcasted_iota(jnp.int32, (rows_y, cols_x), 1) < cols_x - 1
    )
    scale = jnp.where(inside, modulus, 0.0)
    views = shifted(low) + shifted(high)
    both = jnp.concatenate(matrices, axis=0)
    count = both.shape[0] // 2
    strips = []
    for y in range(0, rows_y, GROUP):
        leading, second = terms_of(jnp.concatenate([view[y : y + GROUP] for view in views], axis=0), 2)
        found = times(both, leading)
        force = found[:count] + (found[count:] + times(matrices[0], second))
        strips.append(force.reshape(-1, GROUP, cols_x) * scale[y : y + GROUP][None])
    return jnp.concatenate(strips, axis=1)


def on_nodes(forces):
    sums = []
    for k in range(forces.shape[0] // 4):
        straight, crossed = [
            forces[k * 4 + c] + pltpu.roll(forces[k * 4 + 2 + c], 1, 0) for c in range(2)
        ]
        sums.append(-(straight + pltpu.roll(crossed, 1, 1)))
    return sums


def edge_part(upward, own_ref, halo_ref, blocks_ref):
    components = own_ref.shape[0] - 1
    size = blocks_ref.shape[1]
    rows = size // 2
    start = jnp.where(upward, 0, rows)
    matrices = [
        blocks_ref[pl.ds(pl.multiple_of(term * size + start, 16), rows)] for term in range(2)
    ]
    low = [jnp.where(upward, own_ref[k], halo_ref[k]) for k in range(components + 1)]
    high = [jnp.where(upward, halo_ref[k], own_ref[k]) for k in range(components)]
    return on_nodes(element_forces(matrices, low[:components], high, low[components]))


def internal_kernel(
    disp_ref, modulus_ref, stiffness_ref, mass_ref, own_ref, halo_ref, out_ref, blocks_ref, inverse_ref
):
    inverse_ref[...] = 1.0 / mass_ref[...]
    components, layers, rows_y, cols_x = disp_ref.shape
    dofs = 8 * components
    half = dofs // 2
    size = dofs * GROUP

    row = lax.broadcasted_iota(jnp.int32, (size, dofs), 0) >> halves(GROUP)
    upper = (row >= half).astype(jnp.int32)
    inner = row - half * upper
    dof = (inner >> 2) * 8 + upper * 4 + (inner & 3)
    pick = (dof == lax.broadcasted_iota(jnp.int32, (size, dofs), 1)).astype(F32).astype(BF16)
    diagonal = (lax.broadcasted_iota(jnp.int32, (size, size), 0) & (GROUP - 1)) == (
        lax.broadcasted_iota(jnp.int32, (size, size), 1) & (GROUP - 1)
    )
    for i, term in enumerate(terms_of(stiffness_ref[...], 2)):
        wide = times_turned(times(pick, term).astype(BF16), pick)
        blocks_ref[i * size : (i + 1) * size] = jnp.where(diagonal, wide, 0.0).astype(BF16)

    blocks = [blocks_ref[i * size : (i + 1) * size] for i in range(2)]
    sums = [[0.0] * components for _ in range(layers)]
    for e in range(layers - 1):
        pair = [[disp_ref[k, e + a] for k in range(components)] for a in range(2)]
        forces = element_forces(blocks, pair[0], pair[1], modulus_ref[e])
        for a in range(2):
            part = on_nodes(forces[a * half : (a + 1) * half])
            sums[e + a] = [x + y for x, y in zip(sums[e + a], part)]
    upward = lax.axis_index("sub") == 0
    edge = edge_part(upward, own_ref, halo_ref, blocks_ref)
    at = jnp.where(upward, layers - 1, 0)
    for layer in range(layers):
        for k in range(components):
            out_ref[k, layer] = sums[layer][k] + jnp.where(at == layer, edge[k], 0.0)


def on_core(kernel, outs, flops, moved, **more):
    return pl.pallas_call(
        kernel,
        out_shape=outs,
        compiler_params=pltpu.CompilerParams(vmem_limit_bytes=48 * 1024 * 1024),
        cost_estimate=pl.CostEstimate(flops=flops, bytes_accessed=moved, transcendentals=0),
        **more,
    )


def swapped(block, axis, first):
    size = lax.axis_size(axis)
    route = []
    for i in range(first, size - 1, 2):
        route += [(i, i + 1), (i + 1, i)]
    return lax.ppermute(block, axis, route)


def shards(
    displacement,
    modulus,
    node_mass,
    stiffness,
    face_nodes,
    pair_mortar,
    pair_rank,
    pair_face,
    pair_count,
    pair_shape,
    pair_weight,
    pair_gap,
    pair_normal,
):
    components, layers, rows_y, cols_x = displacement.shape
    face_count = face_nodes.shape[1]
    pair_total = pair_mortar.shape[0]
    domains = lax.axis_size("dom")
    capacity = max(2, 2 * pair_total // domains)

    points = pair_weight.shape[0]
    full = points // 8 * 8
    group = LANES // capacity
    word_rows = 5 * full + 16
    heights = tuple(-(-rows // (8 * group)) * 8 for rows in (4 * full, full + 16))
    rows_high = 12 * face_count // LANES
    line = (1, pair_total)

    def first(*refs):
        first_kernel(capacity, heights, *refs)

    def last(*refs):
        last_kernel(capacity, heights, *refs)

    def shaped(shape, dtype=F32):
        return jax.ShapeDtypeStruct(shape, dtype)

    arrays = [
        face_nodes,
        displacement,
        pair_mortar.reshape(line),
        pair_rank.reshape(line),
        pair_face.reshape(line),
        pair_count.reshape(line),
        pair_weight,
        pair_normal,
        pair_gap,
        jnp.swapaxes(pair_shape, 0, 1),
        modulus,
        node_mass,
    ]
    edge = shaped((components + 1, rows_y, cols_x))
    in_hbm = pl.BlockSpec(memory_space=pltpu.HBM)
    in_vmem = pl.BlockSpec(memory_space=pltpu.VMEM)
    kept = [displacement, *arrays[5:-1]]
    sent, rows, words, turned, mortar, rank, face, nodes, mass, inner, outer = on_core(
        first,
        [
            shaped((domains, rows_high + sum(heights), LANES)),
            shaped((12 * face_count // cols_x, cols_x)),
            shaped((word_rows, pair_total)),
            shaped((4 * full + 8, pair_total)),
            shaped(line, jnp.int32),
            shaped(line, jnp.int32),
            shaped(line, jnp.int32),
            shaped(face_nodes.shape, jnp.int32),
            shaped(node_mass.shape),
            edge,
            edge,
        ],
        900_000_000,
        1_500_000,
        in_specs=[in_hbm] * len(arrays),
        out_specs=[in_hbm] + [in_vmem] * 10,
        scratch_shapes=[pltpu.VMEM(x.shape, x.dtype) for x in kept]
        + [
            pltpu.VMEM((rows_high, LANES), F32),
            pltpu.VMEM((domains, heights[0], LANES), F32),
            pltpu.VMEM((domains, heights[1], LANES), F32),
            pltpu.SemaphoreType.DMA((len(arrays),)),
            pltpu.SemaphoreType.DMA((3, domains)),
        ],
    )(*[pltpu.with_memory_space_constraint(x, pltpu.HBM) for x in arrays])
    order = [place_in_group(domain, domains) for domain in range(domains)]
    got = lax.all_to_all(
        sent, "dom", split_axis=0, concat_axis=0, axis_index_groups=[order], tiled=True
    )
    inner_halo = swapped(inner, ("dom", "sub"), 0)
    outer_halo = swapped(outer, ("dom", "sub"), 1)
    size = 8 * components * GROUP
    internal, blocks, inverse = on_core(
        internal_kernel,
        [shaped(displacement.shape), shaped((2 * size, size), BF16), shaped(mass.shape)],
        1_000_000_000,
        700_000,
    )(displacement, modulus, stiffness, mass, inner, inner_halo)
    return on_core(last, shaped(displacement.shape), 1_000_000_000, 1_500_000)(
        got, rows, words, turned, mortar, rank, face, nodes, inverse, internal, blocks, outer, outer_halo
    )


def solution(mesh):
    placed = (
        P(None, ("runs", "dom", "sub"), None, None),
        P(("runs", "dom", "sub"), None, None),
        P(("runs", "dom", "sub"), None, None),
        P(),
        P(None, ("runs", "dom", "sub")),
        P(("runs", "dom", "sub")),
        P(("runs", "dom", "sub"), None),
        P(("runs", "dom", "sub")),
        P(("runs", "dom", "sub")),
        P(None, None, ("runs", "dom", "sub")),
        P(None, ("runs", "dom", "sub")),
        P(None, ("runs", "dom", "sub")),
        P(None, ("runs", "dom", "sub")),
    )
    return jax.shard_map(
        shards,
        mesh=mesh,
        in_specs=placed,
        out_specs=P(None, ("runs", "dom", "sub"), None, None),
        check_vma=False,
    )
```

```python
import jax
import jax.numpy as jnp
from jax import lax
from jax.experimental import pallas as pl
from jax.experimental.pallas import tpu as pltpu
from jax.sharding import PartitionSpec as P

F32 = jnp.float32
BF16 = jnp.bfloat16
LANES = 128


def terms_of(x, count):
    terms = []
    for _ in range(count):
        terms.append(x.astype(BF16))
        x = x - terms[-1].astype(F32)
    return terms


def stacked_terms(x):
    return jnp.concatenate(terms_of(x, 2), axis=0)


def summed(stacked):
    rows = stacked.shape[0] // 2
    return stacked[:rows] + stacked[rows:]


def marks(index, count):
    shape = (16, index.shape[1])
    rows = lax.broadcasted_iota(jnp.int32, shape, 0).astype(jnp.int16)
    index = jnp.broadcast_to(index, shape).astype(jnp.int16)
    tiles = [
        jnp.where(rows == index - jnp.int16(start), jnp.ones((), BF16), jnp.zeros((), BF16))
        for start in range(0, count, 16)
    ]
    return jnp.concatenate(tiles, axis=0)


def times(left, right):
    return jnp.dot(left, right, preferred_element_type=F32)


def times_turned(left, right):
    return lax.dot_general(left, right, (((1,), (1,)), ((), ())), preferred_element_type=F32)


def halves(power):
    return power.bit_length() - 1


def looked_up(table, face, at):
    both = summed(times(stacked_terms(table), at))
    return jnp.where(face < table.shape[1], both[:12], both[12:])


def folded(placed, height, capacity, domain):
    group = LANES // capacity
    tile, spot = domain // group, domain % group
    part = lax.broadcasted_iota(jnp.int32, (height, LANES), 1) >> halves(capacity)
    block = None
    for j in range(group):
        piece = placed[j * height : (j + 1) * height, tile * LANES : (tile + 1) * LANES]
        if j != spot:
            piece = pltpu.roll(piece, (j - spot) * capacity % LANES, 1)
        block = piece if block is None else jnp.where(part == j, piece, block)
    return block


def unfolded(got_ref, start, height, capacity):
    group = LANES // capacity
    part = lax.broadcasted_iota(jnp.int32, (height, LANES), 1) >> halves(capacity)
    pieces = []
    for j in range(group):
        tiles = []
        for first in range(0, got_ref.shape[0], group):
            block = None
            for spot in range(group):
                piece = got_ref[first + spot, start : start + height]
                if j != spot:
                    piece = pltpu.roll(piece, (spot - j) * capacity % LANES, 1)
                block = piece if block is None else jnp.where(part == spot, piece, block)
            tiles.append(block)
        pieces.append(jnp.concatenate(tiles, axis=1))
    return jnp.concatenate(pieces, axis=0)


def routed(words, rows, place):
    extra = rows - words.shape[0]
    if extra:
        words = jnp.concatenate([words, jnp.zeros((extra, words.shape[1]), F32)], axis=0)
    return summed(times_turned(stacked_terms(words), place))


def weighted_pressure(words, full, remote_rows):
    tail = 5 * full
    normal = words[tail + 5 : tail + 8]
    gap, last = words[4 * full : tail], words[tail + 4 : tail + 5]
    for node in range(4):
        across = sum(
            normal[k : k + 1] * remote_rows[k * 4 + node : k * 4 + node + 1] for k in range(3)
        )
        gap = gap + words[node * full : (node + 1) * full] * across
        last = last + words[tail + node : tail + node + 1] * across
    return jnp.maximum(-gap, 0.0), jnp.maximum(-last, 0.0), normal


def loads_on(shapes, full, tail, pressure, last):
    return [
        jnp.sum(pressure * shapes[i * full : (i + 1) * full], axis=0, keepdims=True)
        + last * shapes[tail + i : tail + i + 1]
        for i in range(4)
    ]


def forces_of(normal, loads):
    loads = jnp.concatenate(loads, axis=0)
    return jnp.concatenate([normal[k : k + 1] * loads for k in range(3)], axis=0)


def place_in_group(domain, domains):
    return {0: domains - 1, domains - 1: 0}.get(domain, domain)


def in_pieces(source, target, sems, first):
    shape = source.shape
    if len(shape) == 4:
        parts = [(i, j) for i in range(shape[0]) for j in range(shape[1])]
    elif len(shape) == 3 and shape[0] <= 4:
        parts = [(i,) for i in range(shape[0])]
    elif len(shape) == 3:
        parts = [(pl.ds(start, min(5, shape[0] - start)),) for start in range(0, shape[0], 5)]
    else:
        return [pltpu.make_async_copy(source, target, sems.at[first])]
    return [
        pltpu.make_async_copy(source.at[part], target.at[part], sems.at[first + i])
        for i, part in enumerate(parts)
    ]


def first_kernel(capacity, heights, *refs):
    (
        nodes_hbm, disp_hbm, mortar_hbm, rank_hbm, face_hbm, count_hbm, weight_hbm, normal_hbm,
        gap_hbm, shape_hbm, modulus_hbm, mass_hbm,
        sent_ref, rows_ref, words_ref, turned_ref, mortar_ref, rank_ref, face_ref, nodes, mass_ref,
        inner_ref, outer_ref, top_ref,
        disp, count, weight, normal_v, gap_v, shape, modulus, halved, shapes, gaps, sems, copy_sems,
    ) = refs
    components, layers, rows_y, cols_x = disp.shape
    sources = (
        nodes_hbm, disp_hbm, rank_hbm, face_hbm, mortar_hbm, shape_hbm, count_hbm, weight_hbm,
        normal_hbm, gap_hbm, modulus_hbm, mass_hbm,
    )
    targets = (
        nodes, disp, rank_ref, face_ref, mortar_ref, shape, count, weight, normal_v, gap_v, modulus,
        mass_ref,
    )
    brought = []
    for source, target in zip(sources, targets):
        brought += in_pieces(source, target, sems, len(brought))
    for copy in brought:
        copy.start()

    domains = sent_ref.shape[0]
    pair_total = rank_ref.shape[1]
    face_count = nodes.shape[1]
    strips = layers * rows_y
    late = 2 * layers
    for copy in brought[:-late]:
        copy.wait()
    rank, face, mortar = rank_ref[...], face_ref[...], mortar_ref[...]
    normal = normal_v[...]
    gap = gap_v[...]

    chosen = lax.broadcasted_iota(jnp.int32, (domains, pair_total), 0) == rank
    before = lax.broadcasted_iota(jnp.int32, (pair_total, pair_total), 0) < lax.broadcasted_iota(
        jnp.int32, (pair_total, pair_total), 1
    )
    earlier = times(chosen.astype(F32).astype(BF16), before.astype(F32).astype(BF16))
    slot = jnp.sum(jnp.where(chosen, earlier, 0.0), axis=0, keepdims=True).astype(jnp.int32)
    place = marks(rank * capacity + slot, domains * capacity)

    parts = stacked_terms(disp[...].reshape(components * strips, cols_x))
    numbers = lax.broadcasted_iota(jnp.int32, (strips, face_count), 0)
    folds = face_count // cols_x
    for corner in range(4):
        index = nodes[corner : corner + 1, :]
        strip = index >> halves(cols_x)
        found = summed(times(parts, marks(index & (cols_x - 1), cols_x)))
        found = found.reshape(components, strips, face_count)
        values = jnp.sum(jnp.where((numbers == strip)[None], found, 0.0), axis=1)
        for fold in range(folds):
            for k in range(components):
                at = fold * 12 + k * 4 + corner
                rows_ref[at : at + 1, :] = values[k : k + 1, fold * cols_x : (fold + 1) * cols_x]

    points = gap.shape[0]
    full = points // 8 * 8
    live = lax.broadcasted_iota(jnp.int32, (points, pair_total), 0) < count[...]
    root = jnp.where(live, jnp.sqrt(weight[...]), 0.0)
    weighted = [root * shape[:, node] for node in range(4)]
    long_words = jnp.concatenate([x[:full] for x in weighted], axis=0)
    group = LANES // capacity
    placed = routed(long_words, group * heights[0], place)

    rows = rows_ref[...]
    high = rows.shape[0]
    rows_high = high * cols_x // LANES
    for i in range(cols_x // LANES):
        halved[i * high : (i + 1) * high] = rows[:, i * LANES : (i + 1) * LANES]
    starts = (rows_high, rows_high + heights[0], rows_high + sum(heights))
    copies = []
    for domain in range(domains):
        spot = place_in_group(domain, domains)
        shapes[domain] = folded(placed, heights[0], capacity, domain)
        copies += [
            pltpu.make_async_copy(halved, sent_ref.at[spot, :rows_high], copy_sems.at[0, domain]),
            pltpu.make_async_copy(
                shapes.at[domain],
                sent_ref.at[spot, starts[0] : starts[1]],
                copy_sems.at[1, domain],
            ),
        ]
        for copy in copies[-2:]:
            copy.start()

    mortar_rows = looked_up(rows, mortar, marks(mortar & (cols_x - 1), cols_x))
    for node in range(4):
        across = sum(
            normal[k : k + 1] * mortar_rows[k * 4 + node : k * 4 + node + 1] for k in range(3)
        )
        gap = gap - shape[:, 4 + node] * across
    gap = root * gap
    short_words = jnp.concatenate(
        [gap[:full]]
        + [x[full:] for x in weighted + [gap]]
        + [normal, face.astype(F32), jnp.zeros((7, pair_total), F32)],
        axis=0,
    )
    placed = routed(short_words, group * heights[1], place)
    for domain in range(domains):
        spot = place_in_group(domain, domains)
        gaps[domain] = folded(placed, heights[1], capacity, domain)
        copies.append(
            pltpu.make_async_copy(
                gaps.at[domain], sent_ref.at[spot, starts[1] : starts[2]], copy_sems.at[2, domain]
            )
        )
        copies[-1].start()

    words_ref[: 4 * full] = long_words
    words_ref[4 * full :] = short_words
    for node in range(4):
        turned = root * shape[:, 4 + node]
        turned_ref[node * full : (node + 1) * full] = turned[:full]
        turned_ref[4 * full + node : 4 * full + node + 1] = turned[full:]

    for copy in brought[-late:]:
        copy.wait()
    sub = lax.axis_index("sub")
    for target, layer in ((inner_ref, (1 - sub) * (layers - 1)), (outer_ref, sub * (layers - 1))):
        for k in range(components):
            target[k] = disp[k, layer]
    top_ref[...] = modulus[layers - 1]
    for copy in copies:
        copy.wait()


def last_kernel(
    capacity, heights, got_ref, rows_ref, words_ref, turned_ref, mortar_ref, rank_ref, face_ref, nodes_ref,
    inverse_ref, internal_ref, blocks_ref, own_ref, halo_ref, top_ref, under_ref, out_hbm, out_ref, sems,
):
    domains = got_ref.shape[0]
    components, layers, rows_y, cols_x = out_ref.shape
    strips = layers * rows_y
    face_count = nodes_ref.shape[1]
    pair_total = rank_ref.shape[1]
    folded = rows_ref.shape[0]
    rows_high = folded * cols_x // LANES
    full = (turned_ref.shape[0] - 8) // 4
    own_rows = rows_ref[...]

    rank, face = rank_ref[...], face_ref[...]
    end = domains - 1
    place = jnp.where(rank == 0, end, jnp.where(rank == end, 0, rank))
    at = marks(face & (cols_x - 1), cols_x)
    step = min(domains, 8)

    def add_step(turn, total):
        block = jnp.concatenate(
            [
                got_ref[pl.ds(turn * step, step), i * folded : (i + 1) * folded].reshape(
                    step * folded, LANES
                )
                for i in range(cols_x // LANES)
            ],
            axis=1,
        )
        found = summed(times(stacked_terms(block), at)).reshape(step, folded, pair_total)
        for i in range(step):
            total = total + jnp.where(place == turn * step + i, found[i], 0.0)
        return total

    both = jnp.zeros((folded, pair_total), F32)
    if domains == step:
        both = add_step(0, both)
    else:
        both = lax.fori_loop(0, domains // step, add_step, both)
    remote_rows = jnp.where(face < cols_x, both[:12], both[12:])
    pressure, last, normal = weighted_pressure(words_ref[...], full, remote_rows)
    turned = turned_ref[...]
    mortar_forces = forces_of(-normal, loads_on(turned, full, 4 * full, pressure, last))

    words = jnp.concatenate(
        [
            unfolded(got_ref, rows_high, heights[0], capacity)[: 4 * full],
            unfolded(got_ref, rows_high + heights[0], heights[1], capacity)[: full + 16],
        ],
        axis=0,
    )
    asked = words[5 * full + 8 : 5 * full + 9].astype(jnp.int32)
    asked_at = marks(asked & (cols_x - 1), cols_x)
    remote_rows = looked_up(own_rows, asked, asked_at)
    pressure, last, normal = weighted_pressure(words, full, remote_rows)
    remote_forces = forces_of(normal, loads_on(words, full, 5 * full, pressure, last))

    forces = jnp.concatenate([mortar_forces, remote_forces], axis=1)
    into = jnp.concatenate([mortar_ref[...], asked], axis=1)
    at = jnp.concatenate([marks(mortar_ref[...] & (cols_x - 1), cols_x), asked_at], axis=1)
    forces = jnp.concatenate(
        [jnp.where(into < cols_x, forces, 0.0), jnp.where(into < cols_x, 0.0, forces)], axis=0
    )
    forces = summed(times_turned(stacked_terms(forces), at))
    forces = jnp.concatenate([forces[:12], forces[12:]], axis=1)
    total = jnp.zeros((2 * components * strips, cols_x), F32)
    parts = [term.astype(F32) for term in terms_of(forces, 2)]
    for corner in range(4):
        index = nodes_ref[corner : corner + 1, :]
        strip = marks(index >> halves(cols_x), strips)
        spread = []
        for part in parts:
            for k in range(components):
                at = k * 4 + corner
                row = jnp.broadcast_to(part[at : at + 1], (16, face_count)).astype(BF16)
                spread.append(strip * jnp.concatenate([row] * (strips // 16), axis=0))
        along_x = marks(index & (cols_x - 1), cols_x)
        total = total + times_turned(jnp.concatenate(spread, axis=0), along_x)
    contact = summed(total).reshape(components, layers, rows_y, cols_x)
    upward = lax.axis_index("sub") == 1
    edge = edge_part(upward, own_ref, halo_ref, top_ref, under_ref, blocks_ref)
    at = jnp.where(upward, layers - 1, 0)
    copies = []
    for layer in range(layers):
        for k in range(components):
            nodal = internal_ref[k, layer] + jnp.where(at == layer, edge[k], 0.0)
            out_ref[k, layer] = (nodal + contact[k, layer]) * inverse_ref[layer]
            copies.append(
                pltpu.make_async_copy(
                    out_ref.at[k, layer], out_hbm.at[k, layer], sems.at[k, layer]
                )
            )
            copies[-1].start()
    for copy in copies:
        copy.wait()


GROUP = 8


def shifted(layer):
    views = []
    for part in layer:
        rows_y, cols_x = part.shape
        for moved in (part, pltpu.roll(part, rows_y - 1, 0)):
            views += [moved, pltpu.roll(moved, cols_x - 1, 1)]
    return views


def element_forces(matrices, low, high, modulus):
    rows_y, cols_x = modulus.shape
    inside = (lax.broadcasted_iota(jnp.int32, (rows_y, cols_x), 0) < rows_y - 1) & (
        lax.broadcasted_iota(jnp.int32, (rows_y, cols_x), 1) < cols_x - 1
    )
    scale = jnp.where(inside, modulus, 0.0)
    views = shifted(low) + shifted(high)
    both = jnp.concatenate(matrices, axis=0)
    count = both.shape[0] // 2
    strips = []
    for y in range(0, rows_y, GROUP):
        leading, second = terms_of(jnp.concatenate([view[y : y + GROUP] for view in views], axis=0), 2)
        found = times(both, leading)
        force = found[:count] + (found[count:] + times(matrices[0], second))
        strips.append(force.reshape(-1, GROUP, cols_x) * scale[y : y + GROUP][None])
    return jnp.concatenate(strips, axis=1)


def on_nodes(forces):
    sums = []
    for k in range(forces.shape[0] // 4):
        straight, crossed = [
            forces[k * 4 + c] + pltpu.roll(forces[k * 4 + 2 + c], 1, 0) for c in range(2)
        ]
        sums.append(-(straight + pltpu.roll(crossed, 1, 1)))
    return sums


def edge_part(upward, own_ref, halo_ref, top_ref, under_ref, blocks_ref):
    components = own_ref.shape[0]
    size = blocks_ref.shape[1]
    rows = size // 2
    start = jnp.where(upward, 0, rows)
    matrices = [
        blocks_ref[pl.ds(pl.multiple_of(term * size + start, 16), rows)] for term in range(2)
    ]
    low = [jnp.where(upward, own_ref[k], halo_ref[k]) for k in range(components)]
    high = [jnp.where(upward, halo_ref[k], own_ref[k]) for k in range(components)]
    modulus = jnp.where(upward, top_ref[...], under_ref[...])
    return on_nodes(element_forces(matrices, low, high, modulus))


def internal_kernel(
    disp_ref, modulus_ref, stiffness_ref, mass_ref, own_ref, halo_ref, top_ref, under_ref, out_ref,
    blocks_ref, inverse_ref,
):
    inverse_ref[...] = 1.0 / mass_ref[...]
    components, layers, rows_y, cols_x = disp_ref.shape
    dofs = 8 * components
    half = dofs // 2
    size = dofs * GROUP

    row = lax.broadcasted_iota(jnp.int32, (size, dofs), 0) >> halves(GROUP)
    upper = (row >= half).astype(jnp.int32)
    inner = row - half * upper
    dof = (inner >> 2) * 8 + upper * 4 + (inner & 3)
    pick = (dof == lax.broadcasted_iota(jnp.int32, (size, dofs), 1)).astype(F32).astype(BF16)
    diagonal = (lax.broadcasted_iota(jnp.int32, (size, size), 0) & (GROUP - 1)) == (
        lax.broadcasted_iota(jnp.int32, (size, size), 1) & (GROUP - 1)
    )
    for i, term in enumerate(terms_of(stiffness_ref[...], 2)):
        wide = times_turned(times(pick, term).astype(BF16), pick)
        blocks_ref[i * size : (i + 1) * size] = jnp.where(diagonal, wide, 0.0).astype(BF16)

    blocks = [blocks_ref[i * size : (i + 1) * size] for i in range(2)]
    sums = [[0.0] * components for _ in range(layers)]
    for e in range(layers - 1):
        pair = [[disp_ref[k, e + a] for k in range(components)] for a in range(2)]
        forces = element_forces(blocks, pair[0], pair[1], modulus_ref[e])
        for a in range(2):
            part = on_nodes(forces[a * half : (a + 1) * half])
            sums[e + a] = [x + y for x, y in zip(sums[e + a], part)]
    upward = lax.axis_index("sub") == 0
    edge = edge_part(upward, own_ref, halo_ref, top_ref, under_ref, blocks_ref)
    at = jnp.where(upward, layers - 1, 0)
    for layer in range(layers):
        for k in range(components):
            out_ref[k, layer] = sums[layer][k] + jnp.where(at == layer, edge[k], 0.0)


def on_core(kernel, outs, flops, moved, **more):
    return pl.pallas_call(
        kernel,
        out_shape=outs,
        compiler_params=pltpu.CompilerParams(vmem_limit_bytes=48 * 1024 * 1024),
        cost_estimate=pl.CostEstimate(flops=flops, bytes_accessed=moved, transcendentals=0),
        **more,
    )


def swapped(block, axis, first):
    size = lax.axis_size(axis)
    route = []
    for i in range(first, size - 1, 2):
        route += [(i, i + 1), (i + 1, i)]
    return lax.ppermute(block, axis, route)


def raised(block, axis):
    return lax.ppermute(block, axis, [(i, i + 1) for i in range(lax.axis_size(axis) - 1)])


def shards(
    displacement,
    modulus,
    node_mass,
    stiffness,
    face_nodes,
    pair_mortar,
    pair_rank,
    pair_face,
    pair_count,
    pair_shape,
    pair_weight,
    pair_gap,
    pair_normal,
):
    components, layers, rows_y, cols_x = displacement.shape
    face_count = face_nodes.shape[1]
    pair_total = pair_mortar.shape[0]
    domains = lax.axis_size("dom")
    capacity = max(2, 2 * pair_total // domains)

    points = pair_weight.shape[0]
    full = points // 8 * 8
    group = LANES // capacity
    word_rows = 5 * full + 16
    heights = tuple(-(-rows // (8 * group)) * 8 for rows in (4 * full, full + 16))
    rows_high = 12 * face_count // LANES
    line = (1, pair_total)

    def first(*refs):
        first_kernel(capacity, heights, *refs)

    def last(*refs):
        last_kernel(capacity, heights, *refs)

    def shaped(shape, dtype=F32):
        return jax.ShapeDtypeStruct(shape, dtype)

    arrays = [
        face_nodes,
        displacement,
        pair_mortar.reshape(line),
        pair_rank.reshape(line),
        pair_face.reshape(line),
        pair_count.reshape(line),
        pair_weight,
        pair_normal,
        pair_gap,
        jnp.swapaxes(pair_shape, 0, 1),
        modulus,
        node_mass,
    ]
    edge = shaped((components, rows_y, cols_x))
    in_hbm = pl.BlockSpec(memory_space=pltpu.HBM)
    in_vmem = pl.BlockSpec(memory_space=pltpu.VMEM)
    kept = [displacement, *arrays[5:-1]]
    sent, rows, words, turned, mortar, rank, face, nodes, mass, inner, outer, top = on_core(
        first,
        [
            shaped((domains, rows_high + sum(heights), LANES)),
            shaped((12 * face_count // cols_x, cols_x)),
            shaped((word_rows, pair_total)),
            shaped((4 * full + 8, pair_total)),
            shaped(line, jnp.int32),
            shaped(line, jnp.int32),
            shaped(line, jnp.int32),
            shaped(face_nodes.shape, jnp.int32),
            shaped(node_mass.shape),
            edge,
            edge,
            shaped((rows_y, cols_x)),
        ],
        900_000_000,
        1_500_000,
        in_specs=[in_hbm] * len(arrays),
        out_specs=[in_hbm] + [in_vmem] * 11,
        scratch_shapes=[pltpu.VMEM(x.shape, x.dtype) for x in kept]
        + [
            pltpu.VMEM((rows_high, LANES), F32),
            pltpu.VMEM((domains, heights[0], LANES), F32),
            pltpu.VMEM((domains, heights[1], LANES), F32),
            pltpu.SemaphoreType.DMA((64,)),
            pltpu.SemaphoreType.DMA((3, domains)),
        ],
    )(*[pltpu.with_memory_space_constraint(x, pltpu.HBM) for x in arrays])
    order = [place_in_group(domain, domains) for domain in range(domains)]
    got = lax.all_to_all(
        sent, "dom", split_axis=0, concat_axis=0, axis_index_groups=[order], tiled=True
    )
    inner_halo = swapped(inner, ("dom", "sub"), 0)
    outer_halo = swapped(outer, ("dom", "sub"), 1)
    under = raised(top, ("dom", "sub"))
    size = 8 * components * GROUP
    internal, blocks, inverse = on_core(
        internal_kernel,
        [shaped(displacement.shape), shaped((2 * size, size), BF16), shaped(mass.shape)],
        1_000_000_000,
        700_000,
    )(displacement, modulus, stiffness, mass, inner, inner_halo, top, under)
    return on_core(
        last,
        shaped(displacement.shape),
        1_000_000_000,
        1_500_000,
        out_specs=in_hbm,
        scratch_shapes=[
            pltpu.VMEM(displacement.shape, F32),
            pltpu.SemaphoreType.DMA((components, layers)),
        ],
    )(
        got, rows, words, turned, mortar, rank, face, nodes, inverse, internal, blocks, outer,
        outer_halo, top, under,
    )


def solution(mesh):
    placed = (
        P(None, ("runs", "dom", "sub"), None, None),
        P(("runs", "dom", "sub"), None, None),
        P(("runs", "dom", "sub"), None, None),
        P(),
        P(None, ("runs", "dom", "sub")),
        P(("runs", "dom", "sub")),
        P(("runs", "dom", "sub"), None),
        P(("runs", "dom", "sub")),
        P(("runs", "dom", "sub")),
        P(None, None, ("runs", "dom", "sub")),
        P(None, ("runs", "dom", "sub")),
        P(None, ("runs", "dom", "sub")),
        P(None, ("runs", "dom", "sub")),
    )
    return jax.shard_map(
        shards,
        mesh=mesh,
        in_specs=placed,
        out_specs=P(None, ("runs", "dom", "sub"), None, None),
        check_vma=False,
    )
```

```python
import jax
import jax.numpy as jnp
from jax import lax
from jax.experimental import pallas as pl
from jax.experimental.pallas import tpu as pltpu
from jax.sharding import PartitionSpec as P

F32 = jnp.float32
BF16 = jnp.bfloat16
LANES = 128


def terms_of(x, count):
    terms = []
    for _ in range(count):
        terms.append(x.astype(BF16))
        x = x - terms[-1].astype(F32)
    return terms


def stacked_terms(x):
    return jnp.concatenate(terms_of(x, 2), axis=0)


def summed(stacked):
    rows = stacked.shape[0] // 2
    return stacked[:rows] + stacked[rows:]


def marks(index, count):
    shape = (16, index.shape[1])
    rows = lax.broadcasted_iota(jnp.int32, shape, 0).astype(jnp.int16)
    index = jnp.broadcast_to(index, shape).astype(jnp.int16)
    tiles = [
        jnp.where(rows == index - jnp.int16(start), jnp.ones((), BF16), jnp.zeros((), BF16))
        for start in range(0, count, 16)
    ]
    return jnp.concatenate(tiles, axis=0)


def times(left, right):
    return jnp.dot(left, right, preferred_element_type=F32)


def times_turned(left, right):
    return lax.dot_general(left, right, (((1,), (1,)), ((), ())), preferred_element_type=F32)


def halves(power):
    return power.bit_length() - 1


def looked_up(table, face, at):
    both = summed(times(stacked_terms(table), at))
    return jnp.where(face < table.shape[1], both[:12], both[12:])


def folded(placed, height, capacity, domain):
    group = LANES // capacity
    tile, spot = domain // group, domain % group
    part = lax.broadcasted_iota(jnp.int32, (height, LANES), 1) >> halves(capacity)
    block = None
    for j in range(group):
        piece = placed[j * height : (j + 1) * height, tile * LANES : (tile + 1) * LANES]
        if j != spot:
            piece = pltpu.roll(piece, (j - spot) * capacity % LANES, 1)
        block = piece if block is None else jnp.where(part == j, piece, block)
    return block


def unfolded(got_ref, start, height, capacity):
    group = LANES // capacity
    part = lax.broadcasted_iota(jnp.int32, (height, LANES), 1) >> halves(capacity)
    pieces = []
    for j in range(group):
        tiles = []
        for first in range(0, got_ref.shape[0], group):
            block = None
            for spot in range(group):
                piece = got_ref[first + spot, start : start + height]
                if j != spot:
                    piece = pltpu.roll(piece, (spot - j) * capacity % LANES, 1)
                block = piece if block is None else jnp.where(part == spot, piece, block)
            tiles.append(block)
        pieces.append(jnp.concatenate(tiles, axis=1))
    return jnp.concatenate(pieces, axis=0)


def routed(words, rows, place):
    extra = rows - words.shape[0]
    if extra:
        words = jnp.concatenate([words, jnp.zeros((extra, words.shape[1]), F32)], axis=0)
    return summed(times_turned(stacked_terms(words), place))


def weighted_pressure(words, full, remote_rows):
    tail = 5 * full
    normal = words[tail + 5 : tail + 8]
    gap, last = words[4 * full : tail], words[tail + 4 : tail + 5]
    for node in range(4):
        across = sum(
            normal[k : k + 1] * remote_rows[k * 4 + node : k * 4 + node + 1] for k in range(3)
        )
        gap = gap + words[node * full : (node + 1) * full] * across
        last = last + words[tail + node : tail + node + 1] * across
    return jnp.maximum(-gap, 0.0), jnp.maximum(-last, 0.0), normal


def loads_on(shapes, full, tail, pressure, last):
    return [
        jnp.sum(pressure * shapes[i * full : (i + 1) * full], axis=0, keepdims=True)
        + last * shapes[tail + i : tail + i + 1]
        for i in range(4)
    ]


def forces_of(normal, loads):
    loads = jnp.concatenate(loads, axis=0)
    return jnp.concatenate([normal[k : k + 1] * loads for k in range(3)], axis=0)


def place_in_group(domain, domains):
    return {0: domains - 1, domains - 1: 0}.get(domain, domain)


def first_kernel(capacity, heights, *refs):
    (
        nodes_hbm, disp_hbm, mortar_hbm, rank_hbm, face_hbm, count_hbm, weight_hbm, normal_hbm,
        gap_hbm, shape_hbm, modulus_hbm,
        sent_ref, rows_ref, words_ref, turned_ref, mortar_ref, rank_ref, face_ref, nodes,
        inner_ref, outer_ref,
        disp, count, weight, normal_v, gap_v, shape, modulus, blocks, sems, copy_sems,
    ) = refs
    components, layers, rows_y, cols_x = disp.shape
    sources = (
        nodes_hbm, disp_hbm, rank_hbm, face_hbm, mortar_hbm, shape_hbm, count_hbm, weight_hbm,
        normal_hbm, gap_hbm, modulus_hbm.at[disp.shape[1] - 1],
    )
    targets = (
        nodes, disp, rank_ref, face_ref, mortar_ref, shape, count, weight, normal_v, gap_v, modulus,
    )
    brought = [
        pltpu.make_async_copy(source, target, sems.at[i])
        for i, (source, target) in enumerate(zip(sources, targets))
    ]
    for copy in brought:
        copy.start()

    domains = sent_ref.shape[0]
    pair_total = rank_ref.shape[1]
    face_count = nodes.shape[1]
    strips = layers * rows_y
    for copy in brought[:-1]:
        copy.wait()
    rank, face, mortar = rank_ref[...], face_ref[...], mortar_ref[...]
    normal = normal_v[...]
    gap = gap_v[...]

    chosen = lax.broadcasted_iota(jnp.int32, (domains, pair_total), 0) == rank
    before = lax.broadcasted_iota(jnp.int32, (pair_total, pair_total), 0) < lax.broadcasted_iota(
        jnp.int32, (pair_total, pair_total), 1
    )
    earlier = times(chosen.astype(F32).astype(BF16), before.astype(F32).astype(BF16))
    slot = jnp.sum(jnp.where(chosen, earlier, 0.0), axis=0, keepdims=True).astype(jnp.int32)
    place = marks(rank * capacity + slot, domains * capacity)

    parts = stacked_terms(disp[...].reshape(components * strips, cols_x))
    numbers = lax.broadcasted_iota(jnp.int32, (strips, face_count), 0)
    folds = face_count // cols_x
    for corner in range(4):
        index = nodes[corner : corner + 1, :]
        strip = index >> halves(cols_x)
        found = summed(times(parts, marks(index & (cols_x - 1), cols_x)))
        found = found.reshape(components, strips, face_count)
        values = jnp.sum(jnp.where((numbers == strip)[None], found, 0.0), axis=1)
        for fold in range(folds):
            for k in range(components):
                at = fold * 12 + k * 4 + corner
                rows_ref[at : at + 1, :] = values[k : k + 1, fold * cols_x : (fold + 1) * cols_x]

    points = gap.shape[0]
    full = points // 8 * 8
    live = lax.broadcasted_iota(jnp.int32, (points, pair_total), 0) < count[...]
    root = jnp.where(live, jnp.sqrt(weight[...]), 0.0)
    weighted = [root * shape[:, node] for node in range(4)]
    long_words = jnp.concatenate([x[:full] for x in weighted], axis=0)
    group = LANES // capacity
    placed = routed(long_words, group * heights[0], place)

    rows = rows_ref[...]
    high = rows.shape[0]
    rows_high = high * cols_x // LANES
    halved = jnp.concatenate(
        [rows[:, i * LANES : (i + 1) * LANES] for i in range(cols_x // LANES)], axis=0
    )
    starts = (0, rows_high, rows_high + heights[0], rows_high + sum(heights))
    copies = [
        pltpu.make_async_copy(
            blocks.at[:, start:end], sent_ref.at[:, start:end], copy_sems.at[i]
        )
        for i, (start, end) in enumerate(zip(starts, starts[1:]))
    ]
    for domain in range(domains):
        blocks[domain, :rows_high] = halved
    copies[0].start()
    for domain in range(domains):
        spot = place_in_group(domain, domains)
        blocks[spot, starts[1] : starts[2]] = folded(placed, heights[0], capacity, domain)
    copies[1].start()

    mortar_rows = looked_up(rows, mortar, marks(mortar & (cols_x - 1), cols_x))
    for node in range(4):
        across = sum(
            normal[k : k + 1] * mortar_rows[k * 4 + node : k * 4 + node + 1] for k in range(3)
        )
        gap = gap - shape[:, 4 + node] * across
    gap = root * gap
    short_words = jnp.concatenate(
        [gap[:full]]
        + [x[full:] for x in weighted + [gap]]
        + [normal, face.astype(F32), jnp.zeros((7, pair_total), F32)],
        axis=0,
    )
    placed = routed(short_words, group * heights[1], place)
    for domain in range(domains):
        spot = place_in_group(domain, domains)
        blocks[spot, starts[2] :] = folded(placed, heights[1], capacity, domain)
    copies[2].start()

    words_ref[: 4 * full] = long_words
    words_ref[4 * full :] = short_words
    for node in range(4):
        turned = root * shape[:, 4 + node]
        turned_ref[node * full : (node + 1) * full] = turned[:full]
        turned_ref[4 * full + node : 4 * full + node + 1] = turned[full:]

    brought[-1].wait()
    sub = lax.axis_index("sub")
    for target, layer in ((inner_ref, (1 - sub) * (layers - 1)), (outer_ref, sub * (layers - 1))):
        for k in range(components):
            target[k] = disp[k, layer]
        target[components] = modulus[...]
    for copy in copies:
        copy.wait()


def last_kernel(
    capacity, heights, got_ref, rows_ref, words_ref, turned_ref, mortar_ref, rank_ref, face_ref, nodes_ref,
    inverse_ref, internal_ref, blocks_ref, own_ref, halo_ref, out_ref,
):
    domains = got_ref.shape[0]
    components, layers, rows_y, cols_x = out_ref.shape
    strips = layers * rows_y
    face_count = nodes_ref.shape[1]
    pair_total = rank_ref.shape[1]
    folded = rows_ref.shape[0]
    rows_high = folded * cols_x // LANES
    full = (turned_ref.shape[0] - 8) // 4
    own_rows = rows_ref[...]

    rank, face = rank_ref[...], face_ref[...]
    end = domains - 1
    place = jnp.where(rank == 0, end, jnp.where(rank == end, 0, rank))
    at = marks(face & (cols_x - 1), cols_x)
    step = min(domains, 8)

    def add_step(turn, total):
        block = jnp.concatenate(
            [
                got_ref[pl.ds(turn * step, step), i * folded : (i + 1) * folded].reshape(
                    step * folded, LANES
                )
                for i in range(cols_x // LANES)
            ],
            axis=1,
        )
        found = summed(times(stacked_terms(block), at)).reshape(step, folded, pair_total)
        for i in range(step):
            total = total + jnp.where(place == turn * step + i, found[i], 0.0)
        return total

    both = jnp.zeros((folded, pair_total), F32)
    if domains == step:
        both = add_step(0, both)
    else:
        both = lax.fori_loop(0, domains // step, add_step, both)
    remote_rows = jnp.where(face < cols_x, both[:12], both[12:])
    pressure, last, normal = weighted_pressure(words_ref[...], full, remote_rows)
    turned = turned_ref[...]
    mortar_forces = forces_of(-normal, loads_on(turned, full, 4 * full, pressure, last))

    words = jnp.concatenate(
        [
            unfolded(got_ref, rows_high, heights[0], capacity)[: 4 * full],
            unfolded(got_ref, rows_high + heights[0], heights[1], capacity)[: full + 16],
        ],
        axis=0,
    )
    asked = words[5 * full + 8 : 5 * full + 9].astype(jnp.int32)
    asked_at = marks(asked & (cols_x - 1), cols_x)
    remote_rows = looked_up(own_rows, asked, asked_at)
    pressure, last, normal = weighted_pressure(words, full, remote_rows)
    remote_forces = forces_of(normal, loads_on(words, full, 5 * full, pressure, last))

    forces = jnp.concatenate([mortar_forces, remote_forces], axis=1)
    into = jnp.concatenate([mortar_ref[...], asked], axis=1)
    at = jnp.concatenate([marks(mortar_ref[...] & (cols_x - 1), cols_x), asked_at], axis=1)
    forces = jnp.concatenate(
        [jnp.where(into < cols_x, forces, 0.0), jnp.where(into < cols_x, 0.0, forces)], axis=0
    )
    forces = summed(times_turned(stacked_terms(forces), at))
    forces = jnp.concatenate([forces[:12], forces[12:]], axis=1)
    total = jnp.zeros((2 * components * strips, cols_x), F32)
    parts = [term.astype(F32) for term in terms_of(forces, 2)]
    for corner in range(4):
        index = nodes_ref[corner : corner + 1, :]
        strip = marks(index >> halves(cols_x), strips)
        spread = []
        for part in parts:
            for k in range(components):
                at = k * 4 + corner
                row = jnp.broadcast_to(part[at : at + 1], (16, face_count)).astype(BF16)
                spread.append(strip * jnp.concatenate([row] * (strips // 16), axis=0))
        along_x = marks(index & (cols_x - 1), cols_x)
        total = total + times_turned(jnp.concatenate(spread, axis=0), along_x)
    contact = summed(total).reshape(components, layers, rows_y, cols_x)
    upward = lax.axis_index("sub") == 1
    edge = edge_part(upward, own_ref, halo_ref, blocks_ref)
    at = jnp.where(upward, layers - 1, 0)
    for layer in range(layers):
        for k in range(components):
            nodal = internal_ref[k, layer] + jnp.where(at == layer, edge[k], 0.0)
            out_ref[k, layer] = (nodal + contact[k, layer]) * inverse_ref[layer]


GROUP = 8


def shifted(layer):
    views = []
    for part in layer:
        rows_y, cols_x = part.shape
        for moved in (part, pltpu.roll(part, rows_y - 1, 0)):
            views += [moved, pltpu.roll(moved, cols_x - 1, 1)]
    return views


def element_forces(matrices, low, high, modulus):
    rows_y, cols_x = modulus.shape
    inside = (lax.broadcasted_iota(jnp.int32, (rows_y, cols_x), 0) < rows_y - 1) & (
        lax.broadcasted_iota(jnp.int32, (rows_y, cols_x), 1) < cols_x - 1
    )
    scale = jnp.where(inside, modulus, 0.0)
    views = shifted(low) + shifted(high)
    both = jnp.concatenate(matrices, axis=0)
    count = both.shape[0] // 2
    strips = []
    for y in range(0, rows_y, GROUP):
        leading, second = terms_of(jnp.concatenate([view[y : y + GROUP] for view in views], axis=0), 2)
        found = times(both, leading)
        force = found[:count] + (found[count:] + times(matrices[0], second))
        strips.append(force.reshape(-1, GROUP, cols_x) * scale[y : y + GROUP][None])
    return jnp.concatenate(strips, axis=1)


def on_nodes(forces):
    sums = []
    for k in range(forces.shape[0] // 4):
        straight, crossed = [
            forces[k * 4 + c] + pltpu.roll(forces[k * 4 + 2 + c], 1, 0) for c in range(2)
        ]
        sums.append(-(straight + pltpu.roll(crossed, 1, 1)))
    return sums


def edge_part(upward, own_ref, halo_ref, blocks_ref):
    components = own_ref.shape[0] - 1
    size = blocks_ref.shape[1]
    rows = size // 2
    start = jnp.where(upward, 0, rows)
    matrices = [
        blocks_ref[pl.ds(pl.multiple_of(term * size + start, 16), rows)] for term in range(2)
    ]
    low = [jnp.where(upward, own_ref[k], halo_ref[k]) for k in range(components + 1)]
    high = [jnp.where(upward, halo_ref[k], own_ref[k]) for k in range(components)]
    return on_nodes(element_forces(matrices, low[:components], high, low[components]))


def internal_kernel(
    disp_ref, modulus_ref, stiffness_ref, mass_ref, own_ref, halo_ref, out_ref, blocks_ref, inverse_ref
):
    inverse_ref[...] = 1.0 / mass_ref[...]
    components, layers, rows_y, cols_x = disp_ref.shape
    dofs = 8 * components
    half = dofs // 2
    size = dofs * GROUP

    row = lax.broadcasted_iota(jnp.int32, (size, dofs), 0) >> halves(GROUP)
    upper = (row >= half).astype(jnp.int32)
    inner = row - half * upper
    dof = (inner >> 2) * 8 + upper * 4 + (inner & 3)
    pick = (dof == lax.broadcasted_iota(jnp.int32, (size, dofs), 1)).astype(F32).astype(BF16)
    diagonal = (lax.broadcasted_iota(jnp.int32, (size, size), 0) & (GROUP - 1)) == (
        lax.broadcasted_iota(jnp.int32, (size, size), 1) & (GROUP - 1)
    )
    for i, term in enumerate(terms_of(stiffness_ref[...], 2)):
        wide = times_turned(times(pick, term).astype(BF16), pick)
        blocks_ref[i * size : (i + 1) * size] = jnp.where(diagonal, wide, 0.0).astype(BF16)

    blocks = [blocks_ref[i * size : (i + 1) * size] for i in range(2)]
    sums = [[0.0] * components for _ in range(layers)]
    for e in range(layers - 1):
        pair = [[disp_ref[k, e + a] for k in range(components)] for a in range(2)]
        forces = element_forces(blocks, pair[0], pair[1], modulus_ref[e])
        for a in range(2):
            part = on_nodes(forces[a * half : (a + 1) * half])
            sums[e + a] = [x + y for x, y in zip(sums[e + a], part)]
    upward = lax.axis_index("sub") == 0
    edge = edge_part(upward, own_ref, halo_ref, blocks_ref)
    at = jnp.where(upward, layers - 1, 0)
    for layer in range(layers):
        for k in range(components):
            out_ref[k, layer] = sums[layer][k] + jnp.where(at == layer, edge[k], 0.0)


def on_core(kernel, outs, flops, moved, **more):
    return pl.pallas_call(
        kernel,
        out_shape=outs,
        compiler_params=pltpu.CompilerParams(vmem_limit_bytes=48 * 1024 * 1024),
        cost_estimate=pl.CostEstimate(flops=flops, bytes_accessed=moved, transcendentals=0),
        **more,
    )


def swapped(block, axis, first):
    size = lax.axis_size(axis)
    route = []
    for i in range(first, size - 1, 2):
        route += [(i, i + 1), (i + 1, i)]
    return lax.ppermute(block, axis, route)


def shards(
    displacement,
    modulus,
    node_mass,
    stiffness,
    face_nodes,
    pair_mortar,
    pair_rank,
    pair_face,
    pair_count,
    pair_shape,
    pair_weight,
    pair_gap,
    pair_normal,
):
    components, layers, rows_y, cols_x = displacement.shape
    face_count = face_nodes.shape[1]
    pair_total = pair_mortar.shape[0]
    domains = lax.axis_size("dom")
    capacity = max(2, 2 * pair_total // domains)

    points = pair_weight.shape[0]
    full = points // 8 * 8
    group = LANES // capacity
    word_rows = 5 * full + 16
    heights = tuple(-(-rows // (8 * group)) * 8 for rows in (4 * full, full + 16))
    rows_high = 12 * face_count // LANES
    line = (1, pair_total)

    def first(*refs):
        first_kernel(capacity, heights, *refs)

    def last(*refs):
        last_kernel(capacity, heights, *refs)

    def shaped(shape, dtype=F32):
        return jax.ShapeDtypeStruct(shape, dtype)

    arrays = [
        face_nodes,
        displacement,
        pair_mortar.reshape(line),
        pair_rank.reshape(line),
        pair_face.reshape(line),
        pair_count.reshape(line),
        pair_weight,
        pair_normal,
        pair_gap,
        jnp.swapaxes(pair_shape, 0, 1),
        modulus,
    ]
    edge = shaped((components + 1, rows_y, cols_x))
    in_hbm = pl.BlockSpec(memory_space=pltpu.HBM)
    in_vmem = pl.BlockSpec(memory_space=pltpu.VMEM)
    kept = [displacement, *arrays[5:-1], modulus[0]]
    sent, rows, words, turned, mortar, rank, face, nodes, inner, outer = on_core(
        first,
        [
            shaped((domains, rows_high + sum(heights), LANES)),
            shaped((12 * face_count // cols_x, cols_x)),
            shaped((word_rows, pair_total)),
            shaped((4 * full + 8, pair_total)),
            shaped(line, jnp.int32),
            shaped(line, jnp.int32),
            shaped(line, jnp.int32),
            shaped(face_nodes.shape, jnp.int32),
            edge,
            edge,
        ],
        900_000_000,
        1_500_000,
        in_specs=[in_hbm] * len(arrays),
        out_specs=[in_hbm] + [in_vmem] * 9,
        scratch_shapes=[pltpu.VMEM(x.shape, x.dtype) for x in kept]
        + [
            pltpu.VMEM((domains, rows_high + sum(heights), LANES), F32),
            pltpu.SemaphoreType.DMA((len(arrays),)),
            pltpu.SemaphoreType.DMA((3,)),
        ],
    )(*[pltpu.with_memory_space_constraint(x, pltpu.HBM) for x in arrays])
    order = [place_in_group(domain, domains) for domain in range(domains)]
    got = lax.all_to_all(
        sent, "dom", split_axis=0, concat_axis=0, axis_index_groups=[order], tiled=True
    )
    inner_halo = swapped(inner, ("dom", "sub"), 0)
    outer_halo = swapped(outer, ("dom", "sub"), 1)
    size = 8 * components * GROUP
    internal, blocks, inverse = on_core(
        internal_kernel,
        [shaped(displacement.shape), shaped((2 * size, size), BF16), shaped(node_mass.shape)],
        1_000_000_000,
        700_000,
    )(displacement, modulus, stiffness, node_mass, inner, inner_halo)
    return on_core(last, shaped(displacement.shape), 1_000_000_000, 1_500_000)(
        got, rows, words, turned, mortar, rank, face, nodes, inverse, internal, blocks, outer, outer_halo
    )


def solution(mesh):
    placed = (
        P(None, ("runs", "dom", "sub"), None, None),
        P(("runs", "dom", "sub"), None, None),
        P(("runs", "dom", "sub"), None, None),
        P(),
        P(None, ("runs", "dom", "sub")),
        P(("runs", "dom", "sub")),
        P(("runs", "dom", "sub"), None),
        P(("runs", "dom", "sub")),
        P(("runs", "dom", "sub")),
        P(None, None, ("runs", "dom", "sub")),
        P(None, ("runs", "dom", "sub")),
        P(None, ("runs", "dom", "sub")),
        P(None, ("runs", "dom", "sub")),
    )
    return jax.shard_map(
        shards,
        mesh=mesh,
        in_specs=placed,
        out_specs=P(None, ("runs", "dom", "sub"), None, None),
        check_vma=False,
    )
```

```python
import jax
import jax.numpy as jnp
from jax import lax
from jax.experimental import pallas as pl
from jax.experimental.pallas import tpu as pltpu
from jax.sharding import PartitionSpec as P

F32 = jnp.float32
BF16 = jnp.bfloat16
LANES = 128


def terms_of(x, count):
    terms = []
    for _ in range(count):
        terms.append(x.astype(BF16))
        x = x - terms[-1].astype(F32)
    return terms


def stacked_terms(x):
    return jnp.concatenate(terms_of(x, 2), axis=0)


def summed(stacked):
    rows = stacked.shape[0] // 2
    return stacked[:rows] + stacked[rows:]


def marks(index, count):
    shape = (16, index.shape[1])
    rows = lax.broadcasted_iota(jnp.int32, shape, 0).astype(jnp.int16)
    index = jnp.broadcast_to(index, shape).astype(jnp.int16)
    tiles = [
        jnp.where(rows == index - jnp.int16(start), jnp.ones((), BF16), jnp.zeros((), BF16))
        for start in range(0, count, 16)
    ]
    return jnp.concatenate(tiles, axis=0)


def times(left, right):
    return jnp.dot(left, right, preferred_element_type=F32)


def times_turned(left, right):
    return lax.dot_general(left, right, (((1,), (1,)), ((), ())), preferred_element_type=F32)


def halves(power):
    return power.bit_length() - 1


def looked_up(table, face, at):
    both = summed(times(stacked_terms(table), at))
    return jnp.where(face < table.shape[1], both[:12], both[12:])


def folded(placed, height, capacity, domain):
    group = LANES // capacity
    tile, spot = domain // group, domain % group
    part = lax.broadcasted_iota(jnp.int32, (height, LANES), 1) >> halves(capacity)
    block = None
    for j in range(group):
        piece = placed[j * height : (j + 1) * height, tile * LANES : (tile + 1) * LANES]
        if j != spot:
            piece = pltpu.roll(piece, (j - spot) * capacity % LANES, 1)
        block = piece if block is None else jnp.where(part == j, piece, block)
    return block


def unfolded(got_ref, start, height, capacity):
    group = LANES // capacity
    part = lax.broadcasted_iota(jnp.int32, (height, LANES), 1) >> halves(capacity)
    pieces = []
    for j in range(group):
        tiles = []
        for first in range(0, got_ref.shape[0], group):
            block = None
            for spot in range(group):
                piece = got_ref[first + spot, start : start + height]
                if j != spot:
                    piece = pltpu.roll(piece, (spot - j) * capacity % LANES, 1)
                block = piece if block is None else jnp.where(part == spot, piece, block)
            tiles.append(block)
        pieces.append(jnp.concatenate(tiles, axis=1))
    return jnp.concatenate(pieces, axis=0)


def routed(words, rows, place):
    extra = rows - words.shape[0]
    if extra:
        words = jnp.concatenate([words, jnp.zeros((extra, words.shape[1]), F32)], axis=0)
    return summed(times_turned(stacked_terms(words), place))


def weighted_pressure(words, full, remote_rows):
    tail = 5 * full
    normal = words[tail + 5 : tail + 8]
    gap, last = words[4 * full : tail], words[tail + 4 : tail + 5]
    for node in range(4):
        across = sum(
            normal[k : k + 1] * remote_rows[k * 4 + node : k * 4 + node + 1] for k in range(3)
        )
        gap = gap + words[node * full : (node + 1) * full] * across
        last = last + words[tail + node : tail + node + 1] * across
    return jnp.maximum(-gap, 0.0), jnp.maximum(-last, 0.0), normal


def loads_on(shapes, full, tail, pressure, last):
    return [
        jnp.sum(pressure * shapes[i * full : (i + 1) * full], axis=0, keepdims=True)
        + last * shapes[tail + i : tail + i + 1]
        for i in range(4)
    ]


def forces_of(normal, loads):
    loads = jnp.concatenate(loads, axis=0)
    return jnp.concatenate([normal[k : k + 1] * loads for k in range(3)], axis=0)


def place_in_group(domain, domains):
    half = domains // 2
    if isinstance(domain, int):
        return 2 * (domains - 1 - domain) if domain >= half else 2 * (half - 1 - domain) + 1
    return jnp.where(domain >= half, 2 * (domains - 1 - domain), 2 * (half - 1 - domain) + 1)


def first_kernel(capacity, heights, *refs):
    (
        nodes_hbm, disp_hbm, mortar_hbm, rank_hbm, face_hbm, count_hbm, weight_hbm, normal_hbm,
        gap_hbm, shape_hbm, modulus_hbm,
        sent_ref, rows_ref, words_ref, turned_ref, mortar_ref, rank_ref, face_ref, nodes,
        inner_ref, outer_ref,
        disp, count, weight, normal_v, gap_v, shape, modulus, blocks, sems, copy_sems,
    ) = refs
    components, layers, rows_y, cols_x = disp.shape
    sources = (
        nodes_hbm, disp_hbm, rank_hbm, face_hbm, mortar_hbm, shape_hbm, count_hbm, weight_hbm,
        normal_hbm, gap_hbm, modulus_hbm.at[disp.shape[1] - 1],
    )
    targets = (
        nodes, disp, rank_ref, face_ref, mortar_ref, shape, count, weight, normal_v, gap_v, modulus,
    )
    brought = [
        pltpu.make_async_copy(source, target, sems.at[i])
        for i, (source, target) in enumerate(zip(sources, targets))
    ]
    for copy in brought:
        copy.start()

    domains = sent_ref.shape[0]
    pair_total = rank_ref.shape[1]
    face_count = nodes.shape[1]
    strips = layers * rows_y
    for copy in brought[:-1]:
        copy.wait()
    rank, face, mortar = rank_ref[...], face_ref[...], mortar_ref[...]
    normal = normal_v[...]
    gap = gap_v[...]

    chosen = lax.broadcasted_iota(jnp.int32, (domains, pair_total), 0) == rank
    before = lax.broadcasted_iota(jnp.int32, (pair_total, pair_total), 0) < lax.broadcasted_iota(
        jnp.int32, (pair_total, pair_total), 1
    )
    earlier = times(chosen.astype(F32).astype(BF16), before.astype(F32).astype(BF16))
    slot = jnp.sum(jnp.where(chosen, earlier, 0.0), axis=0, keepdims=True).astype(jnp.int32)
    place = marks(rank * capacity + slot, domains * capacity)

    parts = stacked_terms(disp[...].reshape(components * strips, cols_x))
    numbers = lax.broadcasted_iota(jnp.int32, (strips, face_count), 0)
    folds = face_count // cols_x
    for corner in range(4):
        index = nodes[corner : corner + 1, :]
        strip = index >> halves(cols_x)
        found = summed(times(parts, marks(index & (cols_x - 1), cols_x)))
        found = found.reshape(components, strips, face_count)
        values = jnp.sum(jnp.where((numbers == strip)[None], found, 0.0), axis=1)
        for fold in range(folds):
            for k in range(components):
                at = fold * 12 + k * 4 + corner
                rows_ref[at : at + 1, :] = values[k : k + 1, fold * cols_x : (fold + 1) * cols_x]

    points = gap.shape[0]
    full = points // 8 * 8
    live = lax.broadcasted_iota(jnp.int32, (points, pair_total), 0) < count[...]
    root = jnp.where(live, jnp.sqrt(weight[...]), 0.0)
    weighted = [root * shape[:, node] for node in range(4)]
    long_words = jnp.concatenate([x[:full] for x in weighted], axis=0)
    group = LANES // capacity
    placed = routed(long_words, group * heights[0], place)

    rows = rows_ref[...]
    high = rows.shape[0]
    rows_high = high * cols_x // LANES
    halved = jnp.concatenate(
        [rows[:, i * LANES : (i + 1) * LANES] for i in range(cols_x // LANES)], axis=0
    )
    starts = (0, rows_high, rows_high + heights[0], rows_high + sum(heights))
    copies = [
        pltpu.make_async_copy(
            blocks.at[:, start:end], sent_ref.at[:, start:end], copy_sems.at[i]
        )
        for i, (start, end) in enumerate(zip(starts, starts[1:]))
    ]
    for domain in range(domains):
        blocks[domain, :rows_high] = halved
    copies[0].start()
    for domain in range(domains):
        spot = place_in_group(domain, domains)
        blocks[spot, starts[1] : starts[2]] = folded(placed, heights[0], capacity, domain)
    copies[1].start()

    mortar_rows = looked_up(rows, mortar, marks(mortar & (cols_x - 1), cols_x))
    for node in range(4):
        across = sum(
            normal[k : k + 1] * mortar_rows[k * 4 + node : k * 4 + node + 1] for k in range(3)
        )
        gap = gap - shape[:, 4 + node] * across
    gap = root * gap
    short_words = jnp.concatenate(
        [gap[:full]]
        + [x[full:] for x in weighted + [gap]]
        + [normal, face.astype(F32), jnp.zeros((7, pair_total), F32)],
        axis=0,
    )
    placed = routed(short_words, group * heights[1], place)
    for domain in range(domains):
        spot = place_in_group(domain, domains)
        blocks[spot, starts[2] :] = folded(placed, heights[1], capacity, domain)
    copies[2].start()

    words_ref[: 4 * full] = long_words
    words_ref[4 * full :] = short_words
    for node in range(4):
        turned = root * shape[:, 4 + node]
        turned_ref[node * full : (node + 1) * full] = turned[:full]
        turned_ref[4 * full + node : 4 * full + node + 1] = turned[full:]

    brought[-1].wait()
    sub = lax.axis_index("sub")
    for target, layer in ((inner_ref, (1 - sub) * (layers - 1)), (outer_ref, sub * (layers - 1))):
        for k in range(components):
            target[k] = disp[k, layer]
        target[components] = modulus[...]
    for copy in copies:
        copy.wait()


def last_kernel(
    capacity, heights, got_ref, rows_ref, words_ref, turned_ref, mortar_ref, rank_ref, face_ref, nodes_ref,
    inverse_ref, internal_ref, blocks_ref, own_ref, halo_ref, out_ref,
):
    domains = got_ref.shape[0]
    components, layers, rows_y, cols_x = out_ref.shape
    strips = layers * rows_y
    face_count = nodes_ref.shape[1]
    pair_total = rank_ref.shape[1]
    folded = rows_ref.shape[0]
    rows_high = folded * cols_x // LANES
    full = (turned_ref.shape[0] - 8) // 4
    own_rows = rows_ref[...]

    rank, face = rank_ref[...], face_ref[...]
    place = place_in_group(rank, domains)
    at = marks(face & (cols_x - 1), cols_x)
    step = min(domains, 8)

    def add_step(turn, total):
        block = jnp.concatenate(
            [
                got_ref[pl.ds(turn * step, step), i * folded : (i + 1) * folded].reshape(
                    step * folded, LANES
                )
                for i in range(cols_x // LANES)
            ],
            axis=1,
        )
        found = summed(times(stacked_terms(block), at)).reshape(step, folded, pair_total)
        for i in range(step):
            total = total + jnp.where(place == turn * step + i, found[i], 0.0)
        return total

    both = jnp.zeros((folded, pair_total), F32)
    if domains == step:
        both = add_step(0, both)
    else:
        both = lax.fori_loop(0, domains // step, add_step, both)
    remote_rows = jnp.where(face < cols_x, both[:12], both[12:])
    pressure, last, normal = weighted_pressure(words_ref[...], full, remote_rows)
    turned = turned_ref[...]
    mortar_forces = forces_of(-normal, loads_on(turned, full, 4 * full, pressure, last))

    words = jnp.concatenate(
        [
            unfolded(got_ref, rows_high, heights[0], capacity)[: 4 * full],
            unfolded(got_ref, rows_high + heights[0], heights[1], capacity)[: full + 16],
        ],
        axis=0,
    )
    asked = words[5 * full + 8 : 5 * full + 9].astype(jnp.int32)
    asked_at = marks(asked & (cols_x - 1), cols_x)
    remote_rows = looked_up(own_rows, asked, asked_at)
    pressure, last, normal = weighted_pressure(words, full, remote_rows)
    remote_forces = forces_of(normal, loads_on(words, full, 5 * full, pressure, last))

    forces = jnp.concatenate([mortar_forces, remote_forces], axis=1)
    into = jnp.concatenate([mortar_ref[...], asked], axis=1)
    at = jnp.concatenate([marks(mortar_ref[...] & (cols_x - 1), cols_x), asked_at], axis=1)
    forces = jnp.concatenate(
        [jnp.where(into < cols_x, forces, 0.0), jnp.where(into < cols_x, 0.0, forces)], axis=0
    )
    forces = summed(times_turned(stacked_terms(forces), at))
    forces = jnp.concatenate([forces[:12], forces[12:]], axis=1)
    total = jnp.zeros((2 * components * strips, cols_x), F32)
    parts = [term.astype(F32) for term in terms_of(forces, 2)]
    for corner in range(4):
        index = nodes_ref[corner : corner + 1, :]
        strip = marks(index >> halves(cols_x), strips)
        spread = []
        for part in parts:
            for k in range(components):
                at = k * 4 + corner
                row = jnp.broadcast_to(part[at : at + 1], (16, face_count)).astype(BF16)
                spread.append(strip * jnp.concatenate([row] * (strips // 16), axis=0))
        along_x = marks(index & (cols_x - 1), cols_x)
        total = total + times_turned(jnp.concatenate(spread, axis=0), along_x)
    contact = summed(total).reshape(components, layers, rows_y, cols_x)
    upward = lax.axis_index("sub") == 1
    edge = edge_part(upward, own_ref, halo_ref, blocks_ref)
    at = jnp.where(upward, layers - 1, 0)
    for layer in range(layers):
        for k in range(components):
            nodal = internal_ref[k, layer] + jnp.where(at == layer, edge[k], 0.0)
            out_ref[k, layer] = (nodal + contact[k, layer]) * inverse_ref[layer]


GROUP = 8


def shifted(layer):
    views = []
    for part in layer:
        rows_y, cols_x = part.shape
        for moved in (part, pltpu.roll(part, rows_y - 1, 0)):
            views += [moved, pltpu.roll(moved, cols_x - 1, 1)]
    return views


def element_forces(matrices, low, high, modulus):
    rows_y, cols_x = modulus.shape
    inside = (lax.broadcasted_iota(jnp.int32, (rows_y, cols_x), 0) < rows_y - 1) & (
        lax.broadcasted_iota(jnp.int32, (rows_y, cols_x), 1) < cols_x - 1
    )
    scale = jnp.where(inside, modulus, 0.0)
    views = shifted(low) + shifted(high)
    both = jnp.concatenate(matrices, axis=0)
    count = both.shape[0] // 2
    strips = []
    for y in range(0, rows_y, GROUP):
        leading, second = terms_of(jnp.concatenate([view[y : y + GROUP] for view in views], axis=0), 2)
        found = times(both, leading)
        force = found[:count] + (found[count:] + times(matrices[0], second))
        strips.append(force.reshape(-1, GROUP, cols_x) * scale[y : y + GROUP][None])
    return jnp.concatenate(strips, axis=1)


def on_nodes(forces):
    sums = []
    for k in range(forces.shape[0] // 4):
        straight, crossed = [
            forces[k * 4 + c] + pltpu.roll(forces[k * 4 + 2 + c], 1, 0) for c in range(2)
        ]
        sums.append(-(straight + pltpu.roll(crossed, 1, 1)))
    return sums


def edge_part(upward, own_ref, halo_ref, blocks_ref):
    components = own_ref.shape[0] - 1
    size = blocks_ref.shape[1]
    rows = size // 2
    start = jnp.where(upward, 0, rows)
    matrices = [
        blocks_ref[pl.ds(pl.multiple_of(term * size + start, 16), rows)] for term in range(2)
    ]
    low = [jnp.where(upward, own_ref[k], halo_ref[k]) for k in range(components + 1)]
    high = [jnp.where(upward, halo_ref[k], own_ref[k]) for k in range(components)]
    return on_nodes(element_forces(matrices, low[:components], high, low[components]))


def internal_kernel(
    disp_ref, modulus_ref, stiffness_ref, mass_ref, own_ref, halo_ref, out_ref, blocks_ref, inverse_ref
):
    inverse_ref[...] = 1.0 / mass_ref[...]
    components, layers, rows_y, cols_x = disp_ref.shape
    dofs = 8 * components
    half = dofs // 2
    size = dofs * GROUP

    row = lax.broadcasted_iota(jnp.int32, (size, dofs), 0) >> halves(GROUP)
    upper = (row >= half).astype(jnp.int32)
    inner = row - half * upper
    dof = (inner >> 2) * 8 + upper * 4 + (inner & 3)
    pick = (dof == lax.broadcasted_iota(jnp.int32, (size, dofs), 1)).astype(F32).astype(BF16)
    diagonal = (lax.broadcasted_iota(jnp.int32, (size, size), 0) & (GROUP - 1)) == (
        lax.broadcasted_iota(jnp.int32, (size, size), 1) & (GROUP - 1)
    )
    for i, term in enumerate(terms_of(stiffness_ref[...], 2)):
        wide = times_turned(times(pick, term).astype(BF16), pick)
        blocks_ref[i * size : (i + 1) * size] = jnp.where(diagonal, wide, 0.0).astype(BF16)

    blocks = [blocks_ref[i * size : (i + 1) * size] for i in range(2)]
    sums = [[0.0] * components for _ in range(layers)]
    for e in range(layers - 1):
        pair = [[disp_ref[k, e + a] for k in range(components)] for a in range(2)]
        forces = element_forces(blocks, pair[0], pair[1], modulus_ref[e])
        for a in range(2):
            part = on_nodes(forces[a * half : (a + 1) * half])
            sums[e + a] = [x + y for x, y in zip(sums[e + a], part)]
    upward = lax.axis_index("sub") == 0
    edge = edge_part(upward, own_ref, halo_ref, blocks_ref)
    at = jnp.where(upward, layers - 1, 0)
    for layer in range(layers):
        for k in range(components):
            out_ref[k, layer] = sums[layer][k] + jnp.where(at == layer, edge[k], 0.0)


def on_core(kernel, outs, flops, moved, **more):
    return pl.pallas_call(
        kernel,
        out_shape=outs,
        compiler_params=pltpu.CompilerParams(vmem_limit_bytes=48 * 1024 * 1024),
        cost_estimate=pl.CostEstimate(flops=flops, bytes_accessed=moved, transcendentals=0),
        **more,
    )


def swapped(block, axis, first):
    size = lax.axis_size(axis)
    route = []
    for i in range(first, size - 1, 2):
        route += [(i, i + 1), (i + 1, i)]
    return lax.ppermute(block, axis, route)


def shards(
    displacement,
    modulus,
    node_mass,
    stiffness,
    face_nodes,
    pair_mortar,
    pair_rank,
    pair_face,
    pair_count,
    pair_shape,
    pair_weight,
    pair_gap,
    pair_normal,
):
    components, layers, rows_y, cols_x = displacement.shape
    face_count = face_nodes.shape[1]
    pair_total = pair_mortar.shape[0]
    domains = lax.axis_size("dom")
    capacity = max(2, 2 * pair_total // domains)

    points = pair_weight.shape[0]
    full = points // 8 * 8
    group = LANES // capacity
    word_rows = 5 * full + 16
    heights = tuple(-(-rows // (8 * group)) * 8 for rows in (4 * full, full + 16))
    rows_high = 12 * face_count // LANES
    line = (1, pair_total)

    def first(*refs):
        first_kernel(capacity, heights, *refs)

    def last(*refs):
        last_kernel(capacity, heights, *refs)

    def shaped(shape, dtype=F32):
        return jax.ShapeDtypeStruct(shape, dtype)

    arrays = [
        face_nodes,
        displacement,
        pair_mortar.reshape(line),
        pair_rank.reshape(line),
        pair_face.reshape(line),
        pair_count.reshape(line),
        pair_weight,
        pair_normal,
        pair_gap,
        jnp.swapaxes(pair_shape, 0, 1),
        modulus,
    ]
    edge = shaped((components + 1, rows_y, cols_x))
    in_hbm = pl.BlockSpec(memory_space=pltpu.HBM)
    in_vmem = pl.BlockSpec(memory_space=pltpu.VMEM)
    kept = [displacement, *arrays[5:-1], modulus[0]]
    sent, rows, words, turned, mortar, rank, face, nodes, inner, outer = on_core(
        first,
        [
            shaped((domains, rows_high + sum(heights), LANES)),
            shaped((12 * face_count // cols_x, cols_x)),
            shaped((word_rows, pair_total)),
            shaped((4 * full + 8, pair_total)),
            shaped(line, jnp.int32),
            shaped(line, jnp.int32),
            shaped(line, jnp.int32),
            shaped(face_nodes.shape, jnp.int32),
            edge,
            edge,
        ],
        900_000_000,
        1_500_000,
        in_specs=[in_hbm] * len(arrays),
        out_specs=[in_hbm] + [in_vmem] * 9,
        scratch_shapes=[pltpu.VMEM(x.shape, x.dtype) for x in kept]
        + [
            pltpu.VMEM((domains, rows_high + sum(heights), LANES), F32),
            pltpu.SemaphoreType.DMA((len(arrays),)),
            pltpu.SemaphoreType.DMA((3,)),
        ],
    )(*[pltpu.with_memory_space_constraint(x, pltpu.HBM) for x in arrays])
    order = sorted(range(domains), key=lambda domain: place_in_group(domain, domains))
    got = lax.all_to_all(
        sent, "dom", split_axis=0, concat_axis=0, axis_index_groups=[order], tiled=True
    )
    inner_halo = swapped(inner, ("dom", "sub"), 0)
    outer_halo = swapped(outer, ("dom", "sub"), 1)
    size = 8 * components * GROUP
    internal, blocks, inverse = on_core(
        internal_kernel,
        [shaped(displacement.shape), shaped((2 * size, size), BF16), shaped(node_mass.shape)],
        1_000_000_000,
        700_000,
    )(displacement, modulus, stiffness, node_mass, inner, inner_halo)
    return on_core(last, shaped(displacement.shape), 1_000_000_000, 1_500_000)(
        got, rows, words, turned, mortar, rank, face, nodes, inverse, internal, blocks, outer, outer_halo
    )


def solution(mesh):
    placed = (
        P(None, ("runs", "dom", "sub"), None, None),
        P(("runs", "dom", "sub"), None, None),
        P(("runs", "dom", "sub"), None, None),
        P(),
        P(None, ("runs", "dom", "sub")),
        P(("runs", "dom", "sub")),
        P(("runs", "dom", "sub"), None),
        P(("runs", "dom", "sub")),
        P(("runs", "dom", "sub")),
        P(None, None, ("runs", "dom", "sub")),
        P(None, ("runs", "dom", "sub")),
        P(None, ("runs", "dom", "sub")),
        P(None, ("runs", "dom", "sub")),
    )
    return jax.shard_map(
        shards,
        mesh=mesh,
        in_specs=placed,
        out_specs=P(None, ("runs", "dom", "sub"), None, None),
        check_vma=False,
    )
```

```python
import jax
import jax.numpy as jnp
from jax import lax
from jax.experimental import pallas as pl
from jax.experimental.pallas import tpu as pltpu
from jax.sharding import PartitionSpec as P

F32 = jnp.float32
BF16 = jnp.bfloat16
LANES = 128


def terms_of(x, count):
    terms = []
    for _ in range(count):
        terms.append(x.astype(BF16))
        x = x - terms[-1].astype(F32)
    return terms


def stacked_terms(x):
    return jnp.concatenate(terms_of(x, 2), axis=0)


def summed(stacked):
    rows = stacked.shape[0] // 2
    return stacked[:rows] + stacked[rows:]


def marks(index, count):
    shape = (16, index.shape[1])
    rows = lax.broadcasted_iota(jnp.int32, shape, 0).astype(jnp.int16)
    index = jnp.broadcast_to(index, shape).astype(jnp.int16)
    tiles = [
        jnp.where(rows == index - jnp.int16(start), jnp.ones((), BF16), jnp.zeros((), BF16))
        for start in range(0, count, 16)
    ]
    return jnp.concatenate(tiles, axis=0)


def times(left, right):
    return jnp.dot(left, right, preferred_element_type=F32)


def times_turned(left, right):
    return lax.dot_general(left, right, (((1,), (1,)), ((), ())), preferred_element_type=F32)


def halves(power):
    return power.bit_length() - 1


def looked_up(table, face, at):
    both = summed(times(stacked_terms(table), at))
    return jnp.where(face < table.shape[1], both[:12], both[12:])


def folded(placed, height, capacity, domain):
    group = LANES // capacity
    tile, spot = domain // group, domain % group
    part = lax.broadcasted_iota(jnp.int32, (height, LANES), 1) >> halves(capacity)
    block = None
    for j in range(group):
        piece = placed[j * height : (j + 1) * height, tile * LANES : (tile + 1) * LANES]
        if j != spot:
            piece = pltpu.roll(piece, (j - spot) * capacity % LANES, 1)
        block = piece if block is None else jnp.where(part == j, piece, block)
    return block


def unfolded(got_ref, start, height, capacity):
    group = LANES // capacity
    part = lax.broadcasted_iota(jnp.int32, (height, LANES), 1) >> halves(capacity)
    pieces = []
    for j in range(group):
        tiles = []
        for first in range(0, got_ref.shape[0], group):
            block = None
            for spot in range(group):
                piece = got_ref[first + spot, start : start + height]
                if j != spot:
                    piece = pltpu.roll(piece, (spot - j) * capacity % LANES, 1)
                block = piece if block is None else jnp.where(part == spot, piece, block)
            tiles.append(block)
        pieces.append(jnp.concatenate(tiles, axis=1))
    return jnp.concatenate(pieces, axis=0)


def routed(words, rows, place):
    extra = rows - words.shape[0]
    if extra:
        words = jnp.concatenate([words, jnp.zeros((extra, words.shape[1]), F32)], axis=0)
    return summed(times_turned(stacked_terms(words), place))


def weighted_pressure(words, full, remote_rows):
    tail = 5 * full
    normal = words[tail + 5 : tail + 8]
    gap, last = words[4 * full : tail], words[tail + 4 : tail + 5]
    for node in range(4):
        across = sum(
            normal[k : k + 1] * remote_rows[k * 4 + node : k * 4 + node + 1] for k in range(3)
        )
        gap = gap + words[node * full : (node + 1) * full] * across
        last = last + words[tail + node : tail + node + 1] * across
    return jnp.maximum(-gap, 0.0), jnp.maximum(-last, 0.0), normal


def loads_on(shapes, full, tail, pressure, last):
    return [
        jnp.sum(pressure * shapes[i * full : (i + 1) * full], axis=0, keepdims=True)
        + last * shapes[tail + i : tail + i + 1]
        for i in range(4)
    ]


def forces_of(normal, loads):
    loads = jnp.concatenate(loads, axis=0)
    return jnp.concatenate([normal[k : k + 1] * loads for k in range(3)], axis=0)


def place_in_group(domain, domains):
    return domains - 1 - domain


def first_kernel(capacity, heights, *refs):
    (
        nodes_hbm, disp_hbm, mortar_hbm, rank_hbm, face_hbm, count_hbm, weight_hbm, normal_hbm,
        gap_hbm, shape_hbm, modulus_hbm,
        sent_ref, rows_ref, words_ref, turned_ref, mortar_ref, rank_ref, face_ref, nodes,
        inner_ref, outer_ref,
        disp, count, weight, normal_v, gap_v, shape, modulus, blocks, sems, copy_sems,
    ) = refs
    components, layers, rows_y, cols_x = disp.shape
    sources = (
        nodes_hbm, disp_hbm, rank_hbm, face_hbm, mortar_hbm, shape_hbm, count_hbm, weight_hbm,
        normal_hbm, gap_hbm, modulus_hbm.at[disp.shape[1] - 1],
    )
    targets = (
        nodes, disp, rank_ref, face_ref, mortar_ref, shape, count, weight, normal_v, gap_v, modulus,
    )
    brought = [
        pltpu.make_async_copy(source, target, sems.at[i])
        for i, (source, target) in enumerate(zip(sources, targets))
    ]
    for copy in brought:
        copy.start()

    domains = sent_ref.shape[0]
    pair_total = rank_ref.shape[1]
    face_count = nodes.shape[1]
    strips = layers * rows_y
    for copy in brought[:-1]:
        copy.wait()
    rank, face, mortar = rank_ref[...], face_ref[...], mortar_ref[...]
    normal = normal_v[...]
    gap = gap_v[...]

    chosen = lax.broadcasted_iota(jnp.int32, (domains, pair_total), 0) == rank
    before = lax.broadcasted_iota(jnp.int32, (pair_total, pair_total), 0) < lax.broadcasted_iota(
        jnp.int32, (pair_total, pair_total), 1
    )
    earlier = times(chosen.astype(F32).astype(BF16), before.astype(F32).astype(BF16))
    slot = jnp.sum(jnp.where(chosen, earlier, 0.0), axis=0, keepdims=True).astype(jnp.int32)
    place = marks(rank * capacity + slot, domains * capacity)

    parts = stacked_terms(disp[...].reshape(components * strips, cols_x))
    numbers = lax.broadcasted_iota(jnp.int32, (strips, face_count), 0)
    folds = face_count // cols_x
    for corner in range(4):
        index = nodes[corner : corner + 1, :]
        strip = index >> halves(cols_x)
        found = summed(times(parts, marks(index & (cols_x - 1), cols_x)))
        found = found.reshape(components, strips, face_count)
        values = jnp.sum(jnp.where((numbers == strip)[None], found, 0.0), axis=1)
        for fold in range(folds):
            for k in range(components):
                at = fold * 12 + k * 4 + corner
                rows_ref[at : at + 1, :] = values[k : k + 1, fold * cols_x : (fold + 1) * cols_x]

    points = gap.shape[0]
    full = points // 8 * 8
    live = lax.broadcasted_iota(jnp.int32, (points, pair_total), 0) < count[...]
    root = jnp.where(live, jnp.sqrt(weight[...]), 0.0)
    weighted = [root * shape[:, node] for node in range(4)]
    long_words = jnp.concatenate([x[:full] for x in weighted], axis=0)
    group = LANES // capacity
    placed = routed(long_words, group * heights[0], place)

    rows = rows_ref[...]
    high = rows.shape[0]
    rows_high = high * cols_x // LANES
    halved = jnp.concatenate(
        [rows[:, i * LANES : (i + 1) * LANES] for i in range(cols_x // LANES)], axis=0
    )
    starts = (0, rows_high, rows_high + heights[0], rows_high + sum(heights))
    copies = [
        pltpu.make_async_copy(
            blocks.at[:, start:end], sent_ref.at[:, start:end], copy_sems.at[i]
        )
        for i, (start, end) in enumerate(zip(starts, starts[1:]))
    ]
    for domain in range(domains):
        blocks[domain, :rows_high] = halved
    copies[0].start()
    for domain in range(domains):
        spot = place_in_group(domain, domains)
        blocks[spot, starts[1] : starts[2]] = folded(placed, heights[0], capacity, domain)
    copies[1].start()

    mortar_rows = looked_up(rows, mortar, marks(mortar & (cols_x - 1), cols_x))
    for node in range(4):
        across = sum(
            normal[k : k + 1] * mortar_rows[k * 4 + node : k * 4 + node + 1] for k in range(3)
        )
        gap = gap - shape[:, 4 + node] * across
    gap = root * gap
    short_words = jnp.concatenate(
        [gap[:full]]
        + [x[full:] for x in weighted + [gap]]
        + [normal, face.astype(F32), jnp.zeros((7, pair_total), F32)],
        axis=0,
    )
    placed = routed(short_words, group * heights[1], place)
    for domain in range(domains):
        spot = place_in_group(domain, domains)
        blocks[spot, starts[2] :] = folded(placed, heights[1], capacity, domain)
    copies[2].start()

    words_ref[: 4 * full] = long_words
    words_ref[4 * full :] = short_words
    for node in range(4):
        turned = root * shape[:, 4 + node]
        turned_ref[node * full : (node + 1) * full] = turned[:full]
        turned_ref[4 * full + node : 4 * full + node + 1] = turned[full:]

    brought[-1].wait()
    sub = lax.axis_index("sub")
    for target, layer in ((inner_ref, (1 - sub) * (layers - 1)), (outer_ref, sub * (layers - 1))):
        for k in range(components):
            target[k] = disp[k, layer]
        target[components] = modulus[...]
    for copy in copies:
        copy.wait()


def last_kernel(
    capacity, heights, got_ref, rows_ref, words_ref, turned_ref, mortar_ref, rank_ref, face_ref, nodes_ref,
    inverse_ref, internal_ref, blocks_ref, own_ref, halo_ref, out_ref,
):
    domains = got_ref.shape[0]
    components, layers, rows_y, cols_x = out_ref.shape
    strips = layers * rows_y
    face_count = nodes_ref.shape[1]
    pair_total = rank_ref.shape[1]
    folded = rows_ref.shape[0]
    rows_high = folded * cols_x // LANES
    full = (turned_ref.shape[0] - 8) // 4
    own_rows = rows_ref[...]

    rank, face = rank_ref[...], face_ref[...]
    place = place_in_group(rank, domains)
    at = marks(face & (cols_x - 1), cols_x)
    step = min(domains, 8)

    def add_step(turn, total):
        block = jnp.concatenate(
            [
                got_ref[pl.ds(turn * step, step), i * folded : (i + 1) * folded].reshape(
                    step * folded, LANES
                )
                for i in range(cols_x // LANES)
            ],
            axis=1,
        )
        found = summed(times(stacked_terms(block), at)).reshape(step, folded, pair_total)
        for i in range(step):
            total = total + jnp.where(place == turn * step + i, found[i], 0.0)
        return total

    both = jnp.zeros((folded, pair_total), F32)
    if domains == step:
        both = add_step(0, both)
    else:
        both = lax.fori_loop(0, domains // step, add_step, both)
    remote_rows = jnp.where(face < cols_x, both[:12], both[12:])
    pressure, last, normal = weighted_pressure(words_ref[...], full, remote_rows)
    turned = turned_ref[...]
    mortar_forces = forces_of(-normal, loads_on(turned, full, 4 * full, pressure, last))

    words = jnp.concatenate(
        [
            unfolded(got_ref, rows_high, heights[0], capacity)[: 4 * full],
            unfolded(got_ref, rows_high + heights[0], heights[1], capacity)[: full + 16],
        ],
        axis=0,
    )
    asked = words[5 * full + 8 : 5 * full + 9].astype(jnp.int32)
    asked_at = marks(asked & (cols_x - 1), cols_x)
    remote_rows = looked_up(own_rows, asked, asked_at)
    pressure, last, normal = weighted_pressure(words, full, remote_rows)
    remote_forces = forces_of(normal, loads_on(words, full, 5 * full, pressure, last))

    forces = jnp.concatenate([mortar_forces, remote_forces], axis=1)
    into = jnp.concatenate([mortar_ref[...], asked], axis=1)
    at = jnp.concatenate([marks(mortar_ref[...] & (cols_x - 1), cols_x), asked_at], axis=1)
    forces = jnp.concatenate(
        [jnp.where(into < cols_x, forces, 0.0), jnp.where(into < cols_x, 0.0, forces)], axis=0
    )
    forces = summed(times_turned(stacked_terms(forces), at))
    forces = jnp.concatenate([forces[:12], forces[12:]], axis=1)
    parts = [term.astype(F32) for term in terms_of(forces, 2)]
    spread, along_x = [], []
    for corner in range(4):
        index = nodes_ref[corner : corner + 1, :]
        strip = marks(index >> halves(cols_x), strips)
        rows = []
        for part in parts:
            for k in range(components):
                at = k * 4 + corner
                row = jnp.broadcast_to(part[at : at + 1], (16, face_count)).astype(BF16)
                rows.append(strip * jnp.concatenate([row] * (strips // 16), axis=0))
        spread.append(jnp.concatenate(rows, axis=0))
        along_x.append(marks(index & (cols_x - 1), cols_x))
    total = times_turned(jnp.concatenate(spread, axis=1), jnp.concatenate(along_x, axis=1))
    contact = summed(total).reshape(components, layers, rows_y, cols_x)
    upward = lax.axis_index("sub") == 1
    edge = edge_part(upward, own_ref, halo_ref, blocks_ref)
    at = jnp.where(upward, layers - 1, 0)
    for layer in range(layers):
        for k in range(components):
            nodal = internal_ref[k, layer] + jnp.where(at == layer, edge[k], 0.0)
            out_ref[k, layer] = (nodal + contact[k, layer]) * inverse_ref[layer]


GROUP = 8


def shifted(layer):
    views = []
    for part in layer:
        rows_y, cols_x = part.shape
        for moved in (part, pltpu.roll(part, rows_y - 1, 0)):
            views += [moved, pltpu.roll(moved, cols_x - 1, 1)]
    return views


def element_forces(matrices, low, high, modulus):
    rows_y, cols_x = modulus.shape
    inside = (lax.broadcasted_iota(jnp.int32, (rows_y, cols_x), 0) < rows_y - 1) & (
        lax.broadcasted_iota(jnp.int32, (rows_y, cols_x), 1) < cols_x - 1
    )
    scale = jnp.where(inside, modulus, 0.0)
    views = shifted(low) + shifted(high)
    both = jnp.concatenate(matrices, axis=0)
    count = both.shape[0] // 2
    strips = []
    for y in range(0, rows_y, GROUP):
        leading, second = terms_of(jnp.concatenate([view[y : y + GROUP] for view in views], axis=0), 2)
        found = times(both, leading)
        force = found[:count] + (found[count:] + times(matrices[0], second))
        strips.append(force.reshape(-1, GROUP, cols_x) * scale[y : y + GROUP][None])
    return jnp.concatenate(strips, axis=1)


def on_nodes(forces):
    sums = []
    for k in range(forces.shape[0] // 4):
        straight, crossed = [
            forces[k * 4 + c] + pltpu.roll(forces[k * 4 + 2 + c], 1, 0) for c in range(2)
        ]
        sums.append(-(straight + pltpu.roll(crossed, 1, 1)))
    return sums


def edge_part(upward, own_ref, halo_ref, blocks_ref):
    components = own_ref.shape[0] - 1
    size = blocks_ref.shape[1]
    rows = size // 2
    start = jnp.where(upward, 0, rows)
    matrices = [
        blocks_ref[pl.ds(pl.multiple_of(term * size + start, 16), rows)] for term in range(2)
    ]
    low = [jnp.where(upward, own_ref[k], halo_ref[k]) for k in range(components + 1)]
    high = [jnp.where(upward, halo_ref[k], own_ref[k]) for k in range(components)]
    return on_nodes(element_forces(matrices, low[:components], high, low[components]))


def internal_kernel(
    disp_ref, modulus_ref, stiffness_ref, mass_ref, own_ref, halo_ref, out_ref, blocks_ref, inverse_ref
):
    inverse_ref[...] = 1.0 / mass_ref[...]
    components, layers, rows_y, cols_x = disp_ref.shape
    dofs = 8 * components
    half = dofs // 2
    size = dofs * GROUP

    row = lax.broadcasted_iota(jnp.int32, (size, dofs), 0) >> halves(GROUP)
    upper = (row >= half).astype(jnp.int32)
    inner = row - half * upper
    dof = (inner >> 2) * 8 + upper * 4 + (inner & 3)
    pick = (dof == lax.broadcasted_iota(jnp.int32, (size, dofs), 1)).astype(F32).astype(BF16)
    diagonal = (lax.broadcasted_iota(jnp.int32, (size, size), 0) & (GROUP - 1)) == (
        lax.broadcasted_iota(jnp.int32, (size, size), 1) & (GROUP - 1)
    )
    for i, term in enumerate(terms_of(stiffness_ref[...], 2)):
        wide = times_turned(times(pick, term).astype(BF16), pick)
        blocks_ref[i * size : (i + 1) * size] = jnp.where(diagonal, wide, 0.0).astype(BF16)

    blocks = [blocks_ref[i * size : (i + 1) * size] for i in range(2)]
    sums = [[0.0] * components for _ in range(layers)]
    for e in range(layers - 1):
        pair = [[disp_ref[k, e + a] for k in range(components)] for a in range(2)]
        forces = element_forces(blocks, pair[0], pair[1], modulus_ref[e])
        for a in range(2):
            part = on_nodes(forces[a * half : (a + 1) * half])
            sums[e + a] = [x + y for x, y in zip(sums[e + a], part)]
    upward = lax.axis_index("sub") == 0
    edge = edge_part(upward, own_ref, halo_ref, blocks_ref)
    at = jnp.where(upward, layers - 1, 0)
    for layer in range(layers):
        for k in range(components):
            out_ref[k, layer] = sums[layer][k] + jnp.where(at == layer, edge[k], 0.0)


def on_core(kernel, outs, flops, moved, **more):
    return pl.pallas_call(
        kernel,
        out_shape=outs,
        compiler_params=pltpu.CompilerParams(vmem_limit_bytes=48 * 1024 * 1024),
        cost_estimate=pl.CostEstimate(flops=flops, bytes_accessed=moved, transcendentals=0),
        **more,
    )


def swapped(block, axis, first):
    size = lax.axis_size(axis)
    route = []
    for i in range(first, size - 1, 2):
        route += [(i, i + 1), (i + 1, i)]
    return lax.ppermute(block, axis, route)


def shards(
    displacement,
    modulus,
    node_mass,
    stiffness,
    face_nodes,
    pair_mortar,
    pair_rank,
    pair_face,
    pair_count,
    pair_shape,
    pair_weight,
    pair_gap,
    pair_normal,
):
    components, layers, rows_y, cols_x = displacement.shape
    face_count = face_nodes.shape[1]
    pair_total = pair_mortar.shape[0]
    domains = lax.axis_size("dom")
    capacity = max(2, 2 * pair_total // domains)

    points = pair_weight.shape[0]
    full = points // 8 * 8
    group = LANES // capacity
    word_rows = 5 * full + 16
    heights = tuple(-(-rows // (8 * group)) * 8 for rows in (4 * full, full + 16))
    rows_high = 12 * face_count // LANES
    line = (1, pair_total)

    def first(*refs):
        first_kernel(capacity, heights, *refs)

    def last(*refs):
        last_kernel(capacity, heights, *refs)

    def shaped(shape, dtype=F32):
        return jax.ShapeDtypeStruct(shape, dtype)

    arrays = [
        face_nodes,
        displacement,
        pair_mortar.reshape(line),
        pair_rank.reshape(line),
        pair_face.reshape(line),
        pair_count.reshape(line),
        pair_weight,
        pair_normal,
        pair_gap,
        jnp.swapaxes(pair_shape, 0, 1),
        modulus,
    ]
    edge = shaped((components + 1, rows_y, cols_x))
    in_hbm = pl.BlockSpec(memory_space=pltpu.HBM)
    in_vmem = pl.BlockSpec(memory_space=pltpu.VMEM)
    kept = [displacement, *arrays[5:-1], modulus[0]]
    sent, rows, words, turned, mortar, rank, face, nodes, inner, outer = on_core(
        first,
        [
            shaped((domains, rows_high + sum(heights), LANES)),
            shaped((12 * face_count // cols_x, cols_x)),
            shaped((word_rows, pair_total)),
            shaped((4 * full + 8, pair_total)),
            shaped(line, jnp.int32),
            shaped(line, jnp.int32),
            shaped(line, jnp.int32),
            shaped(face_nodes.shape, jnp.int32),
            edge,
            edge,
        ],
        900_000_000,
        1_500_000,
        in_specs=[in_hbm] * len(arrays),
        out_specs=[in_hbm] + [in_vmem] * 9,
        scratch_shapes=[pltpu.VMEM(x.shape, x.dtype) for x in kept]
        + [
            pltpu.VMEM((domains, rows_high + sum(heights), LANES), F32),
            pltpu.SemaphoreType.DMA((len(arrays),)),
            pltpu.SemaphoreType.DMA((3,)),
        ],
    )(*[pltpu.with_memory_space_constraint(x, pltpu.HBM) for x in arrays])
    order = [place_in_group(domain, domains) for domain in range(domains)]
    got = lax.all_to_all(
        sent, "dom", split_axis=0, concat_axis=0, axis_index_groups=[order], tiled=True
    )
    inner_halo = swapped(inner, ("dom", "sub"), 0)
    outer_halo = swapped(outer, ("dom", "sub"), 1)
    size = 8 * components * GROUP
    internal, blocks, inverse = on_core(
        internal_kernel,
        [shaped(displacement.shape), shaped((2 * size, size), BF16), shaped(node_mass.shape)],
        1_000_000_000,
        700_000,
    )(displacement, modulus, stiffness, node_mass, inner, inner_halo)
    return on_core(last, shaped(displacement.shape), 1_000_000_000, 1_500_000)(
        got, rows, words, turned, mortar, rank, face, nodes, inverse, internal, blocks, outer, outer_halo
    )


def solution(mesh):
    placed = (
        P(None, ("runs", "dom", "sub"), None, None),
        P(("runs", "dom", "sub"), None, None),
        P(("runs", "dom", "sub"), None, None),
        P(),
        P(None, ("runs", "dom", "sub")),
        P(("runs", "dom", "sub")),
        P(("runs", "dom", "sub"), None),
        P(("runs", "dom", "sub")),
        P(("runs", "dom", "sub")),
        P(None, None, ("runs", "dom", "sub")),
        P(None, ("runs", "dom", "sub")),
        P(None, ("runs", "dom", "sub")),
        P(None, ("runs", "dom", "sub")),
    )
    return jax.shard_map(
        shards,
        mesh=mesh,
        in_specs=placed,
        out_specs=P(None, ("runs", "dom", "sub"), None, None),
        check_vma=False,
    )
```

```python
import jax
import jax.numpy as jnp
from jax import lax
from jax.experimental import pallas as pl
from jax.experimental.pallas import tpu as pltpu
from jax.sharding import PartitionSpec as P

F32 = jnp.float32
BF16 = jnp.bfloat16
LANES = 128


def terms_of(x, count):
    terms = []
    for _ in range(count):
        terms.append(x.astype(BF16))
        x = x - terms[-1].astype(F32)
    return terms


def stacked_terms(x):
    return jnp.concatenate(terms_of(x, 2), axis=0)


def summed(stacked):
    rows = stacked.shape[0] // 2
    return stacked[:rows] + stacked[rows:]


def marks(index, count):
    shape = (16, index.shape[1])
    rows = lax.broadcasted_iota(jnp.int32, shape, 0).astype(jnp.int16)
    index = jnp.broadcast_to(index, shape).astype(jnp.int16)
    tiles = [
        jnp.where(rows == index - jnp.int16(start), jnp.ones((), BF16), jnp.zeros((), BF16))
        for start in range(0, count, 16)
    ]
    return jnp.concatenate(tiles, axis=0)


def times(left, right):
    return jnp.dot(left, right, preferred_element_type=F32)


def times_turned(left, right):
    return lax.dot_general(left, right, (((1,), (1,)), ((), ())), preferred_element_type=F32)


def halves(power):
    return power.bit_length() - 1


def looked_up(table, face, at):
    both = summed(times(stacked_terms(table), at))
    return jnp.where(face < table.shape[1], both[:12], both[12:])


def folded(placed, height, capacity, domain):
    group = LANES // capacity
    tile, spot = domain // group, domain % group
    part = lax.broadcasted_iota(jnp.int32, (height, LANES), 1) >> halves(capacity)
    block = None
    for j in range(group):
        piece = placed[j * height : (j + 1) * height, tile * LANES : (tile + 1) * LANES]
        if j != spot:
            piece = pltpu.roll(piece, (j - spot) * capacity % LANES, 1)
        block = piece if block is None else jnp.where(part == j, piece, block)
    return block


def unfolded(got_ref, start, height, capacity):
    group = LANES // capacity
    part = lax.broadcasted_iota(jnp.int32, (height, LANES), 1) >> halves(capacity)
    pieces = []
    for j in range(group):
        tiles = []
        for first in range(0, got_ref.shape[0], group):
            block = None
            for spot in range(group):
                piece = got_ref[first + spot, start : start + height]
                if j != spot:
                    piece = pltpu.roll(piece, (spot - j) * capacity % LANES, 1)
                block = piece if block is None else jnp.where(part == spot, piece, block)
            tiles.append(block)
        pieces.append(jnp.concatenate(tiles, axis=1))
    return jnp.concatenate(pieces, axis=0)


def routed(words, rows, place):
    extra = rows - words.shape[0]
    if extra:
        words = jnp.concatenate([words, jnp.zeros((extra, words.shape[1]), F32)], axis=0)
    return summed(times_turned(stacked_terms(words), place))


def weighted_pressure(words, full, remote_rows):
    tail = 5 * full
    normal = words[tail + 5 : tail + 8]
    gap, last = words[4 * full : tail], words[tail + 4 : tail + 5]
    for node in range(4):
        across = sum(
            normal[k : k + 1] * remote_rows[k * 4 + node : k * 4 + node + 1] for k in range(3)
        )
        gap = gap + words[node * full : (node + 1) * full] * across
        last = last + words[tail + node : tail + node + 1] * across
    return jnp.maximum(-gap, 0.0), jnp.maximum(-last, 0.0), normal


def loads_on(shapes, full, tail, pressure, last):
    return [
        jnp.sum(pressure * shapes[i * full : (i + 1) * full], axis=0, keepdims=True)
        + last * shapes[tail + i : tail + i + 1]
        for i in range(4)
    ]


def forces_of(normal, loads):
    loads = jnp.concatenate(loads, axis=0)
    return jnp.concatenate([normal[k : k + 1] * loads for k in range(3)], axis=0)


def place_in_group(domain, domains):
    return (domain + 1) % domains


def first_kernel(capacity, heights, *refs):
    (
        nodes_hbm, disp_hbm, mortar_hbm, rank_hbm, face_hbm, count_hbm, weight_hbm, normal_hbm,
        gap_hbm, shape_hbm, modulus_hbm,
        sent_ref, rows_ref, words_ref, turned_ref, mortar_ref, rank_ref, face_ref, nodes,
        inner_ref, outer_ref,
        disp, count, weight, normal_v, gap_v, shape, modulus, blocks, sems, copy_sems,
    ) = refs
    components, layers, rows_y, cols_x = disp.shape
    sources = (
        nodes_hbm, disp_hbm, rank_hbm, face_hbm, mortar_hbm, shape_hbm, count_hbm, weight_hbm,
        normal_hbm, gap_hbm, modulus_hbm.at[disp.shape[1] - 1],
    )
    targets = (
        nodes, disp, rank_ref, face_ref, mortar_ref, shape, count, weight, normal_v, gap_v, modulus,
    )
    brought = [
        pltpu.make_async_copy(source, target, sems.at[i])
        for i, (source, target) in enumerate(zip(sources, targets))
    ]
    for copy in brought:
        copy.start()

    domains = sent_ref.shape[0]
    pair_total = rank_ref.shape[1]
    face_count = nodes.shape[1]
    strips = layers * rows_y
    for copy in brought[:-1]:
        copy.wait()
    rank, face, mortar = rank_ref[...], face_ref[...], mortar_ref[...]
    normal = normal_v[...]
    gap = gap_v[...]

    chosen = lax.broadcasted_iota(jnp.int32, (domains, pair_total), 0) == rank
    before = lax.broadcasted_iota(jnp.int32, (pair_total, pair_total), 0) < lax.broadcasted_iota(
        jnp.int32, (pair_total, pair_total), 1
    )
    earlier = times(chosen.astype(F32).astype(BF16), before.astype(F32).astype(BF16))
    slot = jnp.sum(jnp.where(chosen, earlier, 0.0), axis=0, keepdims=True).astype(jnp.int32)
    place = marks(rank * capacity + slot, domains * capacity)

    parts = stacked_terms(disp[...].reshape(components * strips, cols_x))
    numbers = lax.broadcasted_iota(jnp.int32, (strips, face_count), 0)
    folds = face_count // cols_x
    for corner in range(4):
        index = nodes[corner : corner + 1, :]
        strip = index >> halves(cols_x)
        found = summed(times(parts, marks(index & (cols_x - 1), cols_x)))
        found = found.reshape(components, strips, face_count)
        values = jnp.sum(jnp.where((numbers == strip)[None], found, 0.0), axis=1)
        for fold in range(folds):
            for k in range(components):
                at = fold * 12 + k * 4 + corner
                rows_ref[at : at + 1, :] = values[k : k + 1, fold * cols_x : (fold + 1) * cols_x]

    points = gap.shape[0]
    full = points // 8 * 8
    live = lax.broadcasted_iota(jnp.int32, (points, pair_total), 0) < count[...]
    root = jnp.where(live, jnp.sqrt(weight[...]), 0.0)
    weighted = [root * shape[:, node] for node in range(4)]
    long_words = jnp.concatenate([x[:full] for x in weighted], axis=0)
    group = LANES // capacity
    placed = routed(long_words, group * heights[0], place)

    rows = rows_ref[...]
    high = rows.shape[0]
    rows_high = high * cols_x // LANES
    halved = jnp.concatenate(
        [rows[:, i * LANES : (i + 1) * LANES] for i in range(cols_x // LANES)], axis=0
    )
    starts = (0, rows_high, rows_high + heights[0], rows_high + sum(heights))
    copies = [
        pltpu.make_async_copy(
            blocks.at[:, start:end], sent_ref.at[:, start:end], copy_sems.at[i]
        )
        for i, (start, end) in enumerate(zip(starts, starts[1:]))
    ]
    for domain in range(domains):
        blocks[domain, :rows_high] = halved
    copies[0].start()
    for domain in range(domains):
        spot = place_in_group(domain, domains)
        blocks[spot, starts[1] : starts[2]] = folded(placed, heights[0], capacity, domain)
    copies[1].start()

    mortar_rows = looked_up(rows, mortar, marks(mortar & (cols_x - 1), cols_x))
    for node in range(4):
        across = sum(
            normal[k : k + 1] * mortar_rows[k * 4 + node : k * 4 + node + 1] for k in range(3)
        )
        gap = gap - shape[:, 4 + node] * across
    gap = root * gap
    short_words = jnp.concatenate(
        [gap[:full]]
        + [x[full:] for x in weighted + [gap]]
        + [normal, face.astype(F32), jnp.zeros((7, pair_total), F32)],
        axis=0,
    )
    placed = routed(short_words, group * heights[1], place)
    for domain in range(domains):
        spot = place_in_group(domain, domains)
        blocks[spot, starts[2] :] = folded(placed, heights[1], capacity, domain)
    copies[2].start()

    words_ref[: 4 * full] = long_words
    words_ref[4 * full :] = short_words
    for node in range(4):
        turned = root * shape[:, 4 + node]
        turned_ref[node * full : (node + 1) * full] = turned[:full]
        turned_ref[4 * full + node : 4 * full + node + 1] = turned[full:]

    brought[-1].wait()
    sub = lax.axis_index("sub")
    for target, layer in ((inner_ref, (1 - sub) * (layers - 1)), (outer_ref, sub * (layers - 1))):
        for k in range(components):
            target[k] = disp[k, layer]
        target[components] = modulus[...]
    for copy in copies:
        copy.wait()


def last_kernel(
    capacity, heights, got_ref, rows_ref, words_ref, turned_ref, mortar_ref, rank_ref, face_ref, nodes_ref,
    inverse_ref, internal_ref, blocks_ref, own_ref, halo_ref, out_ref,
):
    domains = got_ref.shape[0]
    components, layers, rows_y, cols_x = out_ref.shape
    strips = layers * rows_y
    face_count = nodes_ref.shape[1]
    pair_total = rank_ref.shape[1]
    folded = rows_ref.shape[0]
    rows_high = folded * cols_x // LANES
    full = (turned_ref.shape[0] - 8) // 4
    own_rows = rows_ref[...]

    rank, face = rank_ref[...], face_ref[...]
    place = place_in_group(rank, domains)
    at = marks(face & (cols_x - 1), cols_x)
    step = min(domains, 8)

    def add_step(turn, total):
        block = jnp.concatenate(
            [
                got_ref[pl.ds(turn * step, step), i * folded : (i + 1) * folded].reshape(
                    step * folded, LANES
                )
                for i in range(cols_x // LANES)
            ],
            axis=1,
        )
        found = summed(times(stacked_terms(block), at)).reshape(step, folded, pair_total)
        for i in range(step):
            total = total + jnp.where(place == turn * step + i, found[i], 0.0)
        return total

    both = jnp.zeros((folded, pair_total), F32)
    if domains == step:
        both = add_step(0, both)
    else:
        both = lax.fori_loop(0, domains // step, add_step, both)
    remote_rows = jnp.where(face < cols_x, both[:12], both[12:])
    pressure, last, normal = weighted_pressure(words_ref[...], full, remote_rows)
    turned = turned_ref[...]
    mortar_forces = forces_of(-normal, loads_on(turned, full, 4 * full, pressure, last))

    words = jnp.concatenate(
        [
            unfolded(got_ref, rows_high, heights[0], capacity)[: 4 * full],
            unfolded(got_ref, rows_high + heights[0], heights[1], capacity)[: full + 16],
        ],
        axis=0,
    )
    asked = words[5 * full + 8 : 5 * full + 9].astype(jnp.int32)
    asked_at = marks(asked & (cols_x - 1), cols_x)
    remote_rows = looked_up(own_rows, asked, asked_at)
    pressure, last, normal = weighted_pressure(words, full, remote_rows)
    remote_forces = forces_of(normal, loads_on(words, full, 5 * full, pressure, last))

    forces = jnp.concatenate([mortar_forces, remote_forces], axis=1)
    into = jnp.concatenate([mortar_ref[...], asked], axis=1)
    at = jnp.concatenate([marks(mortar_ref[...] & (cols_x - 1), cols_x), asked_at], axis=1)
    forces = jnp.concatenate(
        [jnp.where(into < cols_x, forces, 0.0), jnp.where(into < cols_x, 0.0, forces)], axis=0
    )
    forces = summed(times_turned(stacked_terms(forces), at))
    forces = jnp.concatenate([forces[:12], forces[12:]], axis=1)
    parts = [term.astype(F32) for term in terms_of(forces, 2)]
    spread, along_x = [], []
    for corner in range(4):
        index = nodes_ref[corner : corner + 1, :]
        strip = marks(index >> halves(cols_x), strips)
        rows = []
        for part in parts:
            for k in range(components):
                at = k * 4 + corner
                row = jnp.broadcast_to(part[at : at + 1], (16, face_count)).astype(BF16)
                rows.append(strip * jnp.concatenate([row] * (strips // 16), axis=0))
        spread.append(jnp.concatenate(rows, axis=0))
        along_x.append(marks(index & (cols_x - 1), cols_x))
    total = times_turned(jnp.concatenate(spread, axis=1), jnp.concatenate(along_x, axis=1))
    contact = summed(total).reshape(components, layers, rows_y, cols_x)
    upward = lax.axis_index("sub") == 1
    edge = edge_part(upward, own_ref, halo_ref, blocks_ref)
    at = jnp.where(upward, layers - 1, 0)
    for layer in range(layers):
        for k in range(components):
            nodal = internal_ref[k, layer] + jnp.where(at == layer, edge[k], 0.0)
            out_ref[k, layer] = (nodal + contact[k, layer]) * inverse_ref[layer]


GROUP = 8


def shifted(layer):
    views = []
    for part in layer:
        rows_y, cols_x = part.shape
        for moved in (part, pltpu.roll(part, rows_y - 1, 0)):
            views += [moved, pltpu.roll(moved, cols_x - 1, 1)]
    return views


def element_forces(matrices, low, high, modulus):
    rows_y, cols_x = modulus.shape
    inside = (lax.broadcasted_iota(jnp.int32, (rows_y, cols_x), 0) < rows_y - 1) & (
        lax.broadcasted_iota(jnp.int32, (rows_y, cols_x), 1) < cols_x - 1
    )
    scale = jnp.where(inside, modulus, 0.0)
    views = shifted(low) + shifted(high)
    both = jnp.concatenate(matrices, axis=0)
    count = both.shape[0] // 2
    strips = []
    for y in range(0, rows_y, GROUP):
        leading, second = terms_of(jnp.concatenate([view[y : y + GROUP] for view in views], axis=0), 2)
        found = times(both, leading)
        force = found[:count] + (found[count:] + times(matrices[0], second))
        strips.append(force.reshape(-1, GROUP, cols_x) * scale[y : y + GROUP][None])
    return jnp.concatenate(strips, axis=1)


def on_nodes(forces):
    sums = []
    for k in range(forces.shape[0] // 4):
        straight, crossed = [
            forces[k * 4 + c] + pltpu.roll(forces[k * 4 + 2 + c], 1, 0) for c in range(2)
        ]
        sums.append(-(straight + pltpu.roll(crossed, 1, 1)))
    return sums


def edge_part(upward, own_ref, halo_ref, blocks_ref):
    components = own_ref.shape[0] - 1
    size = blocks_ref.shape[1]
    rows = size // 2
    start = jnp.where(upward, 0, rows)
    matrices = [
        blocks_ref[pl.ds(pl.multiple_of(term * size + start, 16), rows)] for term in range(2)
    ]
    low = [jnp.where(upward, own_ref[k], halo_ref[k]) for k in range(components + 1)]
    high = [jnp.where(upward, halo_ref[k], own_ref[k]) for k in range(components)]
    return on_nodes(element_forces(matrices, low[:components], high, low[components]))


def internal_kernel(
    disp_ref, modulus_ref, stiffness_ref, mass_ref, own_ref, halo_ref, out_ref, blocks_ref, inverse_ref
):
    inverse_ref[...] = 1.0 / mass_ref[...]
    components, layers, rows_y, cols_x = disp_ref.shape
    dofs = 8 * components
    half = dofs // 2
    size = dofs * GROUP

    row = lax.broadcasted_iota(jnp.int32, (size, dofs), 0) >> halves(GROUP)
    upper = (row >= half).astype(jnp.int32)
    inner = row - half * upper
    dof = (inner >> 2) * 8 + upper * 4 + (inner & 3)
    pick = (dof == lax.broadcasted_iota(jnp.int32, (size, dofs), 1)).astype(F32).astype(BF16)
    diagonal = (lax.broadcasted_iota(jnp.int32, (size, size), 0) & (GROUP - 1)) == (
        lax.broadcasted_iota(jnp.int32, (size, size), 1) & (GROUP - 1)
    )
    for i, term in enumerate(terms_of(stiffness_ref[...], 2)):
        wide = times_turned(times(pick, term).astype(BF16), pick)
        blocks_ref[i * size : (i + 1) * size] = jnp.where(diagonal, wide, 0.0).astype(BF16)

    blocks = [blocks_ref[i * size : (i + 1) * size] for i in range(2)]
    sums = [[0.0] * components for _ in range(layers)]
    for e in range(layers - 1):
        pair = [[disp_ref[k, e + a] for k in range(components)] for a in range(2)]
        forces = element_forces(blocks, pair[0], pair[1], modulus_ref[e])
        for a in range(2):
            part = on_nodes(forces[a * half : (a + 1) * half])
            sums[e + a] = [x + y for x, y in zip(sums[e + a], part)]
    upward = lax.axis_index("sub") == 0
    edge = edge_part(upward, own_ref, halo_ref, blocks_ref)
    at = jnp.where(upward, layers - 1, 0)
    for layer in range(layers):
        for k in range(components):
            out_ref[k, layer] = sums[layer][k] + jnp.where(at == layer, edge[k], 0.0)


def on_core(kernel, outs, flops, moved, **more):
    return pl.pallas_call(
        kernel,
        out_shape=outs,
        compiler_params=pltpu.CompilerParams(vmem_limit_bytes=48 * 1024 * 1024),
        cost_estimate=pl.CostEstimate(flops=flops, bytes_accessed=moved, transcendentals=0),
        **more,
    )


def swapped(block, axis, first):
    size = lax.axis_size(axis)
    route = []
    for i in range(first, size - 1, 2):
        route += [(i, i + 1), (i + 1, i)]
    return lax.ppermute(block, axis, route)


def shards(
    displacement,
    modulus,
    node_mass,
    stiffness,
    face_nodes,
    pair_mortar,
    pair_rank,
    pair_face,
    pair_count,
    pair_shape,
    pair_weight,
    pair_gap,
    pair_normal,
):
    components, layers, rows_y, cols_x = displacement.shape
    face_count = face_nodes.shape[1]
    pair_total = pair_mortar.shape[0]
    domains = lax.axis_size("dom")
    capacity = max(2, 2 * pair_total // domains)

    points = pair_weight.shape[0]
    full = points // 8 * 8
    group = LANES // capacity
    word_rows = 5 * full + 16
    heights = tuple(-(-rows // (8 * group)) * 8 for rows in (4 * full, full + 16))
    rows_high = 12 * face_count // LANES
    line = (1, pair_total)

    def first(*refs):
        first_kernel(capacity, heights, *refs)

    def last(*refs):
        last_kernel(capacity, heights, *refs)

    def shaped(shape, dtype=F32):
        return jax.ShapeDtypeStruct(shape, dtype)

    arrays = [
        face_nodes,
        displacement,
        pair_mortar.reshape(line),
        pair_rank.reshape(line),
        pair_face.reshape(line),
        pair_count.reshape(line),
        pair_weight,
        pair_normal,
        pair_gap,
        jnp.swapaxes(pair_shape, 0, 1),
        modulus,
    ]
    edge = shaped((components + 1, rows_y, cols_x))
    in_hbm = pl.BlockSpec(memory_space=pltpu.HBM)
    in_vmem = pl.BlockSpec(memory_space=pltpu.VMEM)
    kept = [displacement, *arrays[5:-1], modulus[0]]
    sent, rows, words, turned, mortar, rank, face, nodes, inner, outer = on_core(
        first,
        [
            shaped((domains, rows_high + sum(heights), LANES)),
            shaped((12 * face_count // cols_x, cols_x)),
            shaped((word_rows, pair_total)),
            shaped((4 * full + 8, pair_total)),
            shaped(line, jnp.int32),
            shaped(line, jnp.int32),
            shaped(line, jnp.int32),
            shaped(face_nodes.shape, jnp.int32),
            edge,
            edge,
        ],
        900_000_000,
        1_500_000,
        in_specs=[in_hbm] * len(arrays),
        out_specs=[in_hbm] + [in_vmem] * 9,
        scratch_shapes=[pltpu.VMEM(x.shape, x.dtype) for x in kept]
        + [
            pltpu.VMEM((domains, rows_high + sum(heights), LANES), F32),
            pltpu.SemaphoreType.DMA((len(arrays),)),
            pltpu.SemaphoreType.DMA((3,)),
        ],
    )(*[pltpu.with_memory_space_constraint(x, pltpu.HBM) for x in arrays])
    order = sorted(range(domains), key=lambda domain: place_in_group(domain, domains))
    got = lax.all_to_all(
        sent, "dom", split_axis=0, concat_axis=0, axis_index_groups=[order], tiled=True
    )
    inner_halo = swapped(inner, ("dom", "sub"), 0)
    outer_halo = swapped(outer, ("dom", "sub"), 1)
    size = 8 * components * GROUP
    internal, blocks, inverse = on_core(
        internal_kernel,
        [shaped(displacement.shape), shaped((2 * size, size), BF16), shaped(node_mass.shape)],
        1_000_000_000,
        700_000,
    )(displacement, modulus, stiffness, node_mass, inner, inner_halo)
    return on_core(last, shaped(displacement.shape), 1_000_000_000, 1_500_000)(
        got, rows, words, turned, mortar, rank, face, nodes, inverse, internal, blocks, outer, outer_halo
    )


def solution(mesh):
    placed = (
        P(None, ("runs", "dom", "sub"), None, None),
        P(("runs", "dom", "sub"), None, None),
        P(("runs", "dom", "sub"), None, None),
        P(),
        P(None, ("runs", "dom", "sub")),
        P(("runs", "dom", "sub")),
        P(("runs", "dom", "sub"), None),
        P(("runs", "dom", "sub")),
        P(("runs", "dom", "sub")),
        P(None, None, ("runs", "dom", "sub")),
        P(None, ("runs", "dom", "sub")),
        P(None, ("runs", "dom", "sub")),
        P(None, ("runs", "dom", "sub")),
    )
    return jax.shard_map(
        shards,
        mesh=mesh,
        in_specs=placed,
        out_specs=P(None, ("runs", "dom", "sub"), None, None),
        check_vma=False,
    )
```

```python
import jax
import jax.numpy as jnp
from jax import lax
from jax.experimental import pallas as pl
from jax.experimental.pallas import tpu as pltpu
from jax.sharding import PartitionSpec as P

F32 = jnp.float32
BF16 = jnp.bfloat16
LANES = 128


def terms_of(x, count):
    terms = []
    for _ in range(count):
        terms.append(x.astype(BF16))
        x = x - terms[-1].astype(F32)
    return terms


def stacked_terms(x):
    return jnp.concatenate(terms_of(x, 2), axis=0)


def summed(stacked):
    rows = stacked.shape[0] // 2
    return stacked[:rows] + stacked[rows:]


def marks(index, count):
    shape = (16, index.shape[1])
    rows = lax.broadcasted_iota(jnp.int32, shape, 0).astype(jnp.int16)
    index = jnp.broadcast_to(index, shape).astype(jnp.int16)
    tiles = [
        jnp.where(rows == index - jnp.int16(start), jnp.ones((), BF16), jnp.zeros((), BF16))
        for start in range(0, count, 16)
    ]
    return jnp.concatenate(tiles, axis=0)


def times(left, right):
    return jnp.dot(left, right, preferred_element_type=F32)


def times_turned(left, right):
    return lax.dot_general(left, right, (((1,), (1,)), ((), ())), preferred_element_type=F32)


def halves(power):
    return power.bit_length() - 1


def looked_up(table, face, at):
    both = summed(times(stacked_terms(table), at))
    return jnp.where(face < table.shape[1], both[:12], both[12:])


def folded(placed, height, capacity, domain):
    group = LANES // capacity
    tile, spot = domain // group, domain % group
    part = lax.broadcasted_iota(jnp.int32, (height, LANES), 1) >> halves(capacity)
    block = None
    for j in range(group):
        piece = placed[j * height : (j + 1) * height, tile * LANES : (tile + 1) * LANES]
        if j != spot:
            piece = pltpu.roll(piece, (j - spot) * capacity % LANES, 1)
        block = piece if block is None else jnp.where(part == j, piece, block)
    return block


def unfolded(got_ref, block_rows, start, height, capacity):
    group = LANES // capacity
    part = lax.broadcasted_iota(jnp.int32, (height, LANES), 1) >> halves(capacity)
    pieces = []
    for j in range(group):
        tiles = []
        for first in range(0, got_ref.shape[0] // block_rows, group):
            block = None
            for spot in range(group):
                at = (first + spot) * block_rows + start
                piece = got_ref[at : at + height]
                if j != spot:
                    piece = pltpu.roll(piece, (spot - j) * capacity % LANES, 1)
                block = piece if block is None else jnp.where(part == spot, piece, block)
            tiles.append(block)
        pieces.append(jnp.concatenate(tiles, axis=1))
    return jnp.concatenate(pieces, axis=0)


def routed(words, rows, place):
    extra = -(-rows // 16) * 16 - words.shape[0]
    if extra:
        words = jnp.concatenate([words, jnp.zeros((extra, words.shape[1]), F32)], axis=0)
    return summed(times_turned(stacked_terms(words), place))


def weighted_pressure(words, full, remote_rows):
    tail = 5 * full
    normal = words[tail + 5 : tail + 8]
    gap, last = words[4 * full : tail], words[tail + 4 : tail + 5]
    for node in range(4):
        across = sum(
            normal[k : k + 1] * remote_rows[k * 4 + node : k * 4 + node + 1] for k in range(3)
        )
        gap = gap + words[node * full : (node + 1) * full] * across
        last = last + words[tail + node : tail + node + 1] * across
    return jnp.maximum(-gap, 0.0), jnp.maximum(-last, 0.0), normal


def loads_on(shapes, full, tail, pressure, last):
    return [
        jnp.sum(pressure * shapes[i * full : (i + 1) * full], axis=0, keepdims=True)
        + last * shapes[tail + i : tail + i + 1]
        for i in range(4)
    ]


def forces_of(normal, loads):
    loads = jnp.concatenate(loads, axis=0)
    return jnp.concatenate([normal[k : k + 1] * loads for k in range(3)], axis=0)


def place_in_group(domain, domains):
    return {0: domains - 1, domains - 1: 0}.get(domain, domain)


def first_kernel(capacity, heights, *refs):
    (
        nodes_hbm, disp_hbm, mortar_hbm, rank_hbm, face_hbm, count_hbm, weight_hbm, normal_hbm,
        gap_hbm, shape_hbm, modulus_hbm,
        sent_ref, rows_ref, words_ref, turned_ref, mortar_ref, rank_ref, face_ref, nodes,
        inner_ref, outer_ref,
        disp, count, weight, normal_v, gap_v, shape, modulus, blocks, sems, copy_sem,
    ) = refs
    components, layers, rows_y, cols_x = disp.shape
    block_rows = 12 * nodes.shape[1] // LANES + sum(heights)
    sources = (
        nodes_hbm, disp_hbm, rank_hbm, face_hbm, mortar_hbm, shape_hbm, count_hbm, weight_hbm,
        normal_hbm, gap_hbm, modulus_hbm.at[disp.shape[1] - 1],
    )
    targets = (
        nodes, disp, rank_ref, face_ref, mortar_ref, shape, count, weight, normal_v, gap_v, modulus,
    )
    brought = [
        pltpu.make_async_copy(source, target, sems.at[i])
        for i, (source, target) in enumerate(zip(sources, targets))
    ]
    for copy in brought:
        copy.start()

    domains = sent_ref.shape[0] // block_rows
    pair_total = rank_ref.shape[1]
    face_count = nodes.shape[1]
    strips = layers * rows_y
    for copy in brought[:-1]:
        copy.wait()
    rank, face, mortar = rank_ref[...], face_ref[...], mortar_ref[...]
    normal = normal_v[...]
    gap = gap_v[...]

    chosen = lax.broadcasted_iota(jnp.int32, (domains, pair_total), 0) == rank
    before = lax.broadcasted_iota(jnp.int32, (pair_total, pair_total), 0) < lax.broadcasted_iota(
        jnp.int32, (pair_total, pair_total), 1
    )
    earlier = times(chosen.astype(F32).astype(BF16), before.astype(F32).astype(BF16))
    slot = jnp.sum(jnp.where(chosen, earlier, 0.0), axis=0, keepdims=True).astype(jnp.int32)
    place = marks(rank * capacity + slot, domains * capacity)

    parts = stacked_terms(disp[...].reshape(components * strips, cols_x))
    numbers = lax.broadcasted_iota(jnp.int32, (strips, face_count), 0)
    folds = face_count // cols_x
    for corner in range(4):
        index = nodes[corner : corner + 1, :]
        strip = index >> halves(cols_x)
        found = summed(times(parts, marks(index & (cols_x - 1), cols_x)))
        found = found.reshape(components, strips, face_count)
        values = jnp.sum(jnp.where((numbers == strip)[None], found, 0.0), axis=1)
        for fold in range(folds):
            for k in range(components):
                at = fold * 12 + k * 4 + corner
                rows_ref[at : at + 1, :] = values[k : k + 1, fold * cols_x : (fold + 1) * cols_x]

    points = gap.shape[0]
    full = points // 8 * 8
    live = lax.broadcasted_iota(jnp.int32, (points, pair_total), 0) < count[...]
    root = jnp.where(live, jnp.sqrt(weight[...]), 0.0)
    weighted = [root * shape[:, node] for node in range(4)]
    long_words = jnp.concatenate([x[:full] for x in weighted], axis=0)
    group = LANES // capacity
    placed = routed(long_words, group * heights[0], place)

    rows = rows_ref[...]
    high = rows.shape[0]
    rows_high = high * cols_x // LANES
    halved = jnp.concatenate(
        [rows[:, i * LANES : (i + 1) * LANES] for i in range(cols_x // LANES)], axis=0
    )
    for domain in range(domains):
        at = place_in_group(domain, domains) * block_rows
        blocks[at : at + rows_high] = halved
        at += rows_high
        blocks[at : at + heights[0]] = folded(placed, heights[0], capacity, domain)

    mortar_rows = looked_up(rows, mortar, marks(mortar & (cols_x - 1), cols_x))
    for node in range(4):
        across = sum(
            normal[k : k + 1] * mortar_rows[k * 4 + node : k * 4 + node + 1] for k in range(3)
        )
        gap = gap - shape[:, 4 + node] * across
    gap = root * gap
    short_words = jnp.concatenate(
        [gap[:full]]
        + [x[full:] for x in weighted + [gap]]
        + [normal, face.astype(F32)],
        axis=0,
    )
    placed = routed(short_words, group * heights[1], place)
    for domain in range(domains):
        at = place_in_group(domain, domains) * block_rows + rows_high + heights[0]
        blocks[at : at + heights[1]] = folded(placed, heights[1], capacity, domain)
    sending = pltpu.make_async_copy(blocks, sent_ref, copy_sem)
    sending.start()

    words_ref[: 4 * full] = long_words
    words_ref[4 * full :] = short_words
    for node in range(4):
        turned = root * shape[:, 4 + node]
        turned_ref[node * full : (node + 1) * full] = turned[:full]
        turned_ref[4 * full + node : 4 * full + node + 1] = turned[full:]

    brought[-1].wait()
    sub = lax.axis_index("sub")
    for target, layer in ((inner_ref, (1 - sub) * (layers - 1)), (outer_ref, sub * (layers - 1))):
        for k in range(components):
            target[k] = disp[k, layer]
        target[components] = modulus[...]
    sending.wait()


def last_kernel(
    capacity, heights, got_ref, rows_ref, words_ref, turned_ref, mortar_ref, rank_ref, face_ref, nodes_ref,
    inverse_ref, internal_ref, blocks_ref, own_ref, halo_ref, out_ref,
):
    block_rows = 12 * nodes_ref.shape[1] // LANES + sum(heights)
    domains = got_ref.shape[0] // block_rows
    components, layers, rows_y, cols_x = out_ref.shape
    strips = layers * rows_y
    face_count = nodes_ref.shape[1]
    pair_total = rank_ref.shape[1]
    high = rows_ref.shape[0]
    rows_high = high * cols_x // LANES
    full = (turned_ref.shape[0] - 8) // 4
    own_rows = rows_ref[...]

    rank, face = rank_ref[...], face_ref[...]
    end = domains - 1
    place = jnp.where(rank == 0, end, jnp.where(rank == end, 0, rank))
    at = marks(face & (cols_x - 1), cols_x)
    step = min(domains, 8)

    def add_step(turn, total):
        halves_of = [
            jnp.concatenate(
                [
                    got_ref[pl.ds((turn * step + i) * block_rows + j * high, high)]
                    for j in range(cols_x // LANES)
                ],
                axis=1,
            )
            for i in range(step)
        ]
        block = jnp.concatenate(halves_of, axis=0)
        found = summed(times(stacked_terms(block), at)).reshape(step, high, pair_total)
        for i in range(step):
            total = total + jnp.where(place == turn * step + i, found[i], 0.0)
        return total

    both = jnp.zeros((high, pair_total), F32)
    if domains == step:
        both = add_step(0, both)
    else:
        both = lax.fori_loop(0, domains // step, add_step, both)
    remote_rows = jnp.where(face < cols_x, both[:12], both[12:])
    pressure, last, normal = weighted_pressure(words_ref[...], full, remote_rows)
    turned = turned_ref[...]
    mortar_forces = forces_of(-normal, loads_on(turned, full, 4 * full, pressure, last))

    words = jnp.concatenate(
        [
            unfolded(got_ref, block_rows, rows_high, heights[0], capacity)[: 4 * full],
            unfolded(got_ref, block_rows, rows_high + heights[0], heights[1], capacity)[: full + 9],
        ],
        axis=0,
    )
    asked = words[5 * full + 8 : 5 * full + 9].astype(jnp.int32)
    asked_at = marks(asked & (cols_x - 1), cols_x)
    remote_rows = looked_up(own_rows, asked, asked_at)
    pressure, last, normal = weighted_pressure(words, full, remote_rows)
    remote_forces = forces_of(normal, loads_on(words, full, 5 * full, pressure, last))

    forces = jnp.concatenate([mortar_forces, remote_forces], axis=1)
    into = jnp.concatenate([mortar_ref[...], asked], axis=1)
    at = jnp.concatenate([marks(mortar_ref[...] & (cols_x - 1), cols_x), asked_at], axis=1)
    forces = jnp.concatenate(
        [jnp.where(into < cols_x, forces, 0.0), jnp.where(into < cols_x, 0.0, forces)], axis=0
    )
    forces = summed(times_turned(stacked_terms(forces), at))
    forces = jnp.concatenate([forces[:12], forces[12:]], axis=1)
    total = jnp.zeros((2 * components * strips, cols_x), F32)
    parts = [term.astype(F32) for term in terms_of(forces, 2)]
    for corner in range(4):
        index = nodes_ref[corner : corner + 1, :]
        strip = marks(index >> halves(cols_x), strips)
        spread = []
        for part in parts:
            for k in range(components):
                at = k * 4 + corner
                row = jnp.broadcast_to(part[at : at + 1], (16, face_count)).astype(BF16)
                spread.append(strip * jnp.concatenate([row] * (strips // 16), axis=0))
        along_x = marks(index & (cols_x - 1), cols_x)
        total = total + times_turned(jnp.concatenate(spread, axis=0), along_x)
    contact = summed(total).reshape(components, layers, rows_y, cols_x)
    upward = lax.axis_index("sub") == 1
    edge = edge_part(upward, own_ref, halo_ref, blocks_ref)
    at = jnp.where(upward, layers - 1, 0)
    for layer in range(layers):
        for k in range(components):
            nodal = internal_ref[k, layer] + jnp.where(at == layer, edge[k], 0.0)
            out_ref[k, layer] = (nodal + contact[k, layer]) * inverse_ref[layer]


GROUP = 8


def shifted(layer):
    views = []
    for part in layer:
        rows_y, cols_x = part.shape
        for moved in (part, pltpu.roll(part, rows_y - 1, 0)):
            views += [moved, pltpu.roll(moved, cols_x - 1, 1)]
    return views


def element_forces(matrices, low, high, modulus):
    rows_y, cols_x = modulus.shape
    inside = (lax.broadcasted_iota(jnp.int32, (rows_y, cols_x), 0) < rows_y - 1) & (
        lax.broadcasted_iota(jnp.int32, (rows_y, cols_x), 1) < cols_x - 1
    )
    scale = jnp.where(inside, modulus, 0.0)
    views = shifted(low) + shifted(high)
    both = jnp.concatenate(matrices, axis=0)
    count = both.shape[0] // 2
    strips = []
    for y in range(0, rows_y, GROUP):
        leading, second = terms_of(jnp.concatenate([view[y : y + GROUP] for view in views], axis=0), 2)
        found = times(both, leading)
        force = found[:count] + (found[count:] + times(matrices[0], second))
        strips.append(force.reshape(-1, GROUP, cols_x) * scale[y : y + GROUP][None])
    return jnp.concatenate(strips, axis=1)


def on_nodes(forces):
    sums = []
    for k in range(forces.shape[0] // 4):
        straight, crossed = [
            forces[k * 4 + c] + pltpu.roll(forces[k * 4 + 2 + c], 1, 0) for c in range(2)
        ]
        sums.append(-(straight + pltpu.roll(crossed, 1, 1)))
    return sums


def edge_part(upward, own_ref, halo_ref, blocks_ref):
    components = own_ref.shape[0] - 1
    size = blocks_ref.shape[1]
    rows = size // 2
    start = jnp.where(upward, 0, rows)
    matrices = [
        blocks_ref[pl.ds(pl.multiple_of(term * size + start, 16), rows)] for term in range(2)
    ]
    low = [jnp.where(upward, own_ref[k], halo_ref[k]) for k in range(components + 1)]
    high = [jnp.where(upward, halo_ref[k], own_ref[k]) for k in range(components)]
    return on_nodes(element_forces(matrices, low[:components], high, low[components]))


def internal_kernel(
    disp_ref, modulus_ref, stiffness_ref, mass_ref, own_ref, halo_ref, out_ref, blocks_ref, inverse_ref
):
    inverse_ref[...] = 1.0 / mass_ref[...]
    components, layers, rows_y, cols_x = disp_ref.shape
    dofs = 8 * components
    half = dofs // 2
    size = dofs * GROUP

    row = lax.broadcasted_iota(jnp.int32, (size, dofs), 0) >> halves(GROUP)
    upper = (row >= half).astype(jnp.int32)
    inner = row - half * upper
    dof = (inner >> 2) * 8 + upper * 4 + (inner & 3)
    pick = (dof == lax.broadcasted_iota(jnp.int32, (size, dofs), 1)).astype(F32).astype(BF16)
    diagonal = (lax.broadcasted_iota(jnp.int32, (size, size), 0) & (GROUP - 1)) == (
        lax.broadcasted_iota(jnp.int32, (size, size), 1) & (GROUP - 1)
    )
    for i, term in enumerate(terms_of(stiffness_ref[...], 2)):
        wide = times_turned(times(pick, term).astype(BF16), pick)
        blocks_ref[i * size : (i + 1) * size] = jnp.where(diagonal, wide, 0.0).astype(BF16)

    blocks = [blocks_ref[i * size : (i + 1) * size] for i in range(2)]
    sums = [[0.0] * components for _ in range(layers)]
    for e in range(layers - 1):
        pair = [[disp_ref[k, e + a] for k in range(components)] for a in range(2)]
        forces = element_forces(blocks, pair[0], pair[1], modulus_ref[e])
        for a in range(2):
            part = on_nodes(forces[a * half : (a + 1) * half])
            sums[e + a] = [x + y for x, y in zip(sums[e + a], part)]
    upward = lax.axis_index("sub") == 0
    edge = edge_part(upward, own_ref, halo_ref, blocks_ref)
    at = jnp.where(upward, layers - 1, 0)
    for layer in range(layers):
        for k in range(components):
            out_ref[k, layer] = sums[layer][k] + jnp.where(at == layer, edge[k], 0.0)


def on_core(kernel, outs, flops, moved, **more):
    return pl.pallas_call(
        kernel,
        out_shape=outs,
        compiler_params=pltpu.CompilerParams(vmem_limit_bytes=48 * 1024 * 1024),
        cost_estimate=pl.CostEstimate(flops=flops, bytes_accessed=moved, transcendentals=0),
        **more,
    )


def swapped(block, axis, first):
    size = lax.axis_size(axis)
    route = []
    for i in range(first, size - 1, 2):
        route += [(i, i + 1), (i + 1, i)]
    return lax.ppermute(block, axis, route)


def shards(
    displacement,
    modulus,
    node_mass,
    stiffness,
    face_nodes,
    pair_mortar,
    pair_rank,
    pair_face,
    pair_count,
    pair_shape,
    pair_weight,
    pair_gap,
    pair_normal,
):
    components, layers, rows_y, cols_x = displacement.shape
    face_count = face_nodes.shape[1]
    pair_total = pair_mortar.shape[0]
    domains = lax.axis_size("dom")
    capacity = max(2, 2 * pair_total // domains)

    points = pair_weight.shape[0]
    full = points // 8 * 8
    group = LANES // capacity
    word_rows = 5 * full + 9
    heights = tuple(-(-rows // group) for rows in (4 * full, full + 9))
    rows_high = 12 * face_count // LANES
    line = (1, pair_total)

    def first(*refs):
        first_kernel(capacity, heights, *refs)

    def last(*refs):
        last_kernel(capacity, heights, *refs)

    def shaped(shape, dtype=F32):
        return jax.ShapeDtypeStruct(shape, dtype)

    arrays = [
        face_nodes,
        displacement,
        pair_mortar.reshape(line),
        pair_rank.reshape(line),
        pair_face.reshape(line),
        pair_count.reshape(line),
        pair_weight,
        pair_normal,
        pair_gap,
        jnp.swapaxes(pair_shape, 0, 1),
        modulus,
    ]
    edge = shaped((components + 1, rows_y, cols_x))
    in_hbm = pl.BlockSpec(memory_space=pltpu.HBM)
    in_vmem = pl.BlockSpec(memory_space=pltpu.VMEM)
    kept = [displacement, *arrays[5:-1], modulus[0]]
    sent, rows, words, turned, mortar, rank, face, nodes, inner, outer = on_core(
        first,
        [
            shaped((domains * (rows_high + sum(heights)), LANES)),
            shaped((12 * face_count // cols_x, cols_x)),
            shaped((word_rows, pair_total)),
            shaped((4 * full + 8, pair_total)),
            shaped(line, jnp.int32),
            shaped(line, jnp.int32),
            shaped(line, jnp.int32),
            shaped(face_nodes.shape, jnp.int32),
            edge,
            edge,
        ],
        900_000_000,
        1_500_000,
        in_specs=[in_hbm] * len(arrays),
        out_specs=[in_hbm] + [in_vmem] * 9,
        scratch_shapes=[pltpu.VMEM(x.shape, x.dtype) for x in kept]
        + [
            pltpu.VMEM((domains * (rows_high + sum(heights)), LANES), F32),
            pltpu.SemaphoreType.DMA((len(arrays),)),
            pltpu.SemaphoreType.DMA(()),
        ],
    )(*[pltpu.with_memory_space_constraint(x, pltpu.HBM) for x in arrays])
    order = [place_in_group(domain, domains) for domain in range(domains)]
    got = lax.all_to_all(
        sent.reshape(domains, 1, -1),
        "dom",
        split_axis=0,
        concat_axis=0,
        axis_index_groups=[order],
        tiled=True,
    ).reshape(sent.shape)
    inner_halo = swapped(inner, ("dom", "sub"), 0)
    outer_halo = swapped(outer, ("dom", "sub"), 1)
    size = 8 * components * GROUP
    internal, blocks, inverse = on_core(
        internal_kernel,
        [shaped(displacement.shape), shaped((2 * size, size), BF16), shaped(node_mass.shape)],
        1_000_000_000,
        700_000,
    )(displacement, modulus, stiffness, node_mass, inner, inner_halo)
    return on_core(last, shaped(displacement.shape), 1_000_000_000, 1_500_000)(
        got, rows, words, turned, mortar, rank, face, nodes, inverse, internal, blocks, outer, outer_halo
    )


def solution(mesh):
    placed = (
        P(None, ("runs", "dom", "sub"), None, None),
        P(("runs", "dom", "sub"), None, None),
        P(("runs", "dom", "sub"), None, None),
        P(),
        P(None, ("runs", "dom", "sub")),
        P(("runs", "dom", "sub")),
        P(("runs", "dom", "sub"), None),
        P(("runs", "dom", "sub")),
        P(("runs", "dom", "sub")),
        P(None, None, ("runs", "dom", "sub")),
        P(None, ("runs", "dom", "sub")),
        P(None, ("runs", "dom", "sub")),
        P(None, ("runs", "dom", "sub")),
    )
    return jax.shard_map(
        shards,
        mesh=mesh,
        in_specs=placed,
        out_specs=P(None, ("runs", "dom", "sub"), None, None),
        check_vma=False,
    )
```

```python
import jax
import jax.numpy as jnp
from jax import lax
from jax.experimental import pallas as pl
from jax.experimental.pallas import tpu as pltpu
from jax.sharding import PartitionSpec as P

F32 = jnp.float32
BF16 = jnp.bfloat16
LANES = 128


def terms_of(x, count):
    terms = []
    for _ in range(count):
        terms.append(x.astype(BF16))
        x = x - terms[-1].astype(F32)
    return terms


def stacked_terms(x):
    return jnp.concatenate(terms_of(x, 2), axis=0)


def summed(stacked):
    rows = stacked.shape[0] // 2
    return stacked[:rows] + stacked[rows:]


def marks(index, count):
    shape = (16, index.shape[1])
    rows = lax.broadcasted_iota(jnp.int32, shape, 0).astype(jnp.int16)
    index = jnp.broadcast_to(index, shape).astype(jnp.int16)
    tiles = [
        jnp.where(rows == index - jnp.int16(start), jnp.ones((), BF16), jnp.zeros((), BF16))
        for start in range(0, count, 16)
    ]
    return jnp.concatenate(tiles, axis=0)


def times(left, right):
    return jnp.dot(left, right, preferred_element_type=F32)


def times_turned(left, right):
    return lax.dot_general(left, right, (((1,), (1,)), ((), ())), preferred_element_type=F32)


def halves(power):
    return power.bit_length() - 1


def looked_up(table, face, at):
    both = summed(times(stacked_terms(table), at))
    return jnp.where(face < table.shape[1], both[:12], both[12:])


def folded(placed, height, capacity, domain):
    group = LANES // capacity
    tile, spot = domain // group, domain % group
    part = lax.broadcasted_iota(jnp.int32, (height, LANES), 1) >> halves(capacity)
    block = None
    for j in range(group):
        piece = placed[j * height : (j + 1) * height, tile * LANES : (tile + 1) * LANES]
        if j != spot:
            piece = pltpu.roll(piece, (j - spot) * capacity % LANES, 1)
        block = piece if block is None else jnp.where(part == j, piece, block)
    return block


def unfolded(got_ref, block_rows, start, height, capacity):
    group = LANES // capacity
    part = lax.broadcasted_iota(jnp.int32, (height, LANES), 1) >> halves(capacity)
    pieces = []
    for j in range(group):
        tiles = []
        for first in range(0, got_ref.shape[0] // block_rows, group):
            block = None
            for spot in range(group):
                at = (first + spot) * block_rows + start
                piece = got_ref[at : at + height]
                if j != spot:
                    piece = pltpu.roll(piece, (spot - j) * capacity % LANES, 1)
                block = piece if block is None else jnp.where(part == spot, piece, block)
            tiles.append(block)
        pieces.append(jnp.concatenate(tiles, axis=1))
    return jnp.concatenate(pieces, axis=0)


def routed(words, rows, place):
    extra = -(-rows // 16) * 16 - words.shape[0]
    if extra:
        words = jnp.concatenate([words, jnp.zeros((extra, words.shape[1]), F32)], axis=0)
    return summed(times_turned(stacked_terms(words), place))


def weighted_pressure(words, full, remote_rows):
    tail = 5 * full
    normal = words[tail + 5 : tail + 8]
    gap, last = words[4 * full : tail], words[tail + 4 : tail + 5]
    for node in range(4):
        across = sum(
            normal[k : k + 1] * remote_rows[k * 4 + node : k * 4 + node + 1] for k in range(3)
        )
        gap = gap + words[node * full : (node + 1) * full] * across
        last = last + words[tail + node : tail + node + 1] * across
    return jnp.maximum(-gap, 0.0), jnp.maximum(-last, 0.0), normal


def loads_on(shapes, full, tail, pressure, last):
    return [
        jnp.sum(pressure * shapes[i * full : (i + 1) * full], axis=0, keepdims=True)
        + last * shapes[tail + i : tail + i + 1]
        for i in range(4)
    ]


def forces_of(normal, loads):
    loads = jnp.concatenate(loads, axis=0)
    return jnp.concatenate([normal[k : k + 1] * loads for k in range(3)], axis=0)


def place_in_group(domain, domains):
    return {0: domains - 1, domains - 1: 0}.get(domain, domain)


def first_kernel(capacity, heights, *refs):
    (
        nodes_hbm, disp_hbm, mortar_hbm, rank_hbm, face_hbm, count_hbm, weight_hbm, normal_hbm,
        gap_hbm, shape_hbm, modulus_hbm,
        sent_ref, rows_ref, words_ref, turned_ref, mortar_ref, rank_ref, face_ref, nodes,
        inner_ref, outer_ref,
        disp, count, weight, normal_v, gap_v, shape, modulus, blocks, sems, copy_sem,
    ) = refs
    components, layers, rows_y, cols_x = disp.shape
    block_rows = 12 * nodes.shape[1] // LANES + sum(heights)
    sources = (
        nodes_hbm, disp_hbm, rank_hbm, face_hbm, mortar_hbm, shape_hbm, count_hbm, weight_hbm,
        normal_hbm, gap_hbm, modulus_hbm.at[disp.shape[1] - 1],
    )
    targets = (
        nodes, disp, rank_ref, face_ref, mortar_ref, shape, count, weight, normal_v, gap_v, modulus,
    )
    brought = [
        pltpu.make_async_copy(source, target, sems.at[i])
        for i, (source, target) in enumerate(zip(sources, targets))
    ]
    for copy in brought:
        copy.start()

    domains = sent_ref.shape[0] // block_rows
    pair_total = rank_ref.shape[1]
    face_count = nodes.shape[1]
    strips = layers * rows_y
    for copy in brought[:2]:
        copy.wait()
    parts = stacked_terms(disp[...].reshape(components * strips, cols_x))
    numbers = lax.broadcasted_iota(jnp.int32, (strips, face_count), 0)
    folds = face_count // cols_x
    for corner in range(4):
        index = nodes[corner : corner + 1, :]
        strip = index >> halves(cols_x)
        found = summed(times(parts, marks(index & (cols_x - 1), cols_x)))
        found = found.reshape(components, strips, face_count)
        values = jnp.sum(jnp.where((numbers == strip)[None], found, 0.0), axis=1)
        for fold in range(folds):
            for k in range(components):
                at = fold * 12 + k * 4 + corner
                rows_ref[at : at + 1, :] = values[k : k + 1, fold * cols_x : (fold + 1) * cols_x]

    for copy in brought[2:-1]:
        copy.wait()
    rank, face, mortar = rank_ref[...], face_ref[...], mortar_ref[...]
    normal = normal_v[...]
    gap = gap_v[...]

    chosen = lax.broadcasted_iota(jnp.int32, (domains, pair_total), 0) == rank
    before = lax.broadcasted_iota(jnp.int32, (pair_total, pair_total), 0) < lax.broadcasted_iota(
        jnp.int32, (pair_total, pair_total), 1
    )
    earlier = times(chosen.astype(F32).astype(BF16), before.astype(F32).astype(BF16))
    slot = jnp.sum(jnp.where(chosen, earlier, 0.0), axis=0, keepdims=True).astype(jnp.int32)
    place = marks(rank * capacity + slot, domains * capacity)

    points = gap.shape[0]
    full = points // 8 * 8
    live = lax.broadcasted_iota(jnp.int32, (points, pair_total), 0) < count[...]
    root = jnp.where(live, jnp.sqrt(weight[...]), 0.0)
    weighted = [root * shape[:, node] for node in range(4)]
    long_words = jnp.concatenate([x[:full] for x in weighted], axis=0)
    group = LANES // capacity
    placed = routed(long_words, group * heights[0], place)

    rows = rows_ref[...]
    high = rows.shape[0]
    rows_high = high * cols_x // LANES
    halved = jnp.concatenate(
        [rows[:, i * LANES : (i + 1) * LANES] for i in range(cols_x // LANES)], axis=0
    )
    for domain in range(domains):
        at = place_in_group(domain, domains) * block_rows
        blocks[at : at + rows_high] = halved
        at += rows_high
        blocks[at : at + heights[0]] = folded(placed, heights[0], capacity, domain)

    mortar_rows = looked_up(rows, mortar, marks(mortar & (cols_x - 1), cols_x))
    for node in range(4):
        across = sum(
            normal[k : k + 1] * mortar_rows[k * 4 + node : k * 4 + node + 1] for k in range(3)
        )
        gap = gap - shape[:, 4 + node] * across
    gap = root * gap
    short_words = jnp.concatenate(
        [gap[:full]]
        + [x[full:] for x in weighted + [gap]]
        + [normal, face.astype(F32)],
        axis=0,
    )
    placed = routed(short_words, group * heights[1], place)
    for domain in range(domains):
        at = place_in_group(domain, domains) * block_rows + rows_high + heights[0]
        blocks[at : at + heights[1]] = folded(placed, heights[1], capacity, domain)
    sending = pltpu.make_async_copy(blocks, sent_ref, copy_sem)
    sending.start()

    words_ref[: 4 * full] = long_words
    words_ref[4 * full :] = short_words
    for node in range(4):
        turned = root * shape[:, 4 + node]
        turned_ref[node * full : (node + 1) * full] = turned[:full]
        turned_ref[4 * full + node : 4 * full + node + 1] = turned[full:]

    brought[-1].wait()
    sub = lax.axis_index("sub")
    for target, layer in ((inner_ref, (1 - sub) * (layers - 1)), (outer_ref, sub * (layers - 1))):
        for k in range(components):
            target[k] = disp[k, layer]
        target[components] = modulus[...]
    sending.wait()


def last_kernel(
    capacity, heights, got_ref, rows_ref, words_ref, turned_ref, mortar_ref, rank_ref, face_ref, nodes_ref,
    marks_ref, inverse_ref, internal_ref, blocks_ref, own_ref, halo_ref, out_ref,
):
    block_rows = 12 * nodes_ref.shape[1] // LANES + sum(heights)
    domains = got_ref.shape[0] // block_rows
    components, layers, rows_y, cols_x = out_ref.shape
    strips = layers * rows_y
    face_count = nodes_ref.shape[1]
    pair_total = rank_ref.shape[1]
    high = rows_ref.shape[0]
    rows_high = high * cols_x // LANES
    full = (turned_ref.shape[0] - 8) // 4
    own_rows = rows_ref[...]

    rank, face = rank_ref[...], face_ref[...]
    end = domains - 1
    place = jnp.where(rank == 0, end, jnp.where(rank == end, 0, rank))
    at = marks(face & (cols_x - 1), cols_x)
    step = min(domains, 8)

    def add_step(turn, total):
        halves_of = [
            jnp.concatenate(
                [
                    got_ref[pl.ds((turn * step + i) * block_rows + j * high, high)]
                    for j in range(cols_x // LANES)
                ],
                axis=1,
            )
            for i in range(step)
        ]
        block = jnp.concatenate(halves_of, axis=0)
        found = summed(times(stacked_terms(block), at)).reshape(step, high, pair_total)
        for i in range(step):
            total = total + jnp.where(place == turn * step + i, found[i], 0.0)
        return total

    both = jnp.zeros((high, pair_total), F32)
    if domains == step:
        both = add_step(0, both)
    else:
        both = lax.fori_loop(0, domains // step, add_step, both)
    remote_rows = jnp.where(face < cols_x, both[:12], both[12:])
    pressure, last, normal = weighted_pressure(words_ref[...], full, remote_rows)
    turned = turned_ref[...]
    mortar_forces = forces_of(-normal, loads_on(turned, full, 4 * full, pressure, last))

    words = jnp.concatenate(
        [
            unfolded(got_ref, block_rows, rows_high, heights[0], capacity)[: 4 * full],
            unfolded(got_ref, block_rows, rows_high + heights[0], heights[1], capacity)[: full + 9],
        ],
        axis=0,
    )
    asked = words[5 * full + 8 : 5 * full + 9].astype(jnp.int32)
    asked_at = marks(asked & (cols_x - 1), cols_x)
    remote_rows = looked_up(own_rows, asked, asked_at)
    pressure, last, normal = weighted_pressure(words, full, remote_rows)
    remote_forces = forces_of(normal, loads_on(words, full, 5 * full, pressure, last))

    forces = jnp.concatenate([mortar_forces, remote_forces], axis=1)
    into = jnp.concatenate([mortar_ref[...], asked], axis=1)
    at = jnp.concatenate([marks(mortar_ref[...] & (cols_x - 1), cols_x), asked_at], axis=1)
    forces = jnp.concatenate(
        [jnp.where(into < cols_x, forces, 0.0), jnp.where(into < cols_x, 0.0, forces)], axis=0
    )
    forces = summed(times_turned(stacked_terms(forces), at))
    forces = jnp.concatenate([forces[:12], forces[12:]], axis=1)
    total = jnp.zeros((2 * components * strips, cols_x), F32)
    parts = [term.astype(F32) for term in terms_of(forces, 2)]
    for corner in range(4):
        index = nodes_ref[corner : corner + 1, :]
        strip = marks(index >> halves(cols_x), strips)
        spread = []
        for part in parts:
            for k in range(components):
                at = k * 4 + corner
                row = jnp.broadcast_to(part[at : at + 1], (16, face_count)).astype(BF16)
                spread.append(strip * jnp.concatenate([row] * (strips // 16), axis=0))
        total = total + times_turned(jnp.concatenate(spread, axis=0), marks_ref[corner])
    contact = summed(total).reshape(components, layers, rows_y, cols_x)
    upward = lax.axis_index("sub") == 1
    edge = edge_part(upward, own_ref, halo_ref, blocks_ref)
    at = jnp.where(upward, layers - 1, 0)
    for layer in range(layers):
        for k in range(components):
            nodal = internal_ref[k, layer] + jnp.where(at == layer, edge[k], 0.0)
            out_ref[k, layer] = (nodal + contact[k, layer]) * inverse_ref[layer]


GROUP = 8


def shifted(layer):
    views = []
    for part in layer:
        rows_y, cols_x = part.shape
        for moved in (part, pltpu.roll(part, rows_y - 1, 0)):
            views += [moved, pltpu.roll(moved, cols_x - 1, 1)]
    return views


def element_forces(matrices, low, high, modulus):
    rows_y, cols_x = modulus.shape
    inside = (lax.broadcasted_iota(jnp.int32, (rows_y, cols_x), 0) < rows_y - 1) & (
        lax.broadcasted_iota(jnp.int32, (rows_y, cols_x), 1) < cols_x - 1
    )
    scale = jnp.where(inside, modulus, 0.0)
    views = shifted(low) + shifted(high)
    both = jnp.concatenate(matrices, axis=0)
    count = both.shape[0] // 2
    strips = []
    for y in range(0, rows_y, GROUP):
        leading, second = terms_of(jnp.concatenate([view[y : y + GROUP] for view in views], axis=0), 2)
        found = times(both, leading)
        force = found[:count] + (found[count:] + times(matrices[0], second))
        strips.append(force.reshape(-1, GROUP, cols_x) * scale[y : y + GROUP][None])
    return jnp.concatenate(strips, axis=1)


def on_nodes(forces):
    sums = []
    for k in range(forces.shape[0] // 4):
        straight, crossed = [
            forces[k * 4 + c] + pltpu.roll(forces[k * 4 + 2 + c], 1, 0) for c in range(2)
        ]
        sums.append(-(straight + pltpu.roll(crossed, 1, 1)))
    return sums


def edge_part(upward, own_ref, halo_ref, blocks_ref):
    components = own_ref.shape[0] - 1
    size = blocks_ref.shape[1]
    rows = size // 2
    start = jnp.where(upward, 0, rows)
    matrices = [
        blocks_ref[pl.ds(pl.multiple_of(term * size + start, 16), rows)] for term in range(2)
    ]
    low = [jnp.where(upward, own_ref[k], halo_ref[k]) for k in range(components + 1)]
    high = [jnp.where(upward, halo_ref[k], own_ref[k]) for k in range(components)]
    return on_nodes(element_forces(matrices, low[:components], high, low[components]))


def internal_kernel(
    disp_ref, modulus_ref, stiffness_ref, mass_ref, nodes_ref, own_ref, halo_ref, out_ref, blocks_ref,
    inverse_ref, marks_ref,
):
    inverse_ref[...] = 1.0 / mass_ref[...]
    for corner in range(4):
        width = disp_ref.shape[3]
        marks_ref[corner] = marks(nodes_ref[corner : corner + 1, :] & (width - 1), width)
    components, layers, rows_y, cols_x = disp_ref.shape
    dofs = 8 * components
    half = dofs // 2
    size = dofs * GROUP

    row = lax.broadcasted_iota(jnp.int32, (size, dofs), 0) >> halves(GROUP)
    upper = (row >= half).astype(jnp.int32)
    inner = row - half * upper
    dof = (inner >> 2) * 8 + upper * 4 + (inner & 3)
    pick = (dof == lax.broadcasted_iota(jnp.int32, (size, dofs), 1)).astype(F32).astype(BF16)
    diagonal = (lax.broadcasted_iota(jnp.int32, (size, size), 0) & (GROUP - 1)) == (
        lax.broadcasted_iota(jnp.int32, (size, size), 1) & (GROUP - 1)
    )
    for i, term in enumerate(terms_of(stiffness_ref[...], 2)):
        wide = times_turned(times(pick, term).astype(BF16), pick)
        blocks_ref[i * size : (i + 1) * size] = jnp.where(diagonal, wide, 0.0).astype(BF16)

    blocks = [blocks_ref[i * size : (i + 1) * size] for i in range(2)]
    sums = [[0.0] * components for _ in range(layers)]
    for e in range(layers - 1):
        pair = [[disp_ref[k, e + a] for k in range(components)] for a in range(2)]
        forces = element_forces(blocks, pair[0], pair[1], modulus_ref[e])
        for a in range(2):
            part = on_nodes(forces[a * half : (a + 1) * half])
            sums[e + a] = [x + y for x, y in zip(sums[e + a], part)]
    upward = lax.axis_index("sub") == 0
    edge = edge_part(upward, own_ref, halo_ref, blocks_ref)
    at = jnp.where(upward, layers - 1, 0)
    for layer in range(layers):
        for k in range(components):
            out_ref[k, layer] = sums[layer][k] + jnp.where(at == layer, edge[k], 0.0)


def on_core(kernel, outs, flops, moved, **more):
    return pl.pallas_call(
        kernel,
        out_shape=outs,
        compiler_params=pltpu.CompilerParams(vmem_limit_bytes=48 * 1024 * 1024),
        cost_estimate=pl.CostEstimate(flops=flops, bytes_accessed=moved, transcendentals=0),
        **more,
    )


def swapped(block, axis, first):
    size = lax.axis_size(axis)
    route = []
    for i in range(first, size - 1, 2):
        route += [(i, i + 1), (i + 1, i)]
    return lax.ppermute(block, axis, route)


def shards(
    displacement,
    modulus,
    node_mass,
    stiffness,
    face_nodes,
    pair_mortar,
    pair_rank,
    pair_face,
    pair_count,
    pair_shape,
    pair_weight,
    pair_gap,
    pair_normal,
):
    components, layers, rows_y, cols_x = displacement.shape
    face_count = face_nodes.shape[1]
    pair_total = pair_mortar.shape[0]
    domains = lax.axis_size("dom")
    capacity = max(2, 2 * pair_total // domains)

    points = pair_weight.shape[0]
    full = points // 8 * 8
    group = LANES // capacity
    word_rows = 5 * full + 9
    heights = tuple(-(-rows // group) for rows in (4 * full, full + 9))
    rows_high = 12 * face_count // LANES
    line = (1, pair_total)

    def first(*refs):
        first_kernel(capacity, heights, *refs)

    def last(*refs):
        last_kernel(capacity, heights, *refs)

    def shaped(shape, dtype=F32):
        return jax.ShapeDtypeStruct(shape, dtype)

    arrays = [
        face_nodes,
        displacement,
        pair_mortar.reshape(line),
        pair_rank.reshape(line),
        pair_face.reshape(line),
        pair_count.reshape(line),
        pair_weight,
        pair_normal,
        pair_gap,
        jnp.swapaxes(pair_shape, 0, 1),
        modulus,
    ]
    edge = shaped((components + 1, rows_y, cols_x))
    in_hbm = pl.BlockSpec(memory_space=pltpu.HBM)
    in_vmem = pl.BlockSpec(memory_space=pltpu.VMEM)
    kept = [displacement, *arrays[5:-1], modulus[0]]
    sent, rows, words, turned, mortar, rank, face, nodes, inner, outer = on_core(
        first,
        [
            shaped((domains * (rows_high + sum(heights)), LANES)),
            shaped((12 * face_count // cols_x, cols_x)),
            shaped((word_rows, pair_total)),
            shaped((4 * full + 8, pair_total)),
            shaped(line, jnp.int32),
            shaped(line, jnp.int32),
            shaped(line, jnp.int32),
            shaped(face_nodes.shape, jnp.int32),
            edge,
            edge,
        ],
        900_000_000,
        1_500_000,
        in_specs=[in_hbm] * len(arrays),
        out_specs=[in_hbm] + [in_vmem] * 9,
        scratch_shapes=[pltpu.VMEM(x.shape, x.dtype) for x in kept]
        + [
            pltpu.VMEM((domains * (rows_high + sum(heights)), LANES), F32),
            pltpu.SemaphoreType.DMA((len(arrays),)),
            pltpu.SemaphoreType.DMA(()),
        ],
    )(*[pltpu.with_memory_space_constraint(x, pltpu.HBM) for x in arrays])
    order = [place_in_group(domain, domains) for domain in range(domains)]
    got = lax.all_to_all(
        sent.reshape(domains, 1, -1),
        "dom",
        split_axis=0,
        concat_axis=0,
        axis_index_groups=[order],
        tiled=True,
    ).reshape(sent.shape)
    inner_halo = swapped(inner, ("dom", "sub"), 0)
    outer_halo = swapped(outer, ("dom", "sub"), 1)
    size = 8 * components * GROUP
    internal, blocks, inverse, along_x = on_core(
        internal_kernel,
        [shaped(displacement.shape), shaped((2 * size, size), BF16), shaped(node_mass.shape),
            shaped((4, cols_x, face_count), BF16),
        ],
        1_000_000_000,
        700_000,
    )(displacement, modulus, stiffness, node_mass, nodes, inner, inner_halo)
    return on_core(last, shaped(displacement.shape), 1_000_000_000, 1_500_000)(
        got, rows, words, turned, mortar, rank, face, nodes, along_x, inverse, internal, blocks, outer, outer_halo
    )


def solution(mesh):
    placed = (
        P(None, ("runs", "dom", "sub"), None, None),
        P(("runs", "dom", "sub"), None, None),
        P(("runs", "dom", "sub"), None, None),
        P(),
        P(None, ("runs", "dom", "sub")),
        P(("runs", "dom", "sub")),
        P(("runs", "dom", "sub"), None),
        P(("runs", "dom", "sub")),
        P(("runs", "dom", "sub")),
        P(None, None, ("runs", "dom", "sub")),
        P(None, ("runs", "dom", "sub")),
        P(None, ("runs", "dom", "sub")),
        P(None, ("runs", "dom", "sub")),
    )
    return jax.shard_map(
        shards,
        mesh=mesh,
        in_specs=placed,
        out_specs=P(None, ("runs", "dom", "sub"), None, None),
        check_vma=False,
    )
```

```python
import jax
import jax.numpy as jnp
from jax import lax
from jax.experimental import pallas as pl
from jax.experimental.pallas import tpu as pltpu
from jax.sharding import PartitionSpec as P

F32 = jnp.float32
BF16 = jnp.bfloat16
LANES = 128


def terms_of(x, count):
    terms = []
    for _ in range(count):
        terms.append(x.astype(BF16))
        x = x - terms[-1].astype(F32)
    return terms


def stacked_terms(x):
    return jnp.concatenate(terms_of(x, 2), axis=0)


def summed(stacked):
    rows = stacked.shape[0] // 2
    return stacked[:rows] + stacked[rows:]


def marks(index, count):
    shape = (16, index.shape[1])
    rows = lax.broadcasted_iota(jnp.int32, shape, 0).astype(jnp.int16)
    index = jnp.broadcast_to(index, shape).astype(jnp.int16)
    tiles = [
        jnp.where(rows == index - jnp.int16(start), jnp.ones((), BF16), jnp.zeros((), BF16))
        for start in range(0, count, 16)
    ]
    return jnp.concatenate(tiles, axis=0)


def marks_turned(index, count):
    column = jnp.broadcast_to(index.astype(F32), (8, index.shape[1])).T[:, :1]
    columns = lax.broadcasted_iota(jnp.int32, (index.shape[1], count), 1).astype(F32)
    return jnp.where(columns == column, 1.0, 0.0).astype(BF16)


def times(left, right):
    return jnp.dot(left, right, preferred_element_type=F32)


def times_turned(left, right):
    return lax.dot_general(left, right, (((1,), (1,)), ((), ())), preferred_element_type=F32)


def halves(power):
    return power.bit_length() - 1


def looked_up(table, face, at):
    both = summed(times(stacked_terms(table), at))
    return jnp.where(face < table.shape[1], both[:12], both[12:])


def folded(placed, height, capacity, domain):
    group = LANES // capacity
    tile, spot = domain // group, domain % group
    part = lax.broadcasted_iota(jnp.int32, (height, LANES), 1) >> halves(capacity)
    block = None
    for j in range(group):
        piece = placed[j * height : (j + 1) * height, tile * LANES : (tile + 1) * LANES]
        if j != spot:
            piece = pltpu.roll(piece, (j - spot) * capacity % LANES, 1)
        block = piece if block is None else jnp.where(part == j, piece, block)
    return block


def unfolded(got_ref, block_rows, start, height, capacity):
    group = LANES // capacity
    part = lax.broadcasted_iota(jnp.int32, (height, LANES), 1) >> halves(capacity)
    pieces = []
    for j in range(group):
        tiles = []
        for first in range(0, got_ref.shape[0] // block_rows, group):
            block = None
            for spot in range(group):
                at = (first + spot) * block_rows + start
                piece = got_ref[at : at + height]
                if j != spot:
                    piece = pltpu.roll(piece, (spot - j) * capacity % LANES, 1)
                block = piece if block is None else jnp.where(part == spot, piece, block)
            tiles.append(block)
        pieces.append(jnp.concatenate(tiles, axis=1))
    return jnp.concatenate(pieces, axis=0)


def routed(words, rows, place):
    extra = -(-rows // 16) * 16 - words.shape[0]
    if extra:
        words = jnp.concatenate([words, jnp.zeros((extra, words.shape[1]), F32)], axis=0)
    return summed(times(stacked_terms(words), place))


def weighted_pressure(words, full, remote_rows):
    tail = 5 * full
    normal = words[tail + 5 : tail + 8]
    gap, last = words[4 * full : tail], words[tail + 4 : tail + 5]
    for node in range(4):
        across = sum(
            normal[k : k + 1] * remote_rows[k * 4 + node : k * 4 + node + 1] for k in range(3)
        )
        gap = gap + words[node * full : (node + 1) * full] * across
        last = last + words[tail + node : tail + node + 1] * across
    return jnp.maximum(-gap, 0.0), jnp.maximum(-last, 0.0), normal


def loads_on(shapes, full, tail, pressure, last):
    return [
        jnp.sum(pressure * shapes[i * full : (i + 1) * full], axis=0, keepdims=True)
        + last * shapes[tail + i : tail + i + 1]
        for i in range(4)
    ]


def forces_of(normal, loads):
    loads = jnp.concatenate(loads, axis=0)
    return jnp.concatenate([normal[k : k + 1] * loads for k in range(3)], axis=0)


def place_in_group(domain, domains):
    return {0: domains - 1, domains - 1: 0}.get(domain, domain)


def first_kernel(capacity, heights, *refs):
    (
        nodes_hbm, disp_hbm, mortar_hbm, rank_hbm, face_hbm, count_hbm, weight_hbm, normal_hbm,
        gap_hbm, shape_hbm, modulus_hbm,
        sent_ref, rows_ref, words_ref, turned_ref, mortar_ref, rank_ref, face_ref, nodes,
        inner_ref, outer_ref,
        disp, count, weight, normal_v, gap_v, shape, modulus, blocks, sems, copy_sem,
    ) = refs
    components, layers, rows_y, cols_x = disp.shape
    block_rows = 12 * nodes.shape[1] // LANES + sum(heights)
    sources = (
        nodes_hbm, disp_hbm, rank_hbm, face_hbm, mortar_hbm, shape_hbm, count_hbm, weight_hbm,
        normal_hbm, gap_hbm, modulus_hbm.at[disp.shape[1] - 1],
    )
    targets = (
        nodes, disp, rank_ref, face_ref, mortar_ref, shape, count, weight, normal_v, gap_v, modulus,
    )
    brought = [
        pltpu.make_async_copy(source, target, sems.at[i])
        for i, (source, target) in enumerate(zip(sources, targets))
    ]
    for copy in brought:
        copy.start()

    domains = sent_ref.shape[0] // block_rows
    pair_total = rank_ref.shape[1]
    face_count = nodes.shape[1]
    strips = layers * rows_y
    for copy in brought[:-1]:
        copy.wait()
    rank, face, mortar = rank_ref[...], face_ref[...], mortar_ref[...]
    normal = normal_v[...]
    gap = gap_v[...]

    chosen = lax.broadcasted_iota(jnp.int32, (domains, pair_total), 0) == rank
    before = lax.broadcasted_iota(jnp.int32, (pair_total, pair_total), 0) < lax.broadcasted_iota(
        jnp.int32, (pair_total, pair_total), 1
    )
    earlier = times(chosen.astype(F32).astype(BF16), before.astype(F32).astype(BF16))
    slot = jnp.sum(jnp.where(chosen, earlier, 0.0), axis=0, keepdims=True).astype(jnp.int32)
    place = marks_turned(rank * capacity + slot, domains * capacity)

    parts = stacked_terms(disp[...].reshape(components * strips, cols_x))
    numbers = lax.broadcasted_iota(jnp.int32, (strips, face_count), 0)
    folds = face_count // cols_x
    for corner in range(4):
        index = nodes[corner : corner + 1, :]
        strip = index >> halves(cols_x)
        found = summed(times(parts, marks(index & (cols_x - 1), cols_x)))
        found = found.reshape(components, strips, face_count)
        values = jnp.sum(jnp.where((numbers == strip)[None], found, 0.0), axis=1)
        for fold in range(folds):
            for k in range(components):
                at = fold * 12 + k * 4 + corner
                rows_ref[at : at + 1, :] = values[k : k + 1, fold * cols_x : (fold + 1) * cols_x]

    points = gap.shape[0]
    full = points // 8 * 8
    live = lax.broadcasted_iota(jnp.int32, (points, pair_total), 0) < count[...]
    root = jnp.where(live, jnp.sqrt(weight[...]), 0.0)
    weighted = [root * shape[:, node] for node in range(4)]
    long_words = jnp.concatenate([x[:full] for x in weighted], axis=0)
    group = LANES // capacity
    placed = routed(long_words, group * heights[0], place)

    rows = rows_ref[...]
    high = rows.shape[0]
    rows_high = high * cols_x // LANES
    halved = jnp.concatenate(
        [rows[:, i * LANES : (i + 1) * LANES] for i in range(cols_x // LANES)], axis=0
    )
    for domain in range(domains):
        at = place_in_group(domain, domains) * block_rows
        blocks[at : at + rows_high] = halved
        at += rows_high
        blocks[at : at + heights[0]] = folded(placed, heights[0], capacity, domain)

    mortar_rows = looked_up(rows, mortar, marks(mortar & (cols_x - 1), cols_x))
    for node in range(4):
        across = sum(
            normal[k : k + 1] * mortar_rows[k * 4 + node : k * 4 + node + 1] for k in range(3)
        )
        gap = gap - shape[:, 4 + node] * across
    gap = root * gap
    short_words = jnp.concatenate(
        [gap[:full]]
        + [x[full:] for x in weighted + [gap]]
        + [normal, face.astype(F32)],
        axis=0,
    )
    placed = routed(short_words, group * heights[1], place)
    for domain in range(domains):
        at = place_in_group(domain, domains) * block_rows + rows_high + heights[0]
        blocks[at : at + heights[1]] = folded(placed, heights[1], capacity, domain)
    sending = pltpu.make_async_copy(blocks, sent_ref, copy_sem)
    sending.start()

    words_ref[: 4 * full] = long_words
    words_ref[4 * full :] = short_words
    for node in range(4):
        turned = root * shape[:, 4 + node]
        turned_ref[node * full : (node + 1) * full] = turned[:full]
        turned_ref[4 * full + node : 4 * full + node + 1] = turned[full:]

    brought[-1].wait()
    sub = lax.axis_index("sub")
    for target, layer in ((inner_ref, (1 - sub) * (layers - 1)), (outer_ref, sub * (layers - 1))):
        for k in range(components):
            target[k] = disp[k, layer]
        target[components] = modulus[...]
    sending.wait()


def last_kernel(
    capacity, heights, got_ref, rows_ref, words_ref, turned_ref, mortar_ref, rank_ref, face_ref, nodes_ref,
    marks_ref, inverse_ref, internal_ref, blocks_ref, own_ref, halo_ref, out_ref,
):
    block_rows = 12 * nodes_ref.shape[1] // LANES + sum(heights)
    domains = got_ref.shape[0] // block_rows
    components, layers, rows_y, cols_x = out_ref.shape
    strips = layers * rows_y
    face_count = nodes_ref.shape[1]
    pair_total = rank_ref.shape[1]
    high = rows_ref.shape[0]
    rows_high = high * cols_x // LANES
    full = (turned_ref.shape[0] - 8) // 4
    own_rows = rows_ref[...]

    rank, face = rank_ref[...], face_ref[...]
    end = domains - 1
    place = jnp.where(rank == 0, end, jnp.where(rank == end, 0, rank))
    at = marks(face & (cols_x - 1), cols_x)
    step = min(domains, 8)

    def add_step(turn, total):
        halves_of = [
            jnp.concatenate(
                [
                    got_ref[pl.ds((turn * step + i) * block_rows + j * high, high)]
                    for j in range(cols_x // LANES)
                ],
                axis=1,
            )
            for i in range(step)
        ]
        block = jnp.concatenate(halves_of, axis=0)
        found = summed(times(stacked_terms(block), at)).reshape(step, high, pair_total)
        for i in range(step):
            total = total + jnp.where(place == turn * step + i, found[i], 0.0)
        return total

    both = jnp.zeros((high, pair_total), F32)
    if domains == step:
        both = add_step(0, both)
    else:
        both = lax.fori_loop(0, domains // step, add_step, both)
    remote_rows = jnp.where(face < cols_x, both[:12], both[12:])
    pressure, last, normal = weighted_pressure(words_ref[...], full, remote_rows)
    turned = turned_ref[...]
    mortar_forces = forces_of(-normal, loads_on(turned, full, 4 * full, pressure, last))

    words = jnp.concatenate(
        [
            unfolded(got_ref, block_rows, rows_high, heights[0], capacity)[: 4 * full],
            unfolded(got_ref, block_rows, rows_high + heights[0], heights[1], capacity)[: full + 9],
        ],
        axis=0,
    )
    asked = words[5 * full + 8 : 5 * full + 9].astype(jnp.int32)
    asked_at = marks(asked & (cols_x - 1), cols_x)
    remote_rows = looked_up(own_rows, asked, asked_at)
    pressure, last, normal = weighted_pressure(words, full, remote_rows)
    remote_forces = forces_of(normal, loads_on(words, full, 5 * full, pressure, last))

    forces = jnp.concatenate([mortar_forces, remote_forces], axis=1)
    into = jnp.concatenate([mortar_ref[...], asked], axis=1)
    at = jnp.concatenate([marks(mortar_ref[...] & (cols_x - 1), cols_x), asked_at], axis=1)
    forces = jnp.concatenate(
        [jnp.where(into < cols_x, forces, 0.0), jnp.where(into < cols_x, 0.0, forces)], axis=0
    )
    forces = summed(times_turned(stacked_terms(forces), at))
    forces = jnp.concatenate([forces[:12], forces[12:]], axis=1)
    total = jnp.zeros((2 * components * strips, cols_x), F32)
    parts = [term.astype(F32) for term in terms_of(forces, 2)]
    for corner in range(4):
        index = nodes_ref[corner : corner + 1, :]
        strip = marks(index >> halves(cols_x), strips)
        spread = []
        for part in parts:
            for k in range(components):
                at = k * 4 + corner
                row = jnp.broadcast_to(part[at : at + 1], (16, face_count)).astype(BF16)
                spread.append(strip * jnp.concatenate([row] * (strips // 16), axis=0))
        total = total + times(jnp.concatenate(spread, axis=0), marks_ref[corner])
    contact = summed(total).reshape(components, layers, rows_y, cols_x)
    upward = lax.axis_index("sub") == 1
    edge = edge_part(upward, own_ref, halo_ref, blocks_ref)
    at = jnp.where(upward, layers - 1, 0)
    for layer in range(layers):
        for k in range(components):
            nodal = internal_ref[k, layer] + jnp.where(at == layer, edge[k], 0.0)
            out_ref[k, layer] = (nodal + contact[k, layer]) * inverse_ref[layer]


GROUP = 8


def shifted(layer):
    views = []
    for part in layer:
        rows_y, cols_x = part.shape
        for moved in (part, pltpu.roll(part, rows_y - 1, 0)):
            views += [moved, pltpu.roll(moved, cols_x - 1, 1)]
    return views


def element_forces(matrices, low, high, modulus):
    rows_y, cols_x = modulus.shape
    inside = (lax.broadcasted_iota(jnp.int32, (rows_y, cols_x), 0) < rows_y - 1) & (
        lax.broadcasted_iota(jnp.int32, (rows_y, cols_x), 1) < cols_x - 1
    )
    scale = jnp.where(inside, modulus, 0.0)
    views = shifted(low) + shifted(high)
    both = jnp.concatenate(matrices, axis=0)
    count = both.shape[0] // 2
    strips = []
    for y in range(0, rows_y, GROUP):
        leading, second = terms_of(jnp.concatenate([view[y : y + GROUP] for view in views], axis=0), 2)
        found = times(both, leading)
        force = found[:count] + (found[count:] + times(matrices[0], second))
        strips.append(force.reshape(-1, GROUP, cols_x) * scale[y : y + GROUP][None])
    return jnp.concatenate(strips, axis=1)


def on_nodes(forces):
    sums = []
    for k in range(forces.shape[0] // 4):
        straight, crossed = [
            forces[k * 4 + c] + pltpu.roll(forces[k * 4 + 2 + c], 1, 0) for c in range(2)
        ]
        sums.append(-(straight + pltpu.roll(crossed, 1, 1)))
    return sums


def edge_part(upward, own_ref, halo_ref, blocks_ref):
    components = own_ref.shape[0] - 1
    size = blocks_ref.shape[1]
    rows = size // 2
    start = jnp.where(upward, 0, rows)
    matrices = [
        blocks_ref[pl.ds(pl.multiple_of(term * size + start, 16), rows)] for term in range(2)
    ]
    low = [jnp.where(upward, own_ref[k], halo_ref[k]) for k in range(components + 1)]
    high = [jnp.where(upward, halo_ref[k], own_ref[k]) for k in range(components)]
    return on_nodes(element_forces(matrices, low[:components], high, low[components]))


def internal_kernel(
    disp_ref, modulus_ref, stiffness_ref, mass_ref, nodes_ref, own_ref, halo_ref, out_ref, blocks_ref,
    inverse_ref, marks_ref,
):
    inverse_ref[...] = 1.0 / mass_ref[...]
    for corner in range(4):
        width = disp_ref.shape[3]
        marks_ref[corner] = marks_turned(nodes_ref[corner : corner + 1, :] & (width - 1), width)
    components, layers, rows_y, cols_x = disp_ref.shape
    dofs = 8 * components
    half = dofs // 2
    size = dofs * GROUP

    row = lax.broadcasted_iota(jnp.int32, (size, dofs), 0) >> halves(GROUP)
    upper = (row >= half).astype(jnp.int32)
    inner = row - half * upper
    dof = (inner >> 2) * 8 + upper * 4 + (inner & 3)
    pick = (dof == lax.broadcasted_iota(jnp.int32, (size, dofs), 1)).astype(F32).astype(BF16)
    diagonal = (lax.broadcasted_iota(jnp.int32, (size, size), 0) & (GROUP - 1)) == (
        lax.broadcasted_iota(jnp.int32, (size, size), 1) & (GROUP - 1)
    )
    for i, term in enumerate(terms_of(stiffness_ref[...], 2)):
        wide = times_turned(times(pick, term).astype(BF16), pick)
        blocks_ref[i * size : (i + 1) * size] = jnp.where(diagonal, wide, 0.0).astype(BF16)

    blocks = [blocks_ref[i * size : (i + 1) * size] for i in range(2)]
    sums = [[0.0] * components for _ in range(layers)]
    for e in range(layers - 1):
        pair = [[disp_ref[k, e + a] for k in range(components)] for a in range(2)]
        forces = element_forces(blocks, pair[0], pair[1], modulus_ref[e])
        for a in range(2):
            part = on_nodes(forces[a * half : (a + 1) * half])
            sums[e + a] = [x + y for x, y in zip(sums[e + a], part)]
    upward = lax.axis_index("sub") == 0
    edge = edge_part(upward, own_ref, halo_ref, blocks_ref)
    at = jnp.where(upward, layers - 1, 0)
    for layer in range(layers):
        for k in range(components):
            out_ref[k, layer] = sums[layer][k] + jnp.where(at == layer, edge[k], 0.0)


def on_core(kernel, outs, flops, moved, **more):
    return pl.pallas_call(
        kernel,
        out_shape=outs,
        compiler_params=pltpu.CompilerParams(vmem_limit_bytes=48 * 1024 * 1024),
        cost_estimate=pl.CostEstimate(flops=flops, bytes_accessed=moved, transcendentals=0),
        **more,
    )


def swapped(block, axis, first):
    size = lax.axis_size(axis)
    route = []
    for i in range(first, size - 1, 2):
        route += [(i, i + 1), (i + 1, i)]
    return lax.ppermute(block, axis, route)


def shards(
    displacement,
    modulus,
    node_mass,
    stiffness,
    face_nodes,
    pair_mortar,
    pair_rank,
    pair_face,
    pair_count,
    pair_shape,
    pair_weight,
    pair_gap,
    pair_normal,
):
    components, layers, rows_y, cols_x = displacement.shape
    face_count = face_nodes.shape[1]
    pair_total = pair_mortar.shape[0]
    domains = lax.axis_size("dom")
    capacity = max(2, 2 * pair_total // domains)

    points = pair_weight.shape[0]
    full = points // 8 * 8
    group = LANES // capacity
    word_rows = 5 * full + 9
    heights = tuple(-(-rows // group) for rows in (4 * full, full + 9))
    rows_high = 12 * face_count // LANES
    line = (1, pair_total)

    def first(*refs):
        first_kernel(capacity, heights, *refs)

    def last(*refs):
        last_kernel(capacity, heights, *refs)

    def shaped(shape, dtype=F32):
        return jax.ShapeDtypeStruct(shape, dtype)

    arrays = [
        face_nodes,
        displacement,
        pair_mortar.reshape(line),
        pair_rank.reshape(line),
        pair_face.reshape(line),
        pair_count.reshape(line),
        pair_weight,
        pair_normal,
        pair_gap,
        jnp.swapaxes(pair_shape, 0, 1),
        modulus,
    ]
    edge = shaped((components + 1, rows_y, cols_x))
    in_hbm = pl.BlockSpec(memory_space=pltpu.HBM)
    in_vmem = pl.BlockSpec(memory_space=pltpu.VMEM)
    kept = [displacement, *arrays[5:-1], modulus[0]]
    sent, rows, words, turned, mortar, rank, face, nodes, inner, outer = on_core(
        first,
        [
            shaped((domains * (rows_high + sum(heights)), LANES)),
            shaped((12 * face_count // cols_x, cols_x)),
            shaped((word_rows, pair_total)),
            shaped((4 * full + 8, pair_total)),
            shaped(line, jnp.int32),
            shaped(line, jnp.int32),
            shaped(line, jnp.int32),
            shaped(face_nodes.shape, jnp.int32),
            edge,
            edge,
        ],
        900_000_000,
        1_500_000,
        in_specs=[in_hbm] * len(arrays),
        out_specs=[in_hbm] + [in_vmem] * 9,
        scratch_shapes=[pltpu.VMEM(x.shape, x.dtype) for x in kept]
        + [
            pltpu.VMEM((domains * (rows_high + sum(heights)), LANES), F32),
            pltpu.SemaphoreType.DMA((len(arrays),)),
            pltpu.SemaphoreType.DMA(()),
        ],
    )(*[pltpu.with_memory_space_constraint(x, pltpu.HBM) for x in arrays])
    order = [place_in_group(domain, domains) for domain in range(domains)]
    got = lax.all_to_all(
        sent.reshape(domains, 1, -1),
        "dom",
        split_axis=0,
        concat_axis=0,
        axis_index_groups=[order],
        tiled=True,
    ).reshape(sent.shape)
    inner_halo = swapped(inner, ("dom", "sub"), 0)
    outer_halo = swapped(outer, ("dom", "sub"), 1)
    size = 8 * components * GROUP
    internal, blocks, inverse, along_x = on_core(
        internal_kernel,
        [shaped(displacement.shape), shaped((2 * size, size), BF16), shaped(node_mass.shape),
            shaped((4, face_count, cols_x), BF16),
        ],
        1_000_000_000,
        700_000,
    )(displacement, modulus, stiffness, node_mass, nodes, inner, inner_halo)
    return on_core(last, shaped(displacement.shape), 1_000_000_000, 1_500_000)(
        got, rows, words, turned, mortar, rank, face, nodes, along_x, inverse, internal, blocks, outer, outer_halo
    )


def solution(mesh):
    placed = (
        P(None, ("runs", "dom", "sub"), None, None),
        P(("runs", "dom", "sub"), None, None),
        P(("runs", "dom", "sub"), None, None),
        P(),
        P(None, ("runs", "dom", "sub")),
        P(("runs", "dom", "sub")),
        P(("runs", "dom", "sub"), None),
        P(("runs", "dom", "sub")),
        P(("runs", "dom", "sub")),
        P(None, None, ("runs", "dom", "sub")),
        P(None, ("runs", "dom", "sub")),
        P(None, ("runs", "dom", "sub")),
        P(None, ("runs", "dom", "sub")),
    )
    return jax.shard_map(
        shards,
        mesh=mesh,
        in_specs=placed,
        out_specs=P(None, ("runs", "dom", "sub"), None, None),
        check_vma=False,
    )
```

```python
import jax
import jax.numpy as jnp
from jax import lax
from jax.experimental import pallas as pl
from jax.experimental.pallas import tpu as pltpu
from jax.sharding import PartitionSpec as P

F32 = jnp.float32
BF16 = jnp.bfloat16
LANES = 128


def terms_of(x, count):
    terms = []
    for _ in range(count):
        terms.append(x.astype(BF16))
        x = x - terms[-1].astype(F32)
    return terms


def stacked_terms(x):
    return jnp.concatenate(terms_of(x, 2), axis=0)


def summed(stacked):
    rows = stacked.shape[0] // 2
    return stacked[:rows] + stacked[rows:]


def marks(index, count):
    shape = (16, index.shape[1])
    rows = lax.broadcasted_iota(jnp.int32, shape, 0).astype(jnp.int16)
    index = jnp.broadcast_to(index, shape).astype(jnp.int16)
    tiles = [
        jnp.where(rows == index - jnp.int16(start), jnp.ones((), BF16), jnp.zeros((), BF16))
        for start in range(0, count, 16)
    ]
    return jnp.concatenate(tiles, axis=0)


def times(left, right):
    return jnp.dot(left, right, preferred_element_type=F32)


def times_turned(left, right):
    return lax.dot_general(left, right, (((1,), (1,)), ((), ())), preferred_element_type=F32)


def halves(power):
    return power.bit_length() - 1


def looked_up(table, face, at):
    both = summed(times(stacked_terms(table), at))
    return jnp.where(face < table.shape[1], both[:12], both[12:])


def folded(placed, height, capacity, domain):
    group = LANES // capacity
    tile, spot = domain // group, domain % group
    part = lax.broadcasted_iota(jnp.int32, (height, LANES), 1) >> halves(capacity)
    block = None
    for j in range(group):
        piece = placed[j * height : (j + 1) * height, tile * LANES : (tile + 1) * LANES]
        if j != spot:
            piece = pltpu.roll(piece, (j - spot) * capacity % LANES, 1)
        block = piece if block is None else jnp.where(part == j, piece, block)
    return block


def unfolded(got_ref, block_rows, start, height, capacity):
    group = LANES // capacity
    part = lax.broadcasted_iota(jnp.int32, (height, LANES), 1) >> halves(capacity)
    pieces = []
    for j in range(group):
        tiles = []
        for first in range(0, got_ref.shape[0] // block_rows, group):
            block = None
            for spot in range(group):
                at = (first + spot) * block_rows + start
                piece = got_ref[at : at + height]
                if j != spot:
                    piece = pltpu.roll(piece, (spot - j) * capacity % LANES, 1)
                block = piece if block is None else jnp.where(part == spot, piece, block)
            tiles.append(block)
        pieces.append(jnp.concatenate(tiles, axis=1))
    return jnp.concatenate(pieces, axis=0)


def routed(words, rows, place):
    extra = -(-rows // 16) * 16 - words.shape[0]
    if extra:
        words = jnp.concatenate([words, jnp.zeros((extra, words.shape[1]), F32)], axis=0)
    return summed(times_turned(stacked_terms(words), place))


def weighted_pressure(words, full, remote_rows):
    tail = 5 * full
    normal = words[tail + 5 : tail + 8]
    gap, last = words[4 * full : tail], words[tail + 4 : tail + 5]
    for node in range(4):
        across = sum(
            normal[k : k + 1] * remote_rows[k * 4 + node : k * 4 + node + 1] for k in range(3)
        )
        gap = gap + words[node * full : (node + 1) * full] * across
        last = last + words[tail + node : tail + node + 1] * across
    return jnp.maximum(-gap, 0.0), jnp.maximum(-last, 0.0), normal


def loads_on(shapes, full, tail, pressure, last):
    return [
        jnp.sum(pressure * shapes[i * full : (i + 1) * full], axis=0, keepdims=True)
        + last * shapes[tail + i : tail + i + 1]
        for i in range(4)
    ]


def forces_of(normal, loads):
    loads = jnp.concatenate(loads, axis=0)
    return jnp.concatenate([normal[k : k + 1] * loads for k in range(3)], axis=0)


def place_in_group(domain, domains):
    return {0: domains - 1, domains - 1: 0}.get(domain, domain)


def first_kernel(capacity, heights, *refs):
    (
        nodes_hbm, disp_hbm, mortar_hbm, rank_hbm, face_hbm, count_hbm, weight_hbm, normal_hbm,
        gap_hbm, shape_hbm, modulus_hbm,
        sent_ref, rows_ref, words_ref, turned_ref, mortar_ref, rank_ref, face_ref, nodes,
        inner_ref, outer_ref,
        disp, count, weight, normal_v, gap_v, shape, modulus, blocks, sems, copy_sem,
    ) = refs
    components, layers, rows_y, cols_x = disp.shape
    block_rows = 12 * nodes.shape[1] // LANES + sum(heights)
    sources = (
        nodes_hbm, disp_hbm, rank_hbm, face_hbm, mortar_hbm, shape_hbm, count_hbm, weight_hbm,
        normal_hbm, gap_hbm, modulus_hbm.at[disp.shape[1] - 1],
    )
    targets = (
        nodes, disp, rank_ref, face_ref, mortar_ref, shape, count, weight, normal_v, gap_v, modulus,
    )
    brought = [
        pltpu.make_async_copy(source, target, sems.at[i])
        for i, (source, target) in enumerate(zip(sources, targets))
    ]
    for copy in brought:
        copy.start()

    domains = sent_ref.shape[0] // block_rows
    pair_total = rank_ref.shape[1]
    face_count = nodes.shape[1]
    strips = layers * rows_y
    for copy in brought[:-1]:
        copy.wait()
    rank, face, mortar = rank_ref[...], face_ref[...], mortar_ref[...]
    normal = normal_v[...]
    gap = gap_v[...]

    chosen = lax.broadcasted_iota(jnp.int32, (domains, pair_total), 0) == rank
    before = lax.broadcasted_iota(jnp.int32, (pair_total, pair_total), 0) < lax.broadcasted_iota(
        jnp.int32, (pair_total, pair_total), 1
    )
    earlier = times(chosen.astype(F32).astype(BF16), before.astype(F32).astype(BF16))
    slot = jnp.sum(jnp.where(chosen, earlier, 0.0), axis=0, keepdims=True).astype(jnp.int32)
    place = marks(rank * capacity + slot, domains * capacity)

    parts = stacked_terms(disp[...].reshape(components * strips, cols_x))
    numbers = lax.broadcasted_iota(jnp.int32, (strips, face_count), 0)
    folds = face_count // cols_x
    for corner in range(4):
        index = nodes[corner : corner + 1, :]
        strip = index >> halves(cols_x)
        found = summed(times(parts, marks(index & (cols_x - 1), cols_x)))
        found = found.reshape(components, strips, face_count)
        values = jnp.sum(jnp.where((numbers == strip)[None], found, 0.0), axis=1)
        for fold in range(folds):
            for k in range(components):
                at = fold * 12 + k * 4 + corner
                rows_ref[at : at + 1, :] = values[k : k + 1, fold * cols_x : (fold + 1) * cols_x]

    points = gap.shape[0]
    full = points // 8 * 8
    live = lax.broadcasted_iota(jnp.int32, (points, pair_total), 0) < count[...]
    root = jnp.where(live, jnp.sqrt(weight[...]), 0.0)
    weighted = [root * shape[:, node] for node in range(4)]
    long_words = jnp.concatenate([x[:full] for x in weighted], axis=0)
    group = LANES // capacity
    placed = routed(long_words, group * heights[0], place)

    rows = rows_ref[...]
    high = rows.shape[0]
    rows_high = high * cols_x // LANES
    halved = jnp.concatenate(
        [rows[:, i * LANES : (i + 1) * LANES] for i in range(cols_x // LANES)], axis=0
    )
    for domain in range(domains):
        at = place_in_group(domain, domains) * block_rows
        blocks[at : at + rows_high] = halved
        at += rows_high
        blocks[at : at + heights[0]] = folded(placed, heights[0], capacity, domain)

    mortar_rows = looked_up(rows, mortar, marks(mortar & (cols_x - 1), cols_x))
    for node in range(4):
        across = sum(
            normal[k : k + 1] * mortar_rows[k * 4 + node : k * 4 + node + 1] for k in range(3)
        )
        gap = gap - shape[:, 4 + node] * across
    gap = root * gap
    short_words = jnp.concatenate(
        [gap[:full]]
        + [x[full:] for x in weighted + [gap]]
        + [normal, face.astype(F32)],
        axis=0,
    )
    placed = routed(short_words, group * heights[1], place)
    for domain in range(domains):
        at = place_in_group(domain, domains) * block_rows + rows_high + heights[0]
        blocks[at : at + heights[1]] = folded(placed, heights[1], capacity, domain)
    sending = pltpu.make_async_copy(blocks, sent_ref, copy_sem)
    sending.start()

    words_ref[: 4 * full] = long_words
    words_ref[4 * full :] = short_words
    for node in range(4):
        turned = root * shape[:, 4 + node]
        turned_ref[node * full : (node + 1) * full] = turned[:full]
        turned_ref[4 * full + node : 4 * full + node + 1] = turned[full:]

    brought[-1].wait()
    sub = lax.axis_index("sub")
    for target, layer in ((inner_ref, (1 - sub) * (layers - 1)), (outer_ref, sub * (layers - 1))):
        for k in range(components):
            target[k] = disp[k, layer]
        target[components] = modulus[...]
    sending.wait()


def last_kernel(
    capacity, heights, got_ref, rows_ref, words_ref, turned_ref, mortar_ref, rank_ref, face_ref, nodes_ref,
    inverse_ref, internal_ref, blocks_ref, own_ref, halo_ref, out_hbm, out_ref, sems,
):
    block_rows = 12 * nodes_ref.shape[1] // LANES + sum(heights)
    domains = got_ref.shape[0] // block_rows
    components, layers, rows_y, cols_x = out_ref.shape
    strips = layers * rows_y
    face_count = nodes_ref.shape[1]
    pair_total = rank_ref.shape[1]
    high = rows_ref.shape[0]
    rows_high = high * cols_x // LANES
    full = (turned_ref.shape[0] - 8) // 4
    own_rows = rows_ref[...]

    rank, face = rank_ref[...], face_ref[...]
    end = domains - 1
    place = jnp.where(rank == 0, end, jnp.where(rank == end, 0, rank))
    at = marks(face & (cols_x - 1), cols_x)
    step = min(domains, 8)

    def add_step(turn, total):
        halves_of = [
            jnp.concatenate(
                [
                    got_ref[pl.ds((turn * step + i) * block_rows + j * high, high)]
                    for j in range(cols_x // LANES)
                ],
                axis=1,
            )
            for i in range(step)
        ]
        block = jnp.concatenate(halves_of, axis=0)
        found = summed(times(stacked_terms(block), at)).reshape(step, high, pair_total)
        for i in range(step):
            total = total + jnp.where(place == turn * step + i, found[i], 0.0)
        return total

    both = jnp.zeros((high, pair_total), F32)
    if domains == step:
        both = add_step(0, both)
    else:
        both = lax.fori_loop(0, domains // step, add_step, both)
    remote_rows = jnp.where(face < cols_x, both[:12], both[12:])
    pressure, last, normal = weighted_pressure(words_ref[...], full, remote_rows)
    turned = turned_ref[...]
    mortar_forces = forces_of(-normal, loads_on(turned, full, 4 * full, pressure, last))

    words = jnp.concatenate(
        [
            unfolded(got_ref, block_rows, rows_high, heights[0], capacity)[: 4 * full],
            unfolded(got_ref, block_rows, rows_high + heights[0], heights[1], capacity)[: full + 9],
        ],
        axis=0,
    )
    asked = words[5 * full + 8 : 5 * full + 9].astype(jnp.int32)
    asked_at = marks(asked & (cols_x - 1), cols_x)
    remote_rows = looked_up(own_rows, asked, asked_at)
    pressure, last, normal = weighted_pressure(words, full, remote_rows)
    remote_forces = forces_of(normal, loads_on(words, full, 5 * full, pressure, last))

    forces = jnp.concatenate([mortar_forces, remote_forces], axis=1)
    into = jnp.concatenate([mortar_ref[...], asked], axis=1)
    at = jnp.concatenate([marks(mortar_ref[...] & (cols_x - 1), cols_x), asked_at], axis=1)
    forces = jnp.concatenate(
        [jnp.where(into < cols_x, forces, 0.0), jnp.where(into < cols_x, 0.0, forces)], axis=0
    )
    forces = summed(times_turned(stacked_terms(forces), at))
    forces = jnp.concatenate([forces[:12], forces[12:]], axis=1)
    parts = [term.astype(F32) for term in terms_of(forces, 2)]
    indices = [nodes_ref[corner : corner + 1, :] for corner in range(4)]
    along_x = [marks(index & (cols_x - 1), cols_x) for index in indices]
    strip = [marks(index >> halves(cols_x), strips) for index in indices]
    upward = lax.axis_index("sub") == 1
    edge = edge_part(upward, own_ref, halo_ref, blocks_ref)
    at_edge = jnp.where(upward, layers - 1, 0)
    copies = []
    for layer in range(layers):
        total = jnp.zeros((2 * components * rows_y, cols_x), F32)
        for corner in range(4):
            here = strip[corner][layer * rows_y : (layer + 1) * rows_y]
            spread = []
            for part in parts:
                for k in range(components):
                    at = k * 4 + corner
                    row = jnp.broadcast_to(part[at : at + 1], (16, face_count)).astype(BF16)
                    spread.append(here * jnp.concatenate([row] * (rows_y // 16), axis=0))
            total = total + times_turned(jnp.concatenate(spread, axis=0), along_x[corner])
        contact = summed(total).reshape(components, rows_y, cols_x)
        for k in range(components):
            nodal = internal_ref[k, layer] + jnp.where(at_edge == layer, edge[k], 0.0)
            out_ref[k, layer] = (nodal + contact[k]) * inverse_ref[layer]
        copies.append(
            pltpu.make_async_copy(out_ref.at[:, layer], out_hbm.at[:, layer], sems.at[layer])
        )
        copies[-1].start()
    for copy in copies:
        copy.wait()


GROUP = 8


def shifted(layer):
    views = []
    for part in layer:
        rows_y, cols_x = part.shape
        for moved in (part, pltpu.roll(part, rows_y - 1, 0)):
            views += [moved, pltpu.roll(moved, cols_x - 1, 1)]
    return views


def element_forces(matrices, low, high, modulus):
    rows_y, cols_x = modulus.shape
    inside = (lax.broadcasted_iota(jnp.int32, (rows_y, cols_x), 0) < rows_y - 1) & (
        lax.broadcasted_iota(jnp.int32, (rows_y, cols_x), 1) < cols_x - 1
    )
    scale = jnp.where(inside, modulus, 0.0)
    views = shifted(low) + shifted(high)
    both = jnp.concatenate(matrices, axis=0)
    count = both.shape[0] // 2
    strips = []
    for y in range(0, rows_y, GROUP):
        leading, second = terms_of(jnp.concatenate([view[y : y + GROUP] for view in views], axis=0), 2)
        found = times(both, leading)
        force = found[:count] + (found[count:] + times(matrices[0], second))
        strips.append(force.reshape(-1, GROUP, cols_x) * scale[y : y + GROUP][None])
    return jnp.concatenate(strips, axis=1)


def on_nodes(forces):
    sums = []
    for k in range(forces.shape[0] // 4):
        straight, crossed = [
            forces[k * 4 + c] + pltpu.roll(forces[k * 4 + 2 + c], 1, 0) for c in range(2)
        ]
        sums.append(-(straight + pltpu.roll(crossed, 1, 1)))
    return sums


def edge_part(upward, own_ref, halo_ref, blocks_ref):
    components = own_ref.shape[0] - 1
    size = blocks_ref.shape[1]
    rows = size // 2
    start = jnp.where(upward, 0, rows)
    matrices = [
        blocks_ref[pl.ds(pl.multiple_of(term * size + start, 16), rows)] for term in range(2)
    ]
    low = [jnp.where(upward, own_ref[k], halo_ref[k]) for k in range(components + 1)]
    high = [jnp.where(upward, halo_ref[k], own_ref[k]) for k in range(components)]
    return on_nodes(element_forces(matrices, low[:components], high, low[components]))


def internal_kernel(
    disp_ref, modulus_ref, stiffness_ref, mass_ref, own_ref, halo_ref, out_ref, blocks_ref, inverse_ref
):
    inverse_ref[...] = 1.0 / mass_ref[...]
    components, layers, rows_y, cols_x = disp_ref.shape
    dofs = 8 * components
    half = dofs // 2
    size = dofs * GROUP

    row = lax.broadcasted_iota(jnp.int32, (size, dofs), 0) >> halves(GROUP)
    upper = (row >= half).astype(jnp.int32)
    inner = row - half * upper
    dof = (inner >> 2) * 8 + upper * 4 + (inner & 3)
    pick = (dof == lax.broadcasted_iota(jnp.int32, (size, dofs), 1)).astype(F32).astype(BF16)
    diagonal = (lax.broadcasted_iota(jnp.int32, (size, size), 0) & (GROUP - 1)) == (
        lax.broadcasted_iota(jnp.int32, (size, size), 1) & (GROUP - 1)
    )
    for i, term in enumerate(terms_of(stiffness_ref[...], 2)):
        wide = times_turned(times(pick, term).astype(BF16), pick)
        blocks_ref[i * size : (i + 1) * size] = jnp.where(diagonal, wide, 0.0).astype(BF16)

    blocks = [blocks_ref[i * size : (i + 1) * size] for i in range(2)]
    sums = [[0.0] * components for _ in range(layers)]
    for e in range(layers - 1):
        pair = [[disp_ref[k, e + a] for k in range(components)] for a in range(2)]
        forces = element_forces(blocks, pair[0], pair[1], modulus_ref[e])
        for a in range(2):
            part = on_nodes(forces[a * half : (a + 1) * half])
            sums[e + a] = [x + y for x, y in zip(sums[e + a], part)]
    upward = lax.axis_index("sub") == 0
    edge = edge_part(upward, own_ref, halo_ref, blocks_ref)
    at = jnp.where(upward, layers - 1, 0)
    for layer in range(layers):
        for k in range(components):
            out_ref[k, layer] = sums[layer][k] + jnp.where(at == layer, edge[k], 0.0)


def on_core(kernel, outs, flops, moved, **more):
    return pl.pallas_call(
        kernel,
        out_shape=outs,
        compiler_params=pltpu.CompilerParams(vmem_limit_bytes=48 * 1024 * 1024),
        cost_estimate=pl.CostEstimate(flops=flops, bytes_accessed=moved, transcendentals=0),
        **more,
    )


def swapped(block, axis, first):
    size = lax.axis_size(axis)
    route = []
    for i in range(first, size - 1, 2):
        route += [(i, i + 1), (i + 1, i)]
    return lax.ppermute(block, axis, route)


def shards(
    displacement,
    modulus,
    node_mass,
    stiffness,
    face_nodes,
    pair_mortar,
    pair_rank,
    pair_face,
    pair_count,
    pair_shape,
    pair_weight,
    pair_gap,
    pair_normal,
):
    components, layers, rows_y, cols_x = displacement.shape
    face_count = face_nodes.shape[1]
    pair_total = pair_mortar.shape[0]
    domains = lax.axis_size("dom")
    capacity = max(2, 2 * pair_total // domains)

    points = pair_weight.shape[0]
    full = points // 8 * 8
    group = LANES // capacity
    word_rows = 5 * full + 9
    heights = tuple(-(-rows // group) for rows in (4 * full, full + 9))
    rows_high = 12 * face_count // LANES
    line = (1, pair_total)

    def first(*refs):
        first_kernel(capacity, heights, *refs)

    def last(*refs):
        last_kernel(capacity, heights, *refs)

    def shaped(shape, dtype=F32):
        return jax.ShapeDtypeStruct(shape, dtype)

    arrays = [
        face_nodes,
        displacement,
        pair_mortar.reshape(line),
        pair_rank.reshape(line),
        pair_face.reshape(line),
        pair_count.reshape(line),
        pair_weight,
        pair_normal,
        pair_gap,
        jnp.swapaxes(pair_shape, 0, 1),
        modulus,
    ]
    edge = shaped((components + 1, rows_y, cols_x))
    in_hbm = pl.BlockSpec(memory_space=pltpu.HBM)
    in_vmem = pl.BlockSpec(memory_space=pltpu.VMEM)
    kept = [displacement, *arrays[5:-1], modulus[0]]
    sent, rows, words, turned, mortar, rank, face, nodes, inner, outer = on_core(
        first,
        [
            shaped((domains * (rows_high + sum(heights)), LANES)),
            shaped((12 * face_count // cols_x, cols_x)),
            shaped((word_rows, pair_total)),
            shaped((4 * full + 8, pair_total)),
            shaped(line, jnp.int32),
            shaped(line, jnp.int32),
            shaped(line, jnp.int32),
            shaped(face_nodes.shape, jnp.int32),
            edge,
            edge,
        ],
        900_000_000,
        1_500_000,
        in_specs=[in_hbm] * len(arrays),
        out_specs=[in_hbm] + [in_vmem] * 9,
        scratch_shapes=[pltpu.VMEM(x.shape, x.dtype) for x in kept]
        + [
            pltpu.VMEM((domains * (rows_high + sum(heights)), LANES), F32),
            pltpu.SemaphoreType.DMA((len(arrays),)),
            pltpu.SemaphoreType.DMA(()),
        ],
    )(*[pltpu.with_memory_space_constraint(x, pltpu.HBM) for x in arrays])
    order = [place_in_group(domain, domains) for domain in range(domains)]
    got = lax.all_to_all(
        sent.reshape(domains, 1, -1),
        "dom",
        split_axis=0,
        concat_axis=0,
        axis_index_groups=[order],
        tiled=True,
    ).reshape(sent.shape)
    inner_halo = swapped(inner, ("dom", "sub"), 0)
    outer_halo = swapped(outer, ("dom", "sub"), 1)
    size = 8 * components * GROUP
    internal, blocks, inverse = on_core(
        internal_kernel,
        [shaped(displacement.shape), shaped((2 * size, size), BF16), shaped(node_mass.shape)],
        1_000_000_000,
        700_000,
    )(displacement, modulus, stiffness, node_mass, inner, inner_halo)
    return on_core(
        last,
        shaped(displacement.shape),
        1_000_000_000,
        1_500_000,
        out_specs=in_hbm,
        scratch_shapes=[
            pltpu.VMEM(displacement.shape, F32),
            pltpu.SemaphoreType.DMA((layers,)),
        ],
    )(
        got, rows, words, turned, mortar, rank, face, nodes, inverse, internal, blocks, outer,
        outer_halo,
    )


def solution(mesh):
    placed = (
        P(None, ("runs", "dom", "sub"), None, None),
        P(("runs", "dom", "sub"), None, None),
        P(("runs", "dom", "sub"), None, None),
        P(),
        P(None, ("runs", "dom", "sub")),
        P(("runs", "dom", "sub")),
        P(("runs", "dom", "sub"), None),
        P(("runs", "dom", "sub")),
        P(("runs", "dom", "sub")),
        P(None, None, ("runs", "dom", "sub")),
        P(None, ("runs", "dom", "sub")),
        P(None, ("runs", "dom", "sub")),
        P(None, ("runs", "dom", "sub")),
    )
    return jax.shard_map(
        shards,
        mesh=mesh,
        in_specs=placed,
        out_specs=P(None, ("runs", "dom", "sub"), None, None),
        check_vma=False,
    )
```

```python
import jax
import jax.numpy as jnp
from jax import lax
from jax.experimental import pallas as pl
from jax.experimental.pallas import tpu as pltpu
from jax.sharding import PartitionSpec as P

F32 = jnp.float32
BF16 = jnp.bfloat16
LANES = 128


def terms_of(x, count):
    terms = []
    for _ in range(count):
        terms.append(x.astype(BF16))
        x = x - terms[-1].astype(F32)
    return terms


def stacked_terms(x):
    return jnp.concatenate(terms_of(x, 2), axis=0)


def summed(stacked):
    rows = stacked.shape[0] // 2
    return stacked[:rows] + stacked[rows:]


def marks(index, count):
    shape = (16, index.shape[1])
    rows = lax.broadcasted_iota(jnp.int32, shape, 0).astype(jnp.int16)
    index = jnp.broadcast_to(index, shape).astype(jnp.int16)
    tiles = [
        jnp.where(rows == index - jnp.int16(start), jnp.ones((), BF16), jnp.zeros((), BF16))
        for start in range(0, count, 16)
    ]
    return jnp.concatenate(tiles, axis=0)


def times(left, right):
    return jnp.dot(left, right, preferred_element_type=F32)


def times_turned(left, right):
    return lax.dot_general(left, right, (((1,), (1,)), ((), ())), preferred_element_type=F32)


def halves(power):
    return power.bit_length() - 1


def looked_up(table, face, at):
    both = summed(times(stacked_terms(table), at))
    return jnp.where(face < table.shape[1], both[:12], both[12:])


def folded(placed, height, capacity, domain):
    group = LANES // capacity
    tile, spot = domain // group, domain % group
    part = lax.broadcasted_iota(jnp.int32, (height, LANES), 1) >> halves(capacity)
    block = None
    for j in range(group):
        piece = placed[j * height : (j + 1) * height, tile * LANES : (tile + 1) * LANES]
        if j != spot:
            piece = pltpu.roll(piece, (j - spot) * capacity % LANES, 1)
        block = piece if block is None else jnp.where(part == j, piece, block)
    return block


def unfolded(got_ref, block_rows, start, height, capacity):
    group = LANES // capacity
    part = lax.broadcasted_iota(jnp.int32, (height, LANES), 1) >> halves(capacity)
    pieces = []
    for j in range(group):
        tiles = []
        for first in range(0, got_ref.shape[0] // block_rows, group):
            block = None
            for spot in range(group):
                at = (first + spot) * block_rows + start
                piece = got_ref[at : at + height]
                if j != spot:
                    piece = pltpu.roll(piece, (spot - j) * capacity % LANES, 1)
                block = piece if block is None else jnp.where(part == spot, piece, block)
            tiles.append(block)
        pieces.append(jnp.concatenate(tiles, axis=1))
    return jnp.concatenate(pieces, axis=0)


def routed(words, rows, place):
    extra = -(-rows // 16) * 16 - words.shape[0]
    if extra:
        words = jnp.concatenate([words, jnp.zeros((extra, words.shape[1]), F32)], axis=0)
    return summed(times_turned(stacked_terms(words), place))


def weighted_pressure(words, full, remote_rows):
    tail = 5 * full
    normal = words[tail + 5 : tail + 8]
    gap, last = words[4 * full : tail], words[tail + 4 : tail + 5]
    for node in range(4):
        across = sum(
            normal[k : k + 1] * remote_rows[k * 4 + node : k * 4 + node + 1] for k in range(3)
        )
        gap = gap + words[node * full : (node + 1) * full] * across
        last = last + words[tail + node : tail + node + 1] * across
    return jnp.maximum(-gap, 0.0), jnp.maximum(-last, 0.0), normal


def loads_on(shapes, full, tail, pressure, last):
    return [
        jnp.sum(pressure * shapes[i * full : (i + 1) * full], axis=0, keepdims=True)
        + last * shapes[tail + i : tail + i + 1]
        for i in range(4)
    ]


def forces_of(normal, loads):
    loads = jnp.concatenate(loads, axis=0)
    return jnp.concatenate([normal[k : k + 1] * loads for k in range(3)], axis=0)


def place_in_group(domain, domains):
    return {0: domains - 1, domains - 1: 0}.get(domain, domain)


def first_kernel(capacity, heights, *refs):
    (
        nodes_hbm, disp_hbm, mortar_hbm, rank_hbm, face_hbm, count_hbm, weight_hbm, normal_hbm,
        gap_hbm, shape_hbm, modulus_hbm,
        sent_ref, rows_ref, words_ref, turned_ref, mortar_ref, rank_ref, face_ref, nodes,
        inner_ref, outer_ref,
        disp, count, weight, normal_v, gap_v, shape, modulus, blocks, sems, copy_sems,
    ) = refs
    components, layers, rows_y, cols_x = disp.shape
    block_rows = 12 * nodes.shape[1] // LANES + sum(heights)
    sources = (
        nodes_hbm, disp_hbm, rank_hbm, face_hbm, mortar_hbm, shape_hbm, count_hbm, weight_hbm,
        normal_hbm, gap_hbm, modulus_hbm.at[disp.shape[1] - 1],
    )
    targets = (
        nodes, disp, rank_ref, face_ref, mortar_ref, shape, count, weight, normal_v, gap_v, modulus,
    )
    brought = [
        pltpu.make_async_copy(source, target, sems.at[i])
        for i, (source, target) in enumerate(zip(sources, targets))
    ]
    for copy in brought:
        copy.start()

    domains = sent_ref.shape[0] // block_rows
    pair_total = rank_ref.shape[1]
    face_count = nodes.shape[1]
    strips = layers * rows_y
    for copy in brought[:-1]:
        copy.wait()
    rank, face, mortar = rank_ref[...], face_ref[...], mortar_ref[...]
    normal = normal_v[...]
    gap = gap_v[...]

    chosen = lax.broadcasted_iota(jnp.int32, (domains, pair_total), 0) == rank
    before = lax.broadcasted_iota(jnp.int32, (pair_total, pair_total), 0) < lax.broadcasted_iota(
        jnp.int32, (pair_total, pair_total), 1
    )
    earlier = times(chosen.astype(F32).astype(BF16), before.astype(F32).astype(BF16))
    slot = jnp.sum(jnp.where(chosen, earlier, 0.0), axis=0, keepdims=True).astype(jnp.int32)
    place = marks(rank * capacity + slot, domains * capacity)

    parts = stacked_terms(disp[...].reshape(components * strips, cols_x))
    numbers = lax.broadcasted_iota(jnp.int32, (strips, face_count), 0)
    folds = face_count // cols_x
    for corner in range(4):
        index = nodes[corner : corner + 1, :]
        strip = index >> halves(cols_x)
        found = summed(times(parts, marks(index & (cols_x - 1), cols_x)))
        found = found.reshape(components, strips, face_count)
        values = jnp.sum(jnp.where((numbers == strip)[None], found, 0.0), axis=1)
        for fold in range(folds):
            for k in range(components):
                at = fold * 12 + k * 4 + corner
                rows_ref[at : at + 1, :] = values[k : k + 1, fold * cols_x : (fold + 1) * cols_x]

    points = gap.shape[0]
    full = points // 8 * 8
    live = lax.broadcasted_iota(jnp.int32, (points, pair_total), 0) < count[...]
    root = jnp.where(live, jnp.sqrt(weight[...]), 0.0)
    weighted = [root * shape[:, node] for node in range(4)]
    long_words = jnp.concatenate([x[:full] for x in weighted], axis=0)
    group = LANES // capacity
    placed = routed(long_words, group * heights[0], place)

    rows = rows_ref[...]
    high = rows.shape[0]
    rows_high = high * cols_x // LANES
    halved = jnp.concatenate(
        [rows[:, i * LANES : (i + 1) * LANES] for i in range(cols_x // LANES)], axis=0
    )
    for domain in range(domains):
        at = place_in_group(domain, domains) * block_rows
        blocks[at : at + rows_high] = halved
        at += rows_high
        blocks[at : at + heights[0]] = folded(placed, heights[0], capacity, domain)

    mortar_rows = looked_up(rows, mortar, marks(mortar & (cols_x - 1), cols_x))
    for node in range(4):
        across = sum(
            normal[k : k + 1] * mortar_rows[k * 4 + node : k * 4 + node + 1] for k in range(3)
        )
        gap = gap - shape[:, 4 + node] * across
    gap = root * gap
    short_words = jnp.concatenate(
        [gap[:full]]
        + [x[full:] for x in weighted + [gap]]
        + [normal, face.astype(F32)],
        axis=0,
    )
    placed = routed(short_words, group * heights[1], place)
    members = sorted(range(domains), key=lambda domain: place_in_group(domain, domains))
    chunk = sent_ref.shape[0] // copy_sems.shape[0]
    copies = []
    for spot, domain in enumerate(members):
        at = spot * block_rows + rows_high + heights[0]
        blocks[at : at + heights[1]] = folded(placed, heights[1], capacity, domain)
        if (spot + 1) * block_rows % chunk == 0:
            part = pl.ds((spot + 1) * block_rows - chunk, chunk)
            copies.append(
                pltpu.make_async_copy(
                    blocks.at[part], sent_ref.at[part], copy_sems.at[len(copies)]
                )
            )
            copies[-1].start()

    words_ref[: 4 * full] = long_words
    words_ref[4 * full :] = short_words
    for node in range(4):
        turned = root * shape[:, 4 + node]
        turned_ref[node * full : (node + 1) * full] = turned[:full]
        turned_ref[4 * full + node : 4 * full + node + 1] = turned[full:]

    brought[-1].wait()
    sub = lax.axis_index("sub")
    for target, layer in ((inner_ref, (1 - sub) * (layers - 1)), (outer_ref, sub * (layers - 1))):
        for k in range(components):
            target[k] = disp[k, layer]
        target[components] = modulus[...]
    for copy in copies:
        copy.wait()


def last_kernel(
    capacity, heights, got_ref, rows_ref, words_ref, turned_ref, mortar_ref, rank_ref, face_ref, nodes_ref,
    inverse_ref, internal_ref, blocks_ref, own_ref, halo_ref, out_hbm, out_ref, sems,
):
    block_rows = 12 * nodes_ref.shape[1] // LANES + sum(heights)
    domains = got_ref.shape[0] // block_rows
    components, layers, rows_y, cols_x = out_ref.shape
    strips = layers * rows_y
    face_count = nodes_ref.shape[1]
    pair_total = rank_ref.shape[1]
    high = rows_ref.shape[0]
    rows_high = high * cols_x // LANES
    full = (turned_ref.shape[0] - 8) // 4
    own_rows = rows_ref[...]

    rank, face = rank_ref[...], face_ref[...]
    end = domains - 1
    place = jnp.where(rank == 0, end, jnp.where(rank == end, 0, rank))
    at = marks(face & (cols_x - 1), cols_x)
    step = min(domains, 8)

    def add_step(turn, total):
        halves_of = [
            jnp.concatenate(
                [
                    got_ref[pl.ds((turn * step + i) * block_rows + j * high, high)]
                    for j in range(cols_x // LANES)
                ],
                axis=1,
            )
            for i in range(step)
        ]
        block = jnp.concatenate(halves_of, axis=0)
        found = summed(times(stacked_terms(block), at)).reshape(step, high, pair_total)
        for i in range(step):
            total = total + jnp.where(place == turn * step + i, found[i], 0.0)
        return total

    both = jnp.zeros((high, pair_total), F32)
    if domains == step:
        both = add_step(0, both)
    else:
        both = lax.fori_loop(0, domains // step, add_step, both)
    remote_rows = jnp.where(face < cols_x, both[:12], both[12:])
    pressure, last, normal = weighted_pressure(words_ref[...], full, remote_rows)
    turned = turned_ref[...]
    mortar_forces = forces_of(-normal, loads_on(turned, full, 4 * full, pressure, last))

    words = jnp.concatenate(
        [
            unfolded(got_ref, block_rows, rows_high, heights[0], capacity)[: 4 * full],
            unfolded(got_ref, block_rows, rows_high + heights[0], heights[1], capacity)[: full + 9],
        ],
        axis=0,
    )
    asked = words[5 * full + 8 : 5 * full + 9].astype(jnp.int32)
    asked_at = marks(asked & (cols_x - 1), cols_x)
    remote_rows = looked_up(own_rows, asked, asked_at)
    pressure, last, normal = weighted_pressure(words, full, remote_rows)
    remote_forces = forces_of(normal, loads_on(words, full, 5 * full, pressure, last))

    forces = jnp.concatenate([mortar_forces, remote_forces], axis=1)
    into = jnp.concatenate([mortar_ref[...], asked], axis=1)
    at = jnp.concatenate([marks(mortar_ref[...] & (cols_x - 1), cols_x), asked_at], axis=1)
    forces = jnp.concatenate(
        [jnp.where(into < cols_x, forces, 0.0), jnp.where(into < cols_x, 0.0, forces)], axis=0
    )
    forces = summed(times_turned(stacked_terms(forces), at))
    forces = jnp.concatenate([forces[:12], forces[12:]], axis=1)
    parts = [term.astype(F32) for term in terms_of(forces, 2)]
    indices = [nodes_ref[corner : corner + 1, :] for corner in range(4)]
    along_x = [marks(index & (cols_x - 1), cols_x) for index in indices]
    strip = [marks(index >> halves(cols_x), strips) for index in indices]
    upward = lax.axis_index("sub") == 1
    edge = edge_part(upward, own_ref, halo_ref, blocks_ref)
    at_edge = jnp.where(upward, layers - 1, 0)
    copies = []
    for layer in range(layers):
        total = jnp.zeros((2 * components * rows_y, cols_x), F32)
        for corner in range(4):
            here = strip[corner][layer * rows_y : (layer + 1) * rows_y]
            spread = []
            for part in parts:
                for k in range(components):
                    at = k * 4 + corner
                    row = jnp.broadcast_to(part[at : at + 1], (16, face_count)).astype(BF16)
                    spread.append(here * jnp.concatenate([row] * (rows_y // 16), axis=0))
            total = total + times_turned(jnp.concatenate(spread, axis=0), along_x[corner])
        contact = summed(total).reshape(components, rows_y, cols_x)
        for k in range(components):
            nodal = internal_ref[k, layer] + jnp.where(at_edge == layer, edge[k], 0.0)
            out_ref[k, layer] = (nodal + contact[k]) * inverse_ref[layer]
        copies.append(
            pltpu.make_async_copy(out_ref.at[:, layer], out_hbm.at[:, layer], sems.at[layer])
        )
        copies[-1].start()
    for copy in copies:
        copy.wait()


GROUP = 8


def shifted(layer):
    views = []
    for part in layer:
        rows_y, cols_x = part.shape
        for moved in (part, pltpu.roll(part, rows_y - 1, 0)):
            views += [moved, pltpu.roll(moved, cols_x - 1, 1)]
    return views


def element_forces(matrices, low, high, modulus):
    rows_y, cols_x = modulus.shape
    inside = (lax.broadcasted_iota(jnp.int32, (rows_y, cols_x), 0) < rows_y - 1) & (
        lax.broadcasted_iota(jnp.int32, (rows_y, cols_x), 1) < cols_x - 1
    )
    scale = jnp.where(inside, modulus, 0.0)
    views = shifted(low) + shifted(high)
    both = jnp.concatenate(matrices, axis=0)
    count = both.shape[0] // 2
    strips = []
    for y in range(0, rows_y, GROUP):
        leading, second = terms_of(jnp.concatenate([view[y : y + GROUP] for view in views], axis=0), 2)
        found = times(both, leading)
        force = found[:count] + (found[count:] + times(matrices[0], second))
        strips.append(force.reshape(-1, GROUP, cols_x) * scale[y : y + GROUP][None])
    return jnp.concatenate(strips, axis=1)


def on_nodes(forces):
    sums = []
    for k in range(forces.shape[0] // 4):
        straight, crossed = [
            forces[k * 4 + c] + pltpu.roll(forces[k * 4 + 2 + c], 1, 0) for c in range(2)
        ]
        sums.append(-(straight + pltpu.roll(crossed, 1, 1)))
    return sums


def edge_part(upward, own_ref, halo_ref, blocks_ref):
    components = own_ref.shape[0] - 1
    size = blocks_ref.shape[1]
    rows = size // 2
    start = jnp.where(upward, 0, rows)
    matrices = [
        blocks_ref[pl.ds(pl.multiple_of(term * size + start, 16), rows)] for term in range(2)
    ]
    low = [jnp.where(upward, own_ref[k], halo_ref[k]) for k in range(components + 1)]
    high = [jnp.where(upward, halo_ref[k], own_ref[k]) for k in range(components)]
    return on_nodes(element_forces(matrices, low[:components], high, low[components]))


def internal_kernel(
    disp_ref, modulus_ref, stiffness_ref, mass_ref, own_ref, halo_ref, out_ref, blocks_ref, inverse_ref
):
    inverse_ref[...] = 1.0 / mass_ref[...]
    components, layers, rows_y, cols_x = disp_ref.shape
    dofs = 8 * components
    half = dofs // 2
    size = dofs * GROUP

    row = lax.broadcasted_iota(jnp.int32, (size, dofs), 0) >> halves(GROUP)
    upper = (row >= half).astype(jnp.int32)
    inner = row - half * upper
    dof = (inner >> 2) * 8 + upper * 4 + (inner & 3)
    pick = (dof == lax.broadcasted_iota(jnp.int32, (size, dofs), 1)).astype(F32).astype(BF16)
    diagonal = (lax.broadcasted_iota(jnp.int32, (size, size), 0) & (GROUP - 1)) == (
        lax.broadcasted_iota(jnp.int32, (size, size), 1) & (GROUP - 1)
    )
    for i, term in enumerate(terms_of(stiffness_ref[...], 2)):
        wide = times_turned(times(pick, term).astype(BF16), pick)
        blocks_ref[i * size : (i + 1) * size] = jnp.where(diagonal, wide, 0.0).astype(BF16)

    blocks = [blocks_ref[i * size : (i + 1) * size] for i in range(2)]
    sums = [[0.0] * components for _ in range(layers)]
    for e in range(layers - 1):
        pair = [[disp_ref[k, e + a] for k in range(components)] for a in range(2)]
        forces = element_forces(blocks, pair[0], pair[1], modulus_ref[e])
        for a in range(2):
            part = on_nodes(forces[a * half : (a + 1) * half])
            sums[e + a] = [x + y for x, y in zip(sums[e + a], part)]
    upward = lax.axis_index("sub") == 0
    edge = edge_part(upward, own_ref, halo_ref, blocks_ref)
    at = jnp.where(upward, layers - 1, 0)
    for layer in range(layers):
        for k in range(components):
            out_ref[k, layer] = sums[layer][k] + jnp.where(at == layer, edge[k], 0.0)


def on_core(kernel, outs, flops, moved, **more):
    return pl.pallas_call(
        kernel,
        out_shape=outs,
        compiler_params=pltpu.CompilerParams(vmem_limit_bytes=48 * 1024 * 1024),
        cost_estimate=pl.CostEstimate(flops=flops, bytes_accessed=moved, transcendentals=0),
        **more,
    )


def swapped(block, axis, first):
    size = lax.axis_size(axis)
    route = []
    for i in range(first, size - 1, 2):
        route += [(i, i + 1), (i + 1, i)]
    return lax.ppermute(block, axis, route)


def shards(
    displacement,
    modulus,
    node_mass,
    stiffness,
    face_nodes,
    pair_mortar,
    pair_rank,
    pair_face,
    pair_count,
    pair_shape,
    pair_weight,
    pair_gap,
    pair_normal,
):
    components, layers, rows_y, cols_x = displacement.shape
    face_count = face_nodes.shape[1]
    pair_total = pair_mortar.shape[0]
    domains = lax.axis_size("dom")
    capacity = max(2, 2 * pair_total // domains)

    points = pair_weight.shape[0]
    full = points // 8 * 8
    group = LANES // capacity
    word_rows = 5 * full + 9
    heights = tuple(-(-rows // group) for rows in (4 * full, full + 9))
    rows_high = 12 * face_count // LANES
    line = (1, pair_total)

    def first(*refs):
        first_kernel(capacity, heights, *refs)

    def last(*refs):
        last_kernel(capacity, heights, *refs)

    def shaped(shape, dtype=F32):
        return jax.ShapeDtypeStruct(shape, dtype)

    arrays = [
        face_nodes,
        displacement,
        pair_mortar.reshape(line),
        pair_rank.reshape(line),
        pair_face.reshape(line),
        pair_count.reshape(line),
        pair_weight,
        pair_normal,
        pair_gap,
        jnp.swapaxes(pair_shape, 0, 1),
        modulus,
    ]
    edge = shaped((components + 1, rows_y, cols_x))
    in_hbm = pl.BlockSpec(memory_space=pltpu.HBM)
    in_vmem = pl.BlockSpec(memory_space=pltpu.VMEM)
    kept = [displacement, *arrays[5:-1], modulus[0]]
    sent, rows, words, turned, mortar, rank, face, nodes, inner, outer = on_core(
        first,
        [
            shaped((domains * (rows_high + sum(heights)), LANES)),
            shaped((12 * face_count // cols_x, cols_x)),
            shaped((word_rows, pair_total)),
            shaped((4 * full + 8, pair_total)),
            shaped(line, jnp.int32),
            shaped(line, jnp.int32),
            shaped(line, jnp.int32),
            shaped(face_nodes.shape, jnp.int32),
            edge,
            edge,
        ],
        900_000_000,
        1_500_000,
        in_specs=[in_hbm] * len(arrays),
        out_specs=[in_hbm] + [in_vmem] * 9,
        scratch_shapes=[pltpu.VMEM(x.shape, x.dtype) for x in kept]
        + [
            pltpu.VMEM((domains * (rows_high + sum(heights)), LANES), F32),
            pltpu.SemaphoreType.DMA((len(arrays),)),
            pltpu.SemaphoreType.DMA((4,)),
        ],
    )(*[pltpu.with_memory_space_constraint(x, pltpu.HBM) for x in arrays])
    order = [place_in_group(domain, domains) for domain in range(domains)]
    got = lax.all_to_all(
        sent.reshape(domains, 1, -1),
        "dom",
        split_axis=0,
        concat_axis=0,
        axis_index_groups=[order],
        tiled=True,
    ).reshape(sent.shape)
    inner_halo = swapped(inner, ("dom", "sub"), 0)
    outer_halo = swapped(outer, ("dom", "sub"), 1)
    size = 8 * components * GROUP
    internal, blocks, inverse = on_core(
        internal_kernel,
        [shaped(displacement.shape), shaped((2 * size, size), BF16), shaped(node_mass.shape)],
        1_000_000_000,
        700_000,
    )(displacement, modulus, stiffness, node_mass, inner, inner_halo)
    return on_core(
        last,
        shaped(displacement.shape),
        1_000_000_000,
        1_500_000,
        out_specs=in_hbm,
        scratch_shapes=[
            pltpu.VMEM(displacement.shape, F32),
            pltpu.SemaphoreType.DMA((layers,)),
        ],
    )(
        got, rows, words, turned, mortar, rank, face, nodes, inverse, internal, blocks, outer,
        outer_halo,
    )


def solution(mesh):
    placed = (
        P(None, ("runs", "dom", "sub"), None, None),
        P(("runs", "dom", "sub"), None, None),
        P(("runs", "dom", "sub"), None, None),
        P(),
        P(None, ("runs", "dom", "sub")),
        P(("runs", "dom", "sub")),
        P(("runs", "dom", "sub"), None),
        P(("runs", "dom", "sub")),
        P(("runs", "dom", "sub")),
        P(None, None, ("runs", "dom", "sub")),
        P(None, ("runs", "dom", "sub")),
        P(None, ("runs", "dom", "sub")),
        P(None, ("runs", "dom", "sub")),
    )
    return jax.shard_map(
        shards,
        mesh=mesh,
        in_specs=placed,
        out_specs=P(None, ("runs", "dom", "sub"), None, None),
        check_vma=False,
    )
```

```python
import jax
import jax.numpy as jnp
from jax import lax
from jax.experimental import pallas as pl
from jax.experimental.pallas import tpu as pltpu
from jax.sharding import PartitionSpec as P

F32 = jnp.float32
BF16 = jnp.bfloat16
LANES = 128


def terms_of(x, count):
    terms = []
    for _ in range(count):
        terms.append(x.astype(BF16))
        x = x - terms[-1].astype(F32)
    return terms


def stacked_terms(x):
    return jnp.concatenate(terms_of(x, 2), axis=0)


def summed(stacked):
    rows = stacked.shape[0] // 2
    return stacked[:rows] + stacked[rows:]


def marks(index, count):
    shape = (16, index.shape[1])
    rows = lax.broadcasted_iota(jnp.int32, shape, 0).astype(jnp.int16)
    index = jnp.broadcast_to(index, shape).astype(jnp.int16)
    tiles = [
        jnp.where(rows == index - jnp.int16(start), jnp.ones((), BF16), jnp.zeros((), BF16))
        for start in range(0, count, 16)
    ]
    return jnp.concatenate(tiles, axis=0)


def times(left, right):
    return jnp.dot(left, right, preferred_element_type=F32)


def times_turned(left, right):
    return lax.dot_general(left, right, (((1,), (1,)), ((), ())), preferred_element_type=F32)


def halves(power):
    return power.bit_length() - 1


def looked_up(table, face, at):
    both = summed(times(stacked_terms(table), at))
    return jnp.where(face < table.shape[1], both[:12], both[12:])


def folded(placed, height, capacity, domain):
    group = LANES // capacity
    tile, spot = domain // group, domain % group
    part = lax.broadcasted_iota(jnp.int32, (height, LANES), 1) >> halves(capacity)
    block = None
    for j in range(group):
        piece = placed[j * height : (j + 1) * height, tile * LANES : (tile + 1) * LANES]
        if j != spot:
            piece = pltpu.roll(piece, (j - spot) * capacity % LANES, 1)
        block = piece if block is None else jnp.where(part == j, piece, block)
    return block


def unfolded(got_ref, block_rows, start, height, capacity):
    group = LANES // capacity
    part = lax.broadcasted_iota(jnp.int32, (height, LANES), 1) >> halves(capacity)
    pieces = []
    for j in range(group):
        tiles = []
        for first in range(0, got_ref.shape[0] // block_rows, group):
            block = None
            for spot in range(group):
                at = (first + spot) * block_rows + start
                piece = got_ref[at : at + height]
                if j != spot:
                    piece = pltpu.roll(piece, (spot - j) * capacity % LANES, 1)
                block = piece if block is None else jnp.where(part == spot, piece, block)
            tiles.append(block)
        pieces.append(jnp.concatenate(tiles, axis=1))
    return jnp.concatenate(pieces, axis=0)


def routed(words, rows, place):
    extra = -(-rows // 16) * 16 - words.shape[0]
    if extra:
        words = jnp.concatenate([words, jnp.zeros((extra, words.shape[1]), F32)], axis=0)
    return summed(times_turned(stacked_terms(words), place))


def weighted_pressure(words, full, remote_rows):
    tail = 5 * full
    normal = words[tail + 5 : tail + 8]
    gap, last = words[4 * full : tail], words[tail + 4 : tail + 5]
    for node in range(4):
        across = sum(
            normal[k : k + 1] * remote_rows[k * 4 + node : k * 4 + node + 1] for k in range(3)
        )
        gap = gap + words[node * full : (node + 1) * full] * across
        last = last + words[tail + node : tail + node + 1] * across
    return jnp.maximum(-gap, 0.0), jnp.maximum(-last, 0.0), normal


def loads_on(shapes, full, tail, pressure, last):
    return [
        jnp.sum(pressure * shapes[i * full : (i + 1) * full], axis=0, keepdims=True)
        + last * shapes[tail + i : tail + i + 1]
        for i in range(4)
    ]


def forces_of(normal, loads):
    loads = jnp.concatenate(loads, axis=0)
    return jnp.concatenate([normal[k : k + 1] * loads for k in range(3)], axis=0)


def place_in_group(domain, domains):
    return {0: domains - 1, domains - 1: 0}.get(domain, domain)


def first_kernel(capacity, heights, *refs):
    (
        nodes_hbm, disp_hbm, mortar_hbm, rank_hbm, face_hbm, count_hbm, weight_hbm, normal_hbm,
        gap_hbm, shape_hbm, modulus_hbm,
        sent_ref, rows_ref, words_ref, turned_ref, mortar_ref, rank_ref, face_ref, nodes,
        inner_ref, outer_ref,
        disp, count, weight, normal_v, gap_v, shape, modulus, blocks, sems, copy_sem,
    ) = refs
    components, layers, rows_y, cols_x = disp.shape
    block_rows = 12 * nodes.shape[1] // LANES + sum(heights)
    pieces = [pl.ds(start, LANES) for start in range(0, shape_hbm.shape[1], LANES)]
    sources = (
        nodes_hbm, disp_hbm, rank_hbm, face_hbm, mortar_hbm,
        *[shape_hbm.at[:, piece] for piece in pieces],
        count_hbm, weight_hbm, normal_hbm, gap_hbm, modulus_hbm.at[disp.shape[1] - 1],
    )
    targets = (
        nodes, disp, rank_ref, face_ref, mortar_ref, *[shape.at[i, : shape_hbm.shape[0]] for i in range(len(pieces))],
        count, weight, normal_v, gap_v, modulus,
    )
    brought = [
        pltpu.make_async_copy(source, target, sems.at[i])
        for i, (source, target) in enumerate(zip(sources, targets))
    ]
    for copy in brought:
        copy.start()

    domains = sent_ref.shape[0] // block_rows
    pair_total = rank_ref.shape[1]
    face_count = nodes.shape[1]
    strips = layers * rows_y
    for copy in brought[:-1]:
        copy.wait()
    rank, face, mortar = rank_ref[...], face_ref[...], mortar_ref[...]
    normal = normal_v[...]
    gap = gap_v[...]

    chosen = lax.broadcasted_iota(jnp.int32, (domains, pair_total), 0) == rank
    before = lax.broadcasted_iota(jnp.int32, (pair_total, pair_total), 0) < lax.broadcasted_iota(
        jnp.int32, (pair_total, pair_total), 1
    )
    earlier = times(chosen.astype(F32).astype(BF16), before.astype(F32).astype(BF16))
    slot = jnp.sum(jnp.where(chosen, earlier, 0.0), axis=0, keepdims=True).astype(jnp.int32)
    place = marks(rank * capacity + slot, domains * capacity)

    parts = stacked_terms(disp[...].reshape(components * strips, cols_x))
    numbers = lax.broadcasted_iota(jnp.int32, (strips, face_count), 0)
    folds = face_count // cols_x
    for corner in range(4):
        index = nodes[corner : corner + 1, :]
        strip = index >> halves(cols_x)
        found = summed(times(parts, marks(index & (cols_x - 1), cols_x)))
        found = found.reshape(components, strips, face_count)
        values = jnp.sum(jnp.where((numbers == strip)[None], found, 0.0), axis=1)
        for fold in range(folds):
            for k in range(components):
                at = fold * 12 + k * 4 + corner
                rows_ref[at : at + 1, :] = values[k : k + 1, fold * cols_x : (fold + 1) * cols_x]

    points = gap.shape[0]

    def shape_of(node):
        return jnp.concatenate(
            [shape[i, pl.ds(node, points, 8)] for i in range(pair_total // LANES)], axis=1
        )

    full = points // 8 * 8
    live = lax.broadcasted_iota(jnp.int32, (points, pair_total), 0) < count[...]
    root = jnp.where(live, jnp.sqrt(weight[...]), 0.0)
    weighted = [root * shape_of(node) for node in range(4)]
    long_words = jnp.concatenate([x[:full] for x in weighted], axis=0)
    group = LANES // capacity
    placed = routed(long_words, group * heights[0], place)

    rows = rows_ref[...]
    high = rows.shape[0]
    rows_high = high * cols_x // LANES
    halved = jnp.concatenate(
        [rows[:, i * LANES : (i + 1) * LANES] for i in range(cols_x // LANES)], axis=0
    )
    for domain in range(domains):
        at = place_in_group(domain, domains) * block_rows
        blocks[at : at + rows_high] = halved
        at += rows_high
        blocks[at : at + heights[0]] = folded(placed, heights[0], capacity, domain)

    mortar_rows = looked_up(rows, mortar, marks(mortar & (cols_x - 1), cols_x))
    for node in range(4):
        across = sum(
            normal[k : k + 1] * mortar_rows[k * 4 + node : k * 4 + node + 1] for k in range(3)
        )
        gap = gap - shape_of(4 + node) * across
    gap = root * gap
    short_words = jnp.concatenate(
        [gap[:full]]
        + [x[full:] for x in weighted + [gap]]
        + [normal, face.astype(F32)],
        axis=0,
    )
    placed = routed(short_words, group * heights[1], place)
    for domain in range(domains):
        at = place_in_group(domain, domains) * block_rows + rows_high + heights[0]
        blocks[at : at + heights[1]] = folded(placed, heights[1], capacity, domain)
    sending = pltpu.make_async_copy(blocks, sent_ref, copy_sem)
    sending.start()

    words_ref[: 4 * full] = long_words
    words_ref[4 * full :] = short_words
    for node in range(4):
        turned = root * shape_of(4 + node)
        turned_ref[node * full : (node + 1) * full] = turned[:full]
        turned_ref[4 * full + node : 4 * full + node + 1] = turned[full:]

    brought[-1].wait()
    sub = lax.axis_index("sub")
    for target, layer in ((inner_ref, (1 - sub) * (layers - 1)), (outer_ref, sub * (layers - 1))):
        for k in range(components):
            target[k] = disp[k, layer]
        target[components] = modulus[...]
    sending.wait()


def last_kernel(
    capacity, heights, got_ref, rows_ref, words_ref, turned_ref, mortar_ref, rank_ref, face_ref, nodes_ref,
    inverse_ref, internal_ref, blocks_ref, own_ref, halo_ref, out_hbm, out_ref, sems,
):
    block_rows = 12 * nodes_ref.shape[1] // LANES + sum(heights)
    domains = got_ref.shape[0] // block_rows
    components, layers, rows_y, cols_x = out_ref.shape
    strips = layers * rows_y
    face_count = nodes_ref.shape[1]
    pair_total = rank_ref.shape[1]
    high = rows_ref.shape[0]
    rows_high = high * cols_x // LANES
    full = (turned_ref.shape[0] - 8) // 4
    own_rows = rows_ref[...]

    rank, face = rank_ref[...], face_ref[...]
    end = domains - 1
    place = jnp.where(rank == 0, end, jnp.where(rank == end, 0, rank))
    at = marks(face & (cols_x - 1), cols_x)
    step = min(domains, 8)

    def add_step(turn, total):
        halves_of = [
            jnp.concatenate(
                [
                    got_ref[pl.ds((turn * step + i) * block_rows + j * high, high)]
                    for j in range(cols_x // LANES)
                ],
                axis=1,
            )
            for i in range(step)
        ]
        block = jnp.concatenate(halves_of, axis=0)
        found = summed(times(stacked_terms(block), at)).reshape(step, high, pair_total)
        for i in range(step):
            total = total + jnp.where(place == turn * step + i, found[i], 0.0)
        return total

    both = jnp.zeros((high, pair_total), F32)
    if domains == step:
        both = add_step(0, both)
    else:
        both = lax.fori_loop(0, domains // step, add_step, both)
    remote_rows = jnp.where(face < cols_x, both[:12], both[12:])
    pressure, last, normal = weighted_pressure(words_ref[...], full, remote_rows)
    turned = turned_ref[...]
    mortar_forces = forces_of(-normal, loads_on(turned, full, 4 * full, pressure, last))

    words = jnp.concatenate(
        [
            unfolded(got_ref, block_rows, rows_high, heights[0], capacity)[: 4 * full],
            unfolded(got_ref, block_rows, rows_high + heights[0], heights[1], capacity)[: full + 9],
        ],
        axis=0,
    )
    asked = words[5 * full + 8 : 5 * full + 9].astype(jnp.int32)
    asked_at = marks(asked & (cols_x - 1), cols_x)
    remote_rows = looked_up(own_rows, asked, asked_at)
    pressure, last, normal = weighted_pressure(words, full, remote_rows)
    remote_forces = forces_of(normal, loads_on(words, full, 5 * full, pressure, last))

    forces = jnp.concatenate([mortar_forces, remote_forces], axis=1)
    into = jnp.concatenate([mortar_ref[...], asked], axis=1)
    at = jnp.concatenate([marks(mortar_ref[...] & (cols_x - 1), cols_x), asked_at], axis=1)
    forces = jnp.concatenate(
        [jnp.where(into < cols_x, forces, 0.0), jnp.where(into < cols_x, 0.0, forces)], axis=0
    )
    forces = summed(times_turned(stacked_terms(forces), at))
    forces = jnp.concatenate([forces[:12], forces[12:]], axis=1)
    parts = [term.astype(F32) for term in terms_of(forces, 2)]
    indices = [nodes_ref[corner : corner + 1, :] for corner in range(4)]
    along_x = [marks(index & (cols_x - 1), cols_x) for index in indices]
    strip = [marks(index >> halves(cols_x), strips) for index in indices]
    upward = lax.axis_index("sub") == 1
    edge = edge_part(upward, own_ref, halo_ref, blocks_ref)
    at_edge = jnp.where(upward, layers - 1, 0)
    copies = []
    for layer in range(layers):
        total = jnp.zeros((2 * components * rows_y, cols_x), F32)
        for corner in range(4):
            here = strip[corner][layer * rows_y : (layer + 1) * rows_y]
            spread = []
            for part in parts:
                for k in range(components):
                    at = k * 4 + corner
                    row = jnp.broadcast_to(part[at : at + 1], (16, face_count)).astype(BF16)
                    spread.append(here * jnp.concatenate([row] * (rows_y // 16), axis=0))
            total = total + times_turned(jnp.concatenate(spread, axis=0), along_x[corner])
        contact = summed(total).reshape(components, rows_y, cols_x)
        for k in range(components):
            nodal = internal_ref[k, layer] + jnp.where(at_edge == layer, edge[k], 0.0)
            out_ref[k, layer] = (nodal + contact[k]) * inverse_ref[layer]
        copies.append(
            pltpu.make_async_copy(out_ref.at[:, layer], out_hbm.at[:, layer], sems.at[layer])
        )
        copies[-1].start()
    for copy in copies:
        copy.wait()


GROUP = 8


def shifted(layer):
    views = []
    for part in layer:
        rows_y, cols_x = part.shape
        for moved in (part, pltpu.roll(part, rows_y - 1, 0)):
            views += [moved, pltpu.roll(moved, cols_x - 1, 1)]
    return views


def element_forces(matrices, low, high, modulus):
    rows_y, cols_x = modulus.shape
    inside = (lax.broadcasted_iota(jnp.int32, (rows_y, cols_x), 0) < rows_y - 1) & (
        lax.broadcasted_iota(jnp.int32, (rows_y, cols_x), 1) < cols_x - 1
    )
    scale = jnp.where(inside, modulus, 0.0)
    views = shifted(low) + shifted(high)
    both = jnp.concatenate(matrices, axis=0)
    count = both.shape[0] // 2
    strips = []
    for y in range(0, rows_y, GROUP):
        leading, second = terms_of(jnp.concatenate([view[y : y + GROUP] for view in views], axis=0), 2)
        found = times(both, leading)
        force = found[:count] + (found[count:] + times(matrices[0], second))
        strips.append(force.reshape(-1, GROUP, cols_x) * scale[y : y + GROUP][None])
    return jnp.concatenate(strips, axis=1)


def on_nodes(forces):
    sums = []
    for k in range(forces.shape[0] // 4):
        straight, crossed = [
            forces[k * 4 + c] + pltpu.roll(forces[k * 4 + 2 + c], 1, 0) for c in range(2)
        ]
        sums.append(-(straight + pltpu.roll(crossed, 1, 1)))
    return sums


def edge_part(upward, own_ref, halo_ref, blocks_ref):
    components = own_ref.shape[0] - 1
    size = blocks_ref.shape[1]
    rows = size // 2
    start = jnp.where(upward, 0, rows)
    matrices = [
        blocks_ref[pl.ds(pl.multiple_of(term * size + start, 16), rows)] for term in range(2)
    ]
    low = [jnp.where(upward, own_ref[k], halo_ref[k]) for k in range(components + 1)]
    high = [jnp.where(upward, halo_ref[k], own_ref[k]) for k in range(components)]
    return on_nodes(element_forces(matrices, low[:components], high, low[components]))


def internal_kernel(
    disp_ref, modulus_ref, stiffness_ref, mass_ref, own_ref, halo_ref, out_ref, blocks_ref, inverse_ref
):
    inverse_ref[...] = 1.0 / mass_ref[...]
    components, layers, rows_y, cols_x = disp_ref.shape
    dofs = 8 * components
    half = dofs // 2
    size = dofs * GROUP

    row = lax.broadcasted_iota(jnp.int32, (size, dofs), 0) >> halves(GROUP)
    upper = (row >= half).astype(jnp.int32)
    inner = row - half * upper
    dof = (inner >> 2) * 8 + upper * 4 + (inner & 3)
    pick = (dof == lax.broadcasted_iota(jnp.int32, (size, dofs), 1)).astype(F32).astype(BF16)
    diagonal = (lax.broadcasted_iota(jnp.int32, (size, size), 0) & (GROUP - 1)) == (
        lax.broadcasted_iota(jnp.int32, (size, size), 1) & (GROUP - 1)
    )
    for i, term in enumerate(terms_of(stiffness_ref[...], 2)):
        wide = times_turned(times(pick, term).astype(BF16), pick)
        blocks_ref[i * size : (i + 1) * size] = jnp.where(diagonal, wide, 0.0).astype(BF16)

    blocks = [blocks_ref[i * size : (i + 1) * size] for i in range(2)]
    sums = [[0.0] * components for _ in range(layers)]
    for e in range(layers - 1):
        pair = [[disp_ref[k, e + a] for k in range(components)] for a in range(2)]
        forces = element_forces(blocks, pair[0], pair[1], modulus_ref[e])
        for a in range(2):
            part = on_nodes(forces[a * half : (a + 1) * half])
            sums[e + a] = [x + y for x, y in zip(sums[e + a], part)]
    upward = lax.axis_index("sub") == 0
    edge = edge_part(upward, own_ref, halo_ref, blocks_ref)
    at = jnp.where(upward, layers - 1, 0)
    for layer in range(layers):
        for k in range(components):
            out_ref[k, layer] = sums[layer][k] + jnp.where(at == layer, edge[k], 0.0)


def on_core(kernel, outs, flops, moved, **more):
    return pl.pallas_call(
        kernel,
        out_shape=outs,
        compiler_params=pltpu.CompilerParams(vmem_limit_bytes=48 * 1024 * 1024),
        cost_estimate=pl.CostEstimate(flops=flops, bytes_accessed=moved, transcendentals=0),
        **more,
    )


def swapped(block, axis, first):
    size = lax.axis_size(axis)
    route = []
    for i in range(first, size - 1, 2):
        route += [(i, i + 1), (i + 1, i)]
    return lax.ppermute(block, axis, route)


def shards(
    displacement,
    modulus,
    node_mass,
    stiffness,
    face_nodes,
    pair_mortar,
    pair_rank,
    pair_face,
    pair_count,
    pair_shape,
    pair_weight,
    pair_gap,
    pair_normal,
):
    components, layers, rows_y, cols_x = displacement.shape
    face_count = face_nodes.shape[1]
    pair_total = pair_mortar.shape[0]
    domains = lax.axis_size("dom")
    capacity = max(2, 2 * pair_total // domains)

    points = pair_weight.shape[0]
    full = points // 8 * 8
    group = LANES // capacity
    word_rows = 5 * full + 9
    heights = tuple(-(-rows // group) for rows in (4 * full, full + 9))
    rows_high = 12 * face_count // LANES
    line = (1, pair_total)

    def first(*refs):
        first_kernel(capacity, heights, *refs)

    def last(*refs):
        last_kernel(capacity, heights, *refs)

    def shaped(shape, dtype=F32):
        return jax.ShapeDtypeStruct(shape, dtype)

    arrays = [
        face_nodes,
        displacement,
        pair_mortar.reshape(line),
        pair_rank.reshape(line),
        pair_face.reshape(line),
        pair_count.reshape(line),
        pair_weight,
        pair_normal,
        pair_gap,
        jnp.swapaxes(pair_shape, 0, 1).reshape(-1, pair_total),
        modulus,
    ]
    edge = shaped((components + 1, rows_y, cols_x))
    in_hbm = pl.BlockSpec(memory_space=pltpu.HBM)
    in_vmem = pl.BlockSpec(memory_space=pltpu.VMEM)
    shapes = shaped((pair_total // LANES, 8 * (full + 8), LANES))
    kept = [displacement, *arrays[5:-2], shapes, shaped((rows_y, cols_x))]
    sent, rows, words, turned, mortar, rank, face, nodes, inner, outer = on_core(
        first,
        [
            shaped((domains * (rows_high + sum(heights)), LANES)),
            shaped((12 * face_count // cols_x, cols_x)),
            shaped((word_rows, pair_total)),
            shaped((4 * full + 8, pair_total)),
            shaped(line, jnp.int32),
            shaped(line, jnp.int32),
            shaped(line, jnp.int32),
            shaped(face_nodes.shape, jnp.int32),
            edge,
            edge,
        ],
        900_000_000,
        1_500_000,
        in_specs=[in_hbm] * len(arrays),
        out_specs=[in_hbm] + [in_vmem] * 9,
        scratch_shapes=[pltpu.VMEM(x.shape, x.dtype) for x in kept]
        + [
            pltpu.VMEM((domains * (rows_high + sum(heights)), LANES), F32),
            pltpu.SemaphoreType.DMA((len(arrays) + pair_total // LANES,)),
            pltpu.SemaphoreType.DMA(()),
        ],
    )(*[pltpu.with_memory_space_constraint(x, pltpu.HBM) for x in arrays])
    order = [place_in_group(domain, domains) for domain in range(domains)]
    got = lax.all_to_all(
        sent.reshape(domains, 1, -1),
        "dom",
        split_axis=0,
        concat_axis=0,
        axis_index_groups=[order],
        tiled=True,
    ).reshape(sent.shape)
    inner_halo = swapped(inner, ("dom", "sub"), 0)
    outer_halo = swapped(outer, ("dom", "sub"), 1)
    size = 8 * components * GROUP
    internal, blocks, inverse = on_core(
        internal_kernel,
        [shaped(displacement.shape), shaped((2 * size, size), BF16), shaped(node_mass.shape)],
        1_000_000_000,
        700_000,
    )(displacement, modulus, stiffness, node_mass, inner, inner_halo)
    return on_core(
        last,
        shaped(displacement.shape),
        1_000_000_000,
        1_500_000,
        out_specs=in_hbm,
        scratch_shapes=[
            pltpu.VMEM(displacement.shape, F32),
            pltpu.SemaphoreType.DMA((layers,)),
        ],
    )(
        got, rows, words, turned, mortar, rank, face, nodes, inverse, internal, blocks, outer,
        outer_halo,
    )


def solution(mesh):
    placed = (
        P(None, ("runs", "dom", "sub"), None, None),
        P(("runs", "dom", "sub"), None, None),
        P(("runs", "dom", "sub"), None, None),
        P(),
        P(None, ("runs", "dom", "sub")),
        P(("runs", "dom", "sub")),
        P(("runs", "dom", "sub"), None),
        P(("runs", "dom", "sub")),
        P(("runs", "dom", "sub")),
        P(None, None, ("runs", "dom", "sub")),
        P(None, ("runs", "dom", "sub")),
        P(None, ("runs", "dom", "sub")),
        P(None, ("runs", "dom", "sub")),
    )
    return jax.shard_map(
        shards,
        mesh=mesh,
        in_specs=placed,
        out_specs=P(None, ("runs", "dom", "sub"), None, None),
        check_vma=False,
    )
```

```python
import jax
import jax.numpy as jnp
from jax import lax
from jax.experimental import pallas as pl
from jax.experimental.pallas import tpu as pltpu
from jax.sharding import PartitionSpec as P

F32 = jnp.float32
BF16 = jnp.bfloat16
LANES = 128


def terms_of(x, count):
    terms = []
    for _ in range(count):
        terms.append(x.astype(BF16))
        x = x - terms[-1].astype(F32)
    return terms


def stacked_terms(x):
    return jnp.concatenate(terms_of(x, 2), axis=0)


def summed(stacked):
    rows = stacked.shape[0] // 2
    return stacked[:rows] + stacked[rows:]


def marks(index, count):
    shape = (16, index.shape[1])
    rows = lax.broadcasted_iota(jnp.int32, shape, 0).astype(jnp.int16)
    index = jnp.broadcast_to(index, shape).astype(jnp.int16)
    tiles = [
        jnp.where(rows == index - jnp.int16(start), jnp.ones((), BF16), jnp.zeros((), BF16))
        for start in range(0, count, 16)
    ]
    return jnp.concatenate(tiles, axis=0)


def times(left, right):
    return jnp.dot(left, right, preferred_element_type=F32)


def times_turned(left, right):
    return lax.dot_general(left, right, (((1,), (1,)), ((), ())), preferred_element_type=F32)


def halves(power):
    return power.bit_length() - 1


def looked_up(table, face, at):
    both = summed(times(stacked_terms(table), at))
    return jnp.where(face < table.shape[1], both[:12], both[12:])


def folded(placed, height, capacity, domain):
    group = LANES // capacity
    tile, spot = domain // group, domain % group
    part = lax.broadcasted_iota(jnp.int32, (height, LANES), 1) >> halves(capacity)
    block = None
    for j in range(group):
        piece = placed[j * height : (j + 1) * height, tile * LANES : (tile + 1) * LANES]
        if j != spot:
            piece = pltpu.roll(piece, (j - spot) * capacity % LANES, 1)
        block = piece if block is None else jnp.where(part == j, piece, block)
    return block


def rows_of(ref, start, count):
    if not isinstance(start, int):
        return ref[pl.ds(start, count)]
    first, end = start // 8 * 8, -(-(start + count) // 8) * 8
    return ref[first:end][start - first : start - first + count]


def unfolded(got_ref, block_rows, start, height, capacity):
    group = LANES // capacity
    part = lax.broadcasted_iota(jnp.int32, (height, LANES), 1) >> halves(capacity)
    pieces = []
    for j in range(group):
        tiles = []
        for first in range(0, got_ref.shape[0] // block_rows, group):
            block = None
            for spot in range(group):
                at = (first + spot) * block_rows + start
                piece = rows_of(got_ref, at, height)
                if j != spot:
                    piece = pltpu.roll(piece, (spot - j) * capacity % LANES, 1)
                block = piece if block is None else jnp.where(part == spot, piece, block)
            tiles.append(block)
        pieces.append(jnp.concatenate(tiles, axis=1))
    return jnp.concatenate(pieces, axis=0)


def routed(words, rows, place):
    extra = -(-rows // 16) * 16 - words.shape[0]
    if extra:
        words = jnp.concatenate([words, jnp.zeros((extra, words.shape[1]), F32)], axis=0)
    return summed(times_turned(stacked_terms(words), place))


def weighted_pressure(words, full, remote_rows):
    tail = 5 * full
    normal = words[tail + 5 : tail + 8]
    gap, last = words[4 * full : tail], words[tail + 4 : tail + 5]
    for node in range(4):
        across = sum(
            normal[k : k + 1] * remote_rows[k * 4 + node : k * 4 + node + 1] for k in range(3)
        )
        gap = gap + words[node * full : (node + 1) * full] * across
        last = last + words[tail + node : tail + node + 1] * across
    return jnp.maximum(-gap, 0.0), jnp.maximum(-last, 0.0), normal


def loads_on(shapes, full, tail, pressure, last):
    return [
        jnp.sum(pressure * shapes[i * full : (i + 1) * full], axis=0, keepdims=True)
        + last * shapes[tail + i : tail + i + 1]
        for i in range(4)
    ]


def forces_of(normal, loads):
    loads = jnp.concatenate(loads, axis=0)
    return jnp.concatenate([normal[k : k + 1] * loads for k in range(3)], axis=0)


def place_in_group(domain, domains):
    return {0: domains - 1, domains - 1: 0}.get(domain, domain)


def first_kernel(capacity, heights, *refs):
    (
        nodes_hbm, disp_hbm, mortar_hbm, rank_hbm, face_hbm, count_hbm, weight_hbm, normal_hbm,
        gap_hbm, shape_hbm, modulus_hbm,
        sent_ref, rows_ref, words_ref, turned_ref, mortar_ref, rank_ref, face_ref, nodes,
        inner_ref, outer_ref,
        disp, count, weight, normal_v, gap_v, shape, modulus, blocks, sems, copy_sem,
    ) = refs
    components, layers, rows_y, cols_x = disp.shape
    block_rows = 12 * nodes.shape[1] // LANES + sum(heights)
    sources = (
        nodes_hbm, disp_hbm, rank_hbm, face_hbm, mortar_hbm, shape_hbm, count_hbm, weight_hbm,
        normal_hbm, gap_hbm, modulus_hbm.at[disp.shape[1] - 1],
    )
    targets = (
        nodes, disp, rank_ref, face_ref, mortar_ref, shape, count, weight, normal_v, gap_v, modulus,
    )
    brought = [
        pltpu.make_async_copy(source, target, sems.at[i])
        for i, (source, target) in enumerate(zip(sources, targets))
    ]
    for copy in brought:
        copy.start()

    domains = sent_ref.shape[0] // block_rows
    pair_total = rank_ref.shape[1]
    face_count = nodes.shape[1]
    strips = layers * rows_y
    for copy in brought[:-1]:
        copy.wait()
    rank, face, mortar = rank_ref[...], face_ref[...], mortar_ref[...]
    normal = normal_v[...]
    gap = gap_v[...]

    chosen = lax.broadcasted_iota(jnp.int32, (domains, pair_total), 0) == rank
    before = lax.broadcasted_iota(jnp.int32, (pair_total, pair_total), 0) < lax.broadcasted_iota(
        jnp.int32, (pair_total, pair_total), 1
    )
    earlier = times(chosen.astype(F32).astype(BF16), before.astype(F32).astype(BF16))
    slot = jnp.sum(jnp.where(chosen, earlier, 0.0), axis=0, keepdims=True).astype(jnp.int32)
    place = marks(rank * capacity + slot, domains * capacity)

    parts = stacked_terms(disp[...].reshape(components * strips, cols_x))
    numbers = lax.broadcasted_iota(jnp.int32, (strips, face_count), 0)
    folds = face_count // cols_x
    for corner in range(4):
        index = nodes[corner : corner + 1, :]
        strip = index >> halves(cols_x)
        found = summed(times(parts, marks(index & (cols_x - 1), cols_x)))
        found = found.reshape(components, strips, face_count)
        values = jnp.sum(jnp.where((numbers == strip)[None], found, 0.0), axis=1)
        for fold in range(folds):
            for k in range(components):
                at = fold * 12 + k * 4 + corner
                rows_ref[at : at + 1, :] = values[k : k + 1, fold * cols_x : (fold + 1) * cols_x]

    points = gap.shape[0]
    full = points // 8 * 8
    live = lax.broadcasted_iota(jnp.int32, (points, pair_total), 0) < count[...]
    root = jnp.where(live, jnp.sqrt(weight[...]), 0.0)
    weighted = [root * shape[:, node] for node in range(4)]
    long_words = jnp.concatenate([x[:full] for x in weighted], axis=0)
    group = LANES // capacity
    placed = routed(long_words, group * heights[0], place)

    rows = rows_ref[...]
    high = rows.shape[0]
    rows_high = high * cols_x // LANES
    halved = jnp.concatenate(
        [rows[:, i * LANES : (i + 1) * LANES] for i in range(cols_x // LANES)], axis=0
    )
    for domain in range(domains):
        at = place_in_group(domain, domains) * block_rows
        blocks[at : at + rows_high] = halved
        at += rows_high
        blocks[at : at + heights[0]] = folded(placed, heights[0], capacity, domain)

    mortar_rows = looked_up(rows, mortar, marks(mortar & (cols_x - 1), cols_x))
    for node in range(4):
        across = sum(
            normal[k : k + 1] * mortar_rows[k * 4 + node : k * 4 + node + 1] for k in range(3)
        )
        gap = gap - shape[:, 4 + node] * across
    gap = root * gap
    short_words = jnp.concatenate(
        [gap[:full]]
        + [x[full:] for x in weighted + [gap]]
        + [normal, face.astype(F32)],
        axis=0,
    )
    placed = routed(short_words, group * heights[1], place)
    for domain in range(domains):
        at = place_in_group(domain, domains) * block_rows + rows_high + heights[0]
        blocks[at : at + heights[1]] = folded(placed, heights[1], capacity, domain)
    sending = pltpu.make_async_copy(blocks.at[: sent_ref.shape[0]], sent_ref, copy_sem)
    sending.start()

    words_ref[: 4 * full] = long_words
    words_ref[4 * full :] = short_words
    for node in range(4):
        turned = root * shape[:, 4 + node]
        turned_ref[node * full : (node + 1) * full] = turned[:full]
        turned_ref[4 * full + node : 4 * full + node + 1] = turned[full:]

    brought[-1].wait()
    sub = lax.axis_index("sub")
    for target, layer in ((inner_ref, (1 - sub) * (layers - 1)), (outer_ref, sub * (layers - 1))):
        for k in range(components):
            target[k] = disp[k, layer]
        target[components] = modulus[...]
    sending.wait()


def last_kernel(
    capacity, heights, got_ref, rows_ref, words_ref, turned_ref, mortar_ref, rank_ref, face_ref, nodes_ref,
    inverse_ref, internal_ref, blocks_ref, own_ref, halo_ref, out_hbm, out_ref, sems,
):
    block_rows = 12 * nodes_ref.shape[1] // LANES + sum(heights)
    domains = got_ref.shape[0] // block_rows
    components, layers, rows_y, cols_x = out_ref.shape
    strips = layers * rows_y
    face_count = nodes_ref.shape[1]
    pair_total = rank_ref.shape[1]
    high = rows_ref.shape[0]
    rows_high = high * cols_x // LANES
    full = (turned_ref.shape[0] - 8) // 4
    own_rows = rows_ref[...]

    rank, face = rank_ref[...], face_ref[...]
    end = domains - 1
    place = jnp.where(rank == 0, end, jnp.where(rank == end, 0, rank))
    at = marks(face & (cols_x - 1), cols_x)
    step = min(domains, 8)

    def add_step(turn, total):
        halves_of = [
            jnp.concatenate(
                [
                    rows_of(got_ref, (turn * step + i) * block_rows + j * high, high)
                    for j in range(cols_x // LANES)
                ],
                axis=1,
            )
            for i in range(step)
        ]
        block = jnp.concatenate(halves_of, axis=0)
        found = summed(times(stacked_terms(block), at)).reshape(step, high, pair_total)
        for i in range(step):
            total = total + jnp.where(place == turn * step + i, found[i], 0.0)
        return total

    both = jnp.zeros((high, pair_total), F32)
    if domains == step:
        both = add_step(0, both)
    else:
        both = lax.fori_loop(0, domains // step, add_step, both)
    remote_rows = jnp.where(face < cols_x, both[:12], both[12:])
    pressure, last, normal = weighted_pressure(words_ref[...], full, remote_rows)
    turned = turned_ref[...]
    mortar_forces = forces_of(-normal, loads_on(turned, full, 4 * full, pressure, last))

    words = jnp.concatenate(
        [
            unfolded(got_ref, block_rows, rows_high, heights[0], capacity)[: 4 * full],
            unfolded(got_ref, block_rows, rows_high + heights[0], heights[1], capacity)[: full + 9],
        ],
        axis=0,
    )
    asked = words[5 * full + 8 : 5 * full + 9].astype(jnp.int32)
    asked_at = marks(asked & (cols_x - 1), cols_x)
    remote_rows = looked_up(own_rows, asked, asked_at)
    pressure, last, normal = weighted_pressure(words, full, remote_rows)
    remote_forces = forces_of(normal, loads_on(words, full, 5 * full, pressure, last))

    forces = jnp.concatenate([mortar_forces, remote_forces], axis=1)
    into = jnp.concatenate([mortar_ref[...], asked], axis=1)
    at = jnp.concatenate([marks(mortar_ref[...] & (cols_x - 1), cols_x), asked_at], axis=1)
    forces = jnp.concatenate(
        [jnp.where(into < cols_x, forces, 0.0), jnp.where(into < cols_x, 0.0, forces)], axis=0
    )
    forces = summed(times_turned(stacked_terms(forces), at))
    forces = jnp.concatenate([forces[:12], forces[12:]], axis=1)
    parts = [term.astype(F32) for term in terms_of(forces, 2)]
    indices = [nodes_ref[corner : corner + 1, :] for corner in range(4)]
    along_x = [marks(index & (cols_x - 1), cols_x) for index in indices]
    strip = [marks(index >> halves(cols_x), strips) for index in indices]
    upward = lax.axis_index("sub") == 1
    edge = edge_part(upward, own_ref, halo_ref, blocks_ref)
    at_edge = jnp.where(upward, layers - 1, 0)
    copies = []
    for layer in range(layers):
        total = jnp.zeros((2 * components * rows_y, cols_x), F32)
        for corner in range(4):
            here = strip[corner][layer * rows_y : (layer + 1) * rows_y]
            spread = []
            for part in parts:
                for k in range(components):
                    at = k * 4 + corner
                    row = jnp.broadcast_to(part[at : at + 1], (16, face_count)).astype(BF16)
                    spread.append(here * jnp.concatenate([row] * (rows_y // 16), axis=0))
            total = total + times_turned(jnp.concatenate(spread, axis=0), along_x[corner])
        contact = summed(total).reshape(components, rows_y, cols_x)
        for k in range(components):
            nodal = internal_ref[k, layer] + jnp.where(at_edge == layer, edge[k], 0.0)
            out_ref[k, layer] = (nodal + contact[k]) * inverse_ref[layer]
        copies.append(
            pltpu.make_async_copy(out_ref.at[:, layer], out_hbm.at[:, layer], sems.at[layer])
        )
        copies[-1].start()
    for copy in copies:
        copy.wait()


GROUP = 8


def shifted(layer):
    views = []
    for part in layer:
        rows_y, cols_x = part.shape
        for moved in (part, pltpu.roll(part, rows_y - 1, 0)):
            views += [moved, pltpu.roll(moved, cols_x - 1, 1)]
    return views


def element_forces(matrices, low, high, modulus):
    rows_y, cols_x = modulus.shape
    inside = (lax.broadcasted_iota(jnp.int32, (rows_y, cols_x), 0) < rows_y - 1) & (
        lax.broadcasted_iota(jnp.int32, (rows_y, cols_x), 1) < cols_x - 1
    )
    scale = jnp.where(inside, modulus, 0.0)
    views = shifted(low) + shifted(high)
    both = jnp.concatenate(matrices, axis=0)
    count = both.shape[0] // 2
    strips = []
    for y in range(0, rows_y, GROUP):
        leading, second = terms_of(jnp.concatenate([view[y : y + GROUP] for view in views], axis=0), 2)
        found = times(both, leading)
        force = found[:count] + (found[count:] + times(matrices[0], second))
        strips.append(force.reshape(-1, GROUP, cols_x) * scale[y : y + GROUP][None])
    return jnp.concatenate(strips, axis=1)


def on_nodes(forces):
    sums = []
    for k in range(forces.shape[0] // 4):
        straight, crossed = [
            forces[k * 4 + c] + pltpu.roll(forces[k * 4 + 2 + c], 1, 0) for c in range(2)
        ]
        sums.append(-(straight + pltpu.roll(crossed, 1, 1)))
    return sums


def edge_part(upward, own_ref, halo_ref, blocks_ref):
    components = own_ref.shape[0] - 1
    size = blocks_ref.shape[1]
    rows = size // 2
    start = jnp.where(upward, 0, rows)
    matrices = [
        blocks_ref[pl.ds(pl.multiple_of(term * size + start, 16), rows)] for term in range(2)
    ]
    low = [jnp.where(upward, own_ref[k], halo_ref[k]) for k in range(components + 1)]
    high = [jnp.where(upward, halo_ref[k], own_ref[k]) for k in range(components)]
    return on_nodes(element_forces(matrices, low[:components], high, low[components]))


def internal_kernel(
    disp_ref, modulus_ref, stiffness_ref, mass_ref, own_ref, halo_ref, out_ref, blocks_ref, inverse_ref
):
    inverse_ref[...] = 1.0 / mass_ref[...]
    components, layers, rows_y, cols_x = disp_ref.shape
    dofs = 8 * components
    half = dofs // 2
    size = dofs * GROUP

    row = lax.broadcasted_iota(jnp.int32, (size, dofs), 0) >> halves(GROUP)
    upper = (row >= half).astype(jnp.int32)
    inner = row - half * upper
    dof = (inner >> 2) * 8 + upper * 4 + (inner & 3)
    pick = (dof == lax.broadcasted_iota(jnp.int32, (size, dofs), 1)).astype(F32).astype(BF16)
    diagonal = (lax.broadcasted_iota(jnp.int32, (size, size), 0) & (GROUP - 1)) == (
        lax.broadcasted_iota(jnp.int32, (size, size), 1) & (GROUP - 1)
    )
    for i, term in enumerate(terms_of(stiffness_ref[...], 2)):
        wide = times_turned(times(pick, term).astype(BF16), pick)
        blocks_ref[i * size : (i + 1) * size] = jnp.where(diagonal, wide, 0.0).astype(BF16)

    blocks = [blocks_ref[i * size : (i + 1) * size] for i in range(2)]
    sums = [[0.0] * components for _ in range(layers)]
    for e in range(layers - 1):
        pair = [[disp_ref[k, e + a] for k in range(components)] for a in range(2)]
        forces = element_forces(blocks, pair[0], pair[1], modulus_ref[e])
        for a in range(2):
            part = on_nodes(forces[a * half : (a + 1) * half])
            sums[e + a] = [x + y for x, y in zip(sums[e + a], part)]
    upward = lax.axis_index("sub") == 0
    edge = edge_part(upward, own_ref, halo_ref, blocks_ref)
    at = jnp.where(upward, layers - 1, 0)
    for layer in range(layers):
        for k in range(components):
            out_ref[k, layer] = sums[layer][k] + jnp.where(at == layer, edge[k], 0.0)


def on_core(kernel, outs, flops, moved, **more):
    return pl.pallas_call(
        kernel,
        out_shape=outs,
        compiler_params=pltpu.CompilerParams(vmem_limit_bytes=48 * 1024 * 1024),
        cost_estimate=pl.CostEstimate(flops=flops, bytes_accessed=moved, transcendentals=0),
        **more,
    )


def swapped(block, axis, first):
    size = lax.axis_size(axis)
    route = []
    for i in range(first, size - 1, 2):
        route += [(i, i + 1), (i + 1, i)]
    return lax.ppermute(block, axis, route)


def shards(
    displacement,
    modulus,
    node_mass,
    stiffness,
    face_nodes,
    pair_mortar,
    pair_rank,
    pair_face,
    pair_count,
    pair_shape,
    pair_weight,
    pair_gap,
    pair_normal,
):
    components, layers, rows_y, cols_x = displacement.shape
    face_count = face_nodes.shape[1]
    pair_total = pair_mortar.shape[0]
    domains = lax.axis_size("dom")
    capacity = max(2, 2 * pair_total // domains)

    points = pair_weight.shape[0]
    full = points // 8 * 8
    group = LANES // capacity
    word_rows = 5 * full + 9
    heights = tuple(-(-rows // group) for rows in (4 * full, full + 9))
    rows_high = 12 * face_count // LANES
    line = (1, pair_total)

    def first(*refs):
        first_kernel(capacity, heights, *refs)

    def last(*refs):
        last_kernel(capacity, heights, *refs)

    def shaped(shape, dtype=F32):
        return jax.ShapeDtypeStruct(shape, dtype)

    arrays = [
        face_nodes,
        displacement,
        pair_mortar.reshape(line),
        pair_rank.reshape(line),
        pair_face.reshape(line),
        pair_count.reshape(line),
        pair_weight,
        pair_normal,
        pair_gap,
        jnp.swapaxes(pair_shape, 0, 1),
        modulus,
    ]
    edge = shaped((components + 1, rows_y, cols_x))
    in_hbm = pl.BlockSpec(memory_space=pltpu.HBM)
    in_vmem = pl.BlockSpec(memory_space=pltpu.VMEM)
    kept = [displacement, *arrays[5:-1], shaped((rows_y, cols_x))]
    sent, rows, words, turned, mortar, rank, face, nodes, inner, outer = on_core(
        first,
        [
            shaped((domains * (rows_high + sum(heights)), LANES)),
            shaped((12 * face_count // cols_x, cols_x)),
            shaped((word_rows, pair_total)),
            shaped((4 * full + 8, pair_total)),
            shaped(line, jnp.int32),
            shaped(line, jnp.int32),
            shaped(line, jnp.int32),
            shaped(face_nodes.shape, jnp.int32),
            edge,
            edge,
        ],
        900_000_000,
        1_500_000,
        in_specs=[in_hbm] * len(arrays),
        out_specs=[in_hbm] + [in_vmem] * 9,
        scratch_shapes=[pltpu.VMEM(x.shape, x.dtype) for x in kept]
        + [
            pltpu.VMEM((domains * (rows_high + sum(heights)) + 8, LANES), F32),
            pltpu.SemaphoreType.DMA((len(arrays),)),
            pltpu.SemaphoreType.DMA(()),
        ],
    )(*[pltpu.with_memory_space_constraint(x, pltpu.HBM) for x in arrays])
    order = [place_in_group(domain, domains) for domain in range(domains)]
    got = lax.all_to_all(
        sent.reshape(domains, 1, -1),
        "dom",
        split_axis=0,
        concat_axis=0,
        axis_index_groups=[order],
        tiled=True,
    ).reshape(sent.shape)
    inner_halo = swapped(inner, ("dom", "sub"), 0)
    outer_halo = swapped(outer, ("dom", "sub"), 1)
    size = 8 * components * GROUP
    internal, blocks, inverse = on_core(
        internal_kernel,
        [shaped(displacement.shape), shaped((2 * size, size), BF16), shaped(node_mass.shape)],
        1_000_000_000,
        700_000,
    )(displacement, modulus, stiffness, node_mass, inner, inner_halo)
    return on_core(
        last,
        shaped(displacement.shape),
        1_000_000_000,
        1_500_000,
        out_specs=in_hbm,
        scratch_shapes=[
            pltpu.VMEM(displacement.shape, F32),
            pltpu.SemaphoreType.DMA((layers,)),
        ],
    )(
        got, rows, words, turned, mortar, rank, face, nodes, inverse, internal, blocks, outer,
        outer_halo,
    )


def solution(mesh):
    placed = (
        P(None, ("runs", "dom", "sub"), None, None),
        P(("runs", "dom", "sub"), None, None),
        P(("runs", "dom", "sub"), None, None),
        P(),
        P(None, ("runs", "dom", "sub")),
        P(("runs", "dom", "sub")),
        P(("runs", "dom", "sub"), None),
        P(("runs", "dom", "sub")),
        P(("runs", "dom", "sub")),
        P(None, None, ("runs", "dom", "sub")),
        P(None, ("runs", "dom", "sub")),
        P(None, ("runs", "dom", "sub")),
        P(None, ("runs", "dom", "sub")),
    )
    return jax.shard_map(
        shards,
        mesh=mesh,
        in_specs=placed,
        out_specs=P(None, ("runs", "dom", "sub"), None, None),
        check_vma=False,
    )
```

```python
import jax
import jax.numpy as jnp
from jax import lax
from jax.experimental import pallas as pl
from jax.experimental.pallas import tpu as pltpu
from jax.sharding import PartitionSpec as P

F32 = jnp.float32
BF16 = jnp.bfloat16
LANES = 128


def terms_of(x, count):
    terms = []
    for _ in range(count):
        terms.append(x.astype(BF16))
        x = x - terms[-1].astype(F32)
    return terms


def stacked_terms(x):
    return jnp.concatenate(terms_of(x, 2), axis=0)


def summed(stacked):
    rows = stacked.shape[0] // 2
    return stacked[:rows] + stacked[rows:]


def marks(index, count):
    shape = (16, index.shape[1])
    rows = lax.broadcasted_iota(jnp.int32, shape, 0).astype(jnp.int16)
    index = jnp.broadcast_to(index, shape).astype(jnp.int16)
    tiles = [
        jnp.where(rows == index - jnp.int16(start), jnp.ones((), BF16), jnp.zeros((), BF16))
        for start in range(0, count, 16)
    ]
    return jnp.concatenate(tiles, axis=0)


def times(left, right):
    return jnp.dot(left, right, preferred_element_type=F32)


def times_turned(left, right):
    return lax.dot_general(left, right, (((1,), (1,)), ((), ())), preferred_element_type=F32)


def halves(power):
    return power.bit_length() - 1


def looked_up(table, face, at):
    both = summed(times(stacked_terms(table), at))
    return jnp.where(face < table.shape[1], both[:12], both[12:])


def folded(placed, height, capacity, domain):
    group = LANES // capacity
    tile, spot = domain // group, domain % group
    part = lax.broadcasted_iota(jnp.int32, (height, LANES), 1) >> halves(capacity)
    block = None
    for j in range(group):
        piece = placed[j * height : (j + 1) * height, tile * LANES : (tile + 1) * LANES]
        if j != spot:
            piece = pltpu.roll(piece, (j - spot) * capacity % LANES, 1)
        block = piece if block is None else jnp.where(part == j, piece, block)
    return block


def rows_of(ref, start, count):
    if not isinstance(start, int):
        return ref[pl.ds(start, count)]
    first, end = start // 8 * 8, -(-(start + count) // 8) * 8
    return ref[first:end][start - first : start - first + count]


def unfolded(got_ref, block_rows, start, height, capacity):
    group = LANES // capacity
    part = lax.broadcasted_iota(jnp.int32, (height, LANES), 1) >> halves(capacity)
    pieces = []
    for j in range(group):
        tiles = []
        for first in range(0, got_ref.shape[0] // block_rows, group):
            block = None
            for spot in range(group):
                at = (first + spot) * block_rows + start
                piece = rows_of(got_ref, at, height)
                if j != spot:
                    piece = pltpu.roll(piece, (spot - j) * capacity % LANES, 1)
                block = piece if block is None else jnp.where(part == spot, piece, block)
            tiles.append(block)
        pieces.append(jnp.concatenate(tiles, axis=1))
    return jnp.concatenate(pieces, axis=0)


def routed(words, rows, place):
    extra = -(-rows // 16) * 16 - words.shape[0]
    if extra:
        words = jnp.concatenate([words, jnp.zeros((extra, words.shape[1]), F32)], axis=0)
    return summed(times_turned(stacked_terms(words), place))


def weighted_pressure(words, full, remote_rows):
    tail = 5 * full
    normal = words[tail + 5 : tail + 8]
    gap, last = words[4 * full : tail], words[tail + 4 : tail + 5]
    for node in range(4):
        across = sum(
            normal[k : k + 1] * remote_rows[k * 4 + node : k * 4 + node + 1] for k in range(3)
        )
        gap = gap + words[node * full : (node + 1) * full] * across
        last = last + words[tail + node : tail + node + 1] * across
    return jnp.maximum(-gap, 0.0), jnp.maximum(-last, 0.0), normal


def loads_on(shapes, full, tail, pressure, last):
    return [
        jnp.sum(pressure * shapes[i * full : (i + 1) * full], axis=0, keepdims=True)
        + last * shapes[tail + i : tail + i + 1]
        for i in range(4)
    ]


def forces_of(normal, loads):
    loads = jnp.concatenate(loads, axis=0)
    return jnp.concatenate([normal[k : k + 1] * loads for k in range(3)], axis=0)


def place_in_group(domain, domains):
    return {0: domains - 1, domains - 1: 0}.get(domain, domain)


def first_kernel(capacity, heights, *refs):
    (
        nodes_hbm, disp_hbm, mortar_hbm, rank_hbm, face_hbm, count_hbm, weight_hbm, normal_hbm,
        gap_hbm, shape_hbm, modulus_hbm,
        sent_ref, rows_ref, words_ref, turned_ref, mortar_ref, rank_ref, face_ref, nodes,
        inner_ref, outer_ref,
        disp, count, weight, normal_v, gap_v, shape, modulus, blocks, sems, copy_sem,
    ) = refs
    components, layers, rows_y, cols_x = disp.shape
    block_rows = 12 * nodes.shape[1] // LANES + sum(heights)
    sources = (
        nodes_hbm, disp_hbm, rank_hbm, face_hbm, mortar_hbm, shape_hbm, count_hbm, weight_hbm,
        normal_hbm, gap_hbm, modulus_hbm.at[disp.shape[1] - 1],
    )
    targets = (
        nodes, disp, rank_ref, face_ref, mortar_ref, shape, count, weight, normal_v, gap_v, modulus,
    )
    brought = [
        pltpu.make_async_copy(source, target, sems.at[i])
        for i, (source, target) in enumerate(zip(sources, targets))
    ]
    for copy in brought:
        copy.start()

    domains = sent_ref.shape[0] // block_rows
    pair_total = rank_ref.shape[1]
    face_count = nodes.shape[1]
    strips = layers * rows_y
    for copy in brought[:-1]:
        copy.wait()
    rank, face, mortar = rank_ref[...], face_ref[...], mortar_ref[...]
    normal = normal_v[...]
    gap = gap_v[...]

    chosen = lax.broadcasted_iota(jnp.int32, (domains, pair_total), 0) == rank
    before = lax.broadcasted_iota(jnp.int32, (pair_total, pair_total), 0) < lax.broadcasted_iota(
        jnp.int32, (pair_total, pair_total), 1
    )
    earlier = times(chosen.astype(F32).astype(BF16), before.astype(F32).astype(BF16))
    slot = jnp.sum(jnp.where(chosen, earlier, 0.0), axis=0, keepdims=True).astype(jnp.int32)
    place = marks(rank * capacity + slot, domains * capacity)

    parts = stacked_terms(disp[...].reshape(components * strips, cols_x))
    numbers = lax.broadcasted_iota(jnp.int32, (strips, face_count), 0)
    folds = face_count // cols_x
    for corner in range(4):
        index = nodes[corner : corner + 1, :]
        strip = index >> halves(cols_x)
        found = summed(times(parts, marks(index & (cols_x - 1), cols_x)))
        found = found.reshape(components, strips, face_count)
        values = jnp.sum(jnp.where((numbers == strip)[None], found, 0.0), axis=1)
        for fold in range(folds):
            for k in range(components):
                at = fold * 12 + k * 4 + corner
                rows_ref[at : at + 1, :] = values[k : k + 1, fold * cols_x : (fold + 1) * cols_x]

    points = gap.shape[0]
    full = points // 8 * 8
    live = lax.broadcasted_iota(jnp.int32, (points, pair_total), 0) < count[...]
    root = jnp.where(live, jnp.sqrt(weight[...]), 0.0)
    weighted = [root * shape[:, node] for node in range(4)]
    long_words = jnp.concatenate([x[:full] for x in weighted], axis=0)
    group = LANES // capacity
    placed = routed(long_words, group * heights[0], place)

    rows = rows_ref[...]
    high = rows.shape[0]
    rows_high = high * cols_x // LANES
    halved = jnp.concatenate(
        [rows[:, i * LANES : (i + 1) * LANES] for i in range(cols_x // LANES)], axis=0
    )
    for domain in range(domains):
        at = place_in_group(domain, domains) * block_rows
        blocks[at : at + rows_high] = halved
        at += rows_high
        blocks[at : at + heights[0]] = folded(placed, heights[0], capacity, domain)

    mortar_rows = looked_up(rows, mortar, marks(mortar & (cols_x - 1), cols_x))
    for node in range(4):
        across = sum(
            normal[k : k + 1] * mortar_rows[k * 4 + node : k * 4 + node + 1] for k in range(3)
        )
        gap = gap - shape[:, 4 + node] * across
    gap = root * gap
    short_words = jnp.concatenate(
        [gap[:full]]
        + [x[full:] for x in weighted + [gap]]
        + [normal, face.astype(F32)],
        axis=0,
    )
    placed = routed(short_words, group * heights[1], place)
    for domain in range(domains):
        at = place_in_group(domain, domains) * block_rows + rows_high + heights[0]
        blocks[at : at + heights[1]] = folded(placed, heights[1], capacity, domain)
    sending = pltpu.make_async_copy(blocks.at[: sent_ref.shape[0]], sent_ref, copy_sem)
    sending.start()

    words_ref[: 4 * full] = long_words
    words_ref[4 * full :] = short_words
    for node in range(4):
        turned = root * shape[:, 4 + node]
        turned_ref[node * full : (node + 1) * full] = turned[:full]
        turned_ref[4 * full + node : 4 * full + node + 1] = turned[full:]

    brought[-1].wait()
    sub = lax.axis_index("sub")
    for target, layer in ((inner_ref, (1 - sub) * (layers - 1)), (outer_ref, sub * (layers - 1))):
        for k in range(components):
            target[k] = disp[k, layer]
        target[components] = modulus[...]
    sending.wait()


def last_kernel(
    capacity, heights, got_ref, rows_ref, words_ref, turned_ref, mortar_ref, rank_ref, face_ref, nodes_ref,
    inverse_ref, internal_ref, out_ref,
):
    block_rows = 12 * nodes_ref.shape[1] // LANES + sum(heights)
    domains = got_ref.shape[0] // block_rows
    components, layers, rows_y, cols_x = out_ref.shape
    strips = layers * rows_y
    face_count = nodes_ref.shape[1]
    pair_total = rank_ref.shape[1]
    high = rows_ref.shape[0]
    rows_high = high * cols_x // LANES
    full = (turned_ref.shape[0] - 8) // 4
    own_rows = rows_ref[...]

    rank, face = rank_ref[...], face_ref[...]
    end = domains - 1
    place = jnp.where(rank == 0, end, jnp.where(rank == end, 0, rank))
    at = marks(face & (cols_x - 1), cols_x)
    step = min(domains, 8)

    def add_step(turn, total):
        halves_of = [
            jnp.concatenate(
                [
                    rows_of(got_ref, (turn * step + i) * block_rows + j * high, high)
                    for j in range(cols_x // LANES)
                ],
                axis=1,
            )
            for i in range(step)
        ]
        block = jnp.concatenate(halves_of, axis=0)
        found = summed(times(stacked_terms(block), at)).reshape(step, high, pair_total)
        for i in range(step):
            total = total + jnp.where(place == turn * step + i, found[i], 0.0)
        return total

    both = jnp.zeros((high, pair_total), F32)
    if domains == step:
        both = add_step(0, both)
    else:
        both = lax.fori_loop(0, domains // step, add_step, both)
    remote_rows = jnp.where(face < cols_x, both[:12], both[12:])
    pressure, last, normal = weighted_pressure(words_ref[...], full, remote_rows)
    turned = turned_ref[...]
    mortar_forces = forces_of(-normal, loads_on(turned, full, 4 * full, pressure, last))

    words = jnp.concatenate(
        [
            unfolded(got_ref, block_rows, rows_high, heights[0], capacity)[: 4 * full],
            unfolded(got_ref, block_rows, rows_high + heights[0], heights[1], capacity)[: full + 9],
        ],
        axis=0,
    )
    asked = words[5 * full + 8 : 5 * full + 9].astype(jnp.int32)
    asked_at = marks(asked & (cols_x - 1), cols_x)
    remote_rows = looked_up(own_rows, asked, asked_at)
    pressure, last, normal = weighted_pressure(words, full, remote_rows)
    remote_forces = forces_of(normal, loads_on(words, full, 5 * full, pressure, last))

    forces = jnp.concatenate([mortar_forces, remote_forces], axis=1)
    into = jnp.concatenate([mortar_ref[...], asked], axis=1)
    at = jnp.concatenate([marks(mortar_ref[...] & (cols_x - 1), cols_x), asked_at], axis=1)
    forces = jnp.concatenate(
        [jnp.where(into < cols_x, forces, 0.0), jnp.where(into < cols_x, 0.0, forces)], axis=0
    )
    forces = summed(times_turned(stacked_terms(forces), at))
    forces = jnp.concatenate([forces[:12], forces[12:]], axis=1)
    parts = [term.astype(F32) for term in terms_of(forces, 2)]
    indices = [nodes_ref[corner : corner + 1, :] for corner in range(4)]
    along_x = [marks(index & (cols_x - 1), cols_x) for index in indices]
    strip = [marks(index >> halves(cols_x), strips) for index in indices]
    for layer in range(layers):
        total = jnp.zeros((2 * components * rows_y, cols_x), F32)
        for corner in range(4):
            here = strip[corner][layer * rows_y : (layer + 1) * rows_y]
            spread = []
            for part in parts:
                for k in range(components):
                    at = k * 4 + corner
                    row = jnp.broadcast_to(part[at : at + 1], (16, face_count)).astype(BF16)
                    spread.append(here * jnp.concatenate([row] * (rows_y // 16), axis=0))
            total = total + times_turned(jnp.concatenate(spread, axis=0), along_x[corner])
        contact = summed(total).reshape(components, rows_y, cols_x)
        for k in range(components):
            out_ref[k, layer] = (internal_ref[k, layer] + contact[k]) * inverse_ref[layer]


def edge_kernel(partial_ref, inverse_ref, blocks_ref, own_ref, halo_ref, out_ref):
    components, layers = out_ref.shape[:2]
    upward = lax.axis_index("sub") == 1
    edge = edge_part(upward, own_ref, halo_ref, blocks_ref)
    at_edge = jnp.where(upward, layers - 1, 0)
    for layer in range(layers):
        for k in range(components):
            added = jnp.where(at_edge == layer, edge[k], 0.0) * inverse_ref[layer]
            out_ref[k, layer] = partial_ref[k, layer] + added


GROUP = 8


def shifted(layer):
    views = []
    for part in layer:
        rows_y, cols_x = part.shape
        for moved in (part, pltpu.roll(part, rows_y - 1, 0)):
            views += [moved, pltpu.roll(moved, cols_x - 1, 1)]
    return views


def element_forces(matrices, low, high, modulus):
    rows_y, cols_x = modulus.shape
    inside = (lax.broadcasted_iota(jnp.int32, (rows_y, cols_x), 0) < rows_y - 1) & (
        lax.broadcasted_iota(jnp.int32, (rows_y, cols_x), 1) < cols_x - 1
    )
    scale = jnp.where(inside, modulus, 0.0)
    views = shifted(low) + shifted(high)
    both = jnp.concatenate(matrices, axis=0)
    count = both.shape[0] // 2
    strips = []
    for y in range(0, rows_y, GROUP):
        leading, second = terms_of(jnp.concatenate([view[y : y + GROUP] for view in views], axis=0), 2)
        found = times(both, leading)
        force = found[:count] + (found[count:] + times(matrices[0], second))
        strips.append(force.reshape(-1, GROUP, cols_x) * scale[y : y + GROUP][None])
    return jnp.concatenate(strips, axis=1)


def on_nodes(forces):
    sums = []
    for k in range(forces.shape[0] // 4):
        straight, crossed = [
            forces[k * 4 + c] + pltpu.roll(forces[k * 4 + 2 + c], 1, 0) for c in range(2)
        ]
        sums.append(-(straight + pltpu.roll(crossed, 1, 1)))
    return sums


def edge_part(upward, own_ref, halo_ref, blocks_ref):
    components = own_ref.shape[0] - 1
    size = blocks_ref.shape[1]
    rows = size // 2
    start = jnp.where(upward, 0, rows)
    matrices = [
        blocks_ref[pl.ds(pl.multiple_of(term * size + start, 16), rows)] for term in range(2)
    ]
    low = [jnp.where(upward, own_ref[k], halo_ref[k]) for k in range(components + 1)]
    high = [jnp.where(upward, halo_ref[k], own_ref[k]) for k in range(components)]
    return on_nodes(element_forces(matrices, low[:components], high, low[components]))


def internal_kernel(
    disp_ref, modulus_ref, stiffness_ref, mass_ref, own_ref, halo_ref, out_ref, blocks_ref, inverse_ref
):
    inverse_ref[...] = 1.0 / mass_ref[...]
    components, layers, rows_y, cols_x = disp_ref.shape
    dofs = 8 * components
    half = dofs // 2
    size = dofs * GROUP

    row = lax.broadcasted_iota(jnp.int32, (size, dofs), 0) >> halves(GROUP)
    upper = (row >= half).astype(jnp.int32)
    inner = row - half * upper
    dof = (inner >> 2) * 8 + upper * 4 + (inner & 3)
    pick = (dof == lax.broadcasted_iota(jnp.int32, (size, dofs), 1)).astype(F32).astype(BF16)
    diagonal = (lax.broadcasted_iota(jnp.int32, (size, size), 0) & (GROUP - 1)) == (
        lax.broadcasted_iota(jnp.int32, (size, size), 1) & (GROUP - 1)
    )
    for i, term in enumerate(terms_of(stiffness_ref[...], 2)):
        wide = times_turned(times(pick, term).astype(BF16), pick)
        blocks_ref[i * size : (i + 1) * size] = jnp.where(diagonal, wide, 0.0).astype(BF16)

    blocks = [blocks_ref[i * size : (i + 1) * size] for i in range(2)]
    sums = [[0.0] * components for _ in range(layers)]
    for e in range(layers - 1):
        pair = [[disp_ref[k, e + a] for k in range(components)] for a in range(2)]
        forces = element_forces(blocks, pair[0], pair[1], modulus_ref[e])
        for a in range(2):
            part = on_nodes(forces[a * half : (a + 1) * half])
            sums[e + a] = [x + y for x, y in zip(sums[e + a], part)]
    upward = lax.axis_index("sub") == 0
    edge = edge_part(upward, own_ref, halo_ref, blocks_ref)
    at = jnp.where(upward, layers - 1, 0)
    for layer in range(layers):
        for k in range(components):
            out_ref[k, layer] = sums[layer][k] + jnp.where(at == layer, edge[k], 0.0)


def on_core(kernel, outs, flops, moved, **more):
    return pl.pallas_call(
        kernel,
        out_shape=outs,
        compiler_params=pltpu.CompilerParams(vmem_limit_bytes=48 * 1024 * 1024),
        cost_estimate=pl.CostEstimate(flops=flops, bytes_accessed=moved, transcendentals=0),
        **more,
    )


def swapped(block, axis, first):
    size = lax.axis_size(axis)
    route = []
    for i in range(first, size - 1, 2):
        route += [(i, i + 1), (i + 1, i)]
    return lax.ppermute(block, axis, route)


def shards(
    displacement,
    modulus,
    node_mass,
    stiffness,
    face_nodes,
    pair_mortar,
    pair_rank,
    pair_face,
    pair_count,
    pair_shape,
    pair_weight,
    pair_gap,
    pair_normal,
):
    components, layers, rows_y, cols_x = displacement.shape
    face_count = face_nodes.shape[1]
    pair_total = pair_mortar.shape[0]
    domains = lax.axis_size("dom")
    capacity = max(2, 2 * pair_total // domains)

    points = pair_weight.shape[0]
    full = points // 8 * 8
    group = LANES // capacity
    word_rows = 5 * full + 9
    heights = tuple(-(-rows // group) for rows in (4 * full, full + 9))
    rows_high = 12 * face_count // LANES
    line = (1, pair_total)

    def first(*refs):
        first_kernel(capacity, heights, *refs)

    def last(*refs):
        last_kernel(capacity, heights, *refs)

    def shaped(shape, dtype=F32):
        return jax.ShapeDtypeStruct(shape, dtype)

    arrays = [
        face_nodes,
        displacement,
        pair_mortar.reshape(line),
        pair_rank.reshape(line),
        pair_face.reshape(line),
        pair_count.reshape(line),
        pair_weight,
        pair_normal,
        pair_gap,
        jnp.swapaxes(pair_shape, 0, 1),
        modulus,
    ]
    edge = shaped((components + 1, rows_y, cols_x))
    in_hbm = pl.BlockSpec(memory_space=pltpu.HBM)
    in_vmem = pl.BlockSpec(memory_space=pltpu.VMEM)
    kept = [displacement, *arrays[5:-1], shaped((rows_y, cols_x))]
    sent, rows, words, turned, mortar, rank, face, nodes, inner, outer = on_core(
        first,
        [
            shaped((domains * (rows_high + sum(heights)), LANES)),
            shaped((12 * face_count // cols_x, cols_x)),
            shaped((word_rows, pair_total)),
            shaped((4 * full + 8, pair_total)),
            shaped(line, jnp.int32),
            shaped(line, jnp.int32),
            shaped(line, jnp.int32),
            shaped(face_nodes.shape, jnp.int32),
            edge,
            edge,
        ],
        900_000_000,
        1_500_000,
        in_specs=[in_hbm] * len(arrays),
        out_specs=[in_hbm] + [in_vmem] * 9,
        scratch_shapes=[pltpu.VMEM(x.shape, x.dtype) for x in kept]
        + [
            pltpu.VMEM((domains * (rows_high + sum(heights)) + 8, LANES), F32),
            pltpu.SemaphoreType.DMA((len(arrays),)),
            pltpu.SemaphoreType.DMA(()),
        ],
    )(*[pltpu.with_memory_space_constraint(x, pltpu.HBM) for x in arrays])
    order = [place_in_group(domain, domains) for domain in range(domains)]
    got = lax.all_to_all(
        sent.reshape(domains, 1, -1),
        "dom",
        split_axis=0,
        concat_axis=0,
        axis_index_groups=[order],
        tiled=True,
    ).reshape(sent.shape)
    inner_halo = swapped(inner, ("dom", "sub"), 0)
    outer_halo = swapped(outer, ("dom", "sub"), 1)
    size = 8 * components * GROUP
    internal, blocks, inverse = on_core(
        internal_kernel,
        [shaped(displacement.shape), shaped((2 * size, size), BF16), shaped(node_mass.shape)],
        1_000_000_000,
        700_000,
    )(displacement, modulus, stiffness, node_mass, inner, inner_halo)
    partial = on_core(last, shaped(displacement.shape), 1_000_000_000, 1_500_000)(
        got, rows, words, turned, mortar, rank, face, nodes, inverse, internal
    )
    return on_core(edge_kernel, shaped(displacement.shape), 200_000_000, 600_000)(
        partial, inverse, blocks, outer, outer_halo
    )


def solution(mesh):
    placed = (
        P(None, ("runs", "dom", "sub"), None, None),
        P(("runs", "dom", "sub"), None, None),
        P(("runs", "dom", "sub"), None, None),
        P(),
        P(None, ("runs", "dom", "sub")),
        P(("runs", "dom", "sub")),
        P(("runs", "dom", "sub"), None),
        P(("runs", "dom", "sub")),
        P(("runs", "dom", "sub")),
        P(None, None, ("runs", "dom", "sub")),
        P(None, ("runs", "dom", "sub")),
        P(None, ("runs", "dom", "sub")),
        P(None, ("runs", "dom", "sub")),
    )
    return jax.shard_map(
        shards,
        mesh=mesh,
        in_specs=placed,
        out_specs=P(None, ("runs", "dom", "sub"), None, None),
        check_vma=False,
    )
```

```python
import jax
import jax.numpy as jnp
from jax import lax
from jax.experimental import pallas as pl
from jax.experimental.pallas import tpu as pltpu
from jax.sharding import PartitionSpec as P

F32 = jnp.float32
BF16 = jnp.bfloat16
LANES = 128


def terms_of(x, count):
    terms = []
    for _ in range(count):
        terms.append(x.astype(BF16))
        x = x - terms[-1].astype(F32)
    return terms


def stacked_terms(x):
    return jnp.concatenate(terms_of(x, 2), axis=0)


def summed(stacked):
    rows = stacked.shape[0] // 2
    return stacked[:rows] + stacked[rows:]


def marks(index, count):
    shape = (16, index.shape[1])
    rows = lax.broadcasted_iota(jnp.int32, shape, 0).astype(jnp.int16)
    index = jnp.broadcast_to(index, shape).astype(jnp.int16)
    tiles = [
        jnp.where(rows == index - jnp.int16(start), jnp.ones((), BF16), jnp.zeros((), BF16))
        for start in range(0, count, 16)
    ]
    return jnp.concatenate(tiles, axis=0)


def times(left, right):
    return jnp.dot(left, right, preferred_element_type=F32)


def times_turned(left, right):
    return lax.dot_general(left, right, (((1,), (1,)), ((), ())), preferred_element_type=F32)


def halves(power):
    return power.bit_length() - 1


def looked_up(table, face, at):
    both = summed(times(stacked_terms(table), at))
    return jnp.where(face < table.shape[1], both[:12], both[12:])


def folded(placed, height, capacity, domain):
    group = LANES // capacity
    tile, spot = domain // group, domain % group
    part = lax.broadcasted_iota(jnp.int32, (height, LANES), 1) >> halves(capacity)
    block = None
    for j in range(group):
        piece = placed[j * height : (j + 1) * height, tile * LANES : (tile + 1) * LANES]
        if j != spot:
            piece = pltpu.roll(piece, (j - spot) * capacity % LANES, 1)
        block = piece if block is None else jnp.where(part == j, piece, block)
    return block


def rows_of(ref, start, count):
    if not isinstance(start, int):
        return ref[pl.ds(start, count)]
    first, end = start // 8 * 8, -(-(start + count) // 8) * 8
    return ref[first:end][start - first : start - first + count]


def unfolded(got_ref, block_rows, start, height, capacity):
    group = LANES // capacity
    part = lax.broadcasted_iota(jnp.int32, (height, LANES), 1) >> halves(capacity)
    pieces = []
    for j in range(group):
        tiles = []
        for first in range(0, got_ref.shape[0] // block_rows, group):
            block = None
            for spot in range(group):
                at = (first + spot) * block_rows + start
                piece = rows_of(got_ref, at, height)
                if j != spot:
                    piece = pltpu.roll(piece, (spot - j) * capacity % LANES, 1)
                block = piece if block is None else jnp.where(part == spot, piece, block)
            tiles.append(block)
        pieces.append(jnp.concatenate(tiles, axis=1))
    return jnp.concatenate(pieces, axis=0)


def routed(words, rows, place):
    extra = -(-rows // 16) * 16 - words.shape[0]
    if extra:
        words = jnp.concatenate([words, jnp.zeros((extra, words.shape[1]), F32)], axis=0)
    return summed(times_turned(stacked_terms(words), place))


def weighted_pressure(words, full, remote_rows):
    tail = 5 * full
    normal = words[tail + 5 : tail + 8]
    gap, last = words[4 * full : tail], words[tail + 4 : tail + 5]
    for node in range(4):
        across = sum(
            normal[k : k + 1] * remote_rows[k * 4 + node : k * 4 + node + 1] for k in range(3)
        )
        gap = gap + words[node * full : (node + 1) * full] * across
        last = last + words[tail + node : tail + node + 1] * across
    return jnp.maximum(-gap, 0.0), jnp.maximum(-last, 0.0), normal


def loads_on(shapes, full, tail, pressure, last):
    return [
        jnp.sum(pressure * shapes[i * full : (i + 1) * full], axis=0, keepdims=True)
        + last * shapes[tail + i : tail + i + 1]
        for i in range(4)
    ]


def forces_of(normal, loads):
    loads = jnp.concatenate(loads, axis=0)
    return jnp.concatenate([normal[k : k + 1] * loads for k in range(3)], axis=0)


def place_in_group(domain, domains):
    return {0: domains - 1, domains - 1: 0}.get(domain, domain)


def first_kernel(capacity, heights, *refs):
    (
        nodes_hbm, disp_hbm, mortar_hbm, rank_hbm, face_hbm, count_hbm, weight_hbm, normal_hbm,
        gap_hbm, shape_hbm, modulus_hbm,
        sent_ref, rows_ref, words_ref, turned_ref, mortar_ref, rank_ref, face_ref, nodes,
        inner_ref, outer_ref,
        disp, count, weight, normal_v, gap_v, shape, modulus, blocks, sems, copy_sem,
    ) = refs
    components, layers, rows_y, cols_x = disp.shape
    block_rows = 12 * nodes.shape[1] // LANES + sum(heights)
    sources = (
        nodes_hbm, disp_hbm, rank_hbm, face_hbm, mortar_hbm, shape_hbm, count_hbm, weight_hbm,
        normal_hbm, gap_hbm, modulus_hbm.at[disp.shape[1] - 1],
    )
    targets = (
        nodes, disp, rank_ref, face_ref, mortar_ref, shape, count, weight, normal_v, gap_v, modulus,
    )
    brought = [
        pltpu.make_async_copy(source, target, sems.at[i])
        for i, (source, target) in enumerate(zip(sources, targets))
    ]
    for copy in brought:
        copy.start()

    domains = sent_ref.shape[0] // block_rows
    pair_total = rank_ref.shape[1]
    face_count = nodes.shape[1]
    strips = layers * rows_y
    for copy in brought[:-1]:
        copy.wait()
    rank, face, mortar = rank_ref[...], face_ref[...], mortar_ref[...]
    normal = normal_v[...]
    gap = gap_v[...]

    chosen = lax.broadcasted_iota(jnp.int32, (domains, pair_total), 0) == rank
    before = lax.broadcasted_iota(jnp.int32, (pair_total, pair_total), 0) < lax.broadcasted_iota(
        jnp.int32, (pair_total, pair_total), 1
    )
    earlier = times(chosen.astype(F32).astype(BF16), before.astype(F32).astype(BF16))
    slot = jnp.sum(jnp.where(chosen, earlier, 0.0), axis=0, keepdims=True).astype(jnp.int32)
    place = marks(rank * capacity + slot, domains * capacity)

    parts = stacked_terms(disp[...].reshape(components * strips, cols_x))
    numbers = lax.broadcasted_iota(jnp.int32, (strips, face_count), 0)
    folds = face_count // cols_x
    for corner in range(4):
        index = nodes[corner : corner + 1, :]
        strip = index >> halves(cols_x)
        found = summed(times(parts, marks(index & (cols_x - 1), cols_x)))
        found = found.reshape(components, strips, face_count)
        values = jnp.sum(jnp.where((numbers == strip)[None], found, 0.0), axis=1)
        for fold in range(folds):
            for k in range(components):
                at = fold * 12 + k * 4 + corner
                rows_ref[at : at + 1, :] = values[k : k + 1, fold * cols_x : (fold + 1) * cols_x]

    points = gap.shape[0]
    full = points // 8 * 8
    live = lax.broadcasted_iota(jnp.int32, (points, pair_total), 0) < count[...]
    root = jnp.where(live, jnp.sqrt(weight[...]), 0.0)
    weighted = [root * shape[:, node] for node in range(4)]
    long_words = jnp.concatenate([x[:full] for x in weighted], axis=0)
    group = LANES // capacity
    placed = routed(long_words, group * heights[0], place)

    rows = rows_ref[...]
    high = rows.shape[0]
    rows_high = high * cols_x // LANES
    halved = jnp.concatenate(
        [rows[:, i * LANES : (i + 1) * LANES] for i in range(cols_x // LANES)], axis=0
    )
    for domain in range(domains):
        at = place_in_group(domain, domains) * block_rows
        blocks[at : at + rows_high] = halved
        at += rows_high
        blocks[at : at + heights[0]] = folded(placed, heights[0], capacity, domain)

    mortar_rows = looked_up(rows, mortar, marks(mortar & (cols_x - 1), cols_x))
    for node in range(4):
        across = sum(
            normal[k : k + 1] * mortar_rows[k * 4 + node : k * 4 + node + 1] for k in range(3)
        )
        gap = gap - shape[:, 4 + node] * across
    gap = root * gap
    short_words = jnp.concatenate(
        [gap[:full]]
        + [x[full:] for x in weighted + [gap]]
        + [normal, face.astype(F32)],
        axis=0,
    )
    placed = routed(short_words, group * heights[1], place)
    for domain in range(domains):
        at = place_in_group(domain, domains) * block_rows + rows_high + heights[0]
        blocks[at : at + heights[1]] = folded(placed, heights[1], capacity, domain)
    sending = pltpu.make_async_copy(blocks.at[: sent_ref.shape[0]], sent_ref, copy_sem)
    sending.start()

    words_ref[: 4 * full] = long_words
    words_ref[4 * full :] = short_words
    for node in range(4):
        turned = root * shape[:, 4 + node]
        turned_ref[node * full : (node + 1) * full] = turned[:full]
        turned_ref[4 * full + node : 4 * full + node + 1] = turned[full:]

    brought[-1].wait()
    sub = lax.axis_index("sub")
    for target, layer in ((inner_ref, (1 - sub) * (layers - 1)), (outer_ref, sub * (layers - 1))):
        for k in range(components):
            target[k] = disp[k, layer]
        target[components] = modulus[...]
    sending.wait()


def last_kernel(
    capacity, heights, got_ref, rows_ref, words_ref, turned_ref, mortar_ref, rank_ref, face_ref, nodes_ref,
    inverse_ref, internal_ref, blocks_ref, part_ref, own_ref, halo_ref, out_hbm, out_ref, sems,
):
    block_rows = 12 * nodes_ref.shape[1] // LANES + sum(heights)
    domains = got_ref.shape[0] // block_rows
    components, layers, rows_y, cols_x = out_ref.shape
    strips = layers * rows_y
    face_count = nodes_ref.shape[1]
    pair_total = rank_ref.shape[1]
    high = rows_ref.shape[0]
    rows_high = high * cols_x // LANES
    full = (turned_ref.shape[0] - 8) // 4
    own_rows = rows_ref[...]

    rank, face = rank_ref[...], face_ref[...]
    end = domains - 1
    place = jnp.where(rank == 0, end, jnp.where(rank == end, 0, rank))
    at = marks(face & (cols_x - 1), cols_x)
    step = min(domains, 8)

    def add_step(turn, total):
        halves_of = [
            jnp.concatenate(
                [
                    rows_of(got_ref, (turn * step + i) * block_rows + j * high, high)
                    for j in range(cols_x // LANES)
                ],
                axis=1,
            )
            for i in range(step)
        ]
        block = jnp.concatenate(halves_of, axis=0)
        found = summed(times(stacked_terms(block), at)).reshape(step, high, pair_total)
        for i in range(step):
            total = total + jnp.where(place == turn * step + i, found[i], 0.0)
        return total

    both = jnp.zeros((high, pair_total), F32)
    if domains == step:
        both = add_step(0, both)
    else:
        both = lax.fori_loop(0, domains // step, add_step, both)
    remote_rows = jnp.where(face < cols_x, both[:12], both[12:])
    pressure, last, normal = weighted_pressure(words_ref[...], full, remote_rows)
    turned = turned_ref[...]
    mortar_forces = forces_of(-normal, loads_on(turned, full, 4 * full, pressure, last))

    words = jnp.concatenate(
        [
            unfolded(got_ref, block_rows, rows_high, heights[0], capacity)[: 4 * full],
            unfolded(got_ref, block_rows, rows_high + heights[0], heights[1], capacity)[: full + 9],
        ],
        axis=0,
    )
    asked = words[5 * full + 8 : 5 * full + 9].astype(jnp.int32)
    asked_at = marks(asked & (cols_x - 1), cols_x)
    remote_rows = looked_up(own_rows, asked, asked_at)
    pressure, last, normal = weighted_pressure(words, full, remote_rows)
    remote_forces = forces_of(normal, loads_on(words, full, 5 * full, pressure, last))

    forces = jnp.concatenate([mortar_forces, remote_forces], axis=1)
    into = jnp.concatenate([mortar_ref[...], asked], axis=1)
    at = jnp.concatenate([marks(mortar_ref[...] & (cols_x - 1), cols_x), asked_at], axis=1)
    forces = jnp.concatenate(
        [jnp.where(into < cols_x, forces, 0.0), jnp.where(into < cols_x, 0.0, forces)], axis=0
    )
    forces = summed(times_turned(stacked_terms(forces), at))
    forces = jnp.concatenate([forces[:12], forces[12:]], axis=1)
    parts = [term.astype(F32) for term in terms_of(forces, 2)]
    indices = [nodes_ref[corner : corner + 1, :] for corner in range(4)]
    along_x = [marks(index & (cols_x - 1), cols_x) for index in indices]
    strip = [marks(index >> halves(cols_x), strips) for index in indices]
    upward = lax.axis_index("sub") == 1
    components_all = halo_ref.shape[0] - 1
    half_rows = blocks_ref.shape[0] // 2
    matrices = [blocks_ref[i * half_rows : (i + 1) * half_rows] for i in range(2)]
    halo = products(matrices, shifted([halo_ref[k] for k in range(components_all)]))
    modulus = jnp.where(upward, own_ref[components_all], halo_ref[components_all])
    edge = on_nodes(scaled(part_ref[...] + halo, modulus))
    at_edge = jnp.where(upward, layers - 1, 0)
    copies = []
    for layer in range(layers):
        total = jnp.zeros((2 * components * rows_y, cols_x), F32)
        for corner in range(4):
            here = strip[corner][layer * rows_y : (layer + 1) * rows_y]
            spread = []
            for part in parts:
                for k in range(components):
                    at = k * 4 + corner
                    row = jnp.broadcast_to(part[at : at + 1], (16, face_count)).astype(BF16)
                    spread.append(here * jnp.concatenate([row] * (rows_y // 16), axis=0))
            total = total + times_turned(jnp.concatenate(spread, axis=0), along_x[corner])
        contact = summed(total).reshape(components, rows_y, cols_x)
        for k in range(components):
            nodal = internal_ref[k, layer] + jnp.where(at_edge == layer, edge[k], 0.0)
            out_ref[k, layer] = (nodal + contact[k]) * inverse_ref[layer]
        copies.append(
            pltpu.make_async_copy(out_ref.at[:, layer], out_hbm.at[:, layer], sems.at[layer])
        )
        copies[-1].start()
    for copy in copies:
        copy.wait()


GROUP = 8


def shifted(layer):
    views = []
    for part in layer:
        rows_y, cols_x = part.shape
        for moved in (part, pltpu.roll(part, rows_y - 1, 0)):
            views += [moved, pltpu.roll(moved, cols_x - 1, 1)]
    return views


def products(matrices, views):
    rows_y, cols_x = views[0].shape
    both = jnp.concatenate(matrices, axis=0)
    count = both.shape[0] // 2
    strips = []
    for y in range(0, rows_y, GROUP):
        leading, second = terms_of(jnp.concatenate([view[y : y + GROUP] for view in views], axis=0), 2)
        found = times(both, leading)
        force = found[:count] + (found[count:] + times(matrices[0], second))
        strips.append(force.reshape(-1, GROUP, cols_x))
    return jnp.concatenate(strips, axis=1)


def scaled(forces, modulus):
    rows_y, cols_x = modulus.shape
    inside = (lax.broadcasted_iota(jnp.int32, (rows_y, cols_x), 0) < rows_y - 1) & (
        lax.broadcasted_iota(jnp.int32, (rows_y, cols_x), 1) < cols_x - 1
    )
    return forces * jnp.where(inside, modulus, 0.0)[None]


def element_forces(matrices, low, high, modulus):
    return scaled(products(matrices, shifted(low) + shifted(high)), modulus)


def on_nodes(forces):
    sums = []
    for k in range(forces.shape[0] // 4):
        straight, crossed = [
            forces[k * 4 + c] + pltpu.roll(forces[k * 4 + 2 + c], 1, 0) for c in range(2)
        ]
        sums.append(-(straight + pltpu.roll(crossed, 1, 1)))
    return sums


def edge_part(upward, own_ref, halo_ref, blocks_ref):
    components = own_ref.shape[0] - 1
    size = blocks_ref.shape[1]
    rows = size // 2
    start = jnp.where(upward, 0, rows)
    matrices = [
        blocks_ref[pl.ds(pl.multiple_of(term * size + start, 16), rows)] for term in range(2)
    ]
    low = [jnp.where(upward, own_ref[k], halo_ref[k]) for k in range(components + 1)]
    high = [jnp.where(upward, halo_ref[k], own_ref[k]) for k in range(components)]
    return on_nodes(element_forces(matrices, low[:components], high, low[components]))


def internal_kernel(
    disp_ref, modulus_ref, stiffness_ref, mass_ref, own_ref, halo_ref, outer_ref, out_ref, inverse_ref,
    far_ref, part_ref, blocks_ref,
):
    inverse_ref[...] = 1.0 / mass_ref[...]
    components, layers, rows_y, cols_x = disp_ref.shape
    dofs = 8 * components
    half = dofs // 2
    size = dofs * GROUP

    row = lax.broadcasted_iota(jnp.int32, (size, dofs), 0) >> halves(GROUP)
    upper = (row >= half).astype(jnp.int32)
    inner = row - half * upper
    dof = (inner >> 2) * 8 + upper * 4 + (inner & 3)
    pick = (dof == lax.broadcasted_iota(jnp.int32, (size, dofs), 1)).astype(F32)
    rows = size // 2
    outward = lax.axis_index("sub") == 1
    near = jnp.where(outward, pick[:rows], pick[rows:]).astype(BF16)
    far = jnp.where(outward, pick[rows:], pick[:rows]).astype(BF16)
    pick = pick.astype(BF16)
    near_blocks = []
    diagonal = (lax.broadcasted_iota(jnp.int32, (size, size), 0) & (GROUP - 1)) == (
        lax.broadcasted_iota(jnp.int32, (size, size), 1) & (GROUP - 1)
    )
    for i, term in enumerate(terms_of(stiffness_ref[...], 2)):
        wide = times_turned(times(pick, term).astype(BF16), pick)
        blocks_ref[i * size : (i + 1) * size] = jnp.where(diagonal, wide, 0.0).astype(BF16)
        tall = times(near, term).astype(BF16)
        same = diagonal[:rows, :rows]
        near_blocks.append(jnp.where(same, times_turned(tall, near), 0.0).astype(BF16))
        far_ref[i * rows : (i + 1) * rows] = jnp.where(same, times_turned(tall, far), 0.0).astype(BF16)
    part_ref[...] = products(near_blocks, shifted([outer_ref[k] for k in range(components)]))

    blocks = [blocks_ref[i * size : (i + 1) * size] for i in range(2)]
    sums = [[0.0] * components for _ in range(layers)]
    for e in range(layers - 1):
        pair = [[disp_ref[k, e + a] for k in range(components)] for a in range(2)]
        forces = element_forces(blocks, pair[0], pair[1], modulus_ref[e])
        for a in range(2):
            part = on_nodes(forces[a * half : (a + 1) * half])
            sums[e + a] = [x + y for x, y in zip(sums[e + a], part)]
    upward = lax.axis_index("sub") == 0
    edge = edge_part(upward, own_ref, halo_ref, blocks_ref)
    at = jnp.where(upward, layers - 1, 0)
    for layer in range(layers):
        for k in range(components):
            out_ref[k, layer] = sums[layer][k] + jnp.where(at == layer, edge[k], 0.0)


def on_core(kernel, outs, flops, moved, **more):
    return pl.pallas_call(
        kernel,
        out_shape=outs,
        compiler_params=pltpu.CompilerParams(vmem_limit_bytes=48 * 1024 * 1024),
        cost_estimate=pl.CostEstimate(flops=flops, bytes_accessed=moved, transcendentals=0),
        **more,
    )


def swapped(block, axis, first):
    size = lax.axis_size(axis)
    route = []
    for i in range(first, size - 1, 2):
        route += [(i, i + 1), (i + 1, i)]
    return lax.ppermute(block, axis, route)


def shards(
    displacement,
    modulus,
    node_mass,
    stiffness,
    face_nodes,
    pair_mortar,
    pair_rank,
    pair_face,
    pair_count,
    pair_shape,
    pair_weight,
    pair_gap,
    pair_normal,
):
    components, layers, rows_y, cols_x = displacement.shape
    face_count = face_nodes.shape[1]
    pair_total = pair_mortar.shape[0]
    domains = lax.axis_size("dom")
    capacity = max(2, 2 * pair_total // domains)

    points = pair_weight.shape[0]
    full = points // 8 * 8
    group = LANES // capacity
    word_rows = 5 * full + 9
    heights = tuple(-(-rows // group) for rows in (4 * full, full + 9))
    rows_high = 12 * face_count // LANES
    line = (1, pair_total)

    def first(*refs):
        first_kernel(capacity, heights, *refs)

    def last(*refs):
        last_kernel(capacity, heights, *refs)

    def shaped(shape, dtype=F32):
        return jax.ShapeDtypeStruct(shape, dtype)

    arrays = [
        face_nodes,
        displacement,
        pair_mortar.reshape(line),
        pair_rank.reshape(line),
        pair_face.reshape(line),
        pair_count.reshape(line),
        pair_weight,
        pair_normal,
        pair_gap,
        jnp.swapaxes(pair_shape, 0, 1),
        modulus,
    ]
    edge = shaped((components + 1, rows_y, cols_x))
    in_hbm = pl.BlockSpec(memory_space=pltpu.HBM)
    in_vmem = pl.BlockSpec(memory_space=pltpu.VMEM)
    kept = [displacement, *arrays[5:-1], shaped((rows_y, cols_x))]
    sent, rows, words, turned, mortar, rank, face, nodes, inner, outer = on_core(
        first,
        [
            shaped((domains * (rows_high + sum(heights)), LANES)),
            shaped((12 * face_count // cols_x, cols_x)),
            shaped((word_rows, pair_total)),
            shaped((4 * full + 8, pair_total)),
            shaped(line, jnp.int32),
            shaped(line, jnp.int32),
            shaped(line, jnp.int32),
            shaped(face_nodes.shape, jnp.int32),
            edge,
            edge,
        ],
        900_000_000,
        1_500_000,
        in_specs=[in_hbm] * len(arrays),
        out_specs=[in_hbm] + [in_vmem] * 9,
        scratch_shapes=[pltpu.VMEM(x.shape, x.dtype) for x in kept]
        + [
            pltpu.VMEM((domains * (rows_high + sum(heights)) + 8, LANES), F32),
            pltpu.SemaphoreType.DMA((len(arrays),)),
            pltpu.SemaphoreType.DMA(()),
        ],
    )(*[pltpu.with_memory_space_constraint(x, pltpu.HBM) for x in arrays])
    order = [place_in_group(domain, domains) for domain in range(domains)]
    got = lax.all_to_all(
        sent.reshape(domains, 1, -1),
        "dom",
        split_axis=0,
        concat_axis=0,
        axis_index_groups=[order],
        tiled=True,
    ).reshape(sent.shape)
    inner_halo = swapped(inner, ("dom", "sub"), 0)
    outer_halo = swapped(outer, ("dom", "sub"), 1)
    size = 8 * components * GROUP
    internal, inverse, far, part = on_core(
        internal_kernel,
        [
            shaped(displacement.shape),
            shaped(node_mass.shape),
            shaped((size, size // 2), BF16),
            shaped((size // 2 // GROUP, rows_y, cols_x)),
        ],
        1_000_000_000,
        700_000,
        scratch_shapes=[pltpu.VMEM((2 * size, size), BF16)],
    )(displacement, modulus, stiffness, node_mass, inner, inner_halo, outer)
    return on_core(
        last,
        shaped(displacement.shape),
        1_000_000_000,
        1_500_000,
        out_specs=in_hbm,
        scratch_shapes=[
            pltpu.VMEM(displacement.shape, F32),
            pltpu.SemaphoreType.DMA((layers,)),
        ],
    )(
        got, rows, words, turned, mortar, rank, face, nodes, inverse, internal, far, part, outer,
        outer_halo,
    )


def solution(mesh):
    placed = (
        P(None, ("runs", "dom", "sub"), None, None),
        P(("runs", "dom", "sub"), None, None),
        P(("runs", "dom", "sub"), None, None),
        P(),
        P(None, ("runs", "dom", "sub")),
        P(("runs", "dom", "sub")),
        P(("runs", "dom", "sub"), None),
        P(("runs", "dom", "sub")),
        P(("runs", "dom", "sub")),
        P(None, None, ("runs", "dom", "sub")),
        P(None, ("runs", "dom", "sub")),
        P(None, ("runs", "dom", "sub")),
        P(None, ("runs", "dom", "sub")),
    )
    return jax.shard_map(
        shards,
        mesh=mesh,
        in_specs=placed,
        out_specs=P(None, ("runs", "dom", "sub"), None, None),
        check_vma=False,
    )
```

```python
import jax
import jax.numpy as jnp
from jax import lax
from jax.experimental import pallas as pl
from jax.experimental.pallas import tpu as pltpu
from jax.sharding import PartitionSpec as P

F32 = jnp.float32
BF16 = jnp.bfloat16
LANES = 128


def terms_of(x, count):
    terms = []
    for _ in range(count):
        terms.append(x.astype(BF16))
        x = x - terms[-1].astype(F32)
    return terms


def stacked_terms(x):
    return jnp.concatenate(terms_of(x, 2), axis=0)


def summed(stacked):
    rows = stacked.shape[0] // 2
    return stacked[:rows] + stacked[rows:]


def marks(index, count):
    shape = (16, index.shape[1])
    rows = lax.broadcasted_iota(jnp.int32, shape, 0).astype(jnp.int16)
    index = jnp.broadcast_to(index, shape).astype(jnp.int16)
    tiles = [
        jnp.where(rows == index - jnp.int16(start), jnp.ones((), BF16), jnp.zeros((), BF16))
        for start in range(0, count, 16)
    ]
    return jnp.concatenate(tiles, axis=0)


def times(left, right):
    return jnp.dot(left, right, preferred_element_type=F32)


def times_turned(left, right):
    return lax.dot_general(left, right, (((1,), (1,)), ((), ())), preferred_element_type=F32)


def halves(power):
    return power.bit_length() - 1


def looked_up(table, face, at):
    both = summed(times(stacked_terms(table), at))
    return jnp.where(face < table.shape[1], both[:12], both[12:])


def folded(placed, height, capacity, domain):
    group = LANES // capacity
    tile, spot = domain // group, domain % group
    part = lax.broadcasted_iota(jnp.int32, (height, LANES), 1) >> halves(capacity)
    block = None
    for j in range(group):
        piece = placed[j * height : (j + 1) * height, tile * LANES : (tile + 1) * LANES]
        if j != spot:
            piece = pltpu.roll(piece, (j - spot) * capacity % LANES, 1)
        block = piece if block is None else jnp.where(part == j, piece, block)
    return block


def rows_of(ref, start, count):
    if not isinstance(start, int):
        return ref[pl.ds(start, count)]
    first, end = start // 8 * 8, -(-(start + count) // 8) * 8
    return ref[first:end][start - first : start - first + count]


def unfolded(got_ref, block_rows, start, height, capacity):
    group = LANES // capacity
    part = lax.broadcasted_iota(jnp.int32, (height, LANES), 1) >> halves(capacity)
    pieces = []
    for j in range(group):
        tiles = []
        for first in range(0, got_ref.shape[0] // block_rows, group):
            block = None
            for spot in range(group):
                at = (first + spot) * block_rows + start
                piece = rows_of(got_ref, at, height)
                if j != spot:
                    piece = pltpu.roll(piece, (spot - j) * capacity % LANES, 1)
                block = piece if block is None else jnp.where(part == spot, piece, block)
            tiles.append(block)
        pieces.append(jnp.concatenate(tiles, axis=1))
    return jnp.concatenate(pieces, axis=0)


def routed(words, rows, place):
    extra = -(-rows // 16) * 16 - words.shape[0]
    if extra:
        words = jnp.concatenate([words, jnp.zeros((extra, words.shape[1]), F32)], axis=0)
    return summed(times_turned(stacked_terms(words), place))


def weighted_pressure(words, full, remote_rows):
    tail = 5 * full
    normal = words[tail + 5 : tail + 8]
    gap, last = words[4 * full : tail], words[tail + 4 : tail + 5]
    for node in range(4):
        across = sum(
            normal[k : k + 1] * remote_rows[k * 4 + node : k * 4 + node + 1] for k in range(3)
        )
        gap = gap + words[node * full : (node + 1) * full] * across
        last = last + words[tail + node : tail + node + 1] * across
    return jnp.maximum(-gap, 0.0), jnp.maximum(-last, 0.0), normal


def loads_on(shapes, full, tail, pressure, last):
    return [
        jnp.sum(pressure * shapes[i * full : (i + 1) * full], axis=0, keepdims=True)
        + last * shapes[tail + i : tail + i + 1]
        for i in range(4)
    ]


def forces_of(normal, loads):
    loads = jnp.concatenate(loads, axis=0)
    return jnp.concatenate([normal[k : k + 1] * loads for k in range(3)], axis=0)


def place_in_group(domain, domains):
    return {0: domains - 1, domains - 1: 0}.get(domain, domain)


def first_kernel(capacity, heights, *refs):
    (
        nodes_hbm, disp_hbm, mortar_hbm, rank_hbm, face_hbm, count_hbm, weight_hbm, normal_hbm,
        gap_hbm, shape_hbm, modulus_hbm,
        sent_ref, rows_ref, words_ref, turned_ref, mortar_ref, rank_ref, face_ref, nodes,
        inner_ref, outer_ref,
        disp, count, weight, normal_v, gap_v, shape, modulus, blocks, sems, copy_sem,
    ) = refs
    components, layers, rows_y, cols_x = disp.shape
    block_rows = 12 * nodes.shape[1] // LANES + sum(heights)
    sources = (
        disp_hbm, shape_hbm, nodes_hbm, gap_hbm, weight_hbm, normal_hbm, rank_hbm, face_hbm,
        mortar_hbm, count_hbm, modulus_hbm.at[disp.shape[1] - 1],
    )
    targets = (
        disp, shape, nodes, gap_v, weight, normal_v, rank_ref, face_ref, mortar_ref, count, modulus,
    )
    brought = [
        pltpu.make_async_copy(source, target, sems.at[i])
        for i, (source, target) in enumerate(zip(sources, targets))
    ]
    for copy in brought:
        copy.start()

    domains = sent_ref.shape[0] // block_rows
    pair_total = rank_ref.shape[1]
    face_count = nodes.shape[1]
    strips = layers * rows_y
    for copy in brought[:-1]:
        copy.wait()
    rank, face, mortar = rank_ref[...], face_ref[...], mortar_ref[...]
    normal = normal_v[...]
    gap = gap_v[...]

    chosen = lax.broadcasted_iota(jnp.int32, (domains, pair_total), 0) == rank
    before = lax.broadcasted_iota(jnp.int32, (pair_total, pair_total), 0) < lax.broadcasted_iota(
        jnp.int32, (pair_total, pair_total), 1
    )
    earlier = times(chosen.astype(F32).astype(BF16), before.astype(F32).astype(BF16))
    slot = jnp.sum(jnp.where(chosen, earlier, 0.0), axis=0, keepdims=True).astype(jnp.int32)
    place = marks(rank * capacity + slot, domains * capacity)

    parts = stacked_terms(disp[...].reshape(components * strips, cols_x))
    numbers = lax.broadcasted_iota(jnp.int32, (strips, face_count), 0)
    folds = face_count // cols_x
    for corner in range(4):
        index = nodes[corner : corner + 1, :]
        strip = index >> halves(cols_x)
        found = summed(times(parts, marks(index & (cols_x - 1), cols_x)))
        found = found.reshape(components, strips, face_count)
        values = jnp.sum(jnp.where((numbers == strip)[None], found, 0.0), axis=1)
        for fold in range(folds):
            for k in range(components):
                at = fold * 12 + k * 4 + corner
                rows_ref[at : at + 1, :] = values[k : k + 1, fold * cols_x : (fold + 1) * cols_x]

    points = gap.shape[0]
    full = points // 8 * 8
    live = lax.broadcasted_iota(jnp.int32, (points, pair_total), 0) < count[...]
    root = jnp.where(live, jnp.sqrt(weight[...]), 0.0)
    weighted = [root * shape[:, node] for node in range(4)]
    long_words = jnp.concatenate([x[:full] for x in weighted], axis=0)
    group = LANES // capacity
    placed = routed(long_words, group * heights[0], place)

    rows = rows_ref[...]
    high = rows.shape[0]
    rows_high = high * cols_x // LANES
    halved = jnp.concatenate(
        [rows[:, i * LANES : (i + 1) * LANES] for i in range(cols_x // LANES)], axis=0
    )
    for domain in range(domains):
        at = place_in_group(domain, domains) * block_rows
        blocks[at : at + rows_high] = halved
        at += rows_high
        blocks[at : at + heights[0]] = folded(placed, heights[0], capacity, domain)

    mortar_rows = looked_up(rows, mortar, marks(mortar & (cols_x - 1), cols_x))
    for node in range(4):
        across = sum(
            normal[k : k + 1] * mortar_rows[k * 4 + node : k * 4 + node + 1] for k in range(3)
        )
        gap = gap - shape[:, 4 + node] * across
    gap = root * gap
    short_words = jnp.concatenate(
        [gap[:full]]
        + [x[full:] for x in weighted + [gap]]
        + [normal, face.astype(F32)],
        axis=0,
    )
    placed = routed(short_words, group * heights[1], place)
    for domain in range(domains):
        at = place_in_group(domain, domains) * block_rows + rows_high + heights[0]
        blocks[at : at + heights[1]] = folded(placed, heights[1], capacity, domain)
    sending = pltpu.make_async_copy(blocks.at[: sent_ref.shape[0]], sent_ref, copy_sem)
    sending.start()

    words_ref[: 4 * full] = long_words
    words_ref[4 * full :] = short_words
    for node in range(4):
        turned = root * shape[:, 4 + node]
        turned_ref[node * full : (node + 1) * full] = turned[:full]
        turned_ref[4 * full + node : 4 * full + node + 1] = turned[full:]

    brought[-1].wait()
    sub = lax.axis_index("sub")
    for target, layer in ((inner_ref, (1 - sub) * (layers - 1)), (outer_ref, sub * (layers - 1))):
        for k in range(components):
            target[k] = disp[k, layer]
        target[components] = modulus[...]
    sending.wait()


def last_kernel(
    capacity, heights, got_ref, rows_ref, words_ref, turned_ref, mortar_ref, rank_ref, face_ref, nodes_ref,
    inverse_ref, internal_ref, blocks_ref, own_ref, halo_ref, out_hbm, out_ref, sems,
):
    block_rows = 12 * nodes_ref.shape[1] // LANES + sum(heights)
    domains = got_ref.shape[0] // block_rows
    components, layers, rows_y, cols_x = out_ref.shape
    strips = layers * rows_y
    face_count = nodes_ref.shape[1]
    pair_total = rank_ref.shape[1]
    high = rows_ref.shape[0]
    rows_high = high * cols_x // LANES
    full = (turned_ref.shape[0] - 8) // 4
    own_rows = rows_ref[...]

    rank, face = rank_ref[...], face_ref[...]
    end = domains - 1
    place = jnp.where(rank == 0, end, jnp.where(rank == end, 0, rank))
    at = marks(face & (cols_x - 1), cols_x)
    step = min(domains, 8)

    def add_step(turn, total):
        halves_of = [
            jnp.concatenate(
                [
                    rows_of(got_ref, (turn * step + i) * block_rows + j * high, high)
                    for j in range(cols_x // LANES)
                ],
                axis=1,
            )
            for i in range(step)
        ]
        block = jnp.concatenate(halves_of, axis=0)
        found = summed(times(stacked_terms(block), at)).reshape(step, high, pair_total)
        for i in range(step):
            total = total + jnp.where(place == turn * step + i, found[i], 0.0)
        return total

    both = jnp.zeros((high, pair_total), F32)
    if domains == step:
        both = add_step(0, both)
    else:
        both = lax.fori_loop(0, domains // step, add_step, both)
    remote_rows = jnp.where(face < cols_x, both[:12], both[12:])
    pressure, last, normal = weighted_pressure(words_ref[...], full, remote_rows)
    turned = turned_ref[...]
    mortar_forces = forces_of(-normal, loads_on(turned, full, 4 * full, pressure, last))

    words = jnp.concatenate(
        [
            unfolded(got_ref, block_rows, rows_high, heights[0], capacity)[: 4 * full],
            unfolded(got_ref, block_rows, rows_high + heights[0], heights[1], capacity)[: full + 9],
        ],
        axis=0,
    )
    asked = words[5 * full + 8 : 5 * full + 9].astype(jnp.int32)
    asked_at = marks(asked & (cols_x - 1), cols_x)
    remote_rows = looked_up(own_rows, asked, asked_at)
    pressure, last, normal = weighted_pressure(words, full, remote_rows)
    remote_forces = forces_of(normal, loads_on(words, full, 5 * full, pressure, last))

    forces = jnp.concatenate([mortar_forces, remote_forces], axis=1)
    into = jnp.concatenate([mortar_ref[...], asked], axis=1)
    at = jnp.concatenate([marks(mortar_ref[...] & (cols_x - 1), cols_x), asked_at], axis=1)
    forces = jnp.concatenate(
        [jnp.where(into < cols_x, forces, 0.0), jnp.where(into < cols_x, 0.0, forces)], axis=0
    )
    forces = summed(times_turned(stacked_terms(forces), at))
    forces = jnp.concatenate([forces[:12], forces[12:]], axis=1)
    parts = [term.astype(F32) for term in terms_of(forces, 2)]
    indices = [nodes_ref[corner : corner + 1, :] for corner in range(4)]
    along_x = [marks(index & (cols_x - 1), cols_x) for index in indices]
    strip = [marks(index >> halves(cols_x), strips) for index in indices]
    upward = lax.axis_index("sub") == 1
    edge = edge_part(upward, own_ref, halo_ref, blocks_ref)
    at_edge = jnp.where(upward, layers - 1, 0)
    copies = []
    for layer in range(layers):
        total = jnp.zeros((2 * components * rows_y, cols_x), F32)
        for corner in range(4):
            here = strip[corner][layer * rows_y : (layer + 1) * rows_y]
            spread = []
            for part in parts:
                for k in range(components):
                    at = k * 4 + corner
                    row = jnp.broadcast_to(part[at : at + 1], (16, face_count)).astype(BF16)
                    spread.append(here * jnp.concatenate([row] * (rows_y // 16), axis=0))
            total = total + times_turned(jnp.concatenate(spread, axis=0), along_x[corner])
        contact = summed(total).reshape(components, rows_y, cols_x)
        for k in range(components):
            nodal = internal_ref[k, layer] + jnp.where(at_edge == layer, edge[k], 0.0)
            out_ref[k, layer] = (nodal + contact[k]) * inverse_ref[layer]
        copies.append(
            pltpu.make_async_copy(out_ref.at[:, layer], out_hbm.at[:, layer], sems.at[layer])
        )
        copies[-1].start()
    for copy in copies:
        copy.wait()


GROUP = 8


def shifted(layer):
    views = []
    for part in layer:
        rows_y, cols_x = part.shape
        for moved in (part, pltpu.roll(part, rows_y - 1, 0)):
            views += [moved, pltpu.roll(moved, cols_x - 1, 1)]
    return views


def element_forces(matrices, low, high, modulus):
    rows_y, cols_x = modulus.shape
    inside = (lax.broadcasted_iota(jnp.int32, (rows_y, cols_x), 0) < rows_y - 1) & (
        lax.broadcasted_iota(jnp.int32, (rows_y, cols_x), 1) < cols_x - 1
    )
    scale = jnp.where(inside, modulus, 0.0)
    views = shifted(low) + shifted(high)
    both = jnp.concatenate(matrices, axis=0)
    count = both.shape[0] // 2
    strips = []
    for y in range(0, rows_y, GROUP):
        leading, second = terms_of(jnp.concatenate([view[y : y + GROUP] for view in views], axis=0), 2)
        found = times(both, leading)
        force = found[:count] + (found[count:] + times(matrices[0], second))
        strips.append(force.reshape(-1, GROUP, cols_x) * scale[y : y + GROUP][None])
    return jnp.concatenate(strips, axis=1)


def on_nodes(forces):
    sums = []
    for k in range(forces.shape[0] // 4):
        straight, crossed = [
            forces[k * 4 + c] + pltpu.roll(forces[k * 4 + 2 + c], 1, 0) for c in range(2)
        ]
        sums.append(-(straight + pltpu.roll(crossed, 1, 1)))
    return sums


def edge_part(upward, own_ref, halo_ref, blocks_ref):
    components = own_ref.shape[0] - 1
    size = blocks_ref.shape[1]
    rows = size // 2
    start = jnp.where(upward, 0, rows)
    matrices = [
        blocks_ref[pl.ds(pl.multiple_of(term * size + start, 16), rows)] for term in range(2)
    ]
    low = [jnp.where(upward, own_ref[k], halo_ref[k]) for k in range(components + 1)]
    high = [jnp.where(upward, halo_ref[k], own_ref[k]) for k in range(components)]
    return on_nodes(element_forces(matrices, low[:components], high, low[components]))


def internal_kernel(
    disp_ref, modulus_ref, stiffness_ref, mass_ref, own_ref, halo_ref, out_ref, blocks_ref, inverse_ref
):
    inverse_ref[...] = 1.0 / mass_ref[...]
    components, layers, rows_y, cols_x = disp_ref.shape
    dofs = 8 * components
    half = dofs // 2
    size = dofs * GROUP

    row = lax.broadcasted_iota(jnp.int32, (size, dofs), 0) >> halves(GROUP)
    upper = (row >= half).astype(jnp.int32)
    inner = row - half * upper
    dof = (inner >> 2) * 8 + upper * 4 + (inner & 3)
    pick = (dof == lax.broadcasted_iota(jnp.int32, (size, dofs), 1)).astype(F32).astype(BF16)
    diagonal = (lax.broadcasted_iota(jnp.int32, (size, size), 0) & (GROUP - 1)) == (
        lax.broadcasted_iota(jnp.int32, (size, size), 1) & (GROUP - 1)
    )
    for i, term in enumerate(terms_of(stiffness_ref[...], 2)):
        wide = times_turned(times(pick, term).astype(BF16), pick)
        blocks_ref[i * size : (i + 1) * size] = jnp.where(diagonal, wide, 0.0).astype(BF16)

    blocks = [blocks_ref[i * size : (i + 1) * size] for i in range(2)]
    sums = [[0.0] * components for _ in range(layers)]
    for e in range(layers - 1):
        pair = [[disp_ref[k, e + a] for k in range(components)] for a in range(2)]
        forces = element_forces(blocks, pair[0], pair[1], modulus_ref[e])
        for a in range(2):
            part = on_nodes(forces[a * half : (a + 1) * half])
            sums[e + a] = [x + y for x, y in zip(sums[e + a], part)]
    upward = lax.axis_index("sub") == 0
    edge = edge_part(upward, own_ref, halo_ref, blocks_ref)
    at = jnp.where(upward, layers - 1, 0)
    for layer in range(layers):
        for k in range(components):
            out_ref[k, layer] = sums[layer][k] + jnp.where(at == layer, edge[k], 0.0)


def on_core(kernel, outs, flops, moved, **more):
    return pl.pallas_call(
        kernel,
        out_shape=outs,
        compiler_params=pltpu.CompilerParams(vmem_limit_bytes=48 * 1024 * 1024),
        cost_estimate=pl.CostEstimate(flops=flops, bytes_accessed=moved, transcendentals=0),
        **more,
    )


def swapped(block, axis, first):
    size = lax.axis_size(axis)
    route = []
    for i in range(first, size - 1, 2):
        route += [(i, i + 1), (i + 1, i)]
    return lax.ppermute(block, axis, route)


def shards(
    displacement,
    modulus,
    node_mass,
    stiffness,
    face_nodes,
    pair_mortar,
    pair_rank,
    pair_face,
    pair_count,
    pair_shape,
    pair_weight,
    pair_gap,
    pair_normal,
):
    components, layers, rows_y, cols_x = displacement.shape
    face_count = face_nodes.shape[1]
    pair_total = pair_mortar.shape[0]
    domains = lax.axis_size("dom")
    capacity = max(2, 2 * pair_total // domains)

    points = pair_weight.shape[0]
    full = points // 8 * 8
    group = LANES // capacity
    word_rows = 5 * full + 9
    heights = tuple(-(-rows // group) for rows in (4 * full, full + 9))
    rows_high = 12 * face_count // LANES
    line = (1, pair_total)

    def first(*refs):
        first_kernel(capacity, heights, *refs)

    def last(*refs):
        last_kernel(capacity, heights, *refs)

    def shaped(shape, dtype=F32):
        return jax.ShapeDtypeStruct(shape, dtype)

    arrays = [
        face_nodes,
        displacement,
        pair_mortar.reshape(line),
        pair_rank.reshape(line),
        pair_face.reshape(line),
        pair_count.reshape(line),
        pair_weight,
        pair_normal,
        pair_gap,
        jnp.swapaxes(pair_shape, 0, 1),
        modulus,
    ]
    edge = shaped((components + 1, rows_y, cols_x))
    in_hbm = pl.BlockSpec(memory_space=pltpu.HBM)
    in_vmem = pl.BlockSpec(memory_space=pltpu.VMEM)
    kept = [displacement, *arrays[5:-1], shaped((rows_y, cols_x))]
    sent, rows, words, turned, mortar, rank, face, nodes, inner, outer = on_core(
        first,
        [
            shaped((domains * (rows_high + sum(heights)), LANES)),
            shaped((12 * face_count // cols_x, cols_x)),
            shaped((word_rows, pair_total)),
            shaped((4 * full + 8, pair_total)),
            shaped(line, jnp.int32),
            shaped(line, jnp.int32),
            shaped(line, jnp.int32),
            shaped(face_nodes.shape, jnp.int32),
            edge,
            edge,
        ],
        900_000_000,
        1_500_000,
        in_specs=[in_hbm] * len(arrays),
        out_specs=[in_hbm] + [in_vmem] * 9,
        scratch_shapes=[pltpu.VMEM(x.shape, x.dtype) for x in kept]
        + [
            pltpu.VMEM((domains * (rows_high + sum(heights)) + 8, LANES), F32),
            pltpu.SemaphoreType.DMA((len(arrays),)),
            pltpu.SemaphoreType.DMA(()),
        ],
    )(*[pltpu.with_memory_space_constraint(x, pltpu.HBM) for x in arrays])
    order = [place_in_group(domain, domains) for domain in range(domains)]
    got = lax.all_to_all(
        sent.reshape(domains, 1, -1),
        "dom",
        split_axis=0,
        concat_axis=0,
        axis_index_groups=[order],
        tiled=True,
    ).reshape(sent.shape)
    inner_halo = swapped(inner, ("dom", "sub"), 0)
    outer_halo = swapped(outer, ("dom", "sub"), 1)
    size = 8 * components * GROUP
    internal, blocks, inverse = on_core(
        internal_kernel,
        [shaped(displacement.shape), shaped((2 * size, size), BF16), shaped(node_mass.shape)],
        1_000_000_000,
        700_000,
    )(displacement, modulus, stiffness, node_mass, inner, inner_halo)
    return on_core(
        last,
        shaped(displacement.shape),
        1_000_000_000,
        1_500_000,
        out_specs=in_hbm,
        scratch_shapes=[
            pltpu.VMEM(displacement.shape, F32),
            pltpu.SemaphoreType.DMA((layers,)),
        ],
    )(
        got, rows, words, turned, mortar, rank, face, nodes, inverse, internal, blocks, outer,
        outer_halo,
    )


def solution(mesh):
    placed = (
        P(None, ("runs", "dom", "sub"), None, None),
        P(("runs", "dom", "sub"), None, None),
        P(("runs", "dom", "sub"), None, None),
        P(),
        P(None, ("runs", "dom", "sub")),
        P(("runs", "dom", "sub")),
        P(("runs", "dom", "sub"), None),
        P(("runs", "dom", "sub")),
        P(("runs", "dom", "sub")),
        P(None, None, ("runs", "dom", "sub")),
        P(None, ("runs", "dom", "sub")),
        P(None, ("runs", "dom", "sub")),
        P(None, ("runs", "dom", "sub")),
    )
    return jax.shard_map(
        shards,
        mesh=mesh,
        in_specs=placed,
        out_specs=P(None, ("runs", "dom", "sub"), None, None),
        check_vma=False,
    )
```
